32 devices in a mesh: grp: 2 (over x), row: 16 (over z, y, core).
Axes of the slice: x: 2, y: 2, z: 4, core: 2. Of those that a mesh axis runs over, the one named last changes fastest.
Arguments:
- activations: bfloat16 [9216, 8192], P(('grp', 'row')), parts along dimension 0, may hold values from -6 to 6
- gradients: bfloat16 [9216, 14336], P(('grp', 'row')), parts along dimension 0, may hold values from -6 to 6
- basis_a: bfloat16 [16384, 512], P(('grp', 'row')), parts along dimension 0, may hold values from -0.0625 to 0.0625
- basis_g: bfloat16 [28672, 512], P(('grp', 'row')), parts along dimension 0, may hold values from -0.0625 to 0.0625
- token_index: int32 [9216], P(('grp', 'row')), parts along dimension 0, may hold values from 0 to 4607, each once
- seq_lengths: int32 [8], P('grp'), parts along dimension 0, may hold values from 1 to 2304, 4608 in all
Outputs:
- eigenvalues: float32 [1024, 512], P(('grp', 'row')), parts along dimension 0
The draws below stay inside these ranges and needn't reach their ends.
There are 2 independent parts, one for each index of `grp`. The reference program is written for one: setup_inputs(seed, part) draws one part's arguments, and reference() takes and returns one part's arrays. A program takes and returns all parts, laid end to end along the dimension named above; each array names one. Nothing has to cross between parts.
Inputs may be any that keep to these rules, and one draw needn't show every extreme that they name: `token_index`: each of 0 to 4607 appears once. `seq_lengths`: the lengths sum to 4608; the longest is exactly 2304.
All inputs are finite; a program needn't handle non-finite values.
Results may differ from the reference program's by a relative error of at most 0.0037.
Values may be sent and summed in bfloat16 or wider, within the bound.
No kernel may reach another device: no remote copies, remote signals or barrier semaphores. Data moves between devices by JAX's collectives and lax.ppermute only.
A program may use at most 128 MiB of HBM per device.

```python
import math
import jax
import jax.numpy as jnp
import numpy as np
from jax import lax

D = 8192
FF = 14336
KA = 512
KG = 512
SEQS = 4
TOKENS = 4608


def with_spikes(array, stream_key, source, target, blocks, factor):
    def block_of(dim):
        return (jnp.arange(array.shape[dim]) // (array.shape[dim] // blocks)).reshape((-1,) + (1,) * (array.ndim - 1 - dim))

    one_side = jax.random.permutation(stream_key, blocks)[block_of(target)]
    far = (block_of(target) + blocks // 2) % blocks
    return jnp.where((block_of(source) == one_side) | (block_of(source) == far), factor * array, array)


def level_of(key, extent, pieces, low, top_value):
    level = 1.0
    for position, blocks in pieces:
        heights = jax.random.uniform(jax.random.fold_in(jax.random.fold_in(key, 6), position), (blocks,), jnp.float32, low / len(pieces), top_value / len(pieces))
        level = level * jnp.repeat(jnp.exp(heights), extent[position] // blocks).reshape((-1,) + (1,) * (len(extent) - 1 - position))
    return level


def length_profile(number_of, total, bound, lean):
    portions = [(1 << 20) // math.isqrt(rank ** lean) + 1 for rank in range(2, number_of + 1)]
    rest, given = total - bound - (number_of - 1), [1] * (number_of - 1)
    while rest > 0:
        free = [i for i in range(number_of - 1) if given[i] < bound]
        whole, budget = sum([portions[i] for i in free]), rest
        for i in free:
            more = min(bound - given[i], max(1, budget * portions[i] // whole), rest)
            given[i] = given[i] + more
            rest = rest - more
    return np.array([bound] + given)


def ragged_sizes(own_key, amount, total, most, slope):
    if amount == 2:
        one = jax.random.randint(own_key, (), max(1, total - most), min(most, total - 1) + 1)
        return jnp.stack([one, total - one])
    tallies = jnp.asarray(length_profile(amount, total, most, slope), jnp.int32)
    twos = (amount - 1) // 2
    source_of, receiver = tallies[1:1 + 2 * twos:2], tallies[2:2 + 2 * twos:2]
    slack = jnp.minimum(source_of - 1, most - receiver)
    shifted = jax.random.randint(jax.random.fold_in(own_key, 1), (twos,), 0, 1 << 20) % (slack + 1)
    tallies = tallies.at[1:1 + 2 * twos:2].set(source_of - shifted).at[2:2 + 2 * twos:2].set(receiver + shifted)
    return tallies[jax.random.permutation(jax.random.fold_in(own_key, 2), amount)]


def normal_values(own_key, shape, spread, reach, cuts=(), held_as=jnp.bfloat16):
    drawn = jax.random.normal(own_key, shape, jnp.float32) * spread
    if len(cuts) > 0:
        drawn = level_of(own_key, shape, cuts, -0.22, 0.18) * drawn
    return jnp.clip(drawn, min=-reach, max=reach).astype(held_as)


def bell_draw_with(rng, shape, deviation, bound, cuts, heavy, kind=jnp.bfloat16):
    drawn = deviation * jax.random.normal(rng, shape, jnp.float32)
    if cuts:
        drawn = drawn * level_of(rng, shape, cuts, -0.22, 0.18)
    return jnp.clip(with_spikes(drawn, jax.random.fold_in(rng, 3), *heavy), -bound, bound).astype(kind)


def setup_inputs(seed: int = 0, part: int = 0) -> dict:
    key_of = jax.random.split(jax.random.key(seed), 7)
    part_splits = jax.random.split(jax.random.fold_in(key_of[6], part), 7)
    activations = normal_values(part_splits[0], (TOKENS, D), 1.0, 6.0, ((0, 16),))
    gradients = normal_values(part_splits[1], (TOKENS, FF), 1.0, 6.0, ((0, 16),))
    basis_a = normal_values(part_splits[2], (D, KA), D ** -0.5, 0.0625, ((0, 16),))
    basis_g = bell_draw_with(part_splits[3], (FF, KG), FF ** -0.5, 0.0625, ((0, 16),), (0, 1, 16, 2.0))
    token_index = jax.random.permutation(part_splits[4], TOKENS).astype(jnp.int32)
    seq_lengths = ragged_sizes(part_splits[5], SEQS, TOKENS, TOKENS // 2, 0).astype(jnp.int32)
    return {"activations": activations, "gradients": gradients, "basis_a": basis_a, "basis_g": basis_g, "token_index": token_index, "seq_lengths": seq_lengths}


def reference(activations, gradients, basis_a, basis_g, token_index, seq_lengths):
    rot_a = jnp.dot(activations, basis_a, preferred_element_type=jnp.float32).astype(jnp.bfloat16)
    rot_g = jnp.dot(gradients, basis_g, preferred_element_type=jnp.float32).astype(jnp.bfloat16)
    ends = jnp.cumsum(seq_lengths).astype(jnp.int32)
    seq_ids = jnp.sum((token_index[:, None] >= ends[None, :]).astype(jnp.int32), axis=1).astype(jnp.int32)
    member = (seq_ids[:, None] == jnp.arange(SEQS, dtype=jnp.int32)[None, :]).astype(jnp.bfloat16)
    masked = (member[:, :, None] * rot_a[:, None, :]).reshape(TOKENS, SEQS * KA)
    per_seq = lax.dot_general(rot_g, masked, (((0,), (0,)), ((), ())), preferred_element_type=jnp.float32)
    per_seq = per_seq.reshape(KG, SEQS, KA)
    total = jnp.sum(seq_lengths).astype(jnp.float32)
    return jnp.sum(per_seq * per_seq, axis=1) / total
```

```python
import functools

import jax
import jax.numpy as jnp
from jax import lax
from jax.experimental import pallas as pl
from jax.experimental.pallas import tpu as pltpu
from jax.sharding import PartitionSpec as P

CORES = 2
VMEM_LIMIT = 56 * 1024 * 1024


def params():
    return pltpu.CompilerParams(vmem_limit_bytes=VMEM_LIMIT)


def whole(shape):
    return pl.BlockSpec(shape, lambda *_: (0,) * len(shape))


class Layout:
    def __init__(self, mesh):
        self.chips = mesh.shape["row"] // CORES
        self.ny = max(1, 4 // mesh.shape["grp"])
        if self.chips % self.ny:
            self.ny = 1
        self.nz = self.chips // self.ny

    def device(self, z, y, core):
        return ((z % self.nz) * self.ny + y % self.ny) * CORES + core

    def everyone(self):
        return [(z, y, c) for z in range(self.nz) for y in range(self.ny) for c in range(CORES)]

    def along_z(self, x, hops):
        pairs = [(self.device(z, y, c), self.device(z + hops, y, c)) for z, y, c in self.everyone()]
        return lax.ppermute(x, "row", pairs)

    def along_y(self, x, hops=1):
        pairs = [(self.device(z, y, c), self.device(z, y + hops, c)) for z, y, c in self.everyone()]
        return lax.ppermute(x, "row", pairs)

    def to_sibling(self, x):
        pairs = [(self.device(z, y, c), self.device(z, y, 1 - c)) for z, y, c in self.everyone()]
        return lax.ppermute(x, "row", pairs)


def sibling_columns(act, core, chips):
    rows, depth = act.shape
    kc = depth // (chips * CORES)
    if kc % 128:
        return split_columns(act, 1 - core[0], chips)

    def kernel(core_ref, x_ref, o_ref):
        o_ref[...] = x_ref[...]

    return pl.pallas_call(
        kernel,
        grid_spec=pltpu.PrefetchScalarGridSpec(
            num_scalar_prefetch=1,
            grid=(chips,),
            in_specs=[pl.BlockSpec((rows, kc), lambda i, core: (0, CORES * i + 1 - core[0]))],
            out_specs=pl.BlockSpec((None, rows, kc), lambda i, core: (i, 0, 0)),
        ),
        out_shape=jax.ShapeDtypeStruct((chips, rows, kc), act.dtype),
        cost_estimate=pl.CostEstimate(flops=0, bytes_accessed=2 * rows * depth, transcendentals=0),
        compiler_params=params(),
        name="sibling_columns",
    )(core, act)


def split_columns(act, core, chips):
    rows, depth = act.shape
    kc = depth // (chips * CORES)
    mine = lax.dynamic_index_in_dim(act.reshape(rows, chips, CORES, kc), core, 2, keepdims=False)
    return mine.transpose(1, 0, 2)


def gather_columns(layout, piece, y_first):
    nz, ny = layout.nz, layout.ny
    by_z = {0: piece}
    for d in range(1, nz // 2 + 1):
        by_z[d] = layout.along_z(by_z[d - 1], 1)
    for d in range(nz - 1, nz // 2, -1):
        by_z[d] = layout.along_z(by_z[(d + 1) % nz], -1)
    found = [(by_z[d], d, 0) for d in range(nz)]
    for h in range(1, ny):
        crossed = {}
        for d in range(nz):
            if y_first and d == nz // 2 and d > 0:
                crossed[d] = layout.along_z(crossed[d - 1], 1)
            else:
                crossed[d] = layout.along_y(by_z[d], h)
        found += [(crossed[d], d, h) for d in range(nz)]
    return found


def partial_rotation(act, sib, found, origin, core):
    rows = act.shape[0]
    kc, width = found[0][0].shape
    count = len(found)
    if kc % 128:
        act = split_columns(act, core[0], count)
        act_spec = pl.BlockSpec((None, rows, kc), lambda i, origin, core: (origin[i], 0, 0))
    else:
        act_spec = pl.BlockSpec(
            (rows, kc), lambda i, origin, core: (0, CORES * origin[i] + core[0])
        )

    def kernel(origin_ref, core_ref, act_ref, sib_ref, *refs):
        chunk_refs, o_ref = refs[:count], refs[count]
        step = pl.program_id(0)
        mine = pl.multiple_of(core_ref[0] * rows, 8)
        other = pl.multiple_of((1 - core_ref[0]) * rows, 8)

        @pl.when(step == 0)
        def _():
            o_ref[...] = jnp.zeros_like(o_ref)

        for i in range(count):
            @pl.when(step == i)
            def _(i=i):
                block = chunk_refs[i][...]
                o_ref[pl.ds(mine, rows), :] += jnp.dot(
                    act_ref[...], block, preferred_element_type=jnp.float32
                )
                o_ref[pl.ds(other, rows), :] += jnp.dot(
                    sib_ref[...], block, preferred_element_type=jnp.float32
                )

    return pl.pallas_call(
        kernel,
        grid_spec=pltpu.PrefetchScalarGridSpec(
            num_scalar_prefetch=2,
            grid=(count,),
            in_specs=[
                act_spec,
                pl.BlockSpec((None, rows, kc), lambda i, origin, core: (origin[i], 0, 0)),
            ]
            + [whole((kc, width))] * count,
            out_specs=whole((CORES * rows, width)),
        ),
        out_shape=jax.ShapeDtypeStruct((CORES * rows, width), jnp.float32),
        cost_estimate=pl.CostEstimate(
            flops=4 * rows * kc * count * width,
            bytes_accessed=2 * count * kc * (2 * rows + width) + 8 * rows * width,
            transcendentals=0,
        ),
        compiler_params=params(),
        name="partial_rotation",
    )(origin, core, act, sib, *[block for block, _, _ in found])


def owned_gradients(layout, mine, other, place, owned):
    nz, ny = layout.nz, layout.ny
    pieces = len(mine)
    tokens, width = mine[0].shape
    kept = nz * ny * owned

    def kernel(place_ref, *refs):
        mine_refs, other_refs, o_ref = refs[:pieces], refs[pieces:2 * pieces], refs[2 * pieces]
        z, y, core = place_ref[0], place_ref[1], place_ref[2]
        slot = lax.broadcasted_iota(jnp.int32, (kept, width), 0)
        column = lax.broadcasted_iota(jnp.int32, (kept, width), 1)
        to_y = lax.rem(y + 1 + slot // (nz * owned), ny)
        to_z = lax.rem(z + lax.rem(slot // owned, nz), nz)
        wanted = ((to_z * ny + to_y) * CORES + core) * owned + lax.rem(slot, owned)
        total = jnp.zeros((kept, tokens), jnp.float32)
        for i in range(pieces):
            rotated = (mine_refs[i][...] + other_refs[i][...]).astype(jnp.bfloat16)
            pick = jnp.where(wanted == column + i * width, 1.0, 0.0).astype(jnp.bfloat16)
            total += lax.dot_general(
                pick, rotated, (((1,), (1,)), ((), ())), preferred_element_type=jnp.float32
            )
        o_ref[...] = total.astype(jnp.bfloat16)

    return pl.pallas_call(
        kernel,
        grid_spec=pltpu.PrefetchScalarGridSpec(
            num_scalar_prefetch=1,
            grid=(1,),
            in_specs=[whole((tokens, width))] * (2 * pieces),
            out_specs=whole((kept, tokens)),
        ),
        out_shape=jax.ShapeDtypeStruct((kept, tokens), jnp.bfloat16),
        cost_estimate=pl.CostEstimate(
            flops=2 * kept * pieces * width * tokens,
            bytes_accessed=8 * pieces * tokens * width + 2 * kept * tokens,
            transcendentals=0,
        ),
        compiler_params=params(),
        name="owned_gradients",
    )(place, *mine, *other)


def chip_sums(layout, grads, mine, other, positions, lengths, owned):
    tokens, width = mine.shape
    seqs = lengths.shape[0]
    kept = grads.shape[0]
    stay = layout.nz * owned
    sent = kept - stay

    def kernel(lengths_ref, grads_ref, mine_ref, other_ref, positions_ref, *refs):
        rotated = mine_ref[...] + other_ref[...]
        position = positions_ref[...]
        begin = jnp.int32(0)
        parts = []
        for s in range(seqs):
            end = begin + lengths_ref[s]
            inside = (position >= begin) & (position < end)
            parts.append(jnp.where(inside, rotated, 0.0).astype(jnp.bfloat16))
            begin = end
        for s in range(seqs):
            sums = jnp.dot(grads_ref[...], parts[s], preferred_element_type=jnp.float32)
            at = pl.ds(s * width, width)
            if sent:
                refs[1][:, at] = sums[:sent].astype(jnp.bfloat16)
            refs[0][:, at] = sums[sent:]

    shapes = [jax.ShapeDtypeStruct((stay, seqs * width), jnp.float32)]
    if sent:
        shapes.append(jax.ShapeDtypeStruct((sent, seqs * width), jnp.bfloat16))
    return pl.pallas_call(
        kernel,
        grid_spec=pltpu.PrefetchScalarGridSpec(
            num_scalar_prefetch=1,
            grid=(1,),
            in_specs=[
                whole((kept, tokens)),
                whole((tokens, width)),
                whole((tokens, width)),
                whole((tokens, 1)),
            ],
            out_specs=[whole(s.shape) for s in shapes],
        ),
        out_shape=shapes,
        cost_estimate=pl.CostEstimate(
            flops=2 * kept * tokens * seqs * width,
            bytes_accessed=8 * tokens * width + 6 * kept * seqs * width,
            transcendentals=0,
        ),
        compiler_params=params(),
        name="chip_sums",
    )(lengths, grads, mine, other, positions)


def pair_sums(layout, stay, crossed, owned):
    nz = layout.nz
    width = stay.shape[1]

    def kernel(*refs):
        total = refs[0][...]
        for i in range(len(crossed)):
            total += refs[1 + i][...].astype(jnp.float32)
        outs = refs[1 + len(crossed):]
        outs[0][...] = total[:owned]
        for d in range(1, nz):
            outs[d][...] = total[d * owned:(d + 1) * owned].astype(jnp.bfloat16)

    shapes = [jax.ShapeDtypeStruct((owned, width), jnp.float32)]
    shapes += [jax.ShapeDtypeStruct((owned, width), jnp.bfloat16)] * (nz - 1)
    return pl.pallas_call(
        kernel,
        grid=(1,),
        in_specs=[whole(stay.shape)] + [whole(c.shape) for c in crossed],
        out_specs=[whole(s.shape) for s in shapes],
        out_shape=shapes,
        cost_estimate=pl.CostEstimate(
            flops=stay.size, bytes_accessed=8 * stay.size, transcendentals=0
        ),
        compiler_params=params(),
        name="pair_sums",
    )(stay, *crossed)


def squares(groups, lengths, owned):
    seqs = lengths.shape[0]
    count = len(groups[0])
    width = groups[0][0].shape[1] // seqs

    def kernel(lengths_ref, *refs):
        o_ref = refs[-1]
        total = lengths_ref[0]
        for s in range(1, seqs):
            total = total + lengths_ref[s]
        over = jnp.full((owned, width), total, jnp.int32).astype(jnp.float32)
        for g in range(len(groups)):
            sums = refs[g * count][...]
            for i in range(1, count):
                sums = sums + refs[g * count + i][...].astype(jnp.float32)
            sums = sums * sums
            acc = sums[:, :width]
            for s in range(1, seqs):
                acc = acc + sums[:, s * width:(s + 1) * width]
            o_ref[:, pl.ds(g * width, width)] = acc / over

    flat = [x for group in groups for x in group]
    return pl.pallas_call(
        kernel,
        grid_spec=pltpu.PrefetchScalarGridSpec(
            num_scalar_prefetch=1,
            grid=(1,),
            in_specs=[whole(x.shape) for x in flat],
            out_specs=whole((owned, len(groups) * width)),
        ),
        out_shape=jax.ShapeDtypeStruct((owned, len(groups) * width), jnp.float32),
        cost_estimate=pl.CostEstimate(
            flops=4 * len(flat) * flat[0].size,
            bytes_accessed=4 * len(flat) * flat[0].size,
            transcendentals=0,
        ),
        compiler_params=params(),
        name="squares",
    )(lengths, *flat)


def shards(layout, activations, gradients, basis_a, basis_g, token_index, seq_lengths):
    nz, ny, chips = layout.nz, layout.ny, layout.chips
    rows = activations.shape[0]
    owned = basis_g.shape[1] // (chips * CORES)
    me = lax.axis_index("row")
    core = lax.rem(me, CORES)
    y = lax.rem(me // CORES, ny)
    z = me // (CORES * ny)
    place = jnp.stack([z, y, core]).astype(jnp.int32)
    core = core.reshape(1).astype(jnp.int32)

    parts_g, parts_a = 2, 2
    wide_g, wide_a = basis_g.shape[1] // parts_g, basis_a.shape[1] // parts_a
    found_g = [
        gather_columns(layout, basis_g[:, i * wide_g:(i + 1) * wide_g], i % 2 == 0)
        for i in range(parts_g)
    ]
    found_a = [
        gather_columns(layout, basis_a[:, i * wide_a:(i + 1) * wide_a], i % 2 == 0)
        for i in range(parts_a)
    ]
    origin = jnp.stack(
        [lax.rem(z - d + nz, nz) * ny + lax.rem(y - h + ny, ny) for _, d, h in found_g[0]]
    ).astype(jnp.int32)

    sib_g = layout.to_sibling(sibling_columns(gradients, core, chips))
    sib_a = layout.to_sibling(sibling_columns(activations, core, chips))
    sib_index = layout.to_sibling(token_index)
    first = core[0] == 0
    positions = jnp.concatenate(
        [jnp.where(first, token_index, sib_index), jnp.where(first, sib_index, token_index)]
    ).reshape(CORES * rows, 1)

    mine_g = [partial_rotation(gradients, sib_g, f, origin, core) for f in found_g]
    other_g = [layout.to_sibling(m) for m in mine_g]
    grads = owned_gradients(layout, mine_g, other_g, place, owned)

    groups = []
    for f in found_a:
        mine = partial_rotation(activations, sib_a, f, origin, core)
        other = layout.to_sibling(mine)
        sums = chip_sums(layout, grads, mine, other, positions, seq_lengths, owned)
        block = nz * owned
        crossed = [
            layout.along_y(sums[1][(h - 1) * block:h * block], h) for h in range(1, ny)
        ]
        outs = pair_sums(layout, sums[0], crossed, owned)
        groups.append([outs[0]] + [layout.along_z(outs[d], d) for d in range(1, nz)])
    return squares(groups, seq_lengths, owned)


def solution(mesh):
    return jax.shard_map(
        functools.partial(shards, Layout(mesh)),
        mesh=mesh,
        in_specs=(
            P(("grp", "row"), None),
            P(("grp", "row"), None),
            P(("grp", "row"), None),
            P(("grp", "row"), None),
            P(("grp", "row")),
            P("grp"),
        ),
        out_specs=P(("grp", "row"), None),
        check_vma=False,
    )
```

```python
import functools

import jax
import jax.numpy as jnp
from jax import lax
from jax.experimental import pallas as pl
from jax.experimental.pallas import tpu as pltpu
from jax.sharding import PartitionSpec as P

CORES = 2
VMEM_LIMIT = 56 * 1024 * 1024


def params():
    return pltpu.CompilerParams(vmem_limit_bytes=VMEM_LIMIT)


def whole(shape):
    return pl.BlockSpec(shape, lambda *_: (0,) * len(shape))


class Layout:
    def __init__(self, mesh):
        self.chips = mesh.shape["row"] // CORES
        self.ny = max(1, 4 // mesh.shape["grp"])
        if self.chips % self.ny:
            self.ny = 1
        self.nz = self.chips // self.ny

    def device(self, z, y, core):
        return ((z % self.nz) * self.ny + y % self.ny) * CORES + core

    def everyone(self):
        return [(z, y, c) for z in range(self.nz) for y in range(self.ny) for c in range(CORES)]

    def origin(self, z, y, d, h):
        return lax.rem(z + (self.nz - d), self.nz) * self.ny + lax.rem(y + (self.ny - h), self.ny)

    def along_z(self, x, hops):
        pairs = [(self.device(z, y, c), self.device(z + hops, y, c)) for z, y, c in self.everyone()]
        return lax.ppermute(x, "row", pairs)

    def along_y(self, x, hops=1):
        pairs = [(self.device(z, y, c), self.device(z, y + hops, c)) for z, y, c in self.everyone()]
        return lax.ppermute(x, "row", pairs)

    def to_sibling(self, x):
        pairs = [(self.device(z, y, c), self.device(z, y, 1 - c)) for z, y, c in self.everyone()]
        return lax.ppermute(x, "row", pairs)


def sibling_columns(act, core, chips):
    rows, depth = act.shape
    kc = depth // (chips * CORES)
    if kc % 128:
        return split_columns(act, 1 - core[0], chips)

    def kernel(core_ref, x_ref, o_ref, sems):
        copies = []
        for i in range(chips):
            at = pl.multiple_of((CORES * i + 1 - core_ref[0]) * kc, 128)
            copies.append(pltpu.make_async_copy(x_ref.at[:, pl.ds(at, kc)], o_ref.at[i], sems.at[i]))
        for copy in copies:
            copy.start()
        for copy in copies:
            copy.wait()

    return pl.pallas_call(
        kernel,
        grid_spec=pltpu.PrefetchScalarGridSpec(
            num_scalar_prefetch=1,
            grid=(1,),
            in_specs=[pl.BlockSpec(memory_space=pl.ANY)],
            out_specs=pl.BlockSpec(memory_space=pl.ANY),
            scratch_shapes=[pltpu.SemaphoreType.DMA((chips,))],
        ),
        out_shape=jax.ShapeDtypeStruct((chips, rows, kc), act.dtype),
        cost_estimate=pl.CostEstimate(flops=0, bytes_accessed=2 * rows * depth, transcendentals=0),
        compiler_params=params(),
        name="sibling_columns",
    )(core, act)


def split_columns(act, core, chips):
    rows, depth = act.shape
    kc = depth // (chips * CORES)
    mine = lax.dynamic_index_in_dim(act.reshape(rows, chips, CORES, kc), core, 2, keepdims=False)
    return mine.transpose(1, 0, 2)


class Links:
    def __init__(self, layout, window):
        self.layout, self.window = layout, window
        self.done = {"z": [], "y": []}

    def send(self, kind, x, hops):
        done = self.done[kind]
        if len(done) >= self.window:
            x, _ = lax.optimization_barrier((x, done[-self.window]))
        move = self.layout.along_z if kind == "z" else self.layout.along_y
        done.append(move(x, hops))
        return done[-1]


def gather_columns(links, piece, split):
    nz, ny = links.layout.nz, links.layout.ny
    middle = nz // 2
    steps = [(d, 1) for d in range(1, middle + 1)] + [(d, -1) for d in range(nz - 1, middle, -1)]
    steps = sorted(steps, key=lambda s: (min(s[0], nz - s[0]), -s[1]))
    by_z, crossed, found = {0: piece}, {}, [(piece, 0, 0)]

    def cross(d):
        for h in range(1, ny):
            if d == middle and split:
                head = links.send("z", crossed[d - 1, h][:split], 1)
                if split == piece.shape[0]:
                    got = [head]
                else:
                    got = [head, links.send("y", by_z[d][split:], h)]
            else:
                got = [links.send("y", by_z[d], h)]
            crossed[d, h] = got[0]
            found.append((got, d, h))

    last = 0
    for d, sign in steps:
        by_z[d] = links.send("z", by_z[(d - sign) % nz], sign)
        found.append(([by_z[d]], d, 0))
        cross(last)
        last = d
    cross(last)
    return [(block if isinstance(block, list) else [block], d, h) for block, d, h in found]


def partial_rotation(layout, act, sib, found, place, total=None):
    rows = act.shape[0]
    count = len(found)
    blocks = [x for parts, _, _ in found for x in parts]
    kc = sum(x.shape[0] for x in found[0][0])
    width = blocks[0].shape[1]
    unaligned = kc % 128 != 0
    if unaligned:
        act = split_columns(act, place[2], sib.shape[0])

    def kernel(place_ref, act_ref, sib_ref, *refs):
        block_refs, refs = refs[:len(blocks)], refs[len(blocks):]
        if total is not None:
            total_ref, refs = refs[0], refs[1:]
        o_ref, rows_buf, block_buf, sems = refs
        z, y, core = place_ref[0], place_ref[1], place_ref[2]
        mine = pl.multiple_of(core * rows, 16)
        other = pl.multiple_of((1 - core) * rows, 16)
        copies, k = [], 0
        for i in range(count):
            q = layout.origin(z, y, *found[i][1:])
            if unaligned:
                own = act_ref.at[q]
            else:
                own = act_ref.at[:, pl.ds(pl.multiple_of((CORES * q + core) * kc, 128), kc)]
            step = [
                pltpu.make_async_copy(own, rows_buf.at[i, pl.ds(mine, rows)], sems.at[i, 0]),
                pltpu.make_async_copy(sib_ref.at[q], rows_buf.at[i, pl.ds(other, rows)], sems.at[i, 1]),
            ]
            start = 0
            for j, x in enumerate(found[i][0]):
                at = block_buf.at[i, pl.ds(start, x.shape[0])]
                step.append(pltpu.make_async_copy(block_refs[k], at, sems.at[i, 2 + j]))
                start += x.shape[0]
                k += 1
            for copy in step:
                copy.start()
            copies.append(step)
        for i in range(count):
            for copy in copies[i]:
                copy.wait()
            product = jnp.dot(rows_buf[i], block_buf[i], preferred_element_type=jnp.float32)
            if i > 0:
                o_ref[...] += product
            elif total is not None:
                o_ref[...] = total_ref[...] + product
            else:
                o_ref[...] = product

    shape = (CORES * rows, width)
    anywhere = pl.BlockSpec(memory_space=pl.ANY)
    return pl.pallas_call(
        kernel,
        grid_spec=pltpu.PrefetchScalarGridSpec(
            num_scalar_prefetch=1,
            grid=(1,),
            in_specs=[anywhere] * (2 + len(blocks)) + ([] if total is None else [whole(shape)]),
            out_specs=whole(shape),
            scratch_shapes=[
                pltpu.VMEM((count, CORES * rows, kc), act.dtype),
                pltpu.VMEM((count, kc, width), act.dtype),
                pltpu.SemaphoreType.DMA((count, 4)),
            ],
        ),
        out_shape=jax.ShapeDtypeStruct(shape, jnp.float32),
        cost_estimate=pl.CostEstimate(
            flops=4 * rows * kc * count * width,
            bytes_accessed=2 * count * kc * (2 * rows + width) + 8 * rows * width,
            transcendentals=0,
        ),
        compiler_params=params(),
        name="partial_rotation",
    )(place, act, sib, *blocks, *([] if total is None else [total]))


def rotate(layout, act, sib, found, place, groups):
    total, at = None, 0
    while at < len(found):
        size = groups[0] if len(groups) == 1 else groups.pop(0)
        part = found[at:at + size]
        total = partial_rotation(layout, act, sib, part, place, total)
        at += size
    return total


def owned_gradients(layout, mine, other, place, owned):
    nz, ny = layout.nz, layout.ny
    pieces = len(mine)
    tokens, width = mine[0].shape
    kept = nz * ny * owned

    def kernel(place_ref, *refs):
        mine_refs, other_refs, o_ref = refs[:pieces], refs[pieces:2 * pieces], refs[2 * pieces]
        z, y, core = place_ref[0], place_ref[1], place_ref[2]
        slot = lax.broadcasted_iota(jnp.int32, (kept, width), 0)
        column = lax.broadcasted_iota(jnp.int32, (kept, width), 1)
        to_y = lax.rem(y + 1 + slot // (nz * owned), ny)
        to_z = lax.rem(z + lax.rem(slot // owned, nz), nz)
        wanted = ((to_z * ny + to_y) * CORES + core) * owned + lax.rem(slot, owned)
        total = jnp.zeros((kept, tokens), jnp.float32)
        for i in range(pieces):
            rotated = (mine_refs[i][...] + other_refs[i][...]).astype(jnp.bfloat16)
            pick = jnp.where(wanted == column + i * width, 1.0, 0.0).astype(jnp.bfloat16)
            total += lax.dot_general(
                pick, rotated, (((1,), (1,)), ((), ())), preferred_element_type=jnp.float32
            )
        o_ref[...] = total.astype(jnp.bfloat16)

    return pl.pallas_call(
        kernel,
        grid_spec=pltpu.PrefetchScalarGridSpec(
            num_scalar_prefetch=1,
            grid=(1,),
            in_specs=[whole((tokens, width))] * (2 * pieces),
            out_specs=whole((kept, tokens)),
        ),
        out_shape=jax.ShapeDtypeStruct((kept, tokens), jnp.bfloat16),
        cost_estimate=pl.CostEstimate(
            flops=2 * kept * pieces * width * tokens,
            bytes_accessed=8 * pieces * tokens * width + 2 * kept * tokens,
            transcendentals=0,
        ),
        compiler_params=params(),
        name="owned_gradients",
    )(place, *mine, *other)


def chip_sums(layout, grads, mine, other, positions, lengths, owned):
    tokens, width = mine.shape
    seqs = lengths.shape[0]
    kept = grads.shape[0]
    stay = layout.nz * owned
    sent = kept - stay

    def kernel(lengths_ref, grads_ref, mine_ref, other_ref, positions_ref, *refs):
        rotated = mine_ref[...] + other_ref[...]
        position = positions_ref[...]
        begin = jnp.int32(0)
        parts = []
        for s in range(seqs):
            end = begin + lengths_ref[s]
            inside = (position >= begin) & (position < end)
            parts.append(jnp.where(inside, rotated, 0.0).astype(jnp.bfloat16))
            begin = end
        for s in range(seqs):
            sums = jnp.dot(grads_ref[...], parts[s], preferred_element_type=jnp.float32)
            at = pl.ds(s * width, width)
            if sent:
                refs[1][:, at] = sums[:sent].astype(jnp.bfloat16)
            refs[0][:, at] = sums[sent:]

    shapes = [jax.ShapeDtypeStruct((stay, seqs * width), jnp.float32)]
    if sent:
        shapes.append(jax.ShapeDtypeStruct((sent, seqs * width), jnp.bfloat16))
    return pl.pallas_call(
        kernel,
        grid_spec=pltpu.PrefetchScalarGridSpec(
            num_scalar_prefetch=1,
            grid=(1,),
            in_specs=[
                whole((kept, tokens)),
                whole((tokens, width)),
                whole((tokens, width)),
                whole((tokens, 1)),
            ],
            out_specs=[whole(s.shape) for s in shapes],
        ),
        out_shape=shapes,
        cost_estimate=pl.CostEstimate(
            flops=2 * kept * tokens * seqs * width,
            bytes_accessed=8 * tokens * width + 6 * kept * seqs * width,
            transcendentals=0,
        ),
        compiler_params=params(),
        name="chip_sums",
    )(lengths, grads, mine, other, positions)


def pair_sums(layout, stay, crossed, owned):
    nz = layout.nz
    width = stay.shape[1]

    def kernel(*refs):
        total = refs[0][...]
        for i in range(len(crossed)):
            total += refs[1 + i][...].astype(jnp.float32)
        outs = refs[1 + len(crossed):]
        outs[0][...] = total[:owned]
        for d in range(1, nz):
            outs[d][...] = total[d * owned:(d + 1) * owned].astype(jnp.bfloat16)

    shapes = [jax.ShapeDtypeStruct((owned, width), jnp.float32)]
    shapes += [jax.ShapeDtypeStruct((owned, width), jnp.bfloat16)] * (nz - 1)
    return pl.pallas_call(
        kernel,
        grid=(1,),
        in_specs=[whole(stay.shape)] + [whole(c.shape) for c in crossed],
        out_specs=[whole(s.shape) for s in shapes],
        out_shape=shapes,
        cost_estimate=pl.CostEstimate(
            flops=stay.size, bytes_accessed=8 * stay.size, transcendentals=0
        ),
        compiler_params=params(),
        name="pair_sums",
    )(stay, *crossed)


def squares(groups, lengths, owned):
    seqs = lengths.shape[0]
    count = len(groups[0])
    width = groups[0][0].shape[1] // seqs

    def kernel(lengths_ref, *refs):
        o_ref = refs[-1]
        total = lengths_ref[0]
        for s in range(1, seqs):
            total = total + lengths_ref[s]
        over = jnp.full((owned, width), total, jnp.int32).astype(jnp.float32)
        for g in range(len(groups)):
            sums = refs[g * count][...]
            for i in range(1, count):
                sums = sums + refs[g * count + i][...].astype(jnp.float32)
            sums = sums * sums
            acc = sums[:, :width]
            for s in range(1, seqs):
                acc = acc + sums[:, s * width:(s + 1) * width]
            o_ref[:, pl.ds(g * width, width)] = acc / over

    flat = [x for group in groups for x in group]
    return pl.pallas_call(
        kernel,
        grid_spec=pltpu.PrefetchScalarGridSpec(
            num_scalar_prefetch=1,
            grid=(1,),
            in_specs=[whole(x.shape) for x in flat],
            out_specs=whole((owned, len(groups) * width)),
        ),
        out_shape=jax.ShapeDtypeStruct((owned, len(groups) * width), jnp.float32),
        cost_estimate=pl.CostEstimate(
            flops=4 * len(flat) * flat[0].size,
            bytes_accessed=4 * len(flat) * flat[0].size,
            transcendentals=0,
        ),
        compiler_params=params(),
        name="squares",
    )(lengths, *flat)


def shards(layout, activations, gradients, basis_a, basis_g, token_index, seq_lengths):
    nz, ny, chips = layout.nz, layout.ny, layout.chips
    rows = activations.shape[0]
    owned = basis_g.shape[1] // (chips * CORES)
    me = lax.axis_index("row")
    core = lax.rem(me, CORES)
    y = lax.rem(me // CORES, ny)
    z = me // (CORES * ny)
    place = jnp.stack([z, y, core]).astype(jnp.int32)
    core = core.reshape(1).astype(jnp.int32)

    links = Links(layout, 2)
    found_g = gather_columns(links, basis_g, basis_g.shape[0] * 4 // 7 if ny > 1 else 0)
    parts_a = 2
    wide = basis_a.shape[1] // parts_a
    found_a = [
        gather_columns(
            links, basis_a[:, i * wide:(i + 1) * wide], basis_a.shape[0] * (i % 2) if ny > 1 else 0
        )
        for i in range(parts_a)
    ]

    sib_g = layout.to_sibling(sibling_columns(gradients, core, chips))
    sib_a = layout.to_sibling(sibling_columns(activations, core, chips))
    sib_index = layout.to_sibling(token_index)
    first = core[0] == 0
    positions = jnp.concatenate(
        [jnp.where(first, token_index, sib_index), jnp.where(first, sib_index, token_index)]
    ).reshape(CORES * rows, 1)

    mine_g = rotate(layout, gradients, sib_g, found_g, place, [4])
    grads = owned_gradients(layout, [mine_g], [layout.to_sibling(mine_g)], place, owned)

    groups = []
    for f in found_a:
        mine = rotate(layout, activations, sib_a, f, place, [7, 4])
        other = layout.to_sibling(mine)
        sums = chip_sums(layout, grads, mine, other, positions, seq_lengths, owned)
        block = nz * owned
        crossed = [
            layout.along_y(sums[1][(h - 1) * block:h * block], h) for h in range(1, ny)
        ]
        outs = pair_sums(layout, sums[0], crossed, owned)
        groups.append([outs[0]] + [layout.along_z(outs[d], d) for d in range(1, nz)])
    return squares(groups, seq_lengths, owned)


def solution(mesh):
    return jax.shard_map(
        functools.partial(shards, Layout(mesh)),
        mesh=mesh,
        in_specs=(
            P(("grp", "row"), None),
            P(("grp", "row"), None),
            P(("grp", "row"), None),
            P(("grp", "row"), None),
            P(("grp", "row")),
            P("grp"),
        ),
        out_specs=P(("grp", "row"), None),
        check_vma=False,
    )
```

```python
import functools

import jax
import jax.numpy as jnp
from jax import lax
from jax.experimental import pallas as pl
from jax.experimental.pallas import tpu as pltpu
from jax.sharding import PartitionSpec as P

CORES = 2
MIB = 1024 * 1024


def params(mib=16):
    return pltpu.CompilerParams(vmem_limit_bytes=mib * MIB)


IN_VMEM = pl.BlockSpec(memory_space=pltpu.VMEM)
IN_SMEM = pl.BlockSpec(memory_space=pltpu.SMEM)
ANYWHERE = pl.BlockSpec(memory_space=pl.ANY)


class Layout:
    def __init__(self, mesh):
        self.chips = mesh.shape["row"] // CORES
        self.ny = max(1, 4 // mesh.shape["grp"])
        if self.chips % self.ny:
            self.ny = 1
        self.nz = self.chips // self.ny

    def device(self, z, y, core):
        return ((z % self.nz) * self.ny + y % self.ny) * CORES + core

    def everyone(self):
        return [(z, y, c) for z in range(self.nz) for y in range(self.ny) for c in range(CORES)]

    def origin(self, z, y, d, h):
        return lax.rem(z + (self.nz - d), self.nz) * self.ny + lax.rem(y + (self.ny - h), self.ny)

    def along_z(self, x, hops):
        pairs = [(self.device(z, y, c), self.device(z + hops, y, c)) for z, y, c in self.everyone()]
        return lax.ppermute(x, "row", pairs)

    def along_y(self, x, hops=1):
        pairs = [(self.device(z, y, c), self.device(z, y + hops, c)) for z, y, c in self.everyone()]
        return lax.ppermute(x, "row", pairs)

    def between_chips(self, x):
        groups = [
            [self.device(z, y, c) for z in range(self.nz) for y in range(self.ny)]
            for c in range(CORES)
        ]
        return lax.all_to_all(x, "row", 0, 0, axis_index_groups=groups, tiled=True)

    def to_sibling(self, x):
        pairs = [(self.device(z, y, c), self.device(z, y, 1 - c)) for z, y, c in self.everyone()]
        return lax.ppermute(x, "row", pairs)


def split_columns(act, core, chips):
    rows, depth = act.shape
    kc = depth // (chips * CORES)
    mine = lax.dynamic_index_in_dim(act.reshape(rows, chips, CORES, kc), core, 2, keepdims=False)
    return mine.transpose(1, 0, 2)


class Links:
    def __init__(self, layout, window):
        self.layout, self.window = layout, window
        self.done = {"z": [], "y": []}

    def send(self, kind, x, hops):
        done = self.done[kind]
        if len(done) >= self.window:
            x, _ = lax.optimization_barrier((x, done[-self.window]))
        move = self.layout.along_z if kind == "z" else self.layout.along_y
        done.append(move(x, hops))
        return done[-1]


def gather_columns(links, piece, split):
    nz, ny = links.layout.nz, links.layout.ny
    middle = nz // 2
    steps = [(d, 1) for d in range(1, middle + 1)] + [(d, -1) for d in range(nz - 1, middle, -1)]
    steps = sorted(steps, key=lambda s: (min(s[0], nz - s[0]), -s[1]))
    by_z, crossed, found = {0: piece}, {}, [(piece, 0, 0)]

    def cross(d):
        for h in range(1, ny):
            if d == middle and split:
                head = links.send("z", crossed[d - 1, h][:split], 1)
                if split == piece.shape[0]:
                    got = [head]
                else:
                    got = [head, links.send("y", by_z[d][split:], h)]
            else:
                got = [links.send("y", by_z[d], h)]
            crossed[d, h] = got[0]
            found.append((got, d, h))

    last = 0
    for d, sign in steps:
        by_z[d] = links.send("z", by_z[(d - sign) % nz], sign)
        found.append(([by_z[d]], d, 0))
        cross(last)
        last = d
    cross(last)
    return [(block if isinstance(block, list) else [block], d, h) for block, d, h in found]


def partial_rotation(layout, act, sib, found, place, total=None):
    rows = act.shape[0]
    count = len(found)
    blocks = [x for parts, _, _ in found for x in parts]
    kc = sum(x.shape[0] for x in found[0][0])
    width = blocks[0].shape[1]
    unaligned = kc % 128 != 0
    if unaligned:
        act = split_columns(act, place[2], layout.chips)
        sib = split_columns(sib, place[2], layout.chips)

    def kernel(place_ref, act_ref, sib_ref, *refs):
        block_refs, refs = refs[:len(blocks)], refs[len(blocks):]
        if total is not None:
            total_ref, refs = refs[0], refs[1:]
        o_ref, rows_buf, block_buf, sems = refs
        z, y, core = place_ref[0], place_ref[1], place_ref[2]
        mine = pl.multiple_of(core * rows, 16)
        other = pl.multiple_of((1 - core) * rows, 16)
        copies, k = [], 0
        for i in range(count):
            q = layout.origin(z, y, *found[i][1:])
            at = 0 if unaligned else pl.multiple_of((CORES * q + core) * kc, 128)
            own, its = [
                ref.at[q] if unaligned else ref.at[:, pl.ds(at, kc)] for ref in (act_ref, sib_ref)
            ]
            step = [
                pltpu.make_async_copy(own, rows_buf.at[i, pl.ds(mine, rows)], sems.at[i, 0]),
                pltpu.make_async_copy(its, rows_buf.at[i, pl.ds(other, rows)], sems.at[i, 1]),
            ]
            start = 0
            for j, x in enumerate(found[i][0]):
                at = block_buf.at[i, pl.ds(start, x.shape[0])]
                step.append(pltpu.make_async_copy(block_refs[k], at, sems.at[i, 2 + j]))
                start += x.shape[0]
                k += 1
            for copy in step:
                copy.start()
            copies.append(step)
        for i in range(count):
            for copy in copies[i]:
                copy.wait()
            product = jnp.dot(rows_buf[i], block_buf[i], preferred_element_type=jnp.float32)
            if i > 0:
                o_ref[...] += product
            elif total is not None:
                o_ref[...] = total_ref[...] + product
            else:
                o_ref[...] = product

    shape = (CORES * rows, width)
    return pl.pallas_call(
        kernel,
        in_specs=[IN_SMEM] + [ANYWHERE] * (2 + len(blocks)) + ([] if total is None else [IN_VMEM]),
        out_specs=IN_VMEM,
        out_shape=jax.ShapeDtypeStruct(shape, jnp.float32),
        scratch_shapes=[
            pltpu.VMEM((count, CORES * rows, kc), act.dtype),
            pltpu.VMEM((count, kc, width), act.dtype),
            pltpu.SemaphoreType.DMA((count, 4)),
        ],
        cost_estimate=pl.CostEstimate(
            flops=4 * rows * kc * count * width,
            bytes_accessed=2 * count * kc * (2 * rows + width) + 8 * rows * width,
            transcendentals=0,
        ),
        compiler_params=params(56),
        name="partial_rotation",
    )(place, act, sib, *blocks, *([] if total is None else [total]))


def rotate(layout, act, sib, found, place, groups):
    total, at = None, 0
    while at < len(found):
        size = groups[0] if len(groups) == 1 else groups.pop(0)
        part = found[at:at + size]
        total = partial_rotation(layout, act, sib, part, place, total)
        at += size
    return total


def owned_gradients(layout, mine, other, place, owned):
    tokens, width = mine.shape
    kept = layout.chips * owned

    def kernel(place_ref, mine_ref, other_ref, o_ref):
        slot = lax.broadcasted_iota(jnp.int32, (kept, width), 0)
        column = lax.broadcasted_iota(jnp.int32, (kept, width), 1)
        wanted = (CORES * (slot // owned) + place_ref[2]) * owned + lax.rem(slot, owned)
        pick = jnp.where(wanted == column, 1.0, 0.0).astype(jnp.bfloat16)
        rotated = (mine_ref[...] + other_ref[...]).astype(jnp.bfloat16)
        picked = lax.dot_general(
            pick, rotated, (((1,), (1,)), ((), ())), preferred_element_type=jnp.float32
        )
        o_ref[...] = picked.astype(jnp.bfloat16)

    return pl.pallas_call(
        kernel,
        in_specs=[IN_SMEM, IN_VMEM, IN_VMEM],
        out_specs=IN_VMEM,
        out_shape=jax.ShapeDtypeStruct((kept, tokens), jnp.bfloat16),
        cost_estimate=pl.CostEstimate(
            flops=2 * kept * width * tokens,
            bytes_accessed=8 * tokens * width + 2 * kept * tokens,
            transcendentals=0,
        ),
        compiler_params=params(),
        name="owned_gradients",
    )(place, mine, other)


def chip_sums(grads, mine, other, positions, lengths):
    tokens, width = mine.shape
    seqs = lengths.shape[0]
    kept = grads.shape[0]

    def kernel(lengths_ref, grads_ref, mine_ref, other_ref, positions_ref, o_ref):
        rotated = mine_ref[...] + other_ref[...]
        position = positions_ref[...]
        begin = jnp.int32(0)
        for s in range(seqs):
            end = begin + lengths_ref[s]
            inside = (position >= begin) & (position < end)
            part = jnp.where(inside, rotated, 0.0).astype(jnp.bfloat16)
            sums = jnp.dot(grads_ref[...], part, preferred_element_type=jnp.float32)
            o_ref[:, pl.ds(s * width, width)] = sums.astype(jnp.bfloat16)
            begin = end

    return pl.pallas_call(
        kernel,
        in_specs=[IN_SMEM] + [IN_VMEM] * 4,
        out_specs=IN_VMEM,
        out_shape=jax.ShapeDtypeStruct((kept, seqs * width), jnp.bfloat16),
        cost_estimate=pl.CostEstimate(
            flops=2 * kept * tokens * seqs * width,
            bytes_accessed=8 * tokens * width + 2 * kept * seqs * width,
            transcendentals=0,
        ),
        compiler_params=params(),
        name="chip_sums",
    )(lengths, grads, mine, other, positions)


def squares(groups, lengths, owned):
    seqs = lengths.shape[0]
    chips = groups[0].shape[0] // owned
    widths = [x.shape[1] // seqs for x in groups]

    def kernel(lengths_ref, *refs):
        o_ref = refs[-1]
        total = lengths_ref[0]
        for s in range(1, seqs):
            total = total + lengths_ref[s]
        at = 0
        for ref, width in zip(refs, widths):
            over = jnp.full((owned, width), total, jnp.int32).astype(jnp.float32)
            sums = ref[...].astype(jnp.float32).reshape(chips, owned, seqs * width).sum(axis=0)
            sums = sums * sums
            acc = sums[:, :width]
            for s in range(1, seqs):
                acc = acc + sums[:, s * width:(s + 1) * width]
            o_ref[:, pl.ds(at, width)] = acc / over
            at += width

    return pl.pallas_call(
        kernel,
        in_specs=[IN_SMEM] + [IN_VMEM] * len(groups),
        out_specs=IN_VMEM,
        out_shape=jax.ShapeDtypeStruct((owned, sum(widths)), jnp.float32),
        cost_estimate=pl.CostEstimate(
            flops=2 * sum(x.size for x in groups),
            bytes_accessed=2 * sum(x.size for x in groups),
            transcendentals=0,
        ),
        compiler_params=params(),
        name="squares",
    )(lengths, *groups)


def shards(layout, activations, gradients, basis_a, basis_g, token_index, seq_lengths):
    nz, ny, chips = layout.nz, layout.ny, layout.chips
    rows = activations.shape[0]
    owned = basis_g.shape[1] // (chips * CORES)
    me = lax.axis_index("row")
    core = lax.rem(me, CORES)
    y = lax.rem(me // CORES, ny)
    z = me // (CORES * ny)
    place = jnp.stack([z, y, core]).astype(jnp.int32)

    links = Links(layout, 2)
    found_g = gather_columns(links, basis_g, basis_g.shape[0] * 4 // 7 if ny > 1 else 0)
    parts_a = 2
    wide = basis_a.shape[1] // parts_a
    found_a = [
        gather_columns(
            links, basis_a[:, i * wide:(i + 1) * wide], basis_a.shape[0] * (i % 2) if ny > 1 else 0
        )
        for i in range(parts_a)
    ]

    sib_g = layout.to_sibling(gradients)
    sib_a = layout.to_sibling(activations)
    sib_index = layout.to_sibling(token_index)
    first = core == 0
    positions = jnp.concatenate(
        [jnp.where(first, token_index, sib_index), jnp.where(first, sib_index, token_index)]
    ).reshape(CORES * rows, 1)

    mine_g = rotate(layout, gradients, sib_g, found_g, place, [4])
    grads = owned_gradients(layout, mine_g, layout.to_sibling(mine_g), place, owned)

    groups = []
    for f in found_a:
        mine = rotate(layout, activations, sib_a, f, place, [7, 4])
        sums = chip_sums(grads, mine, layout.to_sibling(mine), positions, seq_lengths)
        groups.append(layout.between_chips(sums))
    return squares(groups, seq_lengths, owned)


def solution(mesh):
    return jax.shard_map(
        functools.partial(shards, Layout(mesh)),
        mesh=mesh,
        in_specs=(
            P(("grp", "row"), None),
            P(("grp", "row"), None),
            P(("grp", "row"), None),
            P(("grp", "row"), None),
            P(("grp", "row")),
            P("grp"),
        ),
        out_specs=P(("grp", "row"), None),
        check_vma=False,
    )
```

```python
import functools

import jax
import jax.numpy as jnp
from jax import lax
from jax.experimental import pallas as pl
from jax.experimental.pallas import tpu as pltpu
from jax.sharding import PartitionSpec as P

CORES = 2
MIB = 1024 * 1024


def params(mib=16):
    return pltpu.CompilerParams(vmem_limit_bytes=mib * MIB)


IN_VMEM = pl.BlockSpec(memory_space=pltpu.VMEM)
IN_SMEM = pl.BlockSpec(memory_space=pltpu.SMEM)
ANYWHERE = pl.BlockSpec(memory_space=pl.ANY)


class Layout:
    def __init__(self, mesh):
        self.chips = mesh.shape["row"] // CORES
        self.ny = max(1, 4 // mesh.shape["grp"])
        if self.chips % self.ny:
            self.ny = 1
        self.nz = self.chips // self.ny

    def device(self, z, y, core):
        return ((z % self.nz) * self.ny + y % self.ny) * CORES + core

    def everyone(self):
        return [(z, y, c) for z in range(self.nz) for y in range(self.ny) for c in range(CORES)]

    def origin(self, z, y, d, h):
        return lax.rem(z + (self.nz - d), self.nz) * self.ny + lax.rem(y + (self.ny - h), self.ny)

    def along_z(self, x, hops):
        pairs = [(self.device(z, y, c), self.device(z + hops, y, c)) for z, y, c in self.everyone()]
        return lax.ppermute(x, "row", pairs)

    def along_y(self, x, hops=1):
        pairs = [(self.device(z, y, c), self.device(z, y + hops, c)) for z, y, c in self.everyone()]
        return lax.ppermute(x, "row", pairs)

    def between_chips(self, x):
        groups = [
            [self.device(z, y, c) for z in range(self.nz) for y in range(self.ny)]
            for c in range(CORES)
        ]
        return lax.all_to_all(x, "row", 0, 0, axis_index_groups=groups, tiled=True)

    def to_sibling(self, x):
        pairs = [(self.device(z, y, c), self.device(z, y, 1 - c)) for z, y, c in self.everyone()]
        return lax.ppermute(x, "row", pairs)


def split_columns(act, core, chips):
    rows, depth = act.shape
    kc = depth // (chips * CORES)
    mine = lax.dynamic_index_in_dim(act.reshape(rows, chips, CORES, kc), core, 2, keepdims=False)
    return mine.transpose(1, 0, 2)


class Links:
    def __init__(self, layout, window):
        self.layout, self.window = layout, window
        self.done = {"z": [], "y": []}
        self.first = []

    def after(self, *first):
        self.first += first

    def send(self, kind, x, hops):
        done = self.done[kind]
        first = self.first + done[-self.window:len(done) - self.window + 1]
        self.first = []
        if first:
            x = lax.optimization_barrier((x, *first))[0]
        move = self.layout.along_z if kind == "z" else self.layout.along_y
        done.append(move(x, hops))
        return done[-1]


def gather_columns(links, piece, split, *before_last):
    nz, ny = links.layout.nz, links.layout.ny
    middle = nz // 2
    steps = [(d, 1) for d in range(1, middle + 1)] + [(d, -1) for d in range(nz - 1, middle, -1)]
    steps = sorted(steps, key=lambda s: (min(s[0], nz - s[0]), -s[1]))
    by_z, crossed, found = {0: piece}, {}, [(piece, 0, 0)]

    def cross(d):
        for h in range(1, ny):
            if d == middle and split:
                head = links.send("z", crossed[d - 1, h][:split], 1)
                if split == piece.shape[0]:
                    got = [head]
                else:
                    got = [head, links.send("y", by_z[d][split:], h)]
            else:
                got = [links.send("y", by_z[d], h)]
            crossed[d, h] = got[0]
            found.append((got, d, h))

    last = 0
    for d, sign in steps:
        if d == middle:
            links.after(*before_last)
        by_z[d] = links.send("z", by_z[(d - sign) % nz], sign)
        found.append(([by_z[d]], d, 0))
        cross(last)
        last = d
    cross(last)
    return [(block if isinstance(block, list) else [block], d, h) for block, d, h in found]


def partial_rotation(layout, act, sib, found, place, total=None):
    rows = act.shape[0]
    count = len(found)
    blocks = [x for parts, _, _ in found for x in parts]
    kc = sum(x.shape[0] for x in found[0][0])
    width = blocks[0].shape[1]
    unaligned = kc % 128 != 0
    if unaligned:
        act = split_columns(act, place[2], layout.chips)
        sib = split_columns(sib, place[2], layout.chips)

    def kernel(place_ref, act_ref, sib_ref, *refs):
        o_ref = refs[-1]
        z, y, core = place_ref[0], place_ref[1], place_ref[2]
        mine = pl.ds(pl.multiple_of(core * rows, 8), rows)
        other = pl.ds(pl.multiple_of((1 - core) * rows, 8), rows)
        k = 0
        for i in range(count):
            q = layout.origin(z, y, *found[i][1:])
            start = 0
            for x in found[i][0]:
                depth = x.shape[0]
                block = refs[k][...]
                if unaligned:
                    own, its = act_ref[q], sib_ref[q]
                else:
                    at = pl.ds(pl.multiple_of((CORES * q + core) * kc + start, 128), depth)
                    own, its = act_ref[:, at], sib_ref[:, at]
                for place_of, x in ((mine, own), (other, its)):
                    product = jnp.dot(x, block, preferred_element_type=jnp.float32)
                    if k == 0 and total is None:
                        o_ref[place_of, :] = product
                    elif k == 0:
                        o_ref[place_of, :] = refs[len(blocks)][place_of, :] + product
                    else:
                        o_ref[place_of, :] += product
                start += depth
                k += 1

    shape = (CORES * rows, width)
    extra = [] if total is None else [total]
    return pl.pallas_call(
        kernel,
        in_specs=[IN_SMEM] + [IN_VMEM] * (2 + len(blocks) + len(extra)),
        out_specs=IN_VMEM,
        out_shape=jax.ShapeDtypeStruct(shape, jnp.float32),
        cost_estimate=pl.CostEstimate(
            flops=4 * rows * kc * count * width,
            bytes_accessed=2 * count * kc * (2 * rows + width) + 8 * rows * width,
            transcendentals=0,
        ),
        compiler_params=params(),
        name="partial_rotation",
    )(place, act, sib, *blocks, *extra)


def owned_gradients(layout, mine, other, place, owned):
    tokens, width = mine.shape
    kept = layout.chips * owned

    def kernel(place_ref, mine_ref, other_ref, o_ref):
        slot = lax.broadcasted_iota(jnp.int32, (kept, width), 0)
        column = lax.broadcasted_iota(jnp.int32, (kept, width), 1)
        wanted = (CORES * (slot // owned) + place_ref[2]) * owned + lax.rem(slot, owned)
        pick = jnp.where(wanted == column, 1.0, 0.0).astype(jnp.bfloat16)
        rotated = (mine_ref[...] + other_ref[...]).astype(jnp.bfloat16)
        picked = lax.dot_general(
            pick, rotated, (((1,), (1,)), ((), ())), preferred_element_type=jnp.float32
        )
        o_ref[...] = picked.astype(jnp.bfloat16)

    return pl.pallas_call(
        kernel,
        in_specs=[IN_SMEM, IN_VMEM, IN_VMEM],
        out_specs=IN_VMEM,
        out_shape=jax.ShapeDtypeStruct((kept, tokens), jnp.bfloat16),
        cost_estimate=pl.CostEstimate(
            flops=2 * kept * width * tokens,
            bytes_accessed=8 * tokens * width + 2 * kept * tokens,
            transcendentals=0,
        ),
        compiler_params=params(),
        name="owned_gradients",
    )(place, mine, other)


def chip_sums(grads, mine, other, positions, lengths):
    tokens, width = mine.shape
    seqs = lengths.shape[0]
    kept = grads.shape[0]

    def kernel(lengths_ref, grads_ref, mine_ref, other_ref, positions_ref, o_ref):
        rotated = mine_ref[...] + other_ref[...]
        position = positions_ref[...]
        begin = jnp.int32(0)
        for s in range(seqs):
            end = begin + lengths_ref[s]
            inside = (position >= begin) & (position < end)
            part = jnp.where(inside, rotated, 0.0).astype(jnp.bfloat16)
            sums = jnp.dot(grads_ref[...], part, preferred_element_type=jnp.float32)
            o_ref[:, pl.ds(s * width, width)] = sums.astype(jnp.bfloat16)
            begin = end

    return pl.pallas_call(
        kernel,
        in_specs=[IN_SMEM] + [IN_VMEM] * 4,
        out_specs=IN_VMEM,
        out_shape=jax.ShapeDtypeStruct((kept, seqs * width), jnp.bfloat16),
        cost_estimate=pl.CostEstimate(
            flops=2 * kept * tokens * seqs * width,
            bytes_accessed=8 * tokens * width + 2 * kept * seqs * width,
            transcendentals=0,
        ),
        compiler_params=params(),
        name="chip_sums",
    )(lengths, grads, mine, other, positions)


def squares(groups, lengths, owned):
    seqs = lengths.shape[0]
    chips = groups[0].shape[0] // owned
    widths = [x.shape[1] // seqs for x in groups]

    def kernel(lengths_ref, *refs):
        o_ref = refs[-1]
        total = lengths_ref[0]
        for s in range(1, seqs):
            total = total + lengths_ref[s]
        at = 0
        for ref, width in zip(refs, widths):
            over = jnp.full((owned, width), total, jnp.int32).astype(jnp.float32)
            sums = ref[...].astype(jnp.float32).reshape(chips, owned, seqs * width).sum(axis=0)
            sums = sums * sums
            acc = sums[:, :width]
            for s in range(1, seqs):
                acc = acc + sums[:, s * width:(s + 1) * width]
            o_ref[:, pl.ds(at, width)] = acc / over
            at += width

    return pl.pallas_call(
        kernel,
        in_specs=[IN_SMEM] + [IN_VMEM] * len(groups),
        out_specs=IN_VMEM,
        out_shape=jax.ShapeDtypeStruct((owned, sum(widths)), jnp.float32),
        cost_estimate=pl.CostEstimate(
            flops=2 * sum(x.size for x in groups),
            bytes_accessed=2 * sum(x.size for x in groups),
            transcendentals=0,
        ),
        compiler_params=params(),
        name="squares",
    )(lengths, *groups)


def shards(layout, activations, gradients, basis_a, basis_g, token_index, seq_lengths):
    nz, ny, chips = layout.nz, layout.ny, layout.chips
    rows = activations.shape[0]
    owned = basis_g.shape[1] // (chips * CORES)
    me = lax.axis_index("row")
    core = lax.rem(me, CORES)
    y = lax.rem(me // CORES, ny)
    z = me // (CORES * ny)
    place = jnp.stack([z, y, core]).astype(jnp.int32)

    links = Links(layout, 2)
    sib_g = layout.to_sibling(gradients)
    found_g = gather_columns(links, basis_g, basis_g.shape[0] * 4 // 7 if ny > 1 else 0, sib_g)
    later, _ = lax.optimization_barrier((activations, found_g[2 % len(found_g)][0][0]))
    sib_a = layout.to_sibling(later)
    early = partial_rotation(layout, gradients, sib_g, found_g[:4], place)
    links.after(sib_a, early)
    found_a, at = [], 0
    for wide in (basis_a.shape[1] * 3 // 4, basis_a.shape[1] // 4):
        found_a.append(gather_columns(links, basis_a[:, at:at + wide], 0))
        at += wide

    sib_index = layout.to_sibling(token_index)
    first = core == 0
    positions = jnp.concatenate(
        [jnp.where(first, token_index, sib_index), jnp.where(first, sib_index, token_index)]
    ).reshape(CORES * rows, 1)

    mine_g = partial_rotation(layout, gradients, sib_g, found_g[4:], place, early)
    grads = owned_gradients(layout, mine_g, layout.to_sibling(mine_g), place, owned)

    groups = []
    for f in found_a:
        most = partial_rotation(layout, activations, sib_a, f[:-1], place)
        mine = partial_rotation(layout, activations, sib_a, f[-1:], place, most)
        sums = chip_sums(grads, mine, layout.to_sibling(mine), positions, seq_lengths)
        groups.append(layout.between_chips(sums))
    return squares(groups, seq_lengths, owned)


def solution(mesh):
    return jax.shard_map(
        functools.partial(shards, Layout(mesh)),
        mesh=mesh,
        in_specs=(
            P(("grp", "row"), None),
            P(("grp", "row"), None),
            P(("grp", "row"), None),
            P(("grp", "row"), None),
            P(("grp", "row")),
            P("grp"),
        ),
        out_specs=P(("grp", "row"), None),
        check_vma=False,
    )
```

```python
import functools

import jax
import jax.numpy as jnp
from jax import lax
from jax.experimental import pallas as pl
from jax.experimental.pallas import tpu as pltpu
from jax.sharding import PartitionSpec as P

CORES = 2
MIB = 1024 * 1024


def params(mib=16):
    return pltpu.CompilerParams(vmem_limit_bytes=mib * MIB)


IN_VMEM = pl.BlockSpec(memory_space=pltpu.VMEM)
IN_SMEM = pl.BlockSpec(memory_space=pltpu.SMEM)
ANYWHERE = pl.BlockSpec(memory_space=pl.ANY)


class Layout:
    def __init__(self, mesh):
        self.chips = mesh.shape["row"] // CORES
        self.ny = max(1, 4 // mesh.shape["grp"])
        if self.chips % self.ny:
            self.ny = 1
        self.nz = self.chips // self.ny

    def device(self, z, y, core):
        return ((z % self.nz) * self.ny + y % self.ny) * CORES + core

    def everyone(self):
        return [(z, y, c) for z in range(self.nz) for y in range(self.ny) for c in range(CORES)]

    def origin(self, z, y, d, h):
        return lax.rem(z + (self.nz - d), self.nz) * self.ny + lax.rem(y + (self.ny - h), self.ny)

    def along_z(self, x, hops):
        pairs = [(self.device(z, y, c), self.device(z + hops, y, c)) for z, y, c in self.everyone()]
        return lax.ppermute(x, "row", pairs)

    def along_y(self, x, hops=1):
        pairs = [(self.device(z, y, c), self.device(z, y + hops, c)) for z, y, c in self.everyone()]
        return lax.ppermute(x, "row", pairs)

    def between_chips(self, x):
        groups = [
            [self.device(z, y, c) for z in range(self.nz) for y in range(self.ny)]
            for c in range(CORES)
        ]
        return lax.all_to_all(x, "row", 0, 0, axis_index_groups=groups, tiled=True)

    def to_sibling(self, x):
        pairs = [(self.device(z, y, c), self.device(z, y, 1 - c)) for z, y, c in self.everyone()]
        return lax.ppermute(x, "row", pairs)


def split_columns(act, core, chips):
    rows, depth = act.shape
    kc = depth // (chips * CORES)
    mine = lax.dynamic_index_in_dim(act.reshape(rows, chips, CORES, kc), core, 2, keepdims=False)
    return mine.transpose(1, 0, 2)


class Links:
    def __init__(self, layout, window):
        self.layout, self.window = layout, window
        self.done = {"z": [], "y": []}
        self.first = []

    def after(self, *first):
        self.first += first

    def send(self, kind, x, hops):
        done = self.done[kind]
        first = self.first + done[-self.window:len(done) - self.window + 1]
        self.first = []
        if first:
            x = lax.optimization_barrier((x, *first))[0]
        move = self.layout.along_z if kind == "z" else self.layout.along_y
        done.append(move(x, hops))
        return done[-1]


def gather_columns(links, piece, split, gates, before_last=None, begun=()):
    nz, ny = links.layout.nz, links.layout.ny
    middle = nz // 2
    steps = [(d, 1) for d in range(1, middle + 1)] + [(d, -1) for d in range(nz - 1, middle, -1)]
    steps = sorted(steps, key=lambda s: (min(s[0], nz - s[0]), -s[1]))
    by_z, crossed, found = {0: piece, **dict(begun)}, {}, [(piece, 0, 0)]

    def cross(d):
        for h in range(1, ny):
            if d == middle and split:
                head = links.send("z", crossed[d - 1, h][:split], 1)
                if split == piece.shape[0]:
                    got = [head]
                else:
                    got = [head, links.send("y", by_z[d][split:], h)]
            else:
                got = [links.send("y", by_z[d], h)]
            crossed[d, h] = got[0]
            found.append((got, d, h))

    last = 0
    for d, sign in steps:
        links.after(*gates.get(d, ()))
        if d not in by_z:
            by_z[d] = links.send("z", by_z[(d - sign) % nz], sign)
        found.append(([by_z[d]], d, 0))
        cross(last)
        last = d
    if before_last is not None:
        links.after(*before_last(by_z))
    cross(last)
    links.first = []
    return [(block if isinstance(block, list) else [block], d, h) for block, d, h in found]


def partial_rotation(layout, act, sib, found, place, total=None):
    rows = act.shape[0]
    count = len(found)
    blocks = [x for parts, _, _ in found for x in parts]
    kc = sum(x.shape[0] for x in found[0][0])
    width = blocks[0].shape[1]
    unaligned = kc % 128 != 0
    if unaligned:
        act = split_columns(act, place[2], layout.chips)
        sib = split_columns(sib, place[2], layout.chips)

    def kernel(place_ref, act_ref, sib_ref, *refs):
        o_ref = refs[-1]
        z, y, core = place_ref[0], place_ref[1], place_ref[2]
        mine = pl.ds(pl.multiple_of(core * rows, 8), rows)
        other = pl.ds(pl.multiple_of((1 - core) * rows, 8), rows)
        k = 0
        for i in range(count):
            q = layout.origin(z, y, *found[i][1:])
            start = 0
            for x in found[i][0]:
                depth = x.shape[0]
                block = refs[k][...]
                if unaligned:
                    own, its = act_ref[q], sib_ref[q]
                else:
                    at = pl.ds(pl.multiple_of((CORES * q + core) * kc + start, 128), depth)
                    own, its = act_ref[:, at], sib_ref[:, at]
                for place_of, x in ((mine, own), (other, its)):
                    product = jnp.dot(x, block, preferred_element_type=jnp.float32)
                    if k == 0 and total is None:
                        o_ref[place_of, :] = product
                    elif k == 0:
                        o_ref[place_of, :] = refs[len(blocks)][place_of, :] + product
                    else:
                        o_ref[place_of, :] += product
                start += depth
                k += 1

    shape = (CORES * rows, width)
    extra = [] if total is None else [total]
    return pl.pallas_call(
        kernel,
        in_specs=[IN_SMEM] + [IN_VMEM] * (2 + len(blocks) + len(extra)),
        out_specs=IN_VMEM,
        out_shape=jax.ShapeDtypeStruct(shape, jnp.float32),
        cost_estimate=pl.CostEstimate(
            flops=4 * rows * kc * count * width,
            bytes_accessed=2 * count * kc * (2 * rows + width) + 8 * rows * width,
            transcendentals=0,
        ),
        compiler_params=params(),
        name="partial_rotation",
    )(place, act, sib, *blocks, *extra)


def owned_gradients(layout, mine, other, place, owned):
    tokens, width = mine.shape
    kept = layout.chips * owned

    def kernel(place_ref, mine_ref, other_ref, o_ref):
        slot = lax.broadcasted_iota(jnp.int32, (kept, width), 0)
        column = lax.broadcasted_iota(jnp.int32, (kept, width), 1)
        wanted = (CORES * (slot // owned) + place_ref[2]) * owned + lax.rem(slot, owned)
        pick = jnp.where(wanted == column, 1.0, 0.0).astype(jnp.bfloat16)
        rotated = (mine_ref[...] + other_ref[...]).astype(jnp.bfloat16)
        picked = lax.dot_general(
            pick, rotated, (((1,), (1,)), ((), ())), preferred_element_type=jnp.float32
        )
        o_ref[...] = picked.astype(jnp.bfloat16)

    return pl.pallas_call(
        kernel,
        in_specs=[IN_SMEM, IN_VMEM, IN_VMEM],
        out_specs=IN_VMEM,
        out_shape=jax.ShapeDtypeStruct((kept, tokens), jnp.bfloat16),
        cost_estimate=pl.CostEstimate(
            flops=2 * kept * width * tokens,
            bytes_accessed=8 * tokens * width + 2 * kept * tokens,
            transcendentals=0,
        ),
        compiler_params=params(),
        name="owned_gradients",
    )(place, mine, other)


def chip_sums(grads, mine, other, positions, lengths):
    tokens, width = mine.shape
    seqs = lengths.shape[0]
    kept = grads.shape[0]

    def kernel(lengths_ref, grads_ref, mine_ref, other_ref, positions_ref, o_ref):
        rotated = mine_ref[...] + other_ref[...]
        position = positions_ref[...]
        begin = jnp.int32(0)
        for s in range(seqs):
            end = begin + lengths_ref[s]
            inside = (position >= begin) & (position < end)
            part = jnp.where(inside, rotated, 0.0).astype(jnp.bfloat16)
            sums = jnp.dot(grads_ref[...], part, preferred_element_type=jnp.float32)
            o_ref[:, pl.ds(s * width, width)] = sums.astype(jnp.bfloat16)
            begin = end

    return pl.pallas_call(
        kernel,
        in_specs=[IN_SMEM] + [IN_VMEM] * 4,
        out_specs=IN_VMEM,
        out_shape=jax.ShapeDtypeStruct((kept, seqs * width), jnp.bfloat16),
        cost_estimate=pl.CostEstimate(
            flops=2 * kept * tokens * seqs * width,
            bytes_accessed=8 * tokens * width + 2 * kept * seqs * width,
            transcendentals=0,
        ),
        compiler_params=params(),
        name="chip_sums",
    )(lengths, grads, mine, other, positions)


def squares(groups, lengths, owned):
    seqs = lengths.shape[0]
    chips = groups[0].shape[0] // owned
    widths = [x.shape[1] // seqs for x in groups]

    def kernel(lengths_ref, *refs):
        o_ref = refs[-1]
        total = lengths_ref[0]
        for s in range(1, seqs):
            total = total + lengths_ref[s]
        at = 0
        for ref, width in zip(refs, widths):
            over = jnp.full((owned, width), total, jnp.int32).astype(jnp.float32)
            sums = ref[...].astype(jnp.float32).reshape(chips, owned, seqs * width).sum(axis=0)
            sums = sums * sums
            acc = sums[:, :width]
            for s in range(1, seqs):
                acc = acc + sums[:, s * width:(s + 1) * width]
            o_ref[:, pl.ds(at, width)] = acc / over
            at += width

    return pl.pallas_call(
        kernel,
        in_specs=[IN_SMEM] + [IN_VMEM] * len(groups),
        out_specs=IN_VMEM,
        out_shape=jax.ShapeDtypeStruct((owned, sum(widths)), jnp.float32),
        cost_estimate=pl.CostEstimate(
            flops=2 * sum(x.size for x in groups),
            bytes_accessed=2 * sum(x.size for x in groups),
            transcendentals=0,
        ),
        compiler_params=params(),
        name="squares",
    )(lengths, *groups)


def shards(layout, activations, gradients, basis_a, basis_g, token_index, seq_lengths):
    nz, ny, chips = layout.nz, layout.ny, layout.chips
    rows = activations.shape[0]
    owned = basis_g.shape[1] // (chips * CORES)
    me = lax.axis_index("row")
    core = lax.rem(me, CORES)
    y = lax.rem(me // CORES, ny)
    z = me // (CORES * ny)
    place = jnp.stack([z, y, core]).astype(jnp.int32)

    sib_index = layout.to_sibling(token_index)
    first = core == 0
    positions = jnp.concatenate(
        [jnp.where(first, token_index, sib_index), jnp.where(first, sib_index, token_index)]
    ).reshape(CORES * rows, 1)

    links = Links(layout, 2)
    sib_g = layout.to_sibling(gradients)
    sib_a = layout.to_sibling(activations)
    split = basis_g.shape[0] * 4 // 7 if ny > 1 else 0
    found_g = gather_columns(links, basis_g, split, {nz // 2: [sib_g, sib_a]})
    early = partial_rotation(layout, gradients, sib_g, found_g[:4], place)
    mine_g = partial_rotation(layout, gradients, sib_g, found_g[4:], place, early)
    grads = owned_gradients(layout, mine_g, layout.to_sibling(mine_g), place, owned)

    def rotated(found, *before_last):
        most = partial_rotation(layout, activations, sib_a, found[:-1], place)
        blocks, d, h = found[-1]
        if before_last:
            blocks = list(lax.optimization_barrier((*blocks, *before_last))[:len(blocks)])
        mine = partial_rotation(layout, activations, sib_a, [(blocks, d, h)], place, most)
        return mine, layout.to_sibling(mine)

    cut = basis_a.shape[1] * 3 // 4
    head, tail = basis_a[:, :cut], basis_a[:, cut:]
    begun, pairs = {}, []

    def begin_tail(by_z):
        begun[1] = links.send("z", tail, 1)
        return [begun[1]]

    def rotate_head(by_z):
        pairs.append(rotated(found_head, by_z[nz - 1]))
        return [pairs[0][1]]

    links.after(early)
    found_head = gather_columns(links, head, 0, {}, begin_tail)
    found_tail = gather_columns(links, tail, 0, {}, rotate_head, begun)
    sums = chip_sums(grads, *pairs[0], positions, seq_lengths)
    groups = [layout.between_chips(sums)]
    sums = chip_sums(grads, *rotated(found_tail, sums), positions, seq_lengths)
    groups.append(layout.between_chips(sums))
    return squares(groups, seq_lengths, owned)


def solution(mesh):
    return jax.shard_map(
        functools.partial(shards, Layout(mesh)),
        mesh=mesh,
        in_specs=(
            P(("grp", "row"), None),
            P(("grp", "row"), None),
            P(("grp", "row"), None),
            P(("grp", "row"), None),
            P(("grp", "row")),
            P("grp"),
        ),
        out_specs=P(("grp", "row"), None),
        check_vma=False,
    )
```

```python
import functools

import jax
import jax.numpy as jnp
from jax import lax
from jax.experimental import pallas as pl
from jax.experimental.pallas import tpu as pltpu
from jax.sharding import PartitionSpec as P

CORES = 2
MIB = 1024 * 1024


def params(mib=8):
    return pltpu.CompilerParams(vmem_limit_bytes=mib * MIB)


IN_VMEM = pl.BlockSpec(memory_space=pltpu.VMEM)
IN_SMEM = pl.BlockSpec(memory_space=pltpu.SMEM)
ANYWHERE = pl.BlockSpec(memory_space=pl.ANY)


class Layout:
    def __init__(self, mesh):
        self.chips = mesh.shape["row"] // CORES
        self.ny = max(1, 4 // mesh.shape["grp"])
        if self.chips % self.ny:
            self.ny = 1
        self.nz = self.chips // self.ny

    def device(self, z, y, core):
        return ((z % self.nz) * self.ny + y % self.ny) * CORES + core

    def everyone(self):
        return [(z, y, c) for z in range(self.nz) for y in range(self.ny) for c in range(CORES)]

    def origin(self, z, y, d, h):
        return lax.rem(z + (self.nz - d), self.nz) * self.ny + lax.rem(y + (self.ny - h), self.ny)

    def along_z(self, x, hops):
        pairs = [(self.device(z, y, c), self.device(z + hops, y, c)) for z, y, c in self.everyone()]
        return lax.ppermute(x, "row", pairs)

    def along_y(self, x, hops=1):
        pairs = [(self.device(z, y, c), self.device(z, y + hops, c)) for z, y, c in self.everyone()]
        return lax.ppermute(x, "row", pairs)

    def between_chips(self, x):
        groups = [
            [self.device(z, y, c) for z in range(self.nz) for y in range(self.ny)]
            for c in range(CORES)
        ]
        return lax.all_to_all(x, "row", 0, 0, axis_index_groups=groups, tiled=True)

    def to_sibling(self, x):
        pairs = [(self.device(z, y, c), self.device(z, y, 1 - c)) for z, y, c in self.everyone()]
        return lax.ppermute(x, "row", pairs)


def split_columns(act, core, chips):
    rows, depth = act.shape
    kc = depth // (chips * CORES)
    mine = lax.dynamic_index_in_dim(act.reshape(rows, chips, CORES, kc), core, 2, keepdims=False)
    return mine.transpose(1, 0, 2)


class Links:
    def __init__(self, layout, window):
        self.layout, self.window = layout, window
        self.done = {"z": [], "y": []}
        self.first = []

    def after(self, *first):
        self.first += first

    def send(self, kind, x, hops):
        done = self.done[kind]
        first = self.first + done[-self.window:len(done) - self.window + 1]
        self.first = []
        if first:
            x = lax.optimization_barrier((x, *first))[0]
        move = self.layout.along_z if kind == "z" else self.layout.along_y
        done.append(move(x, hops))
        return done[-1]


def gather_columns(links, piece, split, gates):
    nz, ny = links.layout.nz, links.layout.ny
    middle = nz // 2
    steps = [(d, 1) for d in range(1, middle + 1)] + [(d, -1) for d in range(nz - 1, middle, -1)]
    steps = sorted(steps, key=lambda s: (min(s[0], nz - s[0]), -s[1]))
    by_z, crossed, found = {0: piece}, {}, [(piece, 0, 0)]

    def cross(d):
        for h in range(1, ny):
            if d == middle and split:
                head = links.send("z", crossed[d - 1, h][:split], 1)
                if split == piece.shape[0]:
                    got = [head]
                else:
                    got = [head, links.send("y", by_z[d][split:], h)]
            else:
                got = [links.send("y", by_z[d], h)]
            crossed[d, h] = got[0]
            found.append((got, d, h))

    last = 0
    for d, sign in steps:
        links.after(*gates.get(d, ()))
        by_z[d] = links.send("z", by_z[(d - sign) % nz], sign)
        found.append(([by_z[d]], d, 0))
        cross(last)
        last = d
    cross(last)
    return [(block if isinstance(block, list) else [block], d, h) for block, d, h in found]


def partial_rotation(layout, act, sib, found, place, total=None, left=None):
    rows = act.shape[0]
    count = len(found)
    blocks = [x for parts, _, _ in found for x in parts]
    kc = sum(x.shape[0] for x in found[0][0])
    width = blocks[0].shape[1]
    unaligned = kc % 128 != 0
    if unaligned:
        act = split_columns(act, place[2], layout.chips)
        sib = split_columns(sib, place[2], layout.chips)

    extra = [] if total is None else [total]

    def kernel(place_ref, act_ref, sib_ref, *refs):
        o_ref = refs[len(blocks) + len(extra)]
        z, y, core = place_ref[0], place_ref[1], place_ref[2]
        mine = pl.ds(pl.multiple_of(core * rows, 8), rows)
        other = pl.ds(pl.multiple_of((1 - core) * rows, 8), rows)
        k = 0
        if left is not None:
            q = layout.origin(z, y, *left[1:])
            at = pl.ds(0 if unaligned else pl.multiple_of((CORES * q + core) * kc, 128), kc)
            refs[-1][mine, :] = act_ref[q] if unaligned else act_ref[:, at]
            refs[-1][other, :] = sib_ref[q] if unaligned else sib_ref[:, at]
        for i in range(count):
            q = layout.origin(z, y, *found[i][1:])
            start = 0
            for x in found[i][0]:
                depth = x.shape[0]
                block = refs[k][...]
                if unaligned:
                    own, its = act_ref[q], sib_ref[q]
                else:
                    at = pl.ds(pl.multiple_of((CORES * q + core) * kc + start, 128), depth)
                    own, its = act_ref[:, at], sib_ref[:, at]
                for place_of, x in ((mine, own), (other, its)):
                    product = jnp.dot(x, block, preferred_element_type=jnp.float32)
                    if k == 0 and total is None:
                        o_ref[place_of, :] = product
                    elif k == 0:
                        o_ref[place_of, :] = refs[len(blocks)][place_of, :] + product
                    else:
                        o_ref[place_of, :] += product
                start += depth
                k += 1

    shapes = [jax.ShapeDtypeStruct((CORES * rows, width), jnp.float32)]
    if left is not None:
        shapes.append(jax.ShapeDtypeStruct((CORES * rows, kc), act.dtype))
    outs = pl.pallas_call(
        kernel,
        in_specs=[IN_SMEM] + [IN_VMEM] * (2 + len(blocks) + len(extra)),
        out_specs=[IN_VMEM] * len(shapes),
        out_shape=shapes,
        cost_estimate=pl.CostEstimate(
            flops=4 * rows * kc * count * width,
            bytes_accessed=2 * count * kc * (2 * rows + width) + 8 * rows * width,
            transcendentals=0,
        ),
        compiler_params=params(),
        name="partial_rotation",
    )(place, act, sib, *blocks, *extra)
    return outs[0] if left is None else outs


def last_rotation(total, rows, block):
    def kernel(total_ref, rows_ref, block_ref, o_ref):
        o_ref[...] = total_ref[...] + jnp.dot(
            rows_ref[...], block_ref[...], preferred_element_type=jnp.float32
        )

    return pl.pallas_call(
        kernel,
        in_specs=[IN_VMEM] * 3,
        out_specs=IN_VMEM,
        out_shape=jax.ShapeDtypeStruct(total.shape, jnp.float32),
        cost_estimate=pl.CostEstimate(
            flops=2 * rows.size * block.shape[1],
            bytes_accessed=2 * rows.size + 8 * total.size,
            transcendentals=0,
        ),
        compiler_params=params(),
        name="last_rotation",
    )(total, rows, block)


def owned_gradients(layout, mine, other, place, owned):
    tokens, width = mine.shape
    kept = layout.chips * owned

    def kernel(place_ref, mine_ref, other_ref, o_ref):
        slot = lax.broadcasted_iota(jnp.int32, (kept, width), 0)
        column = lax.broadcasted_iota(jnp.int32, (kept, width), 1)
        wanted = (CORES * (slot // owned) + place_ref[2]) * owned + lax.rem(slot, owned)
        pick = jnp.where(wanted == column, 1.0, 0.0).astype(jnp.bfloat16)
        rotated = (mine_ref[...] + other_ref[...]).astype(jnp.bfloat16)
        picked = lax.dot_general(
            pick, rotated, (((1,), (1,)), ((), ())), preferred_element_type=jnp.float32
        )
        o_ref[...] = picked.astype(jnp.bfloat16)

    return pl.pallas_call(
        kernel,
        in_specs=[IN_SMEM, IN_VMEM, IN_VMEM],
        out_specs=IN_VMEM,
        out_shape=jax.ShapeDtypeStruct((kept, tokens), jnp.bfloat16),
        cost_estimate=pl.CostEstimate(
            flops=2 * kept * width * tokens,
            bytes_accessed=8 * tokens * width + 2 * kept * tokens,
            transcendentals=0,
        ),
        compiler_params=params(),
        name="owned_gradients",
    )(place, mine, other)


def chip_sums(grads, mine, other, positions, lengths):
    tokens, width = mine.shape
    seqs = lengths.shape[0]
    kept = grads.shape[0]

    def kernel(lengths_ref, grads_ref, mine_ref, other_ref, positions_ref, o_ref):
        rotated = mine_ref[...] + other_ref[...]
        position = positions_ref[...]
        begin = jnp.int32(0)
        for s in range(seqs):
            end = begin + lengths_ref[s]
            inside = (position >= begin) & (position < end)
            part = jnp.where(inside, rotated, 0.0).astype(jnp.bfloat16)
            sums = jnp.dot(grads_ref[...], part, preferred_element_type=jnp.float32)
            o_ref[:, pl.ds(s * width, width)] = sums.astype(jnp.bfloat16)
            begin = end

    return pl.pallas_call(
        kernel,
        in_specs=[IN_SMEM] + [IN_VMEM] * 4,
        out_specs=IN_VMEM,
        out_shape=jax.ShapeDtypeStruct((kept, seqs * width), jnp.bfloat16),
        cost_estimate=pl.CostEstimate(
            flops=2 * kept * tokens * seqs * width,
            bytes_accessed=8 * tokens * width + 2 * kept * seqs * width,
            transcendentals=0,
        ),
        compiler_params=params(),
        name="chip_sums",
    )(lengths, grads, mine, other, positions)


def squares(groups, lengths, owned):
    seqs = lengths.shape[0]
    chips = groups[0].shape[0] // owned
    widths = [x.shape[1] // seqs for x in groups]

    def kernel(lengths_ref, *refs):
        o_ref = refs[-1]
        total = lengths_ref[0]
        for s in range(1, seqs):
            total = total + lengths_ref[s]
        at = 0
        for ref, width in zip(refs, widths):
            over = jnp.full((owned, width), total, jnp.int32).astype(jnp.float32)
            sums = ref[...].astype(jnp.float32).reshape(chips, owned, seqs * width).sum(axis=0)
            sums = sums * sums
            acc = sums[:, :width]
            for s in range(1, seqs):
                acc = acc + sums[:, s * width:(s + 1) * width]
            o_ref[:, pl.ds(at, width)] = acc / over
            at += width

    return pl.pallas_call(
        kernel,
        in_specs=[IN_SMEM] + [IN_VMEM] * len(groups),
        out_specs=IN_VMEM,
        out_shape=jax.ShapeDtypeStruct((owned, sum(widths)), jnp.float32),
        cost_estimate=pl.CostEstimate(
            flops=2 * sum(x.size for x in groups),
            bytes_accessed=2 * sum(x.size for x in groups),
            transcendentals=0,
        ),
        compiler_params=params(),
        name="squares",
    )(lengths, *groups)


def shards(layout, activations, gradients, basis_a, basis_g, token_index, seq_lengths):
    nz, ny, chips = layout.nz, layout.ny, layout.chips
    rows = activations.shape[0]
    owned = basis_g.shape[1] // (chips * CORES)
    me = lax.axis_index("row")
    core = lax.rem(me, CORES)
    y = lax.rem(me // CORES, ny)
    z = me // (CORES * ny)
    place = jnp.stack([z, y, core]).astype(jnp.int32)

    sib_index = layout.to_sibling(token_index)
    first = core == 0
    positions = jnp.concatenate(
        [jnp.where(first, token_index, sib_index), jnp.where(first, sib_index, token_index)]
    ).reshape(CORES * rows, 1)

    links = Links(layout, 2)
    sib_g = layout.to_sibling(gradients)
    sib_a = layout.to_sibling(activations)
    split = basis_g.shape[0] * 5 // 7 if ny > 1 else 0
    found_g = gather_columns(links, basis_g, split, {nz // 2: [sib_g, sib_a]})
    early = partial_rotation(layout, gradients, sib_g, found_g[:4], place)
    mine_g = partial_rotation(layout, gradients, sib_g, found_g[4:], place, early)
    grads = owned_gradients(layout, mine_g, layout.to_sibling(mine_g), place, owned)

    links.after(early)
    found_a = gather_columns(links, basis_a, 0, {})
    most, rows_left = partial_rotation(
        layout, activations, sib_a, found_a[:-1], place, None, found_a[-1]
    )
    mine_a = last_rotation(most, rows_left, found_a[-1][0][0])
    sums = chip_sums(grads, mine_a, layout.to_sibling(mine_a), positions, seq_lengths)
    groups = [layout.between_chips(sums)]
    return squares(groups, seq_lengths, owned)


def solution(mesh):
    return jax.shard_map(
        functools.partial(shards, Layout(mesh)),
        mesh=mesh,
        in_specs=(
            P(("grp", "row"), None),
            P(("grp", "row"), None),
            P(("grp", "row"), None),
            P(("grp", "row"), None),
            P(("grp", "row")),
            P("grp"),
        ),
        out_specs=P(("grp", "row"), None),
        check_vma=False,
    )
```

```python
import functools

import jax
import jax.numpy as jnp
from jax import lax
from jax.experimental import pallas as pl
from jax.experimental.pallas import tpu as pltpu
from jax.sharding import PartitionSpec as P

CORES = 2
MIB = 1024 * 1024


def params(mib=8):
    return pltpu.CompilerParams(vmem_limit_bytes=mib * MIB)


IN_VMEM = pl.BlockSpec(memory_space=pltpu.VMEM)
IN_SMEM = pl.BlockSpec(memory_space=pltpu.SMEM)
ANYWHERE = pl.BlockSpec(memory_space=pl.ANY)


class Layout:
    def __init__(self, mesh):
        self.chips = mesh.shape["row"] // CORES
        self.ny = max(1, 4 // mesh.shape["grp"])
        if self.chips % self.ny:
            self.ny = 1
        self.nz = self.chips // self.ny

    def device(self, z, y, core):
        return ((z % self.nz) * self.ny + y % self.ny) * CORES + core

    def everyone(self):
        return [(z, y, c) for z in range(self.nz) for y in range(self.ny) for c in range(CORES)]

    def origin(self, z, y, d, h):
        return lax.rem(z + (self.nz - d), self.nz) * self.ny + lax.rem(y + (self.ny - h), self.ny)

    def along_z(self, x, hops):
        pairs = [(self.device(z, y, c), self.device(z + hops, y, c)) for z, y, c in self.everyone()]
        return lax.ppermute(x, "row", pairs)

    def along_y(self, x, hops=1):
        pairs = [(self.device(z, y, c), self.device(z, y + hops, c)) for z, y, c in self.everyone()]
        return lax.ppermute(x, "row", pairs)

    def to_sibling(self, x):
        pairs = [(self.device(z, y, c), self.device(z, y, 1 - c)) for z, y, c in self.everyone()]
        return lax.ppermute(x, "row", pairs)


def split_columns(act, core, chips):
    rows, depth = act.shape
    kc = depth // (chips * CORES)
    mine = lax.dynamic_index_in_dim(act.reshape(rows, chips, CORES, kc), core, 2, keepdims=False)
    return mine.transpose(1, 0, 2)


class Links:
    def __init__(self, layout, window):
        self.layout, self.window = layout, window
        self.done = {"z": [], "y": []}
        self.first = []

    def after(self, *first):
        self.first += first

    def send(self, kind, x, hops):
        done = self.done[kind]
        first = self.first + done[-self.window:len(done) - self.window + 1]
        self.first = []
        if first:
            x = lax.optimization_barrier((x, *first))[0]
        move = self.layout.along_z if kind == "z" else self.layout.along_y
        done.append(move(x, hops))
        return done[-1]


def gather_columns(links, piece, split, gates):
    nz, ny = links.layout.nz, links.layout.ny
    middle = nz // 2
    steps = [(d, 1) for d in range(1, middle + 1)] + [(d, -1) for d in range(nz - 1, middle, -1)]
    steps = sorted(steps, key=lambda s: (min(s[0], nz - s[0]), -s[1]))
    by_z, crossed, found = {0: piece}, {}, [(piece, 0, 0)]

    def cross(d):
        for h in range(1, ny):
            if d == middle and split:
                head = links.send("z", crossed[d - 1, h][:split], 1)
                if split == piece.shape[0]:
                    got = [head]
                else:
                    got = [head, links.send("y", by_z[d][split:], h)]
            else:
                got = [links.send("y", by_z[d], h)]
            crossed[d, h] = got[0]
            found.append((got, d, h))

    last = 0
    for d, sign in steps:
        links.after(*gates.get(d, ()))
        by_z[d] = links.send("z", by_z[(d - sign) % nz], sign)
        found.append(([by_z[d]], d, 0))
        cross(last)
        last = d
    cross(last)
    return [(block if isinstance(block, list) else [block], d, h) for block, d, h in found]


def partial_rotation(layout, act, sib, found, place, total=None, left=None):
    rows = act.shape[0]
    count = len(found)
    blocks = [x for parts, _, _ in found for x in parts]
    kc = sum(x.shape[0] for x in found[0][0])
    width = blocks[0].shape[1]
    unaligned = kc % 128 != 0
    if unaligned:
        act = split_columns(act, place[2], layout.chips)
        sib = split_columns(sib, place[2], layout.chips)

    extra = [] if total is None else [total]

    def kernel(place_ref, act_ref, sib_ref, *refs):
        o_ref = refs[len(blocks) + len(extra)]
        z, y, core = place_ref[0], place_ref[1], place_ref[2]
        mine = pl.ds(pl.multiple_of(core * rows, 8), rows)
        other = pl.ds(pl.multiple_of((1 - core) * rows, 8), rows)
        k = 0
        if left is not None:
            q = layout.origin(z, y, *left[1:])
            at = pl.ds(0 if unaligned else pl.multiple_of((CORES * q + core) * kc, 128), kc)
            refs[-1][mine, :] = act_ref[q] if unaligned else act_ref[:, at]
            refs[-1][other, :] = sib_ref[q] if unaligned else sib_ref[:, at]
        for i in range(count):
            q = layout.origin(z, y, *found[i][1:])
            start = 0
            for x in found[i][0]:
                depth = x.shape[0]
                block = refs[k][...]
                if unaligned:
                    own, its = act_ref[q], sib_ref[q]
                else:
                    at = pl.ds(pl.multiple_of((CORES * q + core) * kc + start, 128), depth)
                    own, its = act_ref[:, at], sib_ref[:, at]
                for place_of, x in ((mine, own), (other, its)):
                    product = jnp.dot(x, block, preferred_element_type=jnp.float32)
                    if k == 0 and total is None:
                        o_ref[place_of, :] = product
                    elif k == 0:
                        o_ref[place_of, :] = refs[len(blocks)][place_of, :] + product
                    else:
                        o_ref[place_of, :] += product
                start += depth
                k += 1

    shapes = [jax.ShapeDtypeStruct((CORES * rows, width), jnp.float32)]
    if left is not None:
        shapes.append(jax.ShapeDtypeStruct((CORES * rows, kc), act.dtype))
    outs = pl.pallas_call(
        kernel,
        in_specs=[IN_SMEM] + [IN_VMEM] * (2 + len(blocks) + len(extra)),
        out_specs=[IN_VMEM] * len(shapes),
        out_shape=shapes,
        cost_estimate=pl.CostEstimate(
            flops=4 * rows * kc * count * width,
            bytes_accessed=2 * count * kc * (2 * rows + width) + 8 * rows * width,
            transcendentals=0,
        ),
        compiler_params=params(),
        name="partial_rotation",
    )(place, act, sib, *blocks, *extra)
    return outs[0] if left is None else outs


def last_rotation(total, rows, blocks):
    width = total.shape[1]

    def kernel(total_ref, rows_ref, *refs):
        sums, at = total_ref[...], 0
        for ref in refs[:-1]:
            x = rows_ref[:, pl.ds(at, ref.shape[0])]
            sums += jnp.dot(x, ref[...], preferred_element_type=jnp.float32)
            at += ref.shape[0]
        refs[-1][...] = sums

    return pl.pallas_call(
        kernel,
        in_specs=[IN_VMEM] * (2 + len(blocks)),
        out_specs=IN_VMEM,
        out_shape=jax.ShapeDtypeStruct(total.shape, jnp.float32),
        cost_estimate=pl.CostEstimate(
            flops=2 * rows.size * width,
            bytes_accessed=2 * rows.size + 8 * total.size,
            transcendentals=0,
        ),
        compiler_params=params(),
        name="last_rotation",
    )(total, rows, *blocks)


def owned_gradients(layout, mine, other, place, owned):
    nz, ny = layout.nz, layout.ny
    tokens, width = mine.shape
    kept = nz * ny * owned

    def kernel(place_ref, mine_ref, other_ref, o_ref):
        slot = lax.broadcasted_iota(jnp.int32, (kept, width), 0)
        column = lax.broadcasted_iota(jnp.int32, (kept, width), 1)
        z, y, core = place_ref[0], place_ref[1], place_ref[2]
        to_y = lax.rem(y + 1 + slot // (nz * owned), ny)
        to_z = lax.rem(z + lax.rem(slot // owned, nz), nz)
        wanted = ((to_z * ny + to_y) * CORES + core) * owned + lax.rem(slot, owned)
        pick = jnp.where(wanted == column, 1.0, 0.0).astype(jnp.bfloat16)
        rotated = (mine_ref[...] + other_ref[...]).astype(jnp.bfloat16)
        picked = lax.dot_general(
            pick, rotated, (((1,), (1,)), ((), ())), preferred_element_type=jnp.float32
        )
        o_ref[...] = picked.astype(jnp.bfloat16)

    return pl.pallas_call(
        kernel,
        in_specs=[IN_SMEM, IN_VMEM, IN_VMEM],
        out_specs=IN_VMEM,
        out_shape=jax.ShapeDtypeStruct((kept, tokens), jnp.bfloat16),
        cost_estimate=pl.CostEstimate(
            flops=2 * kept * width * tokens,
            bytes_accessed=8 * tokens * width + 2 * kept * tokens,
            transcendentals=0,
        ),
        compiler_params=params(),
        name="owned_gradients",
    )(place, mine, other)


def chip_sums(layout, grads, mine, other, positions, lengths, owned, cut):
    nz, ny = layout.nz, layout.ny
    tokens, width = mine.shape
    seqs = lengths.shape[0]
    stay = nz * owned
    rest = width - cut

    def kernel(lengths_ref, grads_ref, mine_ref, other_ref, positions_ref, *refs):
        rotated = mine_ref[...] + other_ref[...]
        position = positions_ref[...]
        begin = jnp.int32(0)
        for s in range(seqs):
            end = begin + lengths_ref[s]
            inside = (position >= begin) & (position < end)
            part = jnp.where(inside, rotated, 0.0).astype(jnp.bfloat16)
            sums = jnp.dot(grads_ref[...], part, preferred_element_type=jnp.float32)
            at = pl.ds(s * cut, cut)
            for d in range(nz):
                for h in range(ny):
                    block = sums[h * stay + d * owned:h * stay + (d + 1) * owned, :cut]
                    refs[d][pl.ds(h * owned, owned), at] = block.astype(refs[d].dtype)
            if rest:
                at = pl.ds(s * rest, rest)
                refs[nz][:, at] = sums[stay:, cut:]
                refs[nz + 1][:, at] = sums[:stay, cut:].astype(jnp.bfloat16)
            begin = end

    shapes = [jax.ShapeDtypeStruct((ny * owned, seqs * cut), jnp.float32)]
    shapes += [jax.ShapeDtypeStruct((ny * owned, seqs * cut), jnp.bfloat16)] * (nz - 1)
    if rest:
        shapes.append(jax.ShapeDtypeStruct((stay, seqs * rest), jnp.float32))
        shapes.append(jax.ShapeDtypeStruct((stay, seqs * rest), jnp.bfloat16))
    return pl.pallas_call(
        kernel,
        in_specs=[IN_SMEM] + [IN_VMEM] * 4,
        out_specs=[IN_VMEM] * len(shapes),
        out_shape=shapes,
        cost_estimate=pl.CostEstimate(
            flops=2 * grads.size * seqs * width,
            bytes_accessed=8 * tokens * width + 2 * grads.shape[0] * seqs * width,
            transcendentals=0,
        ),
        compiler_params=params(),
        name="chip_sums",
    )(lengths, grads, mine, other, positions)


def add_up(kept, came, owned, own):
    count = kept.shape[0] // owned
    width = kept.shape[1]

    def kernel(*refs):
        total = refs[0][...]
        for i in range(len(came)):
            total += refs[1 + i][...].astype(jnp.float32)
        outs = refs[1 + len(came):]
        for i in range(count):
            outs[i][...] = total[i * owned:(i + 1) * owned].astype(outs[i].dtype)

    shapes = [
        jax.ShapeDtypeStruct((owned, width), jnp.float32 if i == own else jnp.bfloat16)
        for i in range(count)
    ]
    return pl.pallas_call(
        kernel,
        in_specs=[IN_VMEM] * (1 + len(came)),
        out_specs=[IN_VMEM] * count,
        out_shape=shapes,
        cost_estimate=pl.CostEstimate(
            flops=kept.size * len(came), bytes_accessed=8 * kept.size, transcendentals=0
        ),
        compiler_params=params(),
        name="add_up",
    )(kept, *came)


def squares(groups, lengths, owned):
    seqs = lengths.shape[0]
    widths = [group[0].shape[1] // seqs for group in groups]

    def kernel(lengths_ref, *refs):
        o_ref = refs[-1]
        tokens = lengths_ref[0]
        for s in range(1, seqs):
            tokens = tokens + lengths_ref[s]
        at, k = 0, 0
        for group, width in zip(groups, widths):
            over = jnp.full((owned, width), tokens, jnp.int32).astype(jnp.float32)
            sums = refs[k][...]
            for ref in refs[k + 1:k + len(group)]:
                sums = sums + ref[...].astype(jnp.float32)
            k += len(group)
            sums = sums * sums
            acc = sums[:, :width]
            for s in range(1, seqs):
                acc = acc + sums[:, s * width:(s + 1) * width]
            o_ref[:, pl.ds(at, width)] = acc / over
            at += width

    flat = [x for group in groups for x in group]
    return pl.pallas_call(
        kernel,
        in_specs=[IN_SMEM] + [IN_VMEM] * len(flat),
        out_specs=IN_VMEM,
        out_shape=jax.ShapeDtypeStruct((owned, sum(widths)), jnp.float32),
        cost_estimate=pl.CostEstimate(
            flops=2 * sum(x.size for x in flat),
            bytes_accessed=2 * sum(x.size for x in flat),
            transcendentals=0,
        ),
        compiler_params=params(),
        name="squares",
    )(lengths, *flat)


def scatter_sums(layout, sums, owned):
    nz, ny = layout.nz, layout.ny
    if ny == 1:
        return [[sums[0]] + [layout.along_z(sums[d], d) for d in range(1, nz)]]
    crossed = [layout.along_y(sums[nz + 1])]
    came = [layout.along_z(sums[d], d) for d in range(1, nz)]
    by_z = add_up(sums[nz], crossed, owned, 0)
    second = [by_z[0]] + [layout.along_z(by_z[d], d) for d in range(1, nz)]
    came[0] = lax.optimization_barrier((came[0], by_z[1]))[0]
    by_y = add_up(sums[0], came, owned, 1)
    return [[by_y[1], layout.along_y(by_y[0])], second]


def shards(layout, activations, gradients, basis_a, basis_g, token_index, seq_lengths):
    nz, ny, chips = layout.nz, layout.ny, layout.chips
    rows = activations.shape[0]
    owned = basis_g.shape[1] // (chips * CORES)
    me = lax.axis_index("row")
    core = lax.rem(me, CORES)
    y = lax.rem(me // CORES, ny)
    z = me // (CORES * ny)
    place = jnp.stack([z, y, core]).astype(jnp.int32)

    sib_index = layout.to_sibling(token_index)
    first = core == 0
    positions = jnp.concatenate(
        [jnp.where(first, token_index, sib_index), jnp.where(first, sib_index, token_index)]
    ).reshape(CORES * rows, 1)

    links = Links(layout, 2)
    sib_g = layout.to_sibling(gradients)
    sib_a = layout.to_sibling(activations)
    split = [basis_g.shape[0] * 4 // 7, basis_a.shape[0] // 2] if ny > 1 else [0, 0]
    found_g = gather_columns(links, basis_g, split[0], {nz // 2: [sib_g, sib_a]})
    early = partial_rotation(layout, gradients, sib_g, found_g[:4], place)
    mine_g = partial_rotation(layout, gradients, sib_g, found_g[4:], place, early)
    grads = owned_gradients(layout, mine_g, layout.to_sibling(mine_g), place, owned)

    links.after(early)
    found_a = gather_columns(links, basis_a, split[1], {})
    most, rows_left = partial_rotation(
        layout, activations, sib_a, found_a[:-1], place, None, found_a[-1]
    )
    mine_a = last_rotation(most, rows_left, found_a[-1][0])
    cut = basis_a.shape[1] // ny
    sums = chip_sums(
        layout, grads, mine_a, layout.to_sibling(mine_a), positions, seq_lengths, owned, cut
    )
    return squares(scatter_sums(layout, sums, owned), seq_lengths, owned)


def solution(mesh):
    return jax.shard_map(
        functools.partial(shards, Layout(mesh)),
        mesh=mesh,
        in_specs=(
            P(("grp", "row"), None),
            P(("grp", "row"), None),
            P(("grp", "row"), None),
            P(("grp", "row"), None),
            P(("grp", "row")),
            P("grp"),
        ),
        out_specs=P(("grp", "row"), None),
        check_vma=False,
    )
```

```python
import functools

import jax
import jax.numpy as jnp
from jax import lax
from jax.experimental import pallas as pl
from jax.experimental.pallas import tpu as pltpu
from jax.sharding import PartitionSpec as P

CORES = 2
MIB = 1024 * 1024


def params(mib=8):
    return pltpu.CompilerParams(vmem_limit_bytes=mib * MIB)


IN_VMEM = pl.BlockSpec(memory_space=pltpu.VMEM)
IN_SMEM = pl.BlockSpec(memory_space=pltpu.SMEM)
ANYWHERE = pl.BlockSpec(memory_space=pl.ANY)


class Layout:
    def __init__(self, mesh):
        self.chips = mesh.shape["row"] // CORES
        self.ny = max(1, 4 // mesh.shape["grp"])
        if self.chips % self.ny:
            self.ny = 1
        self.nz = self.chips // self.ny

    def device(self, z, y, core):
        return ((z % self.nz) * self.ny + y % self.ny) * CORES + core

    def everyone(self):
        return [(z, y, c) for z in range(self.nz) for y in range(self.ny) for c in range(CORES)]

    def origin(self, z, y, d, h):
        return lax.rem(z + (self.nz - d), self.nz) * self.ny + lax.rem(y + (self.ny - h), self.ny)

    def along_z(self, x, hops):
        pairs = [(self.device(z, y, c), self.device(z + hops, y, c)) for z, y, c in self.everyone()]
        return lax.ppermute(x, "row", pairs)

    def along_y(self, x, hops=1):
        pairs = [(self.device(z, y, c), self.device(z, y + hops, c)) for z, y, c in self.everyone()]
        return lax.ppermute(x, "row", pairs)

    def to_sibling(self, x):
        pairs = [(self.device(z, y, c), self.device(z, y, 1 - c)) for z, y, c in self.everyone()]
        return lax.ppermute(x, "row", pairs)


def split_columns(act, core, chips):
    rows, depth = act.shape
    kc = depth // (chips * CORES)
    mine = lax.dynamic_index_in_dim(act.reshape(rows, chips, CORES, kc), core, 2, keepdims=False)
    return mine.transpose(1, 0, 2)


class Links:
    def __init__(self, layout, window):
        self.layout, self.window = layout, window
        self.done = {kind: [] for kind in window}
        self.first = []

    def after(self, *first):
        self.first += first

    def send(self, kind, x, hops):
        done, window = self.done[kind], self.window[kind]
        first = self.first + done[-window:len(done) - window + 1]
        self.first = []
        if first:
            x = lax.optimization_barrier((x, *first))[0]
        move = self.layout.along_z if kind == "z" else self.layout.along_y
        done.append(move(x, hops))
        return done[-1]


class Gather:
    def __init__(self, links, piece, split):
        self.links, self.piece, self.split = links, piece, split
        self.nz, self.ny = links.layout.nz, links.layout.ny
        self.middle = self.nz // 2
        self.by_z, self.crossed, self.found = {0: piece}, {}, [([piece], 0, 0)]
        hops = [(d, 1) for d in range(1, self.middle + 1)]
        hops += [(d, -1) for d in range(self.nz - 1, self.middle, -1)]
        hops.sort(key=lambda s: (min(s[0], self.nz - s[0]), -s[1]))
        self.steps = [(d, sign, last) for (d, sign), (last, _) in zip(hops, [(0, 0)] + hops)]
        self.steps.append((None, 0, hops[-1][0]))

    def step(self):
        d, sign, last = self.steps.pop(0)
        if d is not None:
            self.by_z[d] = self.links.send("z", self.by_z[(d - sign) % self.nz], sign)
            self.found.append(([self.by_z[d]], d, 0))
        for h in range(1, self.ny):
            got = []
            if last == self.middle and self.split:
                got.append(self.links.send("z", self.crossed[last - 1, h][:self.split], 1))
            if not got or self.split < self.piece.shape[0]:
                start = self.split if got else 0
                got.append(self.links.send("y", self.by_z[last][start:], h))
            self.crossed[last, h] = got[0]
            self.found.append((got, last, h))


def partial_rotation(layout, act, sib, found, place, total=None, left=None):
    rows = act.shape[0]
    count = len(found)
    blocks = [x for parts, _, _ in found for x in parts]
    kc = sum(x.shape[0] for x in found[0][0])
    width = blocks[0].shape[1]
    unaligned = kc % 128 != 0
    if unaligned:
        act = split_columns(act, place[2], layout.chips)
        sib = split_columns(sib, place[2], layout.chips)

    extra = [] if total is None else [total]

    def kernel(place_ref, act_ref, sib_ref, *refs):
        o_ref = refs[len(blocks) + len(extra)]
        z, y, core = place_ref[0], place_ref[1], place_ref[2]
        mine = pl.ds(pl.multiple_of(core * rows, 8), rows)
        other = pl.ds(pl.multiple_of((1 - core) * rows, 8), rows)
        k = 0
        if left is not None:
            q = layout.origin(z, y, *left[1:])
            at = pl.ds(0 if unaligned else pl.multiple_of((CORES * q + core) * kc, 128), kc)
            refs[-1][mine, :] = act_ref[q] if unaligned else act_ref[:, at]
            refs[-1][other, :] = sib_ref[q] if unaligned else sib_ref[:, at]
        for i in range(count):
            q = layout.origin(z, y, *found[i][1:])
            start = 0
            for x in found[i][0]:
                depth = x.shape[0]
                block = refs[k][...]
                if unaligned:
                    own, its = act_ref[q], sib_ref[q]
                else:
                    at = pl.ds(pl.multiple_of((CORES * q + core) * kc + start, 128), depth)
                    own, its = act_ref[:, at], sib_ref[:, at]
                for place_of, x in ((mine, own), (other, its)):
                    product = jnp.dot(x, block, preferred_element_type=jnp.float32)
                    if k == 0 and total is None:
                        o_ref[place_of, :] = product
                    elif k == 0:
                        o_ref[place_of, :] = refs[len(blocks)][place_of, :] + product
                    else:
                        o_ref[place_of, :] += product
                start += depth
                k += 1

    shapes = [jax.ShapeDtypeStruct((CORES * rows, width), jnp.float32)]
    if left is not None:
        shapes.append(jax.ShapeDtypeStruct((CORES * rows, kc), act.dtype))
    outs = pl.pallas_call(
        kernel,
        in_specs=[IN_SMEM] + [IN_VMEM] * (2 + len(blocks) + len(extra)),
        out_specs=[IN_VMEM] * len(shapes),
        out_shape=shapes,
        cost_estimate=pl.CostEstimate(
            flops=4 * rows * kc * count * width,
            bytes_accessed=2 * count * kc * (2 * rows + width) + 8 * rows * width,
            transcendentals=0,
        ),
        compiler_params=params(),
        name="partial_rotation",
    )(place, act, sib, *blocks, *extra)
    return outs[0] if left is None else outs


def last_rotation(total, rows, blocks):
    width = total.shape[1]

    def kernel(total_ref, rows_ref, *refs):
        sums, at = total_ref[...], 0
        for ref in refs[:-1]:
            x = rows_ref[:, pl.ds(at, ref.shape[0])]
            sums += jnp.dot(x, ref[...], preferred_element_type=jnp.float32)
            at += ref.shape[0]
        refs[-1][...] = sums

    return pl.pallas_call(
        kernel,
        in_specs=[IN_VMEM] * (2 + len(blocks)),
        out_specs=IN_VMEM,
        out_shape=jax.ShapeDtypeStruct(total.shape, jnp.float32),
        cost_estimate=pl.CostEstimate(
            flops=2 * rows.size * width,
            bytes_accessed=2 * rows.size + 8 * total.size,
            transcendentals=0,
        ),
        compiler_params=params(),
        name="last_rotation",
    )(total, rows, *blocks)


def owned_gradients(layout, mine, other, place, owned):
    nz, ny = layout.nz, layout.ny
    tokens, width = mine.shape
    kept = nz * ny * owned

    def kernel(place_ref, mine_ref, other_ref, o_ref):
        slot = lax.broadcasted_iota(jnp.int32, (kept, width), 0)
        column = lax.broadcasted_iota(jnp.int32, (kept, width), 1)
        z, y, core = place_ref[0], place_ref[1], place_ref[2]
        to_y = lax.rem(y + 1 + slot // (nz * owned), ny)
        to_z = lax.rem(z + lax.rem(slot // owned, nz), nz)
        wanted = ((to_z * ny + to_y) * CORES + core) * owned + lax.rem(slot, owned)
        pick = jnp.where(wanted == column, 1.0, 0.0).astype(jnp.bfloat16)
        rotated = (mine_ref[...] + other_ref[...]).astype(jnp.bfloat16)
        picked = lax.dot_general(
            pick, rotated, (((1,), (1,)), ((), ())), preferred_element_type=jnp.float32
        )
        o_ref[...] = picked.astype(jnp.bfloat16)

    return pl.pallas_call(
        kernel,
        in_specs=[IN_SMEM, IN_VMEM, IN_VMEM],
        out_specs=IN_VMEM,
        out_shape=jax.ShapeDtypeStruct((kept, tokens), jnp.bfloat16),
        cost_estimate=pl.CostEstimate(
            flops=2 * kept * width * tokens,
            bytes_accessed=8 * tokens * width + 2 * kept * tokens,
            transcendentals=0,
        ),
        compiler_params=params(),
        name="owned_gradients",
    )(place, mine, other)


def chip_sums(layout, grads, mine, other, positions, lengths, owned, cut):
    nz, ny = layout.nz, layout.ny
    tokens, width = mine.shape
    seqs = lengths.shape[0]
    stay = nz * owned
    rest = width - cut

    def kernel(lengths_ref, grads_ref, mine_ref, other_ref, positions_ref, *refs):
        rotated = mine_ref[...] + other_ref[...]
        position = positions_ref[...]
        begin = jnp.int32(0)
        for s in range(seqs):
            end = begin + lengths_ref[s]
            inside = (position >= begin) & (position < end)
            part = jnp.where(inside, rotated, 0.0).astype(jnp.bfloat16)
            sums = jnp.dot(grads_ref[...], part, preferred_element_type=jnp.float32)
            at = pl.ds(s * cut, cut)
            for d in range(nz):
                for h in range(ny):
                    block = sums[h * stay + d * owned:h * stay + (d + 1) * owned, :cut]
                    refs[d][pl.ds(h * owned, owned), at] = block.astype(refs[d].dtype)
            if rest:
                at = pl.ds(s * rest, rest)
                refs[nz][:, at] = sums[stay:, cut:]
                refs[nz + 1][:, at] = sums[:stay, cut:].astype(jnp.bfloat16)
            begin = end

    shapes = [jax.ShapeDtypeStruct((ny * owned, seqs * cut), jnp.float32)]
    shapes += [jax.ShapeDtypeStruct((ny * owned, seqs * cut), jnp.bfloat16)] * (nz - 1)
    if rest:
        shapes.append(jax.ShapeDtypeStruct((stay, seqs * rest), jnp.float32))
        shapes.append(jax.ShapeDtypeStruct((stay, seqs * rest), jnp.bfloat16))
    return pl.pallas_call(
        kernel,
        in_specs=[IN_SMEM] + [IN_VMEM] * 4,
        out_specs=[IN_VMEM] * len(shapes),
        out_shape=shapes,
        cost_estimate=pl.CostEstimate(
            flops=2 * grads.size * seqs * width,
            bytes_accessed=8 * tokens * width + 2 * grads.shape[0] * seqs * width,
            transcendentals=0,
        ),
        compiler_params=params(),
        name="chip_sums",
    )(lengths, grads, mine, other, positions)


def add_up(kept, came, owned, own):
    count = kept.shape[0] // owned
    width = kept.shape[1]

    def kernel(*refs):
        total = refs[0][...]
        for i in range(len(came)):
            total += refs[1 + i][...].astype(jnp.float32)
        outs = refs[1 + len(came):]
        for i in range(count):
            outs[i][...] = total[i * owned:(i + 1) * owned].astype(outs[i].dtype)

    shapes = [
        jax.ShapeDtypeStruct((owned, width), jnp.float32 if i == own else jnp.bfloat16)
        for i in range(count)
    ]
    return pl.pallas_call(
        kernel,
        in_specs=[IN_VMEM] * (1 + len(came)),
        out_specs=[IN_VMEM] * count,
        out_shape=shapes,
        cost_estimate=pl.CostEstimate(
            flops=kept.size * len(came), bytes_accessed=8 * kept.size, transcendentals=0
        ),
        compiler_params=params(),
        name="add_up",
    )(kept, *came)


def squares(groups, lengths, owned):
    seqs = lengths.shape[0]
    widths = [group[0].shape[1] // seqs for group in groups]

    def kernel(lengths_ref, *refs):
        o_ref = refs[-1]
        tokens = lengths_ref[0]
        for s in range(1, seqs):
            tokens = tokens + lengths_ref[s]
        at, k = 0, 0
        for group, width in zip(groups, widths):
            over = jnp.full((owned, width), tokens, jnp.int32).astype(jnp.float32)
            sums = refs[k][...]
            for ref in refs[k + 1:k + len(group)]:
                sums = sums + ref[...].astype(jnp.float32)
            k += len(group)
            sums = sums * sums
            acc = sums[:, :width]
            for s in range(1, seqs):
                acc = acc + sums[:, s * width:(s + 1) * width]
            o_ref[:, pl.ds(at, width)] = acc / over
            at += width

    flat = [x for group in groups for x in group]
    return pl.pallas_call(
        kernel,
        in_specs=[IN_SMEM] + [IN_VMEM] * len(flat),
        out_specs=IN_VMEM,
        out_shape=jax.ShapeDtypeStruct((owned, sum(widths)), jnp.float32),
        cost_estimate=pl.CostEstimate(
            flops=2 * sum(x.size for x in flat),
            bytes_accessed=2 * sum(x.size for x in flat),
            transcendentals=0,
        ),
        compiler_params=params(),
        name="squares",
    )(lengths, *flat)


def scatter_sums(layout, sums, owned):
    nz, ny = layout.nz, layout.ny
    if ny == 1:
        return [[sums[0]] + [layout.along_z(sums[d], d) for d in range(1, nz)]]
    crossed = [layout.along_y(sums[nz + 1])]
    came = [layout.along_z(sums[d], d) for d in range(1, nz)]
    by_z = add_up(sums[nz], crossed, owned, 0)
    second = [by_z[0]] + [layout.along_z(by_z[d], d) for d in range(1, nz)]
    came[0] = lax.optimization_barrier((came[0], by_z[1]))[0]
    by_y = add_up(sums[0], came, owned, 1)
    return [[by_y[1], layout.along_y(by_y[0])], second]


def shards(layout, activations, gradients, basis_a, basis_g, token_index, seq_lengths):
    nz, ny, chips = layout.nz, layout.ny, layout.chips
    rows = activations.shape[0]
    owned = basis_g.shape[1] // (chips * CORES)
    me = lax.axis_index("row")
    core = lax.rem(me, CORES)
    y = lax.rem(me // CORES, ny)
    z = me // (CORES * ny)
    place = jnp.stack([z, y, core]).astype(jnp.int32)

    sib_index = layout.to_sibling(token_index)
    first = core == 0
    positions = jnp.concatenate(
        [jnp.where(first, token_index, sib_index), jnp.where(first, sib_index, token_index)]
    ).reshape(CORES * rows, 1)

    links = Links(layout, {"z": 3, "y": 2})
    sib_g = layout.to_sibling(gradients)
    sib_a = layout.to_sibling(activations)
    split = [basis_g.shape[0] * 4 // 7, basis_a.shape[0] // 2] if ny > 1 else [0, 0]
    from_g, from_a = Gather(links, basis_g, split[0]), Gather(links, basis_a, split[1])
    from_g.step()
    from_g.step()
    early = partial_rotation(layout, gradients, sib_g, from_g.found[:4], place)
    links.after(sib_g, sib_a)
    while from_a.steps:
        if len(from_a.steps) == 2:
            links.after(early)
        from_a.step()
        if from_g.steps:
            from_g.step()
    found_g, found_a = from_g.found, from_a.found
    mine_g = partial_rotation(layout, gradients, sib_g, found_g[4:], place, early)
    grads = owned_gradients(layout, mine_g, layout.to_sibling(mine_g), place, owned)

    most, rows_left = partial_rotation(
        layout, activations, sib_a, found_a[:-1], place, None, found_a[-1]
    )
    mine_a = last_rotation(most, rows_left, found_a[-1][0])
    cut = basis_a.shape[1] // ny
    sums = chip_sums(
        layout, grads, mine_a, layout.to_sibling(mine_a), positions, seq_lengths, owned, cut
    )
    return squares(scatter_sums(layout, sums, owned), seq_lengths, owned)


def solution(mesh):
    return jax.shard_map(
        functools.partial(shards, Layout(mesh)),
        mesh=mesh,
        in_specs=(
            P(("grp", "row"), None),
            P(("grp", "row"), None),
            P(("grp", "row"), None),
            P(("grp", "row"), None),
            P(("grp", "row")),
            P("grp"),
        ),
        out_specs=P(("grp", "row"), None),
        check_vma=False,
    )
```

```python
import functools

import jax
import jax.numpy as jnp
from jax import lax
from jax.experimental import pallas as pl
from jax.experimental.pallas import tpu as pltpu
from jax.sharding import PartitionSpec as P

CORES = 2
MIB = 1024 * 1024


def params(mib=8):
    return pltpu.CompilerParams(vmem_limit_bytes=mib * MIB)


IN_VMEM = pl.BlockSpec(memory_space=pltpu.VMEM)
IN_SMEM = pl.BlockSpec(memory_space=pltpu.SMEM)
ANYWHERE = pl.BlockSpec(memory_space=pl.ANY)


class Layout:
    def __init__(self, mesh):
        self.chips = mesh.shape["row"] // CORES
        self.ny = max(1, 4 // mesh.shape["grp"])
        if self.chips % self.ny:
            self.ny = 1
        self.nz = self.chips // self.ny

    def device(self, z, y, core):
        return ((z % self.nz) * self.ny + y % self.ny) * CORES + core

    def everyone(self):
        return [(z, y, c) for z in range(self.nz) for y in range(self.ny) for c in range(CORES)]

    def origin(self, z, y, d, h):
        return lax.rem(z + (self.nz - d), self.nz) * self.ny + lax.rem(y + (self.ny - h), self.ny)

    def along_z(self, x, hops):
        pairs = [(self.device(z, y, c), self.device(z + hops, y, c)) for z, y, c in self.everyone()]
        return lax.ppermute(x, "row", pairs)

    def along_y(self, x, hops=1):
        pairs = [(self.device(z, y, c), self.device(z, y + hops, c)) for z, y, c in self.everyone()]
        return lax.ppermute(x, "row", pairs)

    def to_sibling(self, x):
        pairs = [(self.device(z, y, c), self.device(z, y, 1 - c)) for z, y, c in self.everyone()]
        return lax.ppermute(x, "row", pairs)


def split_columns(act, core, chips):
    rows, depth = act.shape
    kc = depth // (chips * CORES)
    mine = lax.dynamic_index_in_dim(act.reshape(rows, chips, CORES, kc), core, 2, keepdims=False)
    return mine.transpose(1, 0, 2)


class Links:
    def __init__(self, layout, window):
        self.layout, self.window = layout, window
        self.done = {kind: [] for kind in window}
        self.first = []

    def after(self, *first):
        self.first += first

    def send(self, kind, x, hops):
        done, window = self.done[kind], self.window[kind]
        first = self.first + done[-window:len(done) - window + 1]
        self.first = []
        if first:
            x = lax.optimization_barrier((x, *first))[0]
        move = self.layout.along_z if kind == "z" else self.layout.along_y
        done.append(move(x, hops))
        return done[-1]


class Gather:
    def __init__(self, links, piece, split):
        self.links, self.piece, self.split = links, piece, split
        self.nz, self.ny = links.layout.nz, links.layout.ny
        self.middle = self.nz // 2
        self.by_z, self.crossed, self.found = {0: piece}, {}, [([piece], 0, 0)]
        hops = [(d, 1) for d in range(1, self.middle + 1)]
        hops += [(d, -1) for d in range(self.nz - 1, self.middle, -1)]
        hops.sort(key=lambda s: (min(s[0], self.nz - s[0]), -s[1]))
        self.steps = [(d, sign, last) for (d, sign), (last, _) in zip(hops, [(0, 0)] + hops)]
        self.steps.append((None, 0, hops[-1][0]))

    def step(self):
        d, sign, last = self.steps.pop(0)
        if d is not None:
            self.by_z[d] = self.links.send("z", self.by_z[(d - sign) % self.nz], sign)
            self.found.append(([self.by_z[d]], d, 0))
        for h in range(1, self.ny):
            got = []
            if last == self.middle and self.split:
                got.append(self.links.send("z", self.crossed[last - 1, h][:self.split], 1))
            if not got or self.split < self.piece.shape[0]:
                start = self.split if got else 0
                got.append(self.links.send("y", self.by_z[last][start:], h))
            self.crossed[last, h] = got[0]
            self.found.append((got, last, h))


def partial_rotation(layout, act, sib, found, place, total=None, left=None):
    rows = act.shape[0]
    count = len(found)
    blocks = [x for parts, _, _ in found for x in parts]
    kc = sum(x.shape[0] for x in found[0][0])
    width = blocks[0].shape[1]
    unaligned = kc % 128 != 0
    if unaligned:
        act = split_columns(act, place[2], layout.chips)
        sib = split_columns(sib, place[2], layout.chips)

    extra = [] if total is None else [total]

    def kernel(place_ref, act_ref, sib_ref, *refs):
        o_ref = refs[len(blocks) + len(extra)]
        z, y, core = place_ref[0], place_ref[1], place_ref[2]
        mine = pl.ds(pl.multiple_of(core * rows, 8), rows)
        other = pl.ds(pl.multiple_of((1 - core) * rows, 8), rows)
        k = 0
        if left is not None:
            q = layout.origin(z, y, *left[1:])
            at = pl.ds(0 if unaligned else pl.multiple_of((CORES * q + core) * kc, 128), kc)
            refs[-1][mine, :] = act_ref[q] if unaligned else act_ref[:, at]
            refs[-1][other, :] = sib_ref[q] if unaligned else sib_ref[:, at]
        for i in range(count):
            q = layout.origin(z, y, *found[i][1:])
            start = 0
            for x in found[i][0]:
                depth = x.shape[0]
                block = refs[k][...]
                if unaligned:
                    own, its = act_ref[q], sib_ref[q]
                else:
                    at = pl.ds(pl.multiple_of((CORES * q + core) * kc + start, 128), depth)
                    own, its = act_ref[:, at], sib_ref[:, at]
                for place_of, x in ((mine, own), (other, its)):
                    product = jnp.dot(x, block, preferred_element_type=jnp.float32)
                    if k == 0 and total is None:
                        o_ref[place_of, :] = product
                    elif k == 0:
                        o_ref[place_of, :] = refs[len(blocks)][place_of, :] + product
                    else:
                        o_ref[place_of, :] += product
                start += depth
                k += 1

    shapes = [jax.ShapeDtypeStruct((CORES * rows, width), jnp.float32)]
    if left is not None:
        shapes.append(jax.ShapeDtypeStruct((CORES * rows, kc), act.dtype))
    outs = pl.pallas_call(
        kernel,
        in_specs=[IN_SMEM] + [IN_VMEM] * (2 + len(blocks) + len(extra)),
        out_specs=[IN_VMEM] * len(shapes),
        out_shape=shapes,
        cost_estimate=pl.CostEstimate(
            flops=4 * rows * kc * count * width,
            bytes_accessed=2 * count * kc * (2 * rows + width) + 8 * rows * width,
            transcendentals=0,
        ),
        compiler_params=params(),
        name="partial_rotation",
    )(place, act, sib, *blocks, *extra)
    return outs[0] if left is None else outs


def last_rotation(total, rows, blocks):
    width = total.shape[1]

    def kernel(total_ref, rows_ref, *refs):
        sums, at = total_ref[...], 0
        for ref in refs[:-1]:
            x = rows_ref[:, pl.ds(at, ref.shape[0])]
            sums += jnp.dot(x, ref[...], preferred_element_type=jnp.float32)
            at += ref.shape[0]
        refs[-1][...] = sums

    return pl.pallas_call(
        kernel,
        in_specs=[IN_VMEM] * (2 + len(blocks)),
        out_specs=IN_VMEM,
        out_shape=jax.ShapeDtypeStruct(total.shape, jnp.float32),
        cost_estimate=pl.CostEstimate(
            flops=2 * rows.size * width,
            bytes_accessed=2 * rows.size + 8 * total.size,
            transcendentals=0,
        ),
        compiler_params=params(),
        name="last_rotation",
    )(total, rows, *blocks)


def owned_gradients(layout, mine, other, place, owned):
    nz, ny = layout.nz, layout.ny
    tokens, width = mine.shape
    kept = nz * ny * owned

    def kernel(place_ref, mine_ref, other_ref, o_ref):
        slot = lax.broadcasted_iota(jnp.int32, (kept, width), 0)
        column = lax.broadcasted_iota(jnp.int32, (kept, width), 1)
        z, y, core = place_ref[0], place_ref[1], place_ref[2]
        to_y = lax.rem(y + 1 + slot // (nz * owned), ny)
        to_z = lax.rem(z + lax.rem(slot // owned, nz), nz)
        wanted = ((to_z * ny + to_y) * CORES + core) * owned + lax.rem(slot, owned)
        pick = jnp.where(wanted == column, 1.0, 0.0).astype(jnp.bfloat16)
        rotated = (mine_ref[...] + other_ref[...]).astype(jnp.bfloat16)
        picked = lax.dot_general(
            pick, rotated, (((1,), (1,)), ((), ())), preferred_element_type=jnp.float32
        )
        o_ref[...] = picked.astype(jnp.bfloat16)

    return pl.pallas_call(
        kernel,
        in_specs=[IN_SMEM, IN_VMEM, IN_VMEM],
        out_specs=IN_VMEM,
        out_shape=jax.ShapeDtypeStruct((kept, tokens), jnp.bfloat16),
        cost_estimate=pl.CostEstimate(
            flops=2 * kept * width * tokens,
            bytes_accessed=8 * tokens * width + 2 * kept * tokens,
            transcendentals=0,
        ),
        compiler_params=params(),
        name="owned_gradients",
    )(place, mine, other)


def chip_sums(layout, grads, mine, other, positions, lengths, owned, cut):
    nz, ny = layout.nz, layout.ny
    tokens, width = mine.shape
    seqs = lengths.shape[0]
    stay = nz * owned
    rest = width - cut

    def kernel(lengths_ref, grads_ref, mine_ref, other_ref, positions_ref, *refs):
        rotated = mine_ref[...] + other_ref[...]
        position = positions_ref[...]
        begin = jnp.int32(0)
        for s in range(seqs):
            end = begin + lengths_ref[s]
            inside = (position >= begin) & (position < end)
            part = jnp.where(inside, rotated, 0.0).astype(jnp.bfloat16)
            sums = jnp.dot(grads_ref[...], part, preferred_element_type=jnp.float32)
            at = pl.ds(s * cut, cut)
            for d in range(nz):
                for h in range(ny):
                    block = sums[h * stay + d * owned:h * stay + (d + 1) * owned, :cut]
                    refs[d][pl.ds(h * owned, owned), at] = block.astype(refs[d].dtype)
            if rest:
                at = pl.ds(s * rest, rest)
                refs[nz][:, at] = sums[stay:, cut:]
                refs[nz + 1][:, at] = sums[:stay, cut:].astype(jnp.bfloat16)
            begin = end

    shapes = [jax.ShapeDtypeStruct((ny * owned, seqs * cut), jnp.float32)]
    shapes += [jax.ShapeDtypeStruct((ny * owned, seqs * cut), jnp.bfloat16)] * (nz - 1)
    if rest:
        shapes.append(jax.ShapeDtypeStruct((stay, seqs * rest), jnp.float32))
        shapes.append(jax.ShapeDtypeStruct((stay, seqs * rest), jnp.bfloat16))
    return pl.pallas_call(
        kernel,
        in_specs=[IN_SMEM] + [IN_VMEM] * 4,
        out_specs=[IN_VMEM] * len(shapes),
        out_shape=shapes,
        cost_estimate=pl.CostEstimate(
            flops=2 * grads.size * seqs * width,
            bytes_accessed=8 * tokens * width + 2 * grads.shape[0] * seqs * width,
            transcendentals=0,
        ),
        compiler_params=params(),
        name="chip_sums",
    )(lengths, grads, mine, other, positions)


def add_up(kept, came, owned, own):
    count = kept.shape[0] // owned
    width = kept.shape[1]

    def kernel(*refs):
        total = refs[0][...]
        for i in range(len(came)):
            total += refs[1 + i][...].astype(jnp.float32)
        outs = refs[1 + len(came):]
        for i in range(count):
            outs[i][...] = total[i * owned:(i + 1) * owned].astype(outs[i].dtype)

    shapes = [
        jax.ShapeDtypeStruct((owned, width), jnp.float32 if i == own else jnp.bfloat16)
        for i in range(count)
    ]
    return pl.pallas_call(
        kernel,
        in_specs=[IN_VMEM] * (1 + len(came)),
        out_specs=[IN_VMEM] * count,
        out_shape=shapes,
        cost_estimate=pl.CostEstimate(
            flops=kept.size * len(came), bytes_accessed=8 * kept.size, transcendentals=0
        ),
        compiler_params=params(),
        name="add_up",
    )(kept, *came)


def squares(groups, lengths, owned):
    seqs = lengths.shape[0]
    widths = [group[0].shape[1] // seqs for group in groups]

    def kernel(lengths_ref, *refs):
        o_ref = refs[-1]
        tokens = lengths_ref[0]
        for s in range(1, seqs):
            tokens = tokens + lengths_ref[s]
        at, k = 0, 0
        for group, width in zip(groups, widths):
            over = jnp.full((owned, width), tokens, jnp.int32).astype(jnp.float32)
            sums = refs[k][...]
            for ref in refs[k + 1:k + len(group)]:
                sums = sums + ref[...].astype(jnp.float32)
            k += len(group)
            sums = sums * sums
            acc = sums[:, :width]
            for s in range(1, seqs):
                acc = acc + sums[:, s * width:(s + 1) * width]
            o_ref[:, pl.ds(at, width)] = acc / over
            at += width

    flat = [x for group in groups for x in group]
    return pl.pallas_call(
        kernel,
        in_specs=[IN_SMEM] + [IN_VMEM] * len(flat),
        out_specs=IN_VMEM,
        out_shape=jax.ShapeDtypeStruct((owned, sum(widths)), jnp.float32),
        cost_estimate=pl.CostEstimate(
            flops=2 * sum(x.size for x in flat),
            bytes_accessed=2 * sum(x.size for x in flat),
            transcendentals=0,
        ),
        compiler_params=params(),
        name="squares",
    )(lengths, *flat)


def scatter_sums(layout, sums, owned):
    nz, ny = layout.nz, layout.ny
    if ny == 1:
        return [[sums[0]] + [layout.along_z(sums[d], d) for d in range(1, nz)]]
    crossed = [layout.along_y(sums[nz + 1])]
    came = [layout.along_z(sums[d], d) for d in range(1, nz)]
    by_z = add_up(sums[nz], crossed, owned, 0)
    second = [by_z[0]] + [layout.along_z(by_z[d], d) for d in range(1, nz)]
    came[0] = lax.optimization_barrier((came[0], by_z[1]))[0]
    by_y = add_up(sums[0], came, owned, 1)
    return [[by_y[1], layout.along_y(by_y[0])], second]


def shards(layout, activations, gradients, basis_a, basis_g, token_index, seq_lengths):
    nz, ny, chips = layout.nz, layout.ny, layout.chips
    rows = activations.shape[0]
    owned = basis_g.shape[1] // (chips * CORES)
    me = lax.axis_index("row")
    core = lax.rem(me, CORES)
    y = lax.rem(me // CORES, ny)
    z = me // (CORES * ny)
    place = jnp.stack([z, y, core]).astype(jnp.int32)

    sib_index = layout.to_sibling(token_index)
    first = core == 0
    positions = jnp.concatenate(
        [jnp.where(first, token_index, sib_index), jnp.where(first, sib_index, token_index)]
    ).reshape(CORES * rows, 1)

    links = Links(layout, {"z": 3, "y": 2})
    sib_g = layout.to_sibling(gradients)
    sib_a = layout.to_sibling(activations)
    split = [basis_g.shape[0] * 4 // 7, basis_a.shape[0] // 2] if ny > 1 else [0, 0]
    from_g, from_a = Gather(links, basis_g, split[0]), Gather(links, basis_a, split[1])
    from_g.step()
    links.after(from_g.by_z[1])
    from_g.step()
    early = partial_rotation(layout, gradients, sib_g, from_g.found[:4], place)
    links.after(sib_g, sib_a)
    while from_a.steps:
        if len(from_a.steps) == 2:
            links.after(early)
        from_a.step()
        if from_g.steps:
            from_g.step()
    found_g, found_a = from_g.found, from_a.found
    mine_g = partial_rotation(layout, gradients, sib_g, found_g[4:], place, early)
    grads = owned_gradients(layout, mine_g, layout.to_sibling(mine_g), place, owned)

    most, rows_left = partial_rotation(
        layout, activations, sib_a, found_a[:-1], place, None, found_a[-1]
    )
    mine_a = last_rotation(most, rows_left, found_a[-1][0])
    cut = basis_a.shape[1] // ny
    sums = chip_sums(
        layout, grads, mine_a, layout.to_sibling(mine_a), positions, seq_lengths, owned, cut
    )
    return squares(scatter_sums(layout, sums, owned), seq_lengths, owned)


def solution(mesh):
    return jax.shard_map(
        functools.partial(shards, Layout(mesh)),
        mesh=mesh,
        in_specs=(
            P(("grp", "row"), None),
            P(("grp", "row"), None),
            P(("grp", "row"), None),
            P(("grp", "row"), None),
            P(("grp", "row")),
            P("grp"),
        ),
        out_specs=P(("grp", "row"), None),
        check_vma=False,
    )
```

```python
import functools

import jax
import jax.numpy as jnp
from jax import lax
from jax.experimental import pallas as pl
from jax.experimental.pallas import tpu as pltpu
from jax.sharding import PartitionSpec as P

CORES = 2
MIB = 1024 * 1024


def params(mib=8):
    return pltpu.CompilerParams(vmem_limit_bytes=mib * MIB)


IN_VMEM = pl.BlockSpec(memory_space=pltpu.VMEM)
IN_SMEM = pl.BlockSpec(memory_space=pltpu.SMEM)
ANYWHERE = pl.BlockSpec(memory_space=pltpu.HBM)


class Layout:
    def __init__(self, mesh):
        self.chips = mesh.shape["row"] // CORES
        self.ny = max(1, 4 // mesh.shape["grp"])
        if self.chips % self.ny:
            self.ny = 1
        self.nz = self.chips // self.ny

    def device(self, z, y, core):
        return ((z % self.nz) * self.ny + y % self.ny) * CORES + core

    def everyone(self):
        return [(z, y, c) for z in range(self.nz) for y in range(self.ny) for c in range(CORES)]

    def origin(self, z, y, d, h):
        return lax.rem(z + (self.nz - d), self.nz) * self.ny + lax.rem(y + (self.ny - h), self.ny)

    def along_z(self, x, hops):
        pairs = [(self.device(z, y, c), self.device(z + hops, y, c)) for z, y, c in self.everyone()]
        return lax.ppermute(x, "row", pairs)

    def along_y(self, x, hops=1):
        pairs = [(self.device(z, y, c), self.device(z, y + hops, c)) for z, y, c in self.everyone()]
        return lax.ppermute(x, "row", pairs)

    def to_sibling(self, x):
        pairs = [(self.device(z, y, c), self.device(z, y, 1 - c)) for z, y, c in self.everyone()]
        return lax.ppermute(x, "row", pairs)


def split_columns(act, core, chips):
    rows, depth = act.shape
    kc = depth // (chips * CORES)
    mine = lax.dynamic_index_in_dim(act.reshape(rows, chips, CORES, kc), core, 2, keepdims=False)
    return mine.transpose(1, 0, 2)


class Links:
    def __init__(self, layout, window):
        self.layout, self.window = layout, window
        self.done = {"z": [], "y": []}
        self.first = []

    def after(self, *first):
        self.first += first

    def send(self, kind, x, hops):
        done = self.done[kind]
        first = self.first + done[-self.window:len(done) - self.window + 1]
        self.first = []
        if first:
            x = lax.optimization_barrier((x, *first))[0]
        move = self.layout.along_z if kind == "z" else self.layout.along_y
        done.append(move(x, hops))
        return done[-1]


def gather_columns(links, piece, split, gates):
    nz, ny = links.layout.nz, links.layout.ny
    middle = nz // 2
    steps = [(d, 1) for d in range(1, middle + 1)] + [(d, -1) for d in range(nz - 1, middle, -1)]
    steps = sorted(steps, key=lambda s: (min(s[0], nz - s[0]), -s[1]))
    by_z, crossed, found = {0: piece}, {}, [(piece, 0, 0)]

    def cross(d):
        for h in range(1, ny):
            if d == middle and split:
                head = links.send("z", crossed[d - 1, h][:split], 1)
                if split == piece.shape[0]:
                    got = [head]
                else:
                    got = [head, links.send("y", by_z[d][split:], h)]
            else:
                got = [links.send("y", by_z[d], h)]
            crossed[d, h] = got[0]
            found.append((got, d, h))

    last = 0
    for d, sign in steps:
        links.after(*gates.get(d, ()))
        by_z[d] = links.send("z", by_z[(d - sign) % nz], sign)
        found.append(([by_z[d]], d, 0))
        cross(last)
        last = d
    if -1 in gates:
        links.after(*gates[-1](by_z, crossed))
    cross(last)
    links.first = []
    return [(block if isinstance(block, list) else [block], d, h) for block, d, h in found]


def partial_rotation(layout, act, sib, found, place, total=None, left=()):
    rows = act.shape[0]
    count = len(found)
    blocks = [x for parts, _, _ in found for x in parts]
    kc = sum(x.shape[0] for x in found[0][0])
    width = blocks[0].shape[1]
    unaligned = kc % 128 != 0
    if unaligned:
        act = split_columns(act, place[2], layout.chips)
        sib = split_columns(sib, place[2], layout.chips)

    extra = [] if total is None else [total]

    def kernel(place_ref, act_ref, sib_ref, *refs):
        block_refs, refs = refs[:len(blocks)], refs[len(blocks):]
        o_ref = refs[len(extra)]
        rows_buf, block_buf, sems = refs[-3:]
        z, y, core = place_ref[0], place_ref[1], place_ref[2]
        mine = pl.ds(pl.multiple_of(core * rows, 16), rows)
        other = pl.ds(pl.multiple_of((1 - core) * rows, 16), rows)

        def bring_rows(d, h, to, i):
            q = layout.origin(z, y, d, h)
            at = 0 if unaligned else pl.ds(pl.multiple_of((CORES * q + core) * kc, 128), kc)
            own, its = [ref.at[q] if unaligned else ref.at[:, at] for ref in (act_ref, sib_ref)]
            return [
                pltpu.make_async_copy(own, to.at[mine], sems.at[i, 0]),
                pltpu.make_async_copy(its, to.at[other], sems.at[i, 1]),
            ]

        copies, k = [], 0
        for i in range(count):
            parts, d, h = found[i]
            step, at = bring_rows(d, h, rows_buf.at[i], i), 0
            for j, x in enumerate(parts):
                to = block_buf.at[i, pl.ds(at, x.shape[0])]
                step.append(pltpu.make_async_copy(block_refs[k], to, sems.at[i, 2 + j]))
                at += x.shape[0]
                k += 1
            copies.append(step)
        for j, (_, d, h) in enumerate(left):
            copies.append(bring_rows(d, h, refs[len(extra) + 1].at[j], count + j))
        for step in copies:
            for copy in step:
                copy.start()
        for i, step in enumerate(copies):
            for copy in step:
                copy.wait()
            if i >= count:
                continue
            product = jnp.dot(rows_buf[i], block_buf[i], preferred_element_type=jnp.float32)
            if i > 0:
                o_ref[...] += product
            elif extra:
                o_ref[...] = refs[0][...] + product
            else:
                o_ref[...] = product

    shapes = [jax.ShapeDtypeStruct((CORES * rows, width), jnp.float32)]
    if left:
        shapes.append(jax.ShapeDtypeStruct((len(left), CORES * rows, kc), act.dtype))
    outs = pl.pallas_call(
        kernel,
        in_specs=[IN_SMEM] + [ANYWHERE] * (2 + len(blocks)) + [IN_VMEM] * len(extra),
        out_specs=[IN_VMEM] * len(shapes),
        out_shape=shapes,
        scratch_shapes=[
            pltpu.VMEM((count, CORES * rows, kc), act.dtype),
            pltpu.VMEM((count, kc, width), act.dtype),
            pltpu.SemaphoreType.DMA((count + len(left), 4)),
        ],
        cost_estimate=pl.CostEstimate(
            flops=4 * rows * kc * count * width,
            bytes_accessed=2 * count * kc * (2 * rows + width) + 8 * rows * width,
            transcendentals=0,
        ),
        compiler_params=params(32),
        name="partial_rotation",
    )(place, act, sib, *blocks, *extra)
    return outs if left else outs[0]


def last_rotation(total, rows, found):
    width = total.shape[1]
    blocks = [x for parts, _, _ in found for x in parts]

    def kernel(total_ref, rows_ref, *refs):
        sums, k = total_ref[...], 0
        for i, (parts, _, _) in enumerate(found):
            at = 0
            for part in parts:
                x = rows_ref[i, :, pl.ds(at, part.shape[0])]
                sums += jnp.dot(x, refs[k][...], preferred_element_type=jnp.float32)
                at += part.shape[0]
                k += 1
        refs[-1][...] = sums

    return pl.pallas_call(
        kernel,
        in_specs=[IN_VMEM] * (2 + len(blocks)),
        out_specs=IN_VMEM,
        out_shape=jax.ShapeDtypeStruct(total.shape, jnp.float32),
        cost_estimate=pl.CostEstimate(
            flops=2 * rows.size * width,
            bytes_accessed=2 * rows.size + 8 * total.size,
            transcendentals=0,
        ),
        compiler_params=params(),
        name="last_rotation",
    )(total, rows, *blocks)


def owned_gradients(layout, mine, other, place, owned):
    nz, ny = layout.nz, layout.ny
    tokens, width = mine.shape
    kept = nz * ny * owned

    def kernel(place_ref, mine_ref, other_ref, o_ref):
        slot = lax.broadcasted_iota(jnp.int32, (kept, width), 0)
        column = lax.broadcasted_iota(jnp.int32, (kept, width), 1)
        z, y, core = place_ref[0], place_ref[1], place_ref[2]
        to_y = lax.rem(y + 1 + slot // (nz * owned), ny)
        to_z = lax.rem(z + lax.rem(slot // owned, nz), nz)
        wanted = ((to_z * ny + to_y) * CORES + core) * owned + lax.rem(slot, owned)
        pick = jnp.where(wanted == column, 1.0, 0.0).astype(jnp.bfloat16)
        rotated = (mine_ref[...] + other_ref[...]).astype(jnp.bfloat16)
        picked = lax.dot_general(
            pick, rotated, (((1,), (1,)), ((), ())), preferred_element_type=jnp.float32
        )
        o_ref[...] = picked.astype(jnp.bfloat16)

    return pl.pallas_call(
        kernel,
        in_specs=[IN_SMEM, IN_VMEM, IN_VMEM],
        out_specs=IN_VMEM,
        out_shape=jax.ShapeDtypeStruct((kept, tokens), jnp.bfloat16),
        cost_estimate=pl.CostEstimate(
            flops=2 * kept * width * tokens,
            bytes_accessed=8 * tokens * width + 2 * kept * tokens,
            transcendentals=0,
        ),
        compiler_params=params(),
        name="owned_gradients",
    )(place, mine, other)


def chip_sums(layout, grads, mine, other, positions, lengths, owned, cut):
    nz, ny = layout.nz, layout.ny
    tokens, width = mine.shape
    seqs = lengths.shape[0]
    stay = nz * owned
    rest = width - cut

    def kernel(lengths_ref, grads_ref, mine_ref, other_ref, positions_ref, *refs):
        rotated = mine_ref[...] + other_ref[...]
        position = positions_ref[...]
        begin = jnp.int32(0)
        for s in range(seqs):
            end = begin + lengths_ref[s]
            inside = (position >= begin) & (position < end)
            part = jnp.where(inside, rotated, 0.0).astype(jnp.bfloat16)
            sums = jnp.dot(grads_ref[...], part, preferred_element_type=jnp.float32)
            at = pl.ds(s * cut, cut)
            for d in range(nz):
                for h in range(ny):
                    block = sums[h * stay + d * owned:h * stay + (d + 1) * owned, :cut]
                    refs[d][pl.ds(h * owned, owned), at] = block.astype(refs[d].dtype)
            if rest:
                at = pl.ds(s * rest, rest)
                refs[nz][:, at] = sums[stay:, cut:]
                refs[nz + 1][:, at] = sums[:stay, cut:].astype(jnp.bfloat16)
            begin = end

    shapes = [jax.ShapeDtypeStruct((ny * owned, seqs * cut), jnp.float32)]
    shapes += [jax.ShapeDtypeStruct((ny * owned, seqs * cut), jnp.bfloat16)] * (nz - 1)
    if rest:
        shapes.append(jax.ShapeDtypeStruct((stay, seqs * rest), jnp.float32))
        shapes.append(jax.ShapeDtypeStruct((stay, seqs * rest), jnp.bfloat16))
    return pl.pallas_call(
        kernel,
        in_specs=[IN_SMEM] + [IN_VMEM] * 4,
        out_specs=[IN_VMEM] * len(shapes),
        out_shape=shapes,
        cost_estimate=pl.CostEstimate(
            flops=2 * grads.size * seqs * width,
            bytes_accessed=8 * tokens * width + 2 * grads.shape[0] * seqs * width,
            transcendentals=0,
        ),
        compiler_params=params(),
        name="chip_sums",
    )(lengths, grads, mine, other, positions)


def add_up(kept, came, owned, own):
    count = kept.shape[0] // owned
    width = kept.shape[1]

    def kernel(*refs):
        total = refs[0][...]
        for i in range(len(came)):
            total += refs[1 + i][...].astype(jnp.float32)
        outs = refs[1 + len(came):]
        for i in range(count):
            outs[i][...] = total[i * owned:(i + 1) * owned].astype(outs[i].dtype)

    shapes = [
        jax.ShapeDtypeStruct((owned, width), jnp.float32 if i == own else jnp.bfloat16)
        for i in range(count)
    ]
    return pl.pallas_call(
        kernel,
        in_specs=[IN_VMEM] * (1 + len(came)),
        out_specs=[IN_VMEM] * count,
        out_shape=shapes,
        cost_estimate=pl.CostEstimate(
            flops=kept.size * len(came), bytes_accessed=8 * kept.size, transcendentals=0
        ),
        compiler_params=params(),
        name="add_up",
    )(kept, *came)


def squares(groups, lengths, owned):
    seqs = lengths.shape[0]
    widths = [group[0].shape[1] // seqs for group in groups]

    def kernel(lengths_ref, *refs):
        o_ref = refs[-1]
        tokens = lengths_ref[0]
        for s in range(1, seqs):
            tokens = tokens + lengths_ref[s]
        at, k = 0, 0
        for group, width in zip(groups, widths):
            over = jnp.full((owned, width), tokens, jnp.int32).astype(jnp.float32)
            sums = refs[k][...]
            for ref in refs[k + 1:k + len(group)]:
                sums = sums + ref[...].astype(jnp.float32)
            k += len(group)
            sums = sums * sums
            acc = sums[:, :width]
            for s in range(1, seqs):
                acc = acc + sums[:, s * width:(s + 1) * width]
            o_ref[:, pl.ds(at, width)] = acc / over
            at += width

    flat = [x for group in groups for x in group]
    return pl.pallas_call(
        kernel,
        in_specs=[IN_SMEM] + [IN_VMEM] * len(flat),
        out_specs=IN_VMEM,
        out_shape=jax.ShapeDtypeStruct((owned, sum(widths)), jnp.float32),
        cost_estimate=pl.CostEstimate(
            flops=2 * sum(x.size for x in flat),
            bytes_accessed=2 * sum(x.size for x in flat),
            transcendentals=0,
        ),
        compiler_params=params(),
        name="squares",
    )(lengths, *flat)


def scatter_sums(layout, sums, owned):
    nz, ny = layout.nz, layout.ny
    if ny == 1:
        return [[sums[0]] + [layout.along_z(sums[d], d) for d in range(1, nz)]]
    crossed = [layout.along_y(sums[nz + 1])]
    came = [layout.along_z(sums[d], d) for d in range(1, nz)]
    by_z = add_up(sums[nz], crossed, owned, 0)
    second = [by_z[0]] + [layout.along_z(by_z[d], d) for d in range(1, nz)]
    came[0] = lax.optimization_barrier((came[0], by_z[1]))[0]
    by_y = add_up(sums[0], came, owned, 1)
    return [[by_y[1], layout.along_y(by_y[0])], second]


def shards(layout, activations, gradients, basis_a, basis_g, token_index, seq_lengths):
    nz, ny, chips = layout.nz, layout.ny, layout.chips
    rows = activations.shape[0]
    owned = basis_g.shape[1] // (chips * CORES)
    me = lax.axis_index("row")
    core = lax.rem(me, CORES)
    y = lax.rem(me // CORES, ny)
    z = me // (CORES * ny)
    place = jnp.stack([z, y, core]).astype(jnp.int32)

    sib_index = layout.to_sibling(token_index)
    first = core == 0
    positions = jnp.concatenate(
        [jnp.where(first, token_index, sib_index), jnp.where(first, sib_index, token_index)]
    ).reshape(CORES * rows, 1)

    links = Links(layout, 2)
    sib_g = layout.to_sibling(gradients)
    sib_a = layout.to_sibling(activations)
    split = [basis_g.shape[0] * 2 // 7, basis_a.shape[0] // 2] if ny > 1 else [0, 0]
    found_g = gather_columns(links, basis_g, split[0], {nz // 2: [sib_g, sib_a]})
    early = partial_rotation(layout, gradients, sib_g, found_g[:4], place)
    links.after(early)
    late = []

    def rotate_rest(by_z, crossed):
        total = early
        if ny > 1:
            total = lax.optimization_barrier((early, crossed[0, 1]))[0]
        late.append(partial_rotation(layout, gradients, sib_g, found_g[4:], place, total))
        return late

    found_a = gather_columns(links, basis_a, split[1], {-1: rotate_rest})
    mine_g = late[0]
    grads = owned_gradients(layout, mine_g, layout.to_sibling(mine_g), place, owned)

    most, rows_left = partial_rotation(
        layout, activations, sib_a, found_a[:-2], place, None, found_a[-2:]
    )
    most, grads, positions = lax.optimization_barrier((most, grads, positions))
    mine_a = last_rotation(most, rows_left, found_a[-2:])
    cut = basis_a.shape[1] // ny
    sums = chip_sums(
        layout, grads, mine_a, layout.to_sibling(mine_a), positions, seq_lengths, owned, cut
    )
    return squares(scatter_sums(layout, sums, owned), seq_lengths, owned)


def solution(mesh):
    return jax.shard_map(
        functools.partial(shards, Layout(mesh)),
        mesh=mesh,
        in_specs=(
            P(("grp", "row"), None),
            P(("grp", "row"), None),
            P(("grp", "row"), None),
            P(("grp", "row"), None),
            P(("grp", "row")),
            P("grp"),
        ),
        out_specs=P(("grp", "row"), None),
        check_vma=False,
    )
```

```python
import functools

import jax
import jax.numpy as jnp
from jax import lax
from jax.experimental import pallas as pl
from jax.experimental.pallas import tpu as pltpu
from jax.sharding import PartitionSpec as P

CORES = 2
MIB = 1024 * 1024


def params(mib=8):
    return pltpu.CompilerParams(vmem_limit_bytes=mib * MIB)


IN_VMEM = pl.BlockSpec(memory_space=pltpu.VMEM)
IN_SMEM = pl.BlockSpec(memory_space=pltpu.SMEM)
ANYWHERE = pl.BlockSpec(memory_space=pl.ANY)


class Layout:
    def __init__(self, mesh):
        self.chips = mesh.shape["row"] // CORES
        self.ny = max(1, 4 // mesh.shape["grp"])
        if self.chips % self.ny:
            self.ny = 1
        self.nz = self.chips // self.ny

    def device(self, z, y, core):
        return ((z % self.nz) * self.ny + y % self.ny) * CORES + core

    def everyone(self):
        return [(z, y, c) for z in range(self.nz) for y in range(self.ny) for c in range(CORES)]

    def origin(self, z, y, d, h):
        return lax.rem(z + (self.nz - d), self.nz) * self.ny + lax.rem(y + (self.ny - h), self.ny)

    def along_z(self, x, hops):
        pairs = [(self.device(z, y, c), self.device(z + hops, y, c)) for z, y, c in self.everyone()]
        return lax.ppermute(x, "row", pairs)

    def along_y(self, x, hops=1):
        pairs = [(self.device(z, y, c), self.device(z, y + hops, c)) for z, y, c in self.everyone()]
        return lax.ppermute(x, "row", pairs)

    def to_sibling(self, x):
        pairs = [(self.device(z, y, c), self.device(z, y, 1 - c)) for z, y, c in self.everyone()]
        return lax.ppermute(x, "row", pairs)


def split_columns(act, core, chips):
    rows, depth = act.shape
    kc = depth // (chips * CORES)
    mine = lax.dynamic_index_in_dim(act.reshape(rows, chips, CORES, kc), core, 2, keepdims=False)
    return mine.transpose(1, 0, 2)


class Links:
    def __init__(self, layout, window):
        self.layout, self.window = layout, window
        self.done = {"z": [], "y": []}
        self.first = []

    def after(self, *first):
        self.first += first

    def send(self, kind, x, hops):
        done = self.done[kind]
        first = self.first + done[-self.window:len(done) - self.window + 1]
        self.first = []
        if first:
            x = lax.optimization_barrier((x, *first))[0]
        move = self.layout.along_z if kind == "z" else self.layout.along_y
        done.append(move(x, hops))
        return done[-1]


def gather_columns(links, piece, split, gates):
    nz, ny = links.layout.nz, links.layout.ny
    middle = nz // 2
    steps = [(d, 1) for d in range(1, middle + 1)] + [(d, -1) for d in range(nz - 1, middle, -1)]
    steps = sorted(steps, key=lambda s: (min(s[0], nz - s[0]), -s[1]))
    by_z, crossed, found = {0: piece}, {}, [(piece, 0, 0)]

    def cross(d):
        for h in range(1, ny):
            if d == middle and split:
                head = links.send("z", crossed[d - 1, h][:split], 1)
                if split == piece.shape[0]:
                    got = [head]
                else:
                    got = [head, links.send("y", by_z[d][split:], h)]
            else:
                got = [links.send("y", by_z[d], h)]
            crossed[d, h] = got[0]
            found.append((got, d, h))

    last = 0
    for d, sign in steps:
        links.after(*gates.get(d, ()))
        by_z[d] = links.send("z", by_z[(d - sign) % nz], sign)
        found.append(([by_z[d]], d, 0))
        cross(last)
        last = d
    if -1 in gates:
        links.after(*gates[-1])
    cross(last)
    links.first = []
    return [(block if isinstance(block, list) else [block], d, h) for block, d, h in found]


def partial_rotation(layout, act, sib, found, place, total=None, left=()):
    rows = act.shape[0]
    count = len(found)
    blocks = [x for parts, _, _ in found for x in parts]
    kc = sum(x.shape[0] for x in found[0][0])
    width = blocks[0].shape[1]
    unaligned = kc % 128 != 0
    if unaligned:
        act = split_columns(act, place[2], layout.chips)
        sib = split_columns(sib, place[2], layout.chips)

    extra = [] if total is None else [total]

    def kernel(place_ref, act_ref, sib_ref, *refs):
        o_ref = refs[len(blocks) + len(extra)]
        z, y, core = place_ref[0], place_ref[1], place_ref[2]
        mine = pl.ds(pl.multiple_of(core * rows, 8), rows)
        other = pl.ds(pl.multiple_of((1 - core) * rows, 8), rows)
        k = 0
        for j, (_, d, h) in enumerate(left):
            q = layout.origin(z, y, d, h)
            at = pl.ds(0 if unaligned else pl.multiple_of((CORES * q + core) * kc, 128), kc)
            refs[-1][j, mine, :] = act_ref[q] if unaligned else act_ref[:, at]
            refs[-1][j, other, :] = sib_ref[q] if unaligned else sib_ref[:, at]
        for i in range(count):
            q = layout.origin(z, y, *found[i][1:])
            start = 0
            for x in found[i][0]:
                depth = x.shape[0]
                block = refs[k][...]
                if unaligned:
                    own, its = act_ref[q], sib_ref[q]
                else:
                    at = pl.ds(pl.multiple_of((CORES * q + core) * kc + start, 128), depth)
                    own, its = act_ref[:, at], sib_ref[:, at]
                for place_of, x in ((mine, own), (other, its)):
                    product = jnp.dot(x, block, preferred_element_type=jnp.float32)
                    if k == 0 and total is None:
                        o_ref[place_of, :] = product
                    elif k == 0:
                        o_ref[place_of, :] = refs[len(blocks)][place_of, :] + product
                    else:
                        o_ref[place_of, :] += product
                start += depth
                k += 1

    shapes = [jax.ShapeDtypeStruct((CORES * rows, width), jnp.float32)]
    if left:
        shapes.append(jax.ShapeDtypeStruct((len(left), CORES * rows, kc), act.dtype))
    outs = pl.pallas_call(
        kernel,
        in_specs=[IN_SMEM] + [IN_VMEM] * (2 + len(blocks) + len(extra)),
        out_specs=[IN_VMEM] * len(shapes),
        out_shape=shapes,
        cost_estimate=pl.CostEstimate(
            flops=4 * rows * kc * count * width,
            bytes_accessed=2 * count * kc * (2 * rows + width) + 8 * rows * width,
            transcendentals=0,
        ),
        compiler_params=params(),
        name="partial_rotation",
    )(place, act, sib, *blocks, *extra)
    return outs if left else outs[0]


def last_rotation(total, rows, found):
    width = total.shape[1]
    blocks = [x for parts, _, _ in found for x in parts]

    def kernel(total_ref, rows_ref, *refs):
        sums, k = total_ref[...], 0
        for i, (parts, _, _) in enumerate(found):
            at = 0
            for part in parts:
                x = rows_ref[i, :, pl.ds(at, part.shape[0])]
                sums += jnp.dot(x, refs[k][...], preferred_element_type=jnp.float32)
                at += part.shape[0]
                k += 1
        refs[-1][...] = sums

    return pl.pallas_call(
        kernel,
        in_specs=[IN_VMEM] * (2 + len(blocks)),
        out_specs=IN_VMEM,
        out_shape=jax.ShapeDtypeStruct(total.shape, jnp.float32),
        cost_estimate=pl.CostEstimate(
            flops=2 * rows.size * width,
            bytes_accessed=2 * rows.size + 8 * total.size,
            transcendentals=0,
        ),
        compiler_params=params(),
        name="last_rotation",
    )(total, rows, *blocks)


def owned_gradients(layout, mine, other, place, owned):
    nz, ny = layout.nz, layout.ny
    tokens, width = mine.shape
    kept = nz * ny * owned

    def kernel(place_ref, mine_ref, other_ref, o_ref):
        slot = lax.broadcasted_iota(jnp.int32, (kept, width), 0)
        column = lax.broadcasted_iota(jnp.int32, (kept, width), 1)
        z, y, core = place_ref[0], place_ref[1], place_ref[2]
        to_y = lax.rem(y + 1 + slot // (nz * owned), ny)
        to_z = lax.rem(z + lax.rem(slot // owned, nz), nz)
        wanted = ((to_z * ny + to_y) * CORES + core) * owned + lax.rem(slot, owned)
        pick = jnp.where(wanted == column, 1.0, 0.0).astype(jnp.bfloat16)
        rotated = (mine_ref[...] + other_ref[...]).astype(jnp.bfloat16)
        picked = lax.dot_general(
            pick, rotated, (((1,), (1,)), ((), ())), preferred_element_type=jnp.float32
        )
        o_ref[...] = picked.astype(jnp.bfloat16)

    return pl.pallas_call(
        kernel,
        in_specs=[IN_SMEM, IN_VMEM, IN_VMEM],
        out_specs=IN_VMEM,
        out_shape=jax.ShapeDtypeStruct((kept, tokens), jnp.bfloat16),
        cost_estimate=pl.CostEstimate(
            flops=2 * kept * width * tokens,
            bytes_accessed=8 * tokens * width + 2 * kept * tokens,
            transcendentals=0,
        ),
        compiler_params=params(),
        name="owned_gradients",
    )(place, mine, other)


def chip_sums(layout, grads, mine, other, positions, lengths, owned, cut):
    nz, ny = layout.nz, layout.ny
    tokens, width = mine.shape
    seqs = lengths.shape[0]
    stay = nz * owned
    rest = width - cut

    def kernel(lengths_ref, grads_ref, mine_ref, other_ref, positions_ref, *refs):
        rotated = mine_ref[...] + other_ref[...]
        position = positions_ref[...]
        begin = jnp.int32(0)
        for s in range(seqs):
            end = begin + lengths_ref[s]
            inside = (position >= begin) & (position < end)
            part = jnp.where(inside, rotated, 0.0).astype(jnp.bfloat16)
            sums = jnp.dot(grads_ref[...], part, preferred_element_type=jnp.float32)
            at = pl.ds(s * cut, cut)
            for d in range(nz):
                for h in range(ny):
                    block = sums[h * stay + d * owned:h * stay + (d + 1) * owned, :cut]
                    refs[d][pl.ds(h * owned, owned), at] = block.astype(refs[d].dtype)
            if rest:
                at = pl.ds(s * rest, rest)
                refs[nz][:, at] = sums[stay:, cut:]
                refs[nz + 1][:, at] = sums[:stay, cut:].astype(jnp.bfloat16)
            begin = end

    shapes = [jax.ShapeDtypeStruct((ny * owned, seqs * cut), jnp.float32)]
    shapes += [jax.ShapeDtypeStruct((ny * owned, seqs * cut), jnp.bfloat16)] * (nz - 1)
    if rest:
        shapes.append(jax.ShapeDtypeStruct((stay, seqs * rest), jnp.float32))
        shapes.append(jax.ShapeDtypeStruct((stay, seqs * rest), jnp.bfloat16))
    return pl.pallas_call(
        kernel,
        in_specs=[IN_SMEM] + [IN_VMEM] * 4,
        out_specs=[IN_VMEM] * len(shapes),
        out_shape=shapes,
        cost_estimate=pl.CostEstimate(
            flops=2 * grads.size * seqs * width,
            bytes_accessed=8 * tokens * width + 2 * grads.shape[0] * seqs * width,
            transcendentals=0,
        ),
        compiler_params=params(),
        name="chip_sums",
    )(lengths, grads, mine, other, positions)


def add_up(kept, came, owned, own):
    count = kept.shape[0] // owned
    width = kept.shape[1]

    def kernel(*refs):
        total = refs[0][...]
        for i in range(len(came)):
            total += refs[1 + i][...].astype(jnp.float32)
        outs = refs[1 + len(came):]
        for i in range(count):
            outs[i][...] = total[i * owned:(i + 1) * owned].astype(outs[i].dtype)

    shapes = [
        jax.ShapeDtypeStruct((owned, width), jnp.float32 if i == own else jnp.bfloat16)
        for i in range(count)
    ]
    return pl.pallas_call(
        kernel,
        in_specs=[IN_VMEM] * (1 + len(came)),
        out_specs=[IN_VMEM] * count,
        out_shape=shapes,
        cost_estimate=pl.CostEstimate(
            flops=kept.size * len(came), bytes_accessed=8 * kept.size, transcendentals=0
        ),
        compiler_params=params(),
        name="add_up",
    )(kept, *came)


def squares(groups, lengths, owned):
    seqs = lengths.shape[0]
    widths = [group[0].shape[1] // seqs for group in groups]

    def kernel(lengths_ref, *refs):
        o_ref = refs[-1]
        tokens = lengths_ref[0]
        for s in range(1, seqs):
            tokens = tokens + lengths_ref[s]
        at, k = 0, 0
        for group, width in zip(groups, widths):
            over = jnp.full((owned, width), tokens, jnp.int32).astype(jnp.float32)
            sums = refs[k][...]
            for ref in refs[k + 1:k + len(group)]:
                sums = sums + ref[...].astype(jnp.float32)
            k += len(group)
            sums = sums * sums
            acc = sums[:, :width]
            for s in range(1, seqs):
                acc = acc + sums[:, s * width:(s + 1) * width]
            o_ref[:, pl.ds(at, width)] = acc / over
            at += width

    flat = [x for group in groups for x in group]
    return pl.pallas_call(
        kernel,
        in_specs=[IN_SMEM] + [IN_VMEM] * len(flat),
        out_specs=IN_VMEM,
        out_shape=jax.ShapeDtypeStruct((owned, sum(widths)), jnp.float32),
        cost_estimate=pl.CostEstimate(
            flops=2 * sum(x.size for x in flat),
            bytes_accessed=2 * sum(x.size for x in flat),
            transcendentals=0,
        ),
        compiler_params=params(),
        name="squares",
    )(lengths, *flat)


def scatter_sums(layout, sums, owned):
    nz, ny = layout.nz, layout.ny
    if ny == 1:
        return [[sums[0]] + [layout.along_z(sums[d], d) for d in range(1, nz)]]
    crossed = [layout.along_y(sums[nz + 1])]
    came = [layout.along_z(sums[d], d) for d in range(1, nz)]
    by_z = add_up(sums[nz], crossed, owned, 0)
    second = [by_z[0]] + [layout.along_z(by_z[d], d) for d in range(1, nz)]
    came[0] = lax.optimization_barrier((came[0], by_z[1]))[0]
    by_y = add_up(sums[0], came, owned, 1)
    return [[by_y[1], layout.along_y(by_y[0])], second]


def shards(layout, activations, gradients, basis_a, basis_g, token_index, seq_lengths):
    nz, ny, chips = layout.nz, layout.ny, layout.chips
    rows = activations.shape[0]
    owned = basis_g.shape[1] // (chips * CORES)
    me = lax.axis_index("row")
    core = lax.rem(me, CORES)
    y = lax.rem(me // CORES, ny)
    z = me // (CORES * ny)
    place = jnp.stack([z, y, core]).astype(jnp.int32)

    sib_index = layout.to_sibling(token_index)
    first = core == 0
    positions = jnp.concatenate(
        [jnp.where(first, token_index, sib_index), jnp.where(first, sib_index, token_index)]
    ).reshape(CORES * rows, 1)

    links = Links(layout, 2)
    sib_g = layout.to_sibling(gradients)
    sib_a = layout.to_sibling(activations)
    split = [basis_g.shape[0] * 3 // 7, basis_a.shape[0] // 2] if ny > 1 else [0, 0]
    found_g = gather_columns(links, basis_g, split[0], {nz // 2: [sib_g, sib_a]})
    early = partial_rotation(layout, gradients, sib_g, found_g[:4], place)
    mine_g = partial_rotation(layout, gradients, sib_g, found_g[4:], place, early)
    links.after(early)
    found_a = gather_columns(links, basis_a, split[1], {})
    grads = owned_gradients(layout, mine_g, layout.to_sibling(mine_g), place, owned)

    most, rows_left = partial_rotation(
        layout, activations, sib_a, found_a[:-2], place, None, found_a[-2:]
    )
    most, positions = lax.optimization_barrier((most, positions))
    mine_a = last_rotation(most, rows_left, found_a[-2:])
    cut = basis_a.shape[1] // ny
    sums = chip_sums(
        layout, grads, mine_a, layout.to_sibling(mine_a), positions, seq_lengths, owned, cut
    )
    return squares(scatter_sums(layout, sums, owned), seq_lengths, owned)


def solution(mesh):
    return jax.shard_map(
        functools.partial(shards, Layout(mesh)),
        mesh=mesh,
        in_specs=(
            P(("grp", "row"), None),
            P(("grp", "row"), None),
            P(("grp", "row"), None),
            P(("grp", "row"), None),
            P(("grp", "row")),
            P("grp"),
        ),
        out_specs=P(("grp", "row"), None),
        check_vma=False,
    )
```

```python
import functools

import jax
import jax.numpy as jnp
from jax import lax
from jax.experimental import pallas as pl
from jax.experimental.pallas import tpu as pltpu
from jax.sharding import PartitionSpec as P

CORES = 2
MIB = 1024 * 1024


def params(mib=8):
    return pltpu.CompilerParams(vmem_limit_bytes=mib * MIB)


IN_VMEM = pl.BlockSpec(memory_space=pltpu.VMEM)
IN_SMEM = pl.BlockSpec(memory_space=pltpu.SMEM)
ANYWHERE = pl.BlockSpec(memory_space=pl.ANY)


class Layout:
    def __init__(self, mesh):
        self.chips = mesh.shape["row"] // CORES
        self.ny = max(1, 4 // mesh.shape["grp"])
        if self.chips % self.ny:
            self.ny = 1
        self.nz = self.chips // self.ny

    def device(self, z, y, core):
        return ((z % self.nz) * self.ny + y % self.ny) * CORES + core

    def everyone(self):
        return [(z, y, c) for z in range(self.nz) for y in range(self.ny) for c in range(CORES)]

    def origin(self, z, y, d, h):
        return lax.rem(z + (self.nz - d), self.nz) * self.ny + lax.rem(y + (self.ny - h), self.ny)

    def along_z(self, x, hops):
        pairs = [(self.device(z, y, c), self.device(z + hops, y, c)) for z, y, c in self.everyone()]
        return lax.ppermute(x, "row", pairs)

    def along_y(self, x, hops=1):
        pairs = [(self.device(z, y, c), self.device(z, y + hops, c)) for z, y, c in self.everyone()]
        return lax.ppermute(x, "row", pairs)

    def to_sibling(self, x):
        pairs = [(self.device(z, y, c), self.device(z, y, 1 - c)) for z, y, c in self.everyone()]
        return lax.ppermute(x, "row", pairs)


def split_columns(act, core, chips):
    rows, depth = act.shape
    kc = depth // (chips * CORES)
    mine = lax.dynamic_index_in_dim(act.reshape(rows, chips, CORES, kc), core, 2, keepdims=False)
    return mine.transpose(1, 0, 2)


class Links:
    def __init__(self, layout, window):
        self.layout, self.window = layout, window
        self.done = {"z": [], "y": []}
        self.first = []

    def after(self, *first):
        self.first += first

    def send(self, kind, x, hops):
        done = self.done[kind]
        first = self.first + done[-self.window:len(done) - self.window + 1]
        self.first = []
        if first:
            x = lax.optimization_barrier((x, *first))[0]
        move = self.layout.along_z if kind == "z" else self.layout.along_y
        done.append(move(x, hops))
        return done[-1]


def gather_columns(links, piece, split, gates):
    nz, ny = links.layout.nz, links.layout.ny
    middle = nz // 2
    steps = [(d, 1) for d in range(1, middle + 1)] + [(d, -1) for d in range(nz - 1, middle, -1)]
    steps = sorted(steps, key=lambda s: (min(s[0], nz - s[0]), -s[1]))
    by_z, crossed, found = {0: piece}, {}, [([piece], 0, 0)]

    def cross(d):
        for h in range(1, ny):
            if d == middle and split:
                head = links.send("z", crossed[d - 1, h][:split], 1)
                if split == piece.shape[0]:
                    got = [head]
                else:
                    got = [head, links.send("y", by_z[d][split:], h)]
            else:
                got = [links.send("y", by_z[d], h)]
            crossed[d, h] = got[0]
            found.append((got, d, h))

    last = 0
    for d, sign in steps:
        links.after(*gates.get(d, ()))
        by_z[d] = links.send("z", by_z[(d - sign) % nz], sign)
        found.append(([by_z[d]], d, 0))
        cross(last)
        last = d
    if -1 in gates:
        links.after(gates[-1](found))
    cross(last)
    links.first = []
    return found


def partial_rotation(layout, act, sib, found, place, total=None, left=()):
    rows = act.shape[0]
    count = len(found)
    blocks = [x for parts, _, _ in found for x in parts]
    kc = sum(x.shape[0] for x in found[0][0])
    width = blocks[0].shape[1]
    unaligned = kc % 128 != 0
    if unaligned:
        act = split_columns(act, place[2], layout.chips)
        sib = split_columns(sib, place[2], layout.chips)

    extra = [] if total is None else [total]

    def kernel(place_ref, act_ref, sib_ref, *refs):
        o_ref = refs[len(blocks) + len(extra)]
        z, y, core = place_ref[0], place_ref[1], place_ref[2]
        mine = pl.ds(pl.multiple_of(core * rows, 8), rows)
        other = pl.ds(pl.multiple_of((1 - core) * rows, 8), rows)
        k = 0
        for j, (_, d, h) in enumerate(left):
            q = layout.origin(z, y, d, h)
            at = pl.ds(0 if unaligned else pl.multiple_of((CORES * q + core) * kc, 128), kc)
            refs[-1][j, mine, :] = act_ref[q] if unaligned else act_ref[:, at]
            refs[-1][j, other, :] = sib_ref[q] if unaligned else sib_ref[:, at]
        for i in range(count):
            q = layout.origin(z, y, *found[i][1:])
            start = 0
            for x in found[i][0]:
                depth = x.shape[0]
                block = refs[k][...]
                if unaligned:
                    own, its = act_ref[q], sib_ref[q]
                else:
                    at = pl.ds(pl.multiple_of((CORES * q + core) * kc + start, 128), depth)
                    own, its = act_ref[:, at], sib_ref[:, at]
                for place_of, x in ((mine, own), (other, its)):
                    product = jnp.dot(x, block, preferred_element_type=jnp.float32)
                    if k == 0 and total is None:
                        o_ref[place_of, :] = product
                    elif k == 0:
                        o_ref[place_of, :] = refs[len(blocks)][place_of, :] + product
                    else:
                        o_ref[place_of, :] += product
                start += depth
                k += 1

    shapes = [jax.ShapeDtypeStruct((CORES * rows, width), jnp.float32)]
    if left:
        shapes.append(jax.ShapeDtypeStruct((len(left), CORES * rows, kc), act.dtype))
    outs = pl.pallas_call(
        kernel,
        in_specs=[IN_SMEM] + [IN_VMEM] * (2 + len(blocks) + len(extra)),
        out_specs=[IN_VMEM] * len(shapes),
        out_shape=shapes,
        cost_estimate=pl.CostEstimate(
            flops=4 * rows * kc * count * width,
            bytes_accessed=2 * count * kc * (2 * rows + width) + 8 * rows * width,
            transcendentals=0,
        ),
        compiler_params=params(),
        name="partial_rotation",
    )(place, act, sib, *blocks, *extra)
    return outs if left else outs[0]


def last_rotation(total, rows, found):
    width = total.shape[1]
    blocks = [x for parts, _, _ in found for x in parts]

    def kernel(total_ref, rows_ref, *refs):
        sums, k = total_ref[...], 0
        for i, (parts, _, _) in enumerate(found):
            at = 0
            for part in parts:
                x = rows_ref[i, :, pl.ds(at, part.shape[0])]
                sums += jnp.dot(x, refs[k][...], preferred_element_type=jnp.float32)
                at += part.shape[0]
                k += 1
        refs[-1][...] = sums

    return pl.pallas_call(
        kernel,
        in_specs=[IN_VMEM] * (2 + len(blocks)),
        out_specs=IN_VMEM,
        out_shape=jax.ShapeDtypeStruct(total.shape, jnp.float32),
        cost_estimate=pl.CostEstimate(
            flops=2 * rows.size * width,
            bytes_accessed=2 * rows.size + 8 * total.size,
            transcendentals=0,
        ),
        compiler_params=params(),
        name="last_rotation",
    )(total, rows, *blocks)


def owned_gradients(layout, mine, other, place, owned):
    nz, ny = layout.nz, layout.ny
    tokens, width = mine.shape
    kept = nz * ny * owned

    def kernel(place_ref, mine_ref, other_ref, o_ref):
        slot = lax.broadcasted_iota(jnp.int32, (kept, width), 0)
        column = lax.broadcasted_iota(jnp.int32, (kept, width), 1)
        z, y, core = place_ref[0], place_ref[1], place_ref[2]
        to_y = lax.rem(y + 1 + slot // (nz * owned), ny)
        to_z = lax.rem(z + lax.rem(slot // owned, nz), nz)
        wanted = ((to_z * ny + to_y) * CORES + core) * owned + lax.rem(slot, owned)
        pick = jnp.where(wanted == column, 1.0, 0.0).astype(jnp.bfloat16)
        rotated = (mine_ref[...] + other_ref[...]).astype(jnp.bfloat16)
        picked = lax.dot_general(
            pick, rotated, (((1,), (1,)), ((), ())), preferred_element_type=jnp.float32
        )
        o_ref[...] = picked.astype(jnp.bfloat16)

    return pl.pallas_call(
        kernel,
        in_specs=[IN_SMEM, IN_VMEM, IN_VMEM],
        out_specs=IN_VMEM,
        out_shape=jax.ShapeDtypeStruct((kept, tokens), jnp.bfloat16),
        cost_estimate=pl.CostEstimate(
            flops=2 * kept * width * tokens,
            bytes_accessed=8 * tokens * width + 2 * kept * tokens,
            transcendentals=0,
        ),
        compiler_params=params(),
        name="owned_gradients",
    )(place, mine, other)


def chip_sums(layout, grads, mine, other, positions, lengths, owned, cut):
    nz, ny = layout.nz, layout.ny
    tokens, width = mine.shape
    seqs = lengths.shape[0]
    stay = nz * owned
    rest = width - cut

    def kernel(lengths_ref, grads_ref, mine_ref, other_ref, positions_ref, *refs):
        rotated = mine_ref[...] + other_ref[...]
        position = positions_ref[...]
        begin = jnp.int32(0)
        for s in range(seqs):
            end = begin + lengths_ref[s]
            inside = (position >= begin) & (position < end)
            part = jnp.where(inside, rotated, 0.0).astype(jnp.bfloat16)
            sums = jnp.dot(grads_ref[...], part, preferred_element_type=jnp.float32)
            at = pl.ds(s * cut, cut)
            for d in range(nz):
                for h in range(ny):
                    block = sums[h * stay + d * owned:h * stay + (d + 1) * owned, :cut]
                    refs[d][pl.ds(h * owned, owned), at] = block.astype(refs[d].dtype)
            if rest:
                at = pl.ds(s * rest, rest)
                refs[nz][:, at] = sums[stay:, cut:]
                refs[nz + 1][:, at] = sums[:stay, cut:].astype(jnp.bfloat16)
            begin = end

    shapes = [jax.ShapeDtypeStruct((ny * owned, seqs * cut), jnp.float32)]
    shapes += [jax.ShapeDtypeStruct((ny * owned, seqs * cut), jnp.bfloat16)] * (nz - 1)
    if rest:
        shapes.append(jax.ShapeDtypeStruct((stay, seqs * rest), jnp.float32))
        shapes.append(jax.ShapeDtypeStruct((stay, seqs * rest), jnp.bfloat16))
    return pl.pallas_call(
        kernel,
        in_specs=[IN_SMEM] + [IN_VMEM] * 4,
        out_specs=[IN_VMEM] * len(shapes),
        out_shape=shapes,
        cost_estimate=pl.CostEstimate(
            flops=2 * grads.size * seqs * width,
            bytes_accessed=8 * tokens * width + 2 * grads.shape[0] * seqs * width,
            transcendentals=0,
        ),
        compiler_params=params(),
        name="chip_sums",
    )(lengths, grads, mine, other, positions)


def add_up(kept, came, owned, own):
    count = kept.shape[0] // owned
    width = kept.shape[1]

    def kernel(*refs):
        total = refs[0][...]
        for i in range(len(came)):
            total += refs[1 + i][...].astype(jnp.float32)
        outs = refs[1 + len(came):]
        for i in range(count):
            outs[i][...] = total[i * owned:(i + 1) * owned].astype(outs[i].dtype)

    shapes = [
        jax.ShapeDtypeStruct((owned, width), jnp.float32 if i == own else jnp.bfloat16)
        for i in range(count)
    ]
    return pl.pallas_call(
        kernel,
        in_specs=[IN_VMEM] * (1 + len(came)),
        out_specs=[IN_VMEM] * count,
        out_shape=shapes,
        cost_estimate=pl.CostEstimate(
            flops=kept.size * len(came), bytes_accessed=8 * kept.size, transcendentals=0
        ),
        compiler_params=params(),
        name="add_up",
    )(kept, *came)


def squares(groups, lengths, owned):
    seqs = lengths.shape[0]
    widths = [group[0].shape[1] // seqs for group in groups]

    def kernel(lengths_ref, *refs):
        o_ref = refs[-1]
        tokens = lengths_ref[0]
        for s in range(1, seqs):
            tokens = tokens + lengths_ref[s]
        at, k = 0, 0
        for group, width in zip(groups, widths):
            over = jnp.full((owned, width), tokens, jnp.int32).astype(jnp.float32)
            sums = refs[k][...]
            for ref in refs[k + 1:k + len(group)]:
                sums = sums + ref[...].astype(jnp.float32)
            k += len(group)
            sums = sums * sums
            acc = sums[:, :width]
            for s in range(1, seqs):
                acc = acc + sums[:, s * width:(s + 1) * width]
            o_ref[:, pl.ds(at, width)] = acc / over
            at += width

    flat = [x for group in groups for x in group]
    return pl.pallas_call(
        kernel,
        in_specs=[IN_SMEM] + [IN_VMEM] * len(flat),
        out_specs=IN_VMEM,
        out_shape=jax.ShapeDtypeStruct((owned, sum(widths)), jnp.float32),
        cost_estimate=pl.CostEstimate(
            flops=2 * sum(x.size for x in flat),
            bytes_accessed=2 * sum(x.size for x in flat),
            transcendentals=0,
        ),
        compiler_params=params(),
        name="squares",
    )(lengths, *flat)


def scatter_sums(layout, sums, owned):
    nz, ny = layout.nz, layout.ny
    if ny == 1:
        return [[sums[0]] + [layout.along_z(sums[d], d) for d in range(1, nz)]]
    crossed = [layout.along_y(sums[nz + 1])]
    came = [layout.along_z(sums[d], d) for d in range(1, nz)]
    by_z = add_up(sums[nz], crossed, owned, 0)
    second = [by_z[0]] + [layout.along_z(by_z[d], d) for d in range(1, nz)]
    came[0] = lax.optimization_barrier((came[0], by_z[1]))[0]
    by_y = add_up(sums[0], came, owned, 1)
    return [[by_y[1], layout.along_y(by_y[0])], second]


def shards(layout, activations, gradients, basis_a, basis_g, token_index, seq_lengths):
    nz, ny, chips = layout.nz, layout.ny, layout.chips
    rows = activations.shape[0]
    owned = basis_g.shape[1] // (chips * CORES)
    me = lax.axis_index("row")
    core = lax.rem(me, CORES)
    y = lax.rem(me // CORES, ny)
    z = me // (CORES * ny)
    place = jnp.stack([z, y, core]).astype(jnp.int32)

    sib_index = layout.to_sibling(token_index)
    first = core == 0
    positions = jnp.concatenate(
        [jnp.where(first, token_index, sib_index), jnp.where(first, sib_index, token_index)]
    ).reshape(CORES * rows, 1)

    links = Links(layout, 2)
    sib_g = layout.to_sibling(gradients)
    sib_a = layout.to_sibling(activations)
    split = [basis_g.shape[0] * 4 // 7, basis_a.shape[0] // 2] if ny > 1 else [0, 0]
    early = []

    def rotate_early(found):
        early.append(partial_rotation(layout, gradients, sib_g, found[:4], place))
        return early[0]

    gates = {nz // 2: [sib_g, sib_a], -1: rotate_early}
    found_g = gather_columns(links, basis_g, split[0], gates)
    mine_g = partial_rotation(layout, gradients, sib_g, found_g[4:], place, early[0])
    found_a = gather_columns(links, basis_a, split[1], {nz // 2: [mine_g]})
    grads = owned_gradients(layout, mine_g, layout.to_sibling(mine_g), place, owned)

    most, rows_left = partial_rotation(
        layout, activations, sib_a, found_a[:-2], place, None, found_a[-2:]
    )
    most, positions = lax.optimization_barrier((most, positions))
    mine_a = last_rotation(most, rows_left, found_a[-2:])
    cut = basis_a.shape[1] // ny
    sums = chip_sums(
        layout, grads, mine_a, layout.to_sibling(mine_a), positions, seq_lengths, owned, cut
    )
    return squares(scatter_sums(layout, sums, owned), seq_lengths, owned)


def solution(mesh):
    return jax.shard_map(
        functools.partial(shards, Layout(mesh)),
        mesh=mesh,
        in_specs=(
            P(("grp", "row"), None),
            P(("grp", "row"), None),
            P(("grp", "row"), None),
            P(("grp", "row"), None),
            P(("grp", "row")),
            P("grp"),
        ),
        out_specs=P(("grp", "row"), None),
        check_vma=False,
    )
```

```python
import functools

import jax
import jax.numpy as jnp
from jax import lax
from jax.experimental import pallas as pl
from jax.experimental.pallas import tpu as pltpu
from jax.sharding import PartitionSpec as P

CORES = 2
MIB = 1024 * 1024


def params(mib=8):
    return pltpu.CompilerParams(vmem_limit_bytes=mib * MIB)


IN_VMEM = pl.BlockSpec(memory_space=pltpu.VMEM)
IN_SMEM = pl.BlockSpec(memory_space=pltpu.SMEM)
ANYWHERE = pl.BlockSpec(memory_space=pl.ANY)


class Layout:
    def __init__(self, mesh):
        self.chips = mesh.shape["row"] // CORES
        self.ny = max(1, 4 // mesh.shape["grp"])
        if self.chips % self.ny:
            self.ny = 1
        self.nz = self.chips // self.ny

    def device(self, z, y, core):
        return ((z % self.nz) * self.ny + y % self.ny) * CORES + core

    def everyone(self):
        return [(z, y, c) for z in range(self.nz) for y in range(self.ny) for c in range(CORES)]

    def origin(self, z, y, d, h):
        return lax.rem(z + (self.nz - d), self.nz) * self.ny + lax.rem(y + (self.ny - h), self.ny)

    def along_z(self, x, hops):
        pairs = [(self.device(z, y, c), self.device(z + hops, y, c)) for z, y, c in self.everyone()]
        return lax.ppermute(x, "row", pairs)

    def along_y(self, x, hops=1):
        pairs = [(self.device(z, y, c), self.device(z, y + hops, c)) for z, y, c in self.everyone()]
        return lax.ppermute(x, "row", pairs)

    def to_sibling(self, x):
        pairs = [(self.device(z, y, c), self.device(z, y, 1 - c)) for z, y, c in self.everyone()]
        return lax.ppermute(x, "row", pairs)


def split_columns(act, core, chips):
    rows, depth = act.shape
    kc = depth // (chips * CORES)
    mine = lax.dynamic_index_in_dim(act.reshape(rows, chips, CORES, kc), core, 2, keepdims=False)
    return mine.transpose(1, 0, 2)


class Links:
    def __init__(self, layout, window):
        self.layout, self.window = layout, window
        self.done = {"z": [], "y": []}
        self.first = []

    def after(self, *first):
        self.first += first

    def send(self, kind, x, hops):
        done = self.done[kind]
        first = self.first + done[-self.window:len(done) - self.window + 1]
        self.first = []
        if first:
            x = lax.optimization_barrier((x, *first))[0]
        move = self.layout.along_z if kind == "z" else self.layout.along_y
        done.append(move(x, hops))
        return done[-1]


def gather_columns(links, piece, split, gates):
    nz, ny = links.layout.nz, links.layout.ny
    middle = nz // 2
    steps = [(d, 1) for d in range(1, middle + 1)] + [(d, -1) for d in range(nz - 1, middle, -1)]
    steps = sorted(steps, key=lambda s: (min(s[0], nz - s[0]), -s[1]))
    by_z, crossed, found = {0: piece}, {}, [([piece], 0, 0)]

    def cross(d):
        for h in range(1, ny):
            if d == middle and split:
                head = links.send("z", crossed[d - 1, h][:split], 1)
                if split == piece.shape[0]:
                    got = [head]
                else:
                    got = [head, links.send("y", by_z[d][split:], h)]
            else:
                got = [links.send("y", by_z[d], h)]
            crossed[d, h] = got[0]
            found.append((got, d, h))

    last = 0
    for d, sign in steps:
        if d in gates:
            links.after(*gates[d](by_z))
        by_z[d] = links.send("z", by_z[(d - sign) % nz], sign)
        found.append(([by_z[d]], d, 0))
        cross(last)
        last = d
    if -1 in gates:
        links.after(gates[-1](found))
    cross(last)
    links.first = []
    return found


def partial_rotation(layout, act, sib, found, place, total=None, left=()):
    rows = act.shape[0]
    count = len(found)
    blocks = [x for parts, _, _ in found for x in parts]
    kc = sum(x.shape[0] for x in found[0][0])
    width = blocks[0].shape[1]
    unaligned = kc % 128 != 0
    if unaligned:
        act = split_columns(act, place[2], layout.chips)
        sib = split_columns(sib, place[2], layout.chips)

    extra = [] if total is None else [total]

    def kernel(place_ref, act_ref, sib_ref, *refs):
        o_ref = refs[len(blocks) + len(extra)]
        z, y, core = place_ref[0], place_ref[1], place_ref[2]
        mine = pl.ds(pl.multiple_of(core * rows, 8), rows)
        other = pl.ds(pl.multiple_of((1 - core) * rows, 8), rows)
        k = 0
        for j, (_, d, h) in enumerate(left):
            q = layout.origin(z, y, d, h)
            at = pl.ds(0 if unaligned else pl.multiple_of((CORES * q + core) * kc, 128), kc)
            refs[-1][j, mine, :] = act_ref[q] if unaligned else act_ref[:, at]
            refs[-1][j, other, :] = sib_ref[q] if unaligned else sib_ref[:, at]
        for i in range(count):
            q = layout.origin(z, y, *found[i][1:])
            start = 0
            for x in found[i][0]:
                depth = x.shape[0]
                block = refs[k][...]
                if unaligned:
                    own, its = act_ref[q], sib_ref[q]
                else:
                    at = pl.ds(pl.multiple_of((CORES * q + core) * kc + start, 128), depth)
                    own, its = act_ref[:, at], sib_ref[:, at]
                for place_of, x in ((mine, own), (other, its)):
                    product = jnp.dot(x, block, preferred_element_type=jnp.float32)
                    if k == 0 and total is None:
                        o_ref[place_of, :] = product
                    elif k == 0:
                        o_ref[place_of, :] = refs[len(blocks)][place_of, :] + product
                    else:
                        o_ref[place_of, :] += product
                start += depth
                k += 1

    shapes = [jax.ShapeDtypeStruct((CORES * rows, width), jnp.float32)]
    if left:
        shapes.append(jax.ShapeDtypeStruct((len(left), CORES * rows, kc), act.dtype))
    outs = pl.pallas_call(
        kernel,
        in_specs=[IN_SMEM] + [IN_VMEM] * (2 + len(blocks) + len(extra)),
        out_specs=[IN_VMEM] * len(shapes),
        out_shape=shapes,
        cost_estimate=pl.CostEstimate(
            flops=4 * rows * kc * count * width,
            bytes_accessed=2 * count * kc * (2 * rows + width) + 8 * rows * width,
            transcendentals=0,
        ),
        compiler_params=params(),
        name="partial_rotation",
    )(place, act, sib, *blocks, *extra)
    return outs if left else outs[0]


def last_rotation(total, rows, found):
    width = total.shape[1]
    blocks = [x for parts, _, _ in found for x in parts]

    def kernel(total_ref, rows_ref, *refs):
        sums, k = total_ref[...], 0
        for i, (parts, _, _) in enumerate(found):
            at = 0
            for part in parts:
                x = rows_ref[i, :, pl.ds(at, part.shape[0])]
                sums += jnp.dot(x, refs[k][...], preferred_element_type=jnp.float32)
                at += part.shape[0]
                k += 1
        refs[-1][...] = sums

    return pl.pallas_call(
        kernel,
        in_specs=[IN_VMEM] * (2 + len(blocks)),
        out_specs=IN_VMEM,
        out_shape=jax.ShapeDtypeStruct(total.shape, jnp.float32),
        cost_estimate=pl.CostEstimate(
            flops=2 * rows.size * width,
            bytes_accessed=2 * rows.size + 8 * total.size,
            transcendentals=0,
        ),
        compiler_params=params(),
        name="last_rotation",
    )(total, rows, *blocks)


def owned_gradients(layout, mine, other, place, owned):
    nz, ny = layout.nz, layout.ny
    tokens, width = mine.shape
    kept = nz * ny * owned

    def kernel(place_ref, mine_ref, other_ref, o_ref):
        slot = lax.broadcasted_iota(jnp.int32, (kept, width), 0)
        column = lax.broadcasted_iota(jnp.int32, (kept, width), 1)
        z, y, core = place_ref[0], place_ref[1], place_ref[2]
        to_y = lax.rem(y + 1 + slot // (nz * owned), ny)
        to_z = lax.rem(z + lax.rem(slot // owned, nz), nz)
        wanted = ((to_z * ny + to_y) * CORES + core) * owned + lax.rem(slot, owned)
        pick = jnp.where(wanted == column, 1.0, 0.0).astype(jnp.bfloat16)
        rotated = (mine_ref[...] + other_ref[...]).astype(jnp.bfloat16)
        picked = lax.dot_general(
            pick, rotated, (((1,), (1,)), ((), ())), preferred_element_type=jnp.float32
        )
        o_ref[...] = picked.astype(jnp.bfloat16)

    return pl.pallas_call(
        kernel,
        in_specs=[IN_SMEM, IN_VMEM, IN_VMEM],
        out_specs=IN_VMEM,
        out_shape=jax.ShapeDtypeStruct((kept, tokens), jnp.bfloat16),
        cost_estimate=pl.CostEstimate(
            flops=2 * kept * width * tokens,
            bytes_accessed=8 * tokens * width + 2 * kept * tokens,
            transcendentals=0,
        ),
        compiler_params=params(),
        name="owned_gradients",
    )(place, mine, other)


def chip_sums(layout, grads, mine, other, positions, lengths, owned, cut):
    nz, ny = layout.nz, layout.ny
    tokens, width = mine.shape
    seqs = lengths.shape[0]
    stay = nz * owned
    rest = width - cut

    def kernel(lengths_ref, grads_ref, mine_ref, other_ref, positions_ref, *refs):
        rotated = mine_ref[...] + other_ref[...]
        position = positions_ref[...]
        begin = jnp.int32(0)
        for s in range(seqs):
            end = begin + lengths_ref[s]
            inside = (position >= begin) & (position < end)
            part = jnp.where(inside, rotated, 0.0).astype(jnp.bfloat16)
            sums = jnp.dot(grads_ref[...], part, preferred_element_type=jnp.float32)
            at = pl.ds(s * cut, cut)
            for d in range(nz):
                for h in range(ny):
                    block = sums[h * stay + d * owned:h * stay + (d + 1) * owned, :cut]
                    refs[d][pl.ds(h * owned, owned), at] = block.astype(refs[d].dtype)
            if rest:
                at = pl.ds(s * rest, rest)
                refs[nz][:, at] = sums[stay:, cut:]
                refs[nz + 1][:, at] = sums[:stay, cut:].astype(jnp.bfloat16)
            begin = end

    shapes = [jax.ShapeDtypeStruct((ny * owned, seqs * cut), jnp.float32)]
    shapes += [jax.ShapeDtypeStruct((ny * owned, seqs * cut), jnp.bfloat16)] * (nz - 1)
    if rest:
        shapes.append(jax.ShapeDtypeStruct((stay, seqs * rest), jnp.float32))
        shapes.append(jax.ShapeDtypeStruct((stay, seqs * rest), jnp.bfloat16))
    return pl.pallas_call(
        kernel,
        in_specs=[IN_SMEM] + [IN_VMEM] * 4,
        out_specs=[IN_VMEM] * len(shapes),
        out_shape=shapes,
        cost_estimate=pl.CostEstimate(
            flops=2 * grads.size * seqs * width,
            bytes_accessed=8 * tokens * width + 2 * grads.shape[0] * seqs * width,
            transcendentals=0,
        ),
        compiler_params=params(),
        name="chip_sums",
    )(lengths, grads, mine, other, positions)


def add_up(kept, came, owned, own):
    count = kept.shape[0] // owned
    width = kept.shape[1]

    def kernel(*refs):
        total = refs[0][...]
        for i in range(len(came)):
            total += refs[1 + i][...].astype(jnp.float32)
        outs = refs[1 + len(came):]
        for i in range(count):
            outs[i][...] = total[i * owned:(i + 1) * owned].astype(outs[i].dtype)

    shapes = [
        jax.ShapeDtypeStruct((owned, width), jnp.float32 if i == own else jnp.bfloat16)
        for i in range(count)
    ]
    return pl.pallas_call(
        kernel,
        in_specs=[IN_VMEM] * (1 + len(came)),
        out_specs=[IN_VMEM] * count,
        out_shape=shapes,
        cost_estimate=pl.CostEstimate(
            flops=kept.size * len(came), bytes_accessed=8 * kept.size, transcendentals=0
        ),
        compiler_params=params(),
        name="add_up",
    )(kept, *came)


def squares(groups, lengths, owned):
    seqs = lengths.shape[0]
    widths = [group[0].shape[1] // seqs for group in groups]

    def kernel(lengths_ref, *refs):
        o_ref = refs[-1]
        tokens = lengths_ref[0]
        for s in range(1, seqs):
            tokens = tokens + lengths_ref[s]
        at, k = 0, 0
        for group, width in zip(groups, widths):
            over = jnp.full((owned, width), tokens, jnp.int32).astype(jnp.float32)
            sums = refs[k][...]
            for ref in refs[k + 1:k + len(group)]:
                sums = sums + ref[...].astype(jnp.float32)
            k += len(group)
            sums = sums * sums
            acc = sums[:, :width]
            for s in range(1, seqs):
                acc = acc + sums[:, s * width:(s + 1) * width]
            o_ref[:, pl.ds(at, width)] = acc / over
            at += width

    flat = [x for group in groups for x in group]
    return pl.pallas_call(
        kernel,
        in_specs=[IN_SMEM] + [IN_VMEM] * len(flat),
        out_specs=IN_VMEM,
        out_shape=jax.ShapeDtypeStruct((owned, sum(widths)), jnp.float32),
        cost_estimate=pl.CostEstimate(
            flops=2 * sum(x.size for x in flat),
            bytes_accessed=2 * sum(x.size for x in flat),
            transcendentals=0,
        ),
        compiler_params=params(),
        name="squares",
    )(lengths, *flat)


def scatter_sums(layout, sums, owned):
    nz, ny = layout.nz, layout.ny
    if ny == 1:
        return [[sums[0]] + [layout.along_z(sums[d], d) for d in range(1, nz)]]
    crossed = [layout.along_y(sums[nz + 1])]
    came = [layout.along_z(sums[d], d) for d in range(1, nz)]
    by_z = add_up(sums[nz], crossed, owned, 0)
    second = [by_z[0]] + [layout.along_z(by_z[d], d) for d in range(1, nz)]
    came[0] = lax.optimization_barrier((came[0], by_z[1]))[0]
    by_y = add_up(sums[0], came, owned, 1)
    return [[by_y[1], layout.along_y(by_y[0])], second]


def shards(layout, activations, gradients, basis_a, basis_g, token_index, seq_lengths):
    nz, ny, chips = layout.nz, layout.ny, layout.chips
    rows = activations.shape[0]
    owned = basis_g.shape[1] // (chips * CORES)
    me = lax.axis_index("row")
    core = lax.rem(me, CORES)
    y = lax.rem(me // CORES, ny)
    z = me // (CORES * ny)
    place = jnp.stack([z, y, core]).astype(jnp.int32)

    sib_index = layout.to_sibling(token_index)
    first = core == 0
    positions = jnp.concatenate(
        [jnp.where(first, token_index, sib_index), jnp.where(first, sib_index, token_index)]
    ).reshape(CORES * rows, 1)

    links = Links(layout, 2)
    sib_g = layout.to_sibling(gradients)
    sib_a = layout.to_sibling(activations)
    split = [basis_g.shape[0] * 4 // 7, basis_a.shape[0] // 2] if ny > 1 else [0, 0]
    early = []

    def rotate_early(found):
        early.append(partial_rotation(layout, gradients, sib_g, found[:4], place))
        return early[0]

    gates = {
        nz - 1: lambda by_z: [by_z[1]],
        nz // 2: lambda by_z: [sib_g, sib_a],
        -1: rotate_early,
    }
    found_g = gather_columns(links, basis_g, split[0], gates)
    mine_g = partial_rotation(layout, gradients, sib_g, found_g[4:], place, early[0])
    found_a = gather_columns(links, basis_a, split[1], {nz // 2: lambda by_z: [mine_g]})
    grads = owned_gradients(layout, mine_g, layout.to_sibling(mine_g), place, owned)

    most, rows_left = partial_rotation(
        layout, activations, sib_a, found_a[:-2], place, None, found_a[-2:]
    )
    most, positions = lax.optimization_barrier((most, positions))
    mine_a = last_rotation(most, rows_left, found_a[-2:])
    cut = basis_a.shape[1] // ny
    sums = chip_sums(
        layout, grads, mine_a, layout.to_sibling(mine_a), positions, seq_lengths, owned, cut
    )
    return squares(scatter_sums(layout, sums, owned), seq_lengths, owned)


def solution(mesh):
    return jax.shard_map(
        functools.partial(shards, Layout(mesh)),
        mesh=mesh,
        in_specs=(
            P(("grp", "row"), None),
            P(("grp", "row"), None),
            P(("grp", "row"), None),
            P(("grp", "row"), None),
            P(("grp", "row")),
            P("grp"),
        ),
        out_specs=P(("grp", "row"), None),
        check_vma=False,
    )
```

```python
import functools

import jax
import jax.numpy as jnp
from jax import lax
from jax.experimental import pallas as pl
from jax.experimental.pallas import tpu as pltpu
from jax.sharding import PartitionSpec as P

CORES = 2
MIB = 1024 * 1024


def params(mib=8):
    return pltpu.CompilerParams(vmem_limit_bytes=mib * MIB)


IN_VMEM = pl.BlockSpec(memory_space=pltpu.VMEM)
IN_SMEM = pl.BlockSpec(memory_space=pltpu.SMEM)
ANYWHERE = pl.BlockSpec(memory_space=pl.ANY)


def in_hbm(x):
    return pltpu.with_memory_space_constraint(x, pltpu.HBM)


class Layout:
    def __init__(self, mesh):
        self.chips = mesh.shape["row"] // CORES
        self.ny = max(1, 4 // mesh.shape["grp"])
        if self.chips % self.ny:
            self.ny = 1
        self.nz = self.chips // self.ny

    def device(self, z, y, core):
        return ((z % self.nz) * self.ny + y % self.ny) * CORES + core

    def everyone(self):
        return [(z, y, c) for z in range(self.nz) for y in range(self.ny) for c in range(CORES)]

    def origin(self, z, y, d, h):
        return lax.rem(z + (self.nz - d), self.nz) * self.ny + lax.rem(y + (self.ny - h), self.ny)

    def along_z(self, x, hops):
        pairs = [(self.device(z, y, c), self.device(z + hops, y, c)) for z, y, c in self.everyone()]
        return lax.ppermute(x, "row", pairs)

    def along_y(self, x, hops=1):
        pairs = [(self.device(z, y, c), self.device(z, y + hops, c)) for z, y, c in self.everyone()]
        return lax.ppermute(x, "row", pairs)

    def to_sibling(self, x):
        pairs = [(self.device(z, y, c), self.device(z, y, 1 - c)) for z, y, c in self.everyone()]
        return lax.ppermute(x, "row", pairs)


def split_columns(act, core, chips):
    rows, depth = act.shape
    kc = depth // (chips * CORES)
    mine = lax.dynamic_index_in_dim(act.reshape(rows, chips, CORES, kc), core, 2, keepdims=False)
    return mine.transpose(1, 0, 2)


class Links:
    def __init__(self, layout, window):
        self.layout, self.window = layout, window
        self.done = {"z": [], "y": []}
        self.first = []

    def after(self, *first):
        self.first += first

    def send(self, kind, x, hops):
        done = self.done[kind]
        first = self.first + done[-self.window:len(done) - self.window + 1]
        self.first = []
        if first:
            x = lax.optimization_barrier((x, *first))[0]
        move = self.layout.along_z if kind == "z" else self.layout.along_y
        done.append(move(x, hops))
        return done[-1]


def gather_columns(links, piece, split, gates):
    nz, ny = links.layout.nz, links.layout.ny
    middle = nz // 2
    steps = [(d, 1) for d in range(1, middle + 1)] + [(d, -1) for d in range(nz - 1, middle, -1)]
    steps = sorted(steps, key=lambda s: (min(s[0], nz - s[0]), -s[1]))
    by_z, crossed, found = {0: piece}, {}, [([piece], 0, 0)]

    def cross(d):
        for h in range(1, ny):
            if d == middle and split:
                head = links.send("z", crossed[d - 1, h][:split], 1)
                if split == piece.shape[0]:
                    got = [head]
                else:
                    got = [head, links.send("y", by_z[d][split:], h)]
            else:
                got = [links.send("y", by_z[d], h)]
            crossed[d, h] = got[0]
            found.append((got, d, h))

    last = 0
    for d, sign in steps:
        links.after(*gates.get(d, ()))
        by_z[d] = links.send("z", by_z[(d - sign) % nz], sign)
        found.append(([by_z[d]], d, 0))
        cross(last)
        last = d
    if -1 in gates:
        links.after(gates[-1](found))
    cross(last)
    links.first = []
    return found


def partial_rotation(layout, act, sib, found, place, total=None, left=()):
    rows = act.shape[0]
    count = len(found)
    blocks = [x for parts, _, _ in found for x in parts]
    kc = sum(x.shape[0] for x in found[0][0])
    width = blocks[0].shape[1]
    unaligned = kc % 128 != 0
    if unaligned:
        act = split_columns(act, place[2], layout.chips)
        sib = split_columns(sib, place[2], layout.chips)

    extra = [] if total is None else [total]

    def kernel(place_ref, act_ref, sib_ref, *refs):
        block_refs, refs = refs[:len(blocks)], refs[len(blocks):]
        o_ref = refs[len(extra)]
        rows_buf, block_buf, sems = refs[-3:]
        z, y, core = place_ref[0], place_ref[1], place_ref[2]
        mine = pl.ds(pl.multiple_of(core * rows, 16), rows)
        other = pl.ds(pl.multiple_of((1 - core) * rows, 16), rows)

        def bring_rows(d, h, to, i):
            q = layout.origin(z, y, d, h)
            at = 0 if unaligned else pl.ds(pl.multiple_of((CORES * q + core) * kc, 128), kc)
            own, its = [ref.at[q] if unaligned else ref.at[:, at] for ref in (act_ref, sib_ref)]
            return [
                pltpu.make_async_copy(own, to.at[mine], sems.at[i, 0]),
                pltpu.make_async_copy(its, to.at[other], sems.at[i, 1]),
            ]

        copies, k = [], 0
        for i in range(count):
            parts, d, h = found[i]
            step, at = bring_rows(d, h, rows_buf.at[i], i), 0
            for j, x in enumerate(parts):
                to = block_buf.at[i, pl.ds(at, x.shape[0])]
                step.append(pltpu.make_async_copy(block_refs[k], to, sems.at[i, 2 + j]))
                at += x.shape[0]
                k += 1
            copies.append(step)
        for j, (_, d, h) in enumerate(left):
            copies.append(bring_rows(d, h, refs[len(extra) + 1].at[j], count + j))
        for step in copies:
            for copy in step:
                copy.start()
        for i, step in enumerate(copies):
            for copy in step:
                copy.wait()
            if i >= count:
                continue
            product = jnp.dot(rows_buf[i], block_buf[i], preferred_element_type=jnp.float32)
            if i > 0:
                o_ref[...] += product
            elif extra:
                o_ref[...] = refs[0][...] + product
            else:
                o_ref[...] = product

    shapes = [jax.ShapeDtypeStruct((CORES * rows, width), jnp.float32)]
    if left:
        shapes.append(jax.ShapeDtypeStruct((len(left), CORES * rows, kc), act.dtype))
    outs = pl.pallas_call(
        kernel,
        in_specs=[IN_SMEM] + [ANYWHERE] * (2 + len(blocks)) + [IN_VMEM] * len(extra),
        out_specs=[IN_VMEM] * len(shapes),
        out_shape=shapes,
        scratch_shapes=[
            pltpu.VMEM((count, CORES * rows, kc), act.dtype),
            pltpu.VMEM((count, kc, width), act.dtype),
            pltpu.SemaphoreType.DMA((count + len(left), 4)),
        ],
        cost_estimate=pl.CostEstimate(
            flops=4 * rows * kc * count * width,
            bytes_accessed=2 * count * kc * (2 * rows + width) + 8 * rows * width,
            transcendentals=0,
        ),
        compiler_params=params(24),
        name="partial_rotation",
    )(place, *[in_hbm(x) for x in (act, sib, *blocks)], *extra)
    return outs if left else outs[0]


def last_rotation(total, rows, found):
    width = total.shape[1]
    blocks = [x for parts, _, _ in found for x in parts]

    def kernel(total_ref, rows_ref, *refs):
        sums, k = total_ref[...], 0
        for i, (parts, _, _) in enumerate(found):
            at = 0
            for part in parts:
                x = rows_ref[i, :, pl.ds(at, part.shape[0])]
                sums += jnp.dot(x, refs[k][...], preferred_element_type=jnp.float32)
                at += part.shape[0]
                k += 1
        refs[-1][...] = sums

    return pl.pallas_call(
        kernel,
        in_specs=[IN_VMEM] * (2 + len(blocks)),
        out_specs=IN_VMEM,
        out_shape=jax.ShapeDtypeStruct(total.shape, jnp.float32),
        cost_estimate=pl.CostEstimate(
            flops=2 * rows.size * width,
            bytes_accessed=2 * rows.size + 8 * total.size,
            transcendentals=0,
        ),
        compiler_params=params(),
        name="last_rotation",
    )(total, rows, *blocks)


def owned_gradients(layout, mine, other, place, owned):
    nz, ny = layout.nz, layout.ny
    tokens, width = mine.shape
    kept = nz * ny * owned

    def kernel(place_ref, mine_ref, other_ref, o_ref):
        slot = lax.broadcasted_iota(jnp.int32, (kept, width), 0)
        column = lax.broadcasted_iota(jnp.int32, (kept, width), 1)
        z, y, core = place_ref[0], place_ref[1], place_ref[2]
        to_y = lax.rem(y + 1 + slot // (nz * owned), ny)
        to_z = lax.rem(z + lax.rem(slot // owned, nz), nz)
        wanted = ((to_z * ny + to_y) * CORES + core) * owned + lax.rem(slot, owned)
        pick = jnp.where(wanted == column, 1.0, 0.0).astype(jnp.bfloat16)
        rotated = (mine_ref[...] + other_ref[...]).astype(jnp.bfloat16)
        picked = lax.dot_general(
            pick, rotated, (((1,), (1,)), ((), ())), preferred_element_type=jnp.float32
        )
        o_ref[...] = picked.astype(jnp.bfloat16)

    return pl.pallas_call(
        kernel,
        in_specs=[IN_SMEM, IN_VMEM, IN_VMEM],
        out_specs=IN_VMEM,
        out_shape=jax.ShapeDtypeStruct((kept, tokens), jnp.bfloat16),
        cost_estimate=pl.CostEstimate(
            flops=2 * kept * width * tokens,
            bytes_accessed=8 * tokens * width + 2 * kept * tokens,
            transcendentals=0,
        ),
        compiler_params=params(),
        name="owned_gradients",
    )(place, mine, other)


def chip_sums(layout, grads, mine, other, positions, lengths, owned, cut):
    nz, ny = layout.nz, layout.ny
    tokens, width = mine.shape
    seqs = lengths.shape[0]
    stay = nz * owned
    rest = width - cut

    def kernel(lengths_ref, grads_ref, mine_ref, other_ref, positions_ref, *refs):
        rotated = mine_ref[...] + other_ref[...]
        position = positions_ref[...]
        begin = jnp.int32(0)
        for s in range(seqs):
            end = begin + lengths_ref[s]
            inside = (position >= begin) & (position < end)
            part = jnp.where(inside, rotated, 0.0).astype(jnp.bfloat16)
            sums = jnp.dot(grads_ref[...], part, preferred_element_type=jnp.float32)
            at = pl.ds(s * cut, cut)
            for d in range(nz):
                for h in range(ny):
                    block = sums[h * stay + d * owned:h * stay + (d + 1) * owned, :cut]
                    refs[d][pl.ds(h * owned, owned), at] = block.astype(refs[d].dtype)
            if rest:
                at = pl.ds(s * rest, rest)
                refs[nz][:, at] = sums[stay:, cut:]
                refs[nz + 1][:, at] = sums[:stay, cut:].astype(jnp.bfloat16)
            begin = end

    shapes = [jax.ShapeDtypeStruct((ny * owned, seqs * cut), jnp.float32)]
    shapes += [jax.ShapeDtypeStruct((ny * owned, seqs * cut), jnp.bfloat16)] * (nz - 1)
    if rest:
        shapes.append(jax.ShapeDtypeStruct((stay, seqs * rest), jnp.float32))
        shapes.append(jax.ShapeDtypeStruct((stay, seqs * rest), jnp.bfloat16))
    return pl.pallas_call(
        kernel,
        in_specs=[IN_SMEM] + [IN_VMEM] * 4,
        out_specs=[IN_VMEM] * len(shapes),
        out_shape=shapes,
        cost_estimate=pl.CostEstimate(
            flops=2 * grads.size * seqs * width,
            bytes_accessed=8 * tokens * width + 2 * grads.shape[0] * seqs * width,
            transcendentals=0,
        ),
        compiler_params=params(),
        name="chip_sums",
    )(lengths, grads, mine, other, positions)


def add_up(kept, came, owned, own):
    count = kept.shape[0] // owned
    width = kept.shape[1]

    def kernel(*refs):
        total = refs[0][...]
        for i in range(len(came)):
            total += refs[1 + i][...].astype(jnp.float32)
        outs = refs[1 + len(came):]
        for i in range(count):
            outs[i][...] = total[i * owned:(i + 1) * owned].astype(outs[i].dtype)

    shapes = [
        jax.ShapeDtypeStruct((owned, width), jnp.float32 if i == own else jnp.bfloat16)
        for i in range(count)
    ]
    return pl.pallas_call(
        kernel,
        in_specs=[IN_VMEM] * (1 + len(came)),
        out_specs=[IN_VMEM] * count,
        out_shape=shapes,
        cost_estimate=pl.CostEstimate(
            flops=kept.size * len(came), bytes_accessed=8 * kept.size, transcendentals=0
        ),
        compiler_params=params(),
        name="add_up",
    )(kept, *came)


def squares(groups, lengths, owned):
    seqs = lengths.shape[0]
    widths = [group[0].shape[1] // seqs for group in groups]

    def kernel(lengths_ref, *refs):
        o_ref = refs[-1]
        tokens = lengths_ref[0]
        for s in range(1, seqs):
            tokens = tokens + lengths_ref[s]
        at, k = 0, 0
        for group, width in zip(groups, widths):
            over = jnp.full((owned, width), tokens, jnp.int32).astype(jnp.float32)
            sums = refs[k][...]
            for ref in refs[k + 1:k + len(group)]:
                sums = sums + ref[...].astype(jnp.float32)
            k += len(group)
            sums = sums * sums
            acc = sums[:, :width]
            for s in range(1, seqs):
                acc = acc + sums[:, s * width:(s + 1) * width]
            o_ref[:, pl.ds(at, width)] = acc / over
            at += width

    flat = [x for group in groups for x in group]
    return pl.pallas_call(
        kernel,
        in_specs=[IN_SMEM] + [IN_VMEM] * len(flat),
        out_specs=IN_VMEM,
        out_shape=jax.ShapeDtypeStruct((owned, sum(widths)), jnp.float32),
        cost_estimate=pl.CostEstimate(
            flops=2 * sum(x.size for x in flat),
            bytes_accessed=2 * sum(x.size for x in flat),
            transcendentals=0,
        ),
        compiler_params=params(),
        name="squares",
    )(lengths, *flat)


def scatter_sums(layout, sums, owned):
    nz, ny = layout.nz, layout.ny
    if ny == 1:
        return [[sums[0]] + [layout.along_z(sums[d], d) for d in range(1, nz)]]
    crossed = [layout.along_y(sums[nz + 1])]
    came = [layout.along_z(sums[d], d) for d in range(1, nz)]
    by_z = add_up(sums[nz], crossed, owned, 0)
    second = [by_z[0]] + [layout.along_z(by_z[d], d) for d in range(1, nz)]
    came[0] = lax.optimization_barrier((came[0], by_z[1]))[0]
    by_y = add_up(sums[0], came, owned, 1)
    return [[by_y[1], layout.along_y(by_y[0])], second]


def shards(layout, activations, gradients, basis_a, basis_g, token_index, seq_lengths):
    nz, ny, chips = layout.nz, layout.ny, layout.chips
    rows = activations.shape[0]
    owned = basis_g.shape[1] // (chips * CORES)
    me = lax.axis_index("row")
    core = lax.rem(me, CORES)
    y = lax.rem(me // CORES, ny)
    z = me // (CORES * ny)
    place = jnp.stack([z, y, core]).astype(jnp.int32)

    sib_index = layout.to_sibling(token_index)
    first = core == 0
    positions = jnp.concatenate(
        [jnp.where(first, token_index, sib_index), jnp.where(first, sib_index, token_index)]
    ).reshape(CORES * rows, 1)

    links = Links(layout, 2)
    sib_g = layout.to_sibling(gradients)
    sib_a = layout.to_sibling(activations)
    split = [basis_g.shape[0] * 4 // 7, basis_a.shape[0] // 2] if ny > 1 else [0, 0]
    early = []

    def rotate_early(found):
        early.append(partial_rotation(layout, gradients, sib_g, found[:4], place))
        return early[0]

    gates = {nz // 2: [sib_g, sib_a], -1: rotate_early}
    found_g = gather_columns(links, basis_g, split[0], gates)
    mine_g = partial_rotation(layout, gradients, sib_g, found_g[4:], place, early[0])
    found_a = gather_columns(links, basis_a, split[1], {nz // 2: [mine_g]})
    grads = owned_gradients(layout, mine_g, layout.to_sibling(mine_g), place, owned)

    most, rows_left = partial_rotation(
        layout, activations, sib_a, found_a[:-2], place, None, found_a[-2:]
    )
    most, positions = lax.optimization_barrier((most, positions))
    mine_a = last_rotation(most, rows_left, found_a[-2:])
    cut = basis_a.shape[1] // ny
    sums = chip_sums(
        layout, grads, mine_a, layout.to_sibling(mine_a), positions, seq_lengths, owned, cut
    )
    return squares(scatter_sums(layout, sums, owned), seq_lengths, owned)


def solution(mesh):
    return jax.shard_map(
        functools.partial(shards, Layout(mesh)),
        mesh=mesh,
        in_specs=(
            P(("grp", "row"), None),
            P(("grp", "row"), None),
            P(("grp", "row"), None),
            P(("grp", "row"), None),
            P(("grp", "row")),
            P("grp"),
        ),
        out_specs=P(("grp", "row"), None),
        check_vma=False,
    )
```

```python
import functools

import jax
import jax.numpy as jnp
from jax import lax
from jax.experimental import pallas as pl
from jax.experimental.pallas import tpu as pltpu
from jax.sharding import PartitionSpec as P

CORES = 2
MIB = 1024 * 1024


def params(mib=8):
    return pltpu.CompilerParams(vmem_limit_bytes=mib * MIB)


IN_VMEM = pl.BlockSpec(memory_space=pltpu.VMEM)
IN_SMEM = pl.BlockSpec(memory_space=pltpu.SMEM)
ANYWHERE = pl.BlockSpec(memory_space=pl.ANY)


def in_hbm(x):
    return pltpu.with_memory_space_constraint(x, pltpu.HBM)


class Layout:
    def __init__(self, mesh):
        self.chips = mesh.shape["row"] // CORES
        self.ny = max(1, 4 // mesh.shape["grp"])
        if self.chips % self.ny:
            self.ny = 1
        self.nz = self.chips // self.ny

    def device(self, z, y, core):
        return ((z % self.nz) * self.ny + y % self.ny) * CORES + core

    def everyone(self):
        return [(z, y, c) for z in range(self.nz) for y in range(self.ny) for c in range(CORES)]

    def origin(self, z, y, d, h):
        return lax.rem(z + (self.nz - d), self.nz) * self.ny + lax.rem(y + (self.ny - h), self.ny)

    def along_z(self, x, hops):
        pairs = [(self.device(z, y, c), self.device(z + hops, y, c)) for z, y, c in self.everyone()]
        return lax.ppermute(x, "row", pairs)

    def along_y(self, x, hops=1):
        pairs = [(self.device(z, y, c), self.device(z, y + hops, c)) for z, y, c in self.everyone()]
        return lax.ppermute(x, "row", pairs)

    def to_sibling(self, x):
        pairs = [(self.device(z, y, c), self.device(z, y, 1 - c)) for z, y, c in self.everyone()]
        return lax.ppermute(x, "row", pairs)


def split_columns(act, core, chips):
    rows, depth = act.shape
    kc = depth // (chips * CORES)
    mine = lax.dynamic_index_in_dim(act.reshape(rows, chips, CORES, kc), core, 2, keepdims=False)
    return mine.transpose(1, 0, 2)


class Links:
    def __init__(self, layout, window):
        self.layout, self.window = layout, window
        self.done = {"z": [], "y": []}
        self.first = []

    def after(self, *first):
        self.first += first

    def send(self, kind, x, hops):
        done = self.done[kind]
        first = self.first + done[-self.window:len(done) - self.window + 1]
        self.first = []
        if first:
            x = lax.optimization_barrier((x, *first))[0]
        move = self.layout.along_z if kind == "z" else self.layout.along_y
        done.append(move(x, hops))
        return done[-1]


def gather_columns(links, piece, split, gates):
    nz, ny = links.layout.nz, links.layout.ny
    middle = nz // 2
    steps = [(d, 1) for d in range(1, middle + 1)] + [(d, -1) for d in range(nz - 1, middle, -1)]
    steps = sorted(steps, key=lambda s: (min(s[0], nz - s[0]), -s[1]))
    by_z, crossed, found = {0: piece}, {}, [([piece], 0, 0)]

    def cross(d):
        for h in range(1, ny):
            if d == middle and split:
                head = links.send("z", crossed[d - 1, h][:split], 1)
                if -1 in gates:
                    links.after(gates[-1](found))
                if split == piece.shape[0]:
                    got = [head]
                else:
                    got = [head, links.send("y", by_z[d][split:], h)]
            else:
                got = [links.send("y", by_z[d], h)]
            crossed[d, h] = got[0]
            found.append((got, d, h))

    last = 0
    for d, sign in steps:
        links.after(*gates.get(d, ()))
        by_z[d] = links.send("z", by_z[(d - sign) % nz], sign)
        found.append(([by_z[d]], d, 0))
        cross(last)
        last = d
    cross(last)
    links.first = []
    return found


def partial_rotation(layout, act, sib, found, place, total=None, left=()):
    rows = act.shape[0]
    count = len(found)
    blocks = [x for parts, _, _ in found for x in parts]
    kc = sum(x.shape[0] for x in found[0][0])
    width = blocks[0].shape[1]
    unaligned = kc % 128 != 0
    if unaligned:
        act = split_columns(act, place[2], layout.chips)
        sib = split_columns(sib, place[2], layout.chips)

    extra = [] if total is None else [total]

    def kernel(place_ref, act_ref, sib_ref, *refs):
        block_refs, refs = refs[:len(blocks)], refs[len(blocks):]
        o_ref = refs[len(extra)]
        rows_buf, block_buf, sems = refs[-3:]
        z, y, core = place_ref[0], place_ref[1], place_ref[2]
        mine = pl.ds(pl.multiple_of(core * rows, 16), rows)
        other = pl.ds(pl.multiple_of((1 - core) * rows, 16), rows)

        def bring_rows(d, h, to, i):
            q = layout.origin(z, y, d, h)
            at = 0 if unaligned else pl.ds(pl.multiple_of((CORES * q + core) * kc, 128), kc)
            own, its = [ref.at[q] if unaligned else ref.at[:, at] for ref in (act_ref, sib_ref)]
            return [
                pltpu.make_async_copy(own, to.at[mine], sems.at[i, 0]),
                pltpu.make_async_copy(its, to.at[other], sems.at[i, 1]),
            ]

        copies, k = [], 0
        for i in range(count):
            parts, d, h = found[i]
            step, at = bring_rows(d, h, rows_buf.at[i], i), 0
            for j, x in enumerate(parts):
                to = block_buf.at[i, pl.ds(at, x.shape[0])]
                step.append(pltpu.make_async_copy(block_refs[k], to, sems.at[i, 2 + j]))
                at += x.shape[0]
                k += 1
            copies.append(step)
        for j, (_, d, h) in enumerate(left):
            copies.append(bring_rows(d, h, refs[len(extra) + 1].at[j], count + j))
        for step in copies:
            for copy in step:
                copy.start()
        for i, step in enumerate(copies):
            for copy in step:
                copy.wait()
            if i >= count:
                continue
            product = jnp.dot(rows_buf[i], block_buf[i], preferred_element_type=jnp.float32)
            if i > 0:
                o_ref[...] += product
            elif extra:
                o_ref[...] = refs[0][...] + product
            else:
                o_ref[...] = product

    shapes = [jax.ShapeDtypeStruct((CORES * rows, width), jnp.float32)]
    if left:
        shapes.append(jax.ShapeDtypeStruct((len(left), CORES * rows, kc), act.dtype))
    outs = pl.pallas_call(
        kernel,
        in_specs=[IN_SMEM] + [ANYWHERE] * (2 + len(blocks)) + [IN_VMEM] * len(extra),
        out_specs=[IN_VMEM] * len(shapes),
        out_shape=shapes,
        scratch_shapes=[
            pltpu.VMEM((count, CORES * rows, kc), act.dtype),
            pltpu.VMEM((count, kc, width), act.dtype),
            pltpu.SemaphoreType.DMA((count + len(left), 4)),
        ],
        cost_estimate=pl.CostEstimate(
            flops=4 * rows * kc * count * width,
            bytes_accessed=2 * count * kc * (2 * rows + width) + 8 * rows * width,
            transcendentals=0,
        ),
        compiler_params=params(24),
        name="partial_rotation",
    )(place, *[in_hbm(x) for x in (act, sib, *blocks)], *extra)
    return outs if left else outs[0]


def last_rotation(total, rows, found):
    width = total.shape[1]
    blocks = [x for parts, _, _ in found for x in parts]

    def kernel(total_ref, rows_ref, *refs):
        sums, k = total_ref[...], 0
        for i, (parts, _, _) in enumerate(found):
            at = 0
            for part in parts:
                x = rows_ref[i, :, pl.ds(at, part.shape[0])]
                sums += jnp.dot(x, refs[k][...], preferred_element_type=jnp.float32)
                at += part.shape[0]
                k += 1
        refs[-1][...] = sums

    return pl.pallas_call(
        kernel,
        in_specs=[IN_VMEM] * (2 + len(blocks)),
        out_specs=IN_VMEM,
        out_shape=jax.ShapeDtypeStruct(total.shape, jnp.float32),
        cost_estimate=pl.CostEstimate(
            flops=2 * rows.size * width,
            bytes_accessed=2 * rows.size + 8 * total.size,
            transcendentals=0,
        ),
        compiler_params=params(),
        name="last_rotation",
    )(total, rows, *blocks)


def owned_gradients(layout, mine, other, place, owned):
    nz, ny = layout.nz, layout.ny
    tokens, width = mine.shape
    kept = nz * ny * owned

    def kernel(place_ref, mine_ref, other_ref, o_ref):
        slot = lax.broadcasted_iota(jnp.int32, (kept, width), 0)
        column = lax.broadcasted_iota(jnp.int32, (kept, width), 1)
        z, y, core = place_ref[0], place_ref[1], place_ref[2]
        to_y = lax.rem(y + 1 + slot // (nz * owned), ny)
        to_z = lax.rem(z + lax.rem(slot // owned, nz), nz)
        wanted = ((to_z * ny + to_y) * CORES + core) * owned + lax.rem(slot, owned)
        pick = jnp.where(wanted == column, 1.0, 0.0).astype(jnp.bfloat16)
        rotated = (mine_ref[...] + other_ref[...]).astype(jnp.bfloat16)
        picked = lax.dot_general(
            pick, rotated, (((1,), (1,)), ((), ())), preferred_element_type=jnp.float32
        )
        o_ref[...] = picked.astype(jnp.bfloat16)

    return pl.pallas_call(
        kernel,
        in_specs=[IN_SMEM, IN_VMEM, IN_VMEM],
        out_specs=IN_VMEM,
        out_shape=jax.ShapeDtypeStruct((kept, tokens), jnp.bfloat16),
        cost_estimate=pl.CostEstimate(
            flops=2 * kept * width * tokens,
            bytes_accessed=8 * tokens * width + 2 * kept * tokens,
            transcendentals=0,
        ),
        compiler_params=params(),
        name="owned_gradients",
    )(place, mine, other)


def chip_sums(layout, grads, mine, other, positions, lengths, owned, cut):
    nz, ny = layout.nz, layout.ny
    tokens, width = mine.shape
    seqs = lengths.shape[0]
    stay = nz * owned
    rest = width - cut

    def kernel(lengths_ref, grads_ref, mine_ref, other_ref, positions_ref, *refs):
        rotated = mine_ref[...] + other_ref[...]
        position = positions_ref[...]
        begin = jnp.int32(0)
        for s in range(seqs):
            end = begin + lengths_ref[s]
            inside = (position >= begin) & (position < end)
            part = jnp.where(inside, rotated, 0.0).astype(jnp.bfloat16)
            sums = jnp.dot(grads_ref[...], part, preferred_element_type=jnp.float32)
            at = pl.ds(s * cut, cut)
            for d in range(nz):
                for h in range(ny):
                    block = sums[h * stay + d * owned:h * stay + (d + 1) * owned, :cut]
                    refs[d][pl.ds(h * owned, owned), at] = block.astype(refs[d].dtype)
            if rest:
                at = pl.ds(s * rest, rest)
                refs[nz][:, at] = sums[stay:, cut:]
                refs[nz + 1][:, at] = sums[:stay, cut:].astype(jnp.bfloat16)
            begin = end

    shapes = [jax.ShapeDtypeStruct((ny * owned, seqs * cut), jnp.float32)]
    shapes += [jax.ShapeDtypeStruct((ny * owned, seqs * cut), jnp.bfloat16)] * (nz - 1)
    if rest:
        shapes.append(jax.ShapeDtypeStruct((stay, seqs * rest), jnp.float32))
        shapes.append(jax.ShapeDtypeStruct((stay, seqs * rest), jnp.bfloat16))
    return pl.pallas_call(
        kernel,
        in_specs=[IN_SMEM] + [IN_VMEM] * 4,
        out_specs=[IN_VMEM] * len(shapes),
        out_shape=shapes,
        cost_estimate=pl.CostEstimate(
            flops=2 * grads.size * seqs * width,
            bytes_accessed=8 * tokens * width + 2 * grads.shape[0] * seqs * width,
            transcendentals=0,
        ),
        compiler_params=params(),
        name="chip_sums",
    )(lengths, grads, mine, other, positions)


def add_up(kept, came, owned, own):
    count = kept.shape[0] // owned
    width = kept.shape[1]

    def kernel(*refs):
        total = refs[0][...]
        for i in range(len(came)):
            total += refs[1 + i][...].astype(jnp.float32)
        outs = refs[1 + len(came):]
        for i in range(count):
            outs[i][...] = total[i * owned:(i + 1) * owned].astype(outs[i].dtype)

    shapes = [
        jax.ShapeDtypeStruct((owned, width), jnp.float32 if i == own else jnp.bfloat16)
        for i in range(count)
    ]
    return pl.pallas_call(
        kernel,
        in_specs=[IN_VMEM] * (1 + len(came)),
        out_specs=[IN_VMEM] * count,
        out_shape=shapes,
        cost_estimate=pl.CostEstimate(
            flops=kept.size * len(came), bytes_accessed=8 * kept.size, transcendentals=0
        ),
        compiler_params=params(),
        name="add_up",
    )(kept, *came)


def squares(groups, lengths, owned):
    seqs = lengths.shape[0]
    widths = [group[0].shape[1] // seqs for group in groups]

    def kernel(lengths_ref, *refs):
        o_ref = refs[-1]
        tokens = lengths_ref[0]
        for s in range(1, seqs):
            tokens = tokens + lengths_ref[s]
        at, k = 0, 0
        for group, width in zip(groups, widths):
            over = jnp.full((owned, width), tokens, jnp.int32).astype(jnp.float32)
            sums = refs[k][...]
            for ref in refs[k + 1:k + len(group)]:
                sums = sums + ref[...].astype(jnp.float32)
            k += len(group)
            sums = sums * sums
            acc = sums[:, :width]
            for s in range(1, seqs):
                acc = acc + sums[:, s * width:(s + 1) * width]
            o_ref[:, pl.ds(at, width)] = acc / over
            at += width

    flat = [x for group in groups for x in group]
    return pl.pallas_call(
        kernel,
        in_specs=[IN_SMEM] + [IN_VMEM] * len(flat),
        out_specs=IN_VMEM,
        out_shape=jax.ShapeDtypeStruct((owned, sum(widths)), jnp.float32),
        cost_estimate=pl.CostEstimate(
            flops=2 * sum(x.size for x in flat),
            bytes_accessed=2 * sum(x.size for x in flat),
            transcendentals=0,
        ),
        compiler_params=params(),
        name="squares",
    )(lengths, *flat)


def scatter_sums(layout, sums, owned):
    nz, ny = layout.nz, layout.ny
    if ny == 1:
        return [[sums[0]] + [layout.along_z(sums[d], d) for d in range(1, nz)]]
    crossed = [layout.along_y(sums[nz + 1])]
    came = [layout.along_z(sums[d], d) for d in range(1, nz)]
    by_z = add_up(sums[nz], crossed, owned, 0)
    second = [by_z[0]] + [layout.along_z(by_z[d], d) for d in range(1, nz)]
    by_y = add_up(sums[0], came, owned, 1)
    return [[by_y[1], layout.along_y(by_y[0])], second]


def shards(layout, activations, gradients, basis_a, basis_g, token_index, seq_lengths):
    nz, ny, chips = layout.nz, layout.ny, layout.chips
    rows = activations.shape[0]
    owned = basis_g.shape[1] // (chips * CORES)
    me = lax.axis_index("row")
    core = lax.rem(me, CORES)
    y = lax.rem(me // CORES, ny)
    z = me // (CORES * ny)
    place = jnp.stack([z, y, core]).astype(jnp.int32)

    sib_index = layout.to_sibling(token_index)
    first = core == 0
    positions = jnp.concatenate(
        [jnp.where(first, token_index, sib_index), jnp.where(first, sib_index, token_index)]
    ).reshape(CORES * rows, 1)

    links = Links(layout, 2)
    sib_g = layout.to_sibling(gradients)
    sib_a = layout.to_sibling(activations)
    split = [basis_g.shape[0] * 4 // 7, basis_a.shape[0] // 2] if ny > 1 else [0, 0]
    early = []

    def rotate_early(found):
        early.append(partial_rotation(layout, gradients, sib_g, found[:4], place))
        return early[0]

    gates = {nz // 2: [sib_g, sib_a], -1: rotate_early}
    found_g = gather_columns(links, basis_g, split[0], gates)
    if not early:
        rotate_early(found_g)
    mine_g = partial_rotation(layout, gradients, sib_g, found_g[4:], place, early[0])
    found_a = gather_columns(links, basis_a, split[1], {nz // 2: [mine_g]})
    grads = owned_gradients(layout, mine_g, layout.to_sibling(mine_g), place, owned)

    most, rows_left = partial_rotation(
        layout, activations, sib_a, found_a[:-2], place, None, found_a[-2:]
    )
    most, positions = lax.optimization_barrier((most, positions))
    mine_a = last_rotation(most, rows_left, found_a[-2:])
    cut = basis_a.shape[1] // ny**2
    sums = chip_sums(
        layout, grads, mine_a, layout.to_sibling(mine_a), positions, seq_lengths, owned, cut
    )
    return squares(scatter_sums(layout, sums, owned), seq_lengths, owned)


def solution(mesh):
    return jax.shard_map(
        functools.partial(shards, Layout(mesh)),
        mesh=mesh,
        in_specs=(
            P(("grp", "row"), None),
            P(("grp", "row"), None),
            P(("grp", "row"), None),
            P(("grp", "row"), None),
            P(("grp", "row")),
            P("grp"),
        ),
        out_specs=P(("grp", "row"), None),
        check_vma=False,
    )
```

```python
import functools

import jax
import jax.numpy as jnp
from jax import lax
from jax.experimental import pallas as pl
from jax.experimental.pallas import tpu as pltpu
from jax.sharding import PartitionSpec as P

CORES = 2
MIB = 1024 * 1024


def params(mib=8):
    return pltpu.CompilerParams(vmem_limit_bytes=mib * MIB)


IN_VMEM = pl.BlockSpec(memory_space=pltpu.VMEM)
IN_SMEM = pl.BlockSpec(memory_space=pltpu.SMEM)
ANYWHERE = pl.BlockSpec(memory_space=pl.ANY)


def in_hbm(x):
    return pltpu.with_memory_space_constraint(x, pltpu.HBM)


class Layout:
    def __init__(self, mesh):
        self.chips = mesh.shape["row"] // CORES
        self.ny = max(1, 4 // mesh.shape["grp"])
        if self.chips % self.ny:
            self.ny = 1
        self.nz = self.chips // self.ny

    def device(self, z, y, core):
        return ((z % self.nz) * self.ny + y % self.ny) * CORES + core

    def everyone(self):
        return [(z, y, c) for z in range(self.nz) for y in range(self.ny) for c in range(CORES)]

    def origin(self, z, y, d, h):
        return lax.rem(z + (self.nz - d), self.nz) * self.ny + lax.rem(y + (self.ny - h), self.ny)

    def along_z(self, x, hops):
        pairs = [(self.device(z, y, c), self.device(z + hops, y, c)) for z, y, c in self.everyone()]
        return lax.ppermute(x, "row", pairs)

    def along_y(self, x, hops=1):
        pairs = [(self.device(z, y, c), self.device(z, y + hops, c)) for z, y, c in self.everyone()]
        return lax.ppermute(x, "row", pairs)

    def to_sibling(self, x):
        pairs = [(self.device(z, y, c), self.device(z, y, 1 - c)) for z, y, c in self.everyone()]
        return lax.ppermute(x, "row", pairs)


def split_columns(act, core, chips):
    rows, depth = act.shape
    kc = depth // (chips * CORES)
    mine = lax.dynamic_index_in_dim(act.reshape(rows, chips, CORES, kc), core, 2, keepdims=False)
    return mine.transpose(1, 0, 2)


class Links:
    def __init__(self, layout, window):
        self.layout, self.window = layout, window
        self.done = {"z": [], "y": []}
        self.first = []

    def after(self, *first):
        self.first += first

    def send(self, kind, x, hops):
        done = self.done[kind]
        first = self.first + done[-self.window:len(done) - self.window + 1]
        self.first = []
        if first:
            x = lax.optimization_barrier((x, *first))[0]
        move = self.layout.along_z if kind == "z" else self.layout.along_y
        done.append(move(x, hops))
        return done[-1]


def gather_columns(links, piece, split, gates):
    nz, ny = links.layout.nz, links.layout.ny
    middle = nz // 2
    steps = [(d, 1) for d in range(1, middle + 1)] + [(d, -1) for d in range(nz - 1, middle, -1)]
    steps = sorted(steps, key=lambda s: (min(s[0], nz - s[0]), -s[1]))
    by_z, crossed, found = {0: piece}, {}, [([piece], 0, 0)]

    def cross(d):
        for h in range(1, ny):
            if d == middle and split:
                head = links.send("z", crossed[d - 1, h][:split], 1)
                if -1 in gates:
                    links.after(gates[-1](found))
                if split == piece.shape[0]:
                    got = [head]
                else:
                    got = [head, links.send("y", by_z[d][split:], h)]
            else:
                links.after(*gates.get(("y", d), ()))
                got = [links.send("y", by_z[d], h)]
            crossed[d, h] = got[0]
            found.append((got, d, h))

    last = 0
    for d, sign in steps:
        links.after(*gates.get(d, ()))
        by_z[d] = links.send("z", by_z[(d - sign) % nz], sign)
        found.append(([by_z[d]], d, 0))
        cross(last)
        last = d
    cross(last)
    links.first = []
    return found


def partial_rotation(layout, act, sib, found, place, total=None, left=()):
    rows = act.shape[0]
    count = len(found)
    blocks = [x for parts, _, _ in found for x in parts]
    kc = sum(x.shape[0] for x in found[0][0])
    width = blocks[0].shape[1]
    unaligned = kc % 128 != 0
    if unaligned:
        act = split_columns(act, place[2], layout.chips)
        sib = split_columns(sib, place[2], layout.chips)

    extra = [] if total is None else [total]

    def kernel(place_ref, act_ref, sib_ref, *refs):
        block_refs, refs = refs[:len(blocks)], refs[len(blocks):]
        o_ref = refs[len(extra)]
        rows_buf, block_buf, sems = refs[-3:]
        z, y, core = place_ref[0], place_ref[1], place_ref[2]
        mine = pl.ds(pl.multiple_of(core * rows, 16), rows)
        other = pl.ds(pl.multiple_of((1 - core) * rows, 16), rows)

        def bring_rows(d, h, to, i):
            q = layout.origin(z, y, d, h)
            at = 0 if unaligned else pl.ds(pl.multiple_of((CORES * q + core) * kc, 128), kc)
            own, its = [ref.at[q] if unaligned else ref.at[:, at] for ref in (act_ref, sib_ref)]
            return [
                pltpu.make_async_copy(own, to.at[mine], sems.at[i, 0]),
                pltpu.make_async_copy(its, to.at[other], sems.at[i, 1]),
            ]

        copies, k = [], 0
        for i in range(count):
            parts, d, h = found[i]
            step, at = bring_rows(d, h, rows_buf.at[i], i), 0
            for j, x in enumerate(parts):
                to = block_buf.at[i, pl.ds(at, x.shape[0])]
                step.append(pltpu.make_async_copy(block_refs[k], to, sems.at[i, 2 + j]))
                at += x.shape[0]
                k += 1
            copies.append(step)
        for j, (_, d, h) in enumerate(left):
            copies.append(bring_rows(d, h, refs[len(extra) + 1].at[j], count + j))
        for step in copies:
            for copy in step:
                copy.start()
        for i, step in enumerate(copies):
            for copy in step:
                copy.wait()
            if i >= count:
                continue
            product = jnp.dot(rows_buf[i], block_buf[i], preferred_element_type=jnp.float32)
            if i > 0:
                o_ref[...] += product
            elif extra:
                o_ref[...] = refs[0][...] + product
            else:
                o_ref[...] = product

    shapes = [jax.ShapeDtypeStruct((CORES * rows, width), jnp.float32)]
    if left:
        shapes.append(jax.ShapeDtypeStruct((len(left), CORES * rows, kc), act.dtype))
    outs = pl.pallas_call(
        kernel,
        in_specs=[IN_SMEM] + [ANYWHERE] * (2 + len(blocks)) + [IN_VMEM] * len(extra),
        out_specs=[IN_VMEM] * len(shapes),
        out_shape=shapes,
        scratch_shapes=[
            pltpu.VMEM((count, CORES * rows, kc), act.dtype),
            pltpu.VMEM((count, kc, width), act.dtype),
            pltpu.SemaphoreType.DMA((count + len(left), 4)),
        ],
        cost_estimate=pl.CostEstimate(
            flops=4 * rows * kc * count * width,
            bytes_accessed=2 * count * kc * (2 * rows + width) + 8 * rows * width,
            transcendentals=0,
        ),
        compiler_params=params(24),
        name="partial_rotation",
    )(place, *[in_hbm(x) for x in (act, sib, *blocks)], *extra)
    return outs if left else outs[0]


def last_rotation(total, rows, found):
    width = total.shape[1]
    blocks = [x for parts, _, _ in found for x in parts]

    def kernel(total_ref, rows_ref, *refs):
        sums, k = total_ref[...], 0
        for i, (parts, _, _) in enumerate(found):
            at = 0
            for part in parts:
                x = rows_ref[i, :, pl.ds(at, part.shape[0])]
                sums += jnp.dot(x, refs[k][...], preferred_element_type=jnp.float32)
                at += part.shape[0]
                k += 1
        refs[-1][...] = sums

    return pl.pallas_call(
        kernel,
        in_specs=[IN_VMEM] * (2 + len(blocks)),
        out_specs=IN_VMEM,
        out_shape=jax.ShapeDtypeStruct(total.shape, jnp.float32),
        cost_estimate=pl.CostEstimate(
            flops=2 * rows.size * width,
            bytes_accessed=2 * rows.size + 8 * total.size,
            transcendentals=0,
        ),
        compiler_params=params(),
        name="last_rotation",
    )(total, rows, *blocks)


def owned_gradients(layout, mine, other, place, owned):
    nz, ny = layout.nz, layout.ny
    tokens, width = mine.shape
    kept = nz * ny * owned

    def kernel(place_ref, mine_ref, other_ref, o_ref):
        slot = lax.broadcasted_iota(jnp.int32, (kept, width), 0)
        column = lax.broadcasted_iota(jnp.int32, (kept, width), 1)
        z, y, core = place_ref[0], place_ref[1], place_ref[2]
        to_y = lax.rem(y + 1 + slot // (nz * owned), ny)
        to_z = lax.rem(z + lax.rem(slot // owned, nz), nz)
        wanted = ((to_z * ny + to_y) * CORES + core) * owned + lax.rem(slot, owned)
        pick = jnp.where(wanted == column, 1.0, 0.0).astype(jnp.bfloat16)
        rotated = (mine_ref[...] + other_ref[...]).astype(jnp.bfloat16)
        picked = lax.dot_general(
            pick, rotated, (((1,), (1,)), ((), ())), preferred_element_type=jnp.float32
        )
        o_ref[...] = picked.astype(jnp.bfloat16)

    return pl.pallas_call(
        kernel,
        in_specs=[IN_SMEM, IN_VMEM, IN_VMEM],
        out_specs=IN_VMEM,
        out_shape=jax.ShapeDtypeStruct((kept, tokens), jnp.bfloat16),
        cost_estimate=pl.CostEstimate(
            flops=2 * kept * width * tokens,
            bytes_accessed=8 * tokens * width + 2 * kept * tokens,
            transcendentals=0,
        ),
        compiler_params=params(),
        name="owned_gradients",
    )(place, mine, other)


def chip_sums(layout, grads, mine, other, positions, lengths, owned, cut):
    nz, ny = layout.nz, layout.ny
    tokens, width = mine.shape
    seqs = lengths.shape[0]
    stay = nz * owned
    rest = width - cut

    def kernel(lengths_ref, grads_ref, mine_ref, other_ref, positions_ref, *refs):
        rotated = mine_ref[...] + other_ref[...]
        position = positions_ref[...]
        begin = jnp.int32(0)
        for s in range(seqs):
            end = begin + lengths_ref[s]
            inside = (position >= begin) & (position < end)
            part = jnp.where(inside, rotated, 0.0).astype(jnp.bfloat16)
            sums = jnp.dot(grads_ref[...], part, preferred_element_type=jnp.float32)
            at = pl.ds(s * cut, cut)
            for d in range(nz):
                for h in range(ny):
                    block = sums[h * stay + d * owned:h * stay + (d + 1) * owned, :cut]
                    refs[d][pl.ds(h * owned, owned), at] = block.astype(refs[d].dtype)
            if rest:
                at = pl.ds(s * rest, rest)
                refs[nz][:, at] = sums[stay:, cut:]
                refs[nz + 1][:, at] = sums[:stay, cut:].astype(jnp.bfloat16)
            begin = end

    shapes = [jax.ShapeDtypeStruct((ny * owned, seqs * cut), jnp.float32)]
    shapes += [jax.ShapeDtypeStruct((ny * owned, seqs * cut), jnp.bfloat16)] * (nz - 1)
    if rest:
        shapes.append(jax.ShapeDtypeStruct((stay, seqs * rest), jnp.float32))
        shapes.append(jax.ShapeDtypeStruct((stay, seqs * rest), jnp.bfloat16))
    return pl.pallas_call(
        kernel,
        in_specs=[IN_SMEM] + [IN_VMEM] * 4,
        out_specs=[IN_VMEM] * len(shapes),
        out_shape=shapes,
        cost_estimate=pl.CostEstimate(
            flops=2 * grads.size * seqs * width,
            bytes_accessed=8 * tokens * width + 2 * grads.shape[0] * seqs * width,
            transcendentals=0,
        ),
        compiler_params=params(),
        name="chip_sums",
    )(lengths, grads, mine, other, positions)


def add_up(kept, came, owned, own):
    count = kept.shape[0] // owned
    width = kept.shape[1]

    def kernel(*refs):
        total = refs[0][...]
        for i in range(len(came)):
            total += refs[1 + i][...].astype(jnp.float32)
        outs = refs[1 + len(came):]
        for i in range(count):
            outs[i][...] = total[i * owned:(i + 1) * owned].astype(outs[i].dtype)

    shapes = [
        jax.ShapeDtypeStruct((owned, width), jnp.float32 if i == own else jnp.bfloat16)
        for i in range(count)
    ]
    return pl.pallas_call(
        kernel,
        in_specs=[IN_VMEM] * (1 + len(came)),
        out_specs=[IN_VMEM] * count,
        out_shape=shapes,
        cost_estimate=pl.CostEstimate(
            flops=kept.size * len(came), bytes_accessed=8 * kept.size, transcendentals=0
        ),
        compiler_params=params(),
        name="add_up",
    )(kept, *came)


def squares(groups, lengths, owned):
    seqs = lengths.shape[0]
    widths = [group[0].shape[1] // seqs for group in groups]

    def kernel(lengths_ref, *refs):
        o_ref = refs[-1]
        tokens = lengths_ref[0]
        for s in range(1, seqs):
            tokens = tokens + lengths_ref[s]
        at, k = 0, 0
        for group, width in zip(groups, widths):
            over = jnp.full((owned, width), tokens, jnp.int32).astype(jnp.float32)
            sums = refs[k][...]
            for ref in refs[k + 1:k + len(group)]:
                sums = sums + ref[...].astype(jnp.float32)
            k += len(group)
            sums = sums * sums
            acc = sums[:, :width]
            for s in range(1, seqs):
                acc = acc + sums[:, s * width:(s + 1) * width]
            o_ref[:, pl.ds(at, width)] = acc / over
            at += width

    flat = [x for group in groups for x in group]
    return pl.pallas_call(
        kernel,
        in_specs=[IN_SMEM] + [IN_VMEM] * len(flat),
        out_specs=IN_VMEM,
        out_shape=jax.ShapeDtypeStruct((owned, sum(widths)), jnp.float32),
        cost_estimate=pl.CostEstimate(
            flops=2 * sum(x.size for x in flat),
            bytes_accessed=2 * sum(x.size for x in flat),
            transcendentals=0,
        ),
        compiler_params=params(),
        name="squares",
    )(lengths, *flat)


def scatter_sums(layout, sums, owned):
    nz, ny = layout.nz, layout.ny
    if ny == 1:
        return [[sums[0]] + [layout.along_z(sums[d], d) for d in range(1, nz)]]
    crossed = [layout.along_y(sums[nz + 1])]
    came = [layout.along_z(sums[d], d) for d in range(1, nz)]
    by_z = add_up(sums[nz], crossed, owned, 0)
    second = [by_z[0]] + [layout.along_z(by_z[d], d) for d in range(1, nz)]
    by_y = add_up(sums[0], came, owned, 1)
    return [[by_y[1], layout.along_y(by_y[0])], second]


def shards(layout, activations, gradients, basis_a, basis_g, token_index, seq_lengths):
    nz, ny, chips = layout.nz, layout.ny, layout.chips
    rows = activations.shape[0]
    owned = basis_g.shape[1] // (chips * CORES)
    me = lax.axis_index("row")
    core = lax.rem(me, CORES)
    y = lax.rem(me // CORES, ny)
    z = me // (CORES * ny)
    place = jnp.stack([z, y, core]).astype(jnp.int32)

    sib_index = layout.to_sibling(token_index)
    first = core == 0
    positions = jnp.concatenate(
        [jnp.where(first, token_index, sib_index), jnp.where(first, sib_index, token_index)]
    ).reshape(CORES * rows, 1)

    links = Links(layout, 2)
    sib_g = layout.to_sibling(gradients)
    sib_a = layout.to_sibling(activations)
    split = [basis_g.shape[0] * 4 // 7, basis_a.shape[0] // 2] if ny > 1 else [0, 0]
    early = []

    def rotate_early(found):
        early.append(partial_rotation(layout, gradients, sib_g, found[:4], place))
        return early[0]

    gates = {nz // 2: [sib_g, sib_a], -1: rotate_early}
    found_g = gather_columns(links, basis_g, split[0], gates)
    if not early:
        rotate_early(found_g)
    mine_g = partial_rotation(layout, gradients, sib_g, found_g[4:], place, early[0])
    links.after(early[0])
    found_a = gather_columns(links, basis_a, split[1], {("y", nz - 1): [mine_g]})
    grads = owned_gradients(layout, mine_g, layout.to_sibling(mine_g), place, owned)

    most, rows_left = partial_rotation(
        layout, activations, sib_a, found_a[:-2], place, None, found_a[-2:]
    )
    most, positions = lax.optimization_barrier((most, positions))
    mine_a = last_rotation(most, rows_left, found_a[-2:])
    cut = basis_a.shape[1] // ny**2
    sums = chip_sums(
        layout, grads, mine_a, layout.to_sibling(mine_a), positions, seq_lengths, owned, cut
    )
    return squares(scatter_sums(layout, sums, owned), seq_lengths, owned)


def solution(mesh):
    return jax.shard_map(
        functools.partial(shards, Layout(mesh)),
        mesh=mesh,
        in_specs=(
            P(("grp", "row"), None),
            P(("grp", "row"), None),
            P(("grp", "row"), None),
            P(("grp", "row"), None),
            P(("grp", "row")),
            P("grp"),
        ),
        out_specs=P(("grp", "row"), None),
        check_vma=False,
    )
```

```python
import functools

import jax
import jax.numpy as jnp
from jax import lax
from jax.experimental import pallas as pl
from jax.experimental.pallas import tpu as pltpu
from jax.sharding import PartitionSpec as P

CORES = 2
MIB = 1024 * 1024


def params(mib=8):
    return pltpu.CompilerParams(vmem_limit_bytes=mib * MIB)


IN_VMEM = pl.BlockSpec(memory_space=pltpu.VMEM)
IN_SMEM = pl.BlockSpec(memory_space=pltpu.SMEM)
ANYWHERE = pl.BlockSpec(memory_space=pl.ANY)


def in_hbm(x):
    return pltpu.with_memory_space_constraint(x, pltpu.HBM)


class Layout:
    def __init__(self, mesh):
        self.chips = mesh.shape["row"] // CORES
        self.ny = max(1, 4 // mesh.shape["grp"])
        if self.chips % self.ny:
            self.ny = 1
        self.nz = self.chips // self.ny

    def device(self, z, y, core):
        return ((z % self.nz) * self.ny + y % self.ny) * CORES + core

    def everyone(self):
        return [(z, y, c) for z in range(self.nz) for y in range(self.ny) for c in range(CORES)]

    def origin(self, z, y, d, h):
        return lax.rem(z + (self.nz - d), self.nz) * self.ny + lax.rem(y + (self.ny - h), self.ny)

    def along_z(self, x, hops):
        pairs = [(self.device(z, y, c), self.device(z + hops, y, c)) for z, y, c in self.everyone()]
        return lax.ppermute(x, "row", pairs)

    def along_y(self, x, hops=1):
        pairs = [(self.device(z, y, c), self.device(z, y + hops, c)) for z, y, c in self.everyone()]
        return lax.ppermute(x, "row", pairs)

    def to_sibling(self, x):
        pairs = [(self.device(z, y, c), self.device(z, y, 1 - c)) for z, y, c in self.everyone()]
        return lax.ppermute(x, "row", pairs)


def split_columns(act, core, chips):
    rows, depth = act.shape
    kc = depth // (chips * CORES)
    mine = lax.dynamic_index_in_dim(act.reshape(rows, chips, CORES, kc), core, 2, keepdims=False)
    return mine.transpose(1, 0, 2)


class Links:
    def __init__(self, layout, window):
        self.layout, self.window = layout, window
        self.done = {"z": [], "y": []}
        self.first = []

    def after(self, *first):
        self.first += first

    def send(self, kind, x, hops):
        done = self.done[kind]
        first = self.first + done[-self.window:len(done) - self.window + 1]
        self.first = []
        if first:
            x = lax.optimization_barrier((x, *first))[0]
        move = self.layout.along_z if kind == "z" else self.layout.along_y
        done.append(move(x, hops))
        return done[-1]


def gather_columns(links, piece, split, gates, begun={}):
    nz, ny = links.layout.nz, links.layout.ny
    middle = nz // 2
    steps = [(d, 1) for d in range(1, middle + 1)] + [(d, -1) for d in range(nz - 1, middle, -1)]
    steps = sorted(steps, key=lambda s: (min(s[0], nz - s[0]), -s[1]))
    by_z, crossed, found = {0: piece}, {}, [([piece], 0, 0)]

    def cross(d):
        for h in range(1, ny):
            if d == middle and split:
                head = links.send("z", crossed[d - 1, h][:split], 1)
                if -1 in gates:
                    links.after(gates[-1](found))
                if split == piece.shape[0]:
                    got = [head]
                else:
                    got = [head, links.send("y", by_z[d][split:], h)]
            else:
                gate = gates.get(("y", d), ())
                links.after(*(gate() if callable(gate) else gate))
                got = [begun[h]] if d == 0 and h in begun else [links.send("y", by_z[d], h)]
            crossed[d, h] = got[0]
            found.append((got, d, h))

    last = 0
    for d, sign in steps:
        gate = gates.get(d, ())
        links.after(*(gate(by_z) if callable(gate) else gate))
        by_z[d] = links.send("z", by_z[(d - sign) % nz], sign)
        found.append(([by_z[d]], d, 0))
        cross(last)
        last = d
    cross(last)
    links.first = []
    return found


def partial_rotation(layout, act, sib, found, place, total=None, left=()):
    rows = act.shape[0]
    count = len(found)
    blocks = [x for parts, _, _ in found for x in parts]
    kc = sum(x.shape[0] for x in found[0][0])
    width = blocks[0].shape[1]
    unaligned = kc % 128 != 0
    if unaligned:
        act = split_columns(act, place[2], layout.chips)
        sib = split_columns(sib, place[2], layout.chips)

    extra = [] if total is None else [total]

    def kernel(place_ref, act_ref, sib_ref, *refs):
        block_refs, refs = refs[:len(blocks)], refs[len(blocks):]
        o_ref = refs[len(extra)]
        rows_buf, block_buf, sems = refs[-3:]
        z, y, core = place_ref[0], place_ref[1], place_ref[2]
        mine = pl.ds(pl.multiple_of(core * rows, 16), rows)
        other = pl.ds(pl.multiple_of((1 - core) * rows, 16), rows)

        def bring_rows(d, h, to, i):
            q = layout.origin(z, y, d, h)
            at = 0 if unaligned else pl.ds(pl.multiple_of((CORES * q + core) * kc, 128), kc)
            own, its = [ref.at[q] if unaligned else ref.at[:, at] for ref in (act_ref, sib_ref)]
            return [
                pltpu.make_async_copy(own, to.at[mine], sems.at[i, 0]),
                pltpu.make_async_copy(its, to.at[other], sems.at[i, 1]),
            ]

        copies, k = [], 0
        for i in range(count):
            parts, d, h = found[i]
            step, at = bring_rows(d, h, rows_buf.at[i], i), 0
            for j, x in enumerate(parts):
                to = block_buf.at[i, pl.ds(at, x.shape[0])]
                step.append(pltpu.make_async_copy(block_refs[k], to, sems.at[i, 2 + j]))
                at += x.shape[0]
                k += 1
            copies.append(step)
        for j, (_, d, h) in enumerate(left):
            copies.append(bring_rows(d, h, refs[len(extra) + 1].at[j], count + j))
        for step in copies:
            for copy in step:
                copy.start()
        for i, step in enumerate(copies):
            for copy in step:
                copy.wait()
            if i >= count:
                continue
            product = jnp.dot(rows_buf[i], block_buf[i], preferred_element_type=jnp.float32)
            if i > 0:
                o_ref[...] += product
            elif extra:
                o_ref[...] = refs[0][...] + product
            else:
                o_ref[...] = product

    shapes = [jax.ShapeDtypeStruct((CORES * rows, width), jnp.float32)]
    if left:
        shapes.append(jax.ShapeDtypeStruct((len(left), CORES * rows, kc), act.dtype))
    outs = pl.pallas_call(
        kernel,
        in_specs=[IN_SMEM] + [ANYWHERE] * (2 + len(blocks)) + [IN_VMEM] * len(extra),
        out_specs=[IN_VMEM] * len(shapes),
        out_shape=shapes,
        scratch_shapes=[
            pltpu.VMEM((count, CORES * rows, kc), act.dtype),
            pltpu.VMEM((count, kc, width), act.dtype),
            pltpu.SemaphoreType.DMA((count + len(left), 4)),
        ],
        cost_estimate=pl.CostEstimate(
            flops=4 * rows * kc * count * width,
            bytes_accessed=2 * count * kc * (2 * rows + width) + 8 * rows * width,
            transcendentals=0,
        ),
        compiler_params=params(24),
        name="partial_rotation",
    )(place, *[in_hbm(x) for x in (act, sib, *blocks)], *extra)
    return outs if left else outs[0]


def last_rotation(total, rows, found):
    width = total.shape[1]
    blocks = [x for parts, _, _ in found for x in parts]

    def kernel(total_ref, rows_ref, *refs):
        sums, k = total_ref[...], 0
        for i, (parts, _, _) in enumerate(found):
            at = 0
            for part in parts:
                x = rows_ref[i, :, pl.ds(at, part.shape[0])]
                sums += jnp.dot(x, refs[k][...], preferred_element_type=jnp.float32)
                at += part.shape[0]
                k += 1
        refs[-1][...] = sums

    return pl.pallas_call(
        kernel,
        in_specs=[IN_VMEM] * (2 + len(blocks)),
        out_specs=IN_VMEM,
        out_shape=jax.ShapeDtypeStruct(total.shape, jnp.float32),
        cost_estimate=pl.CostEstimate(
            flops=2 * rows.size * width,
            bytes_accessed=2 * rows.size + 8 * total.size,
            transcendentals=0,
        ),
        compiler_params=params(),
        name="last_rotation",
    )(total, rows, *blocks)


def owned_gradients(layout, mine, other, place, owned):
    nz, ny = layout.nz, layout.ny
    tokens, width = mine.shape
    kept = nz * ny * owned

    def kernel(place_ref, mine_ref, other_ref, o_ref):
        slot = lax.broadcasted_iota(jnp.int32, (kept, width), 0)
        column = lax.broadcasted_iota(jnp.int32, (kept, width), 1)
        z, y, core = place_ref[0], place_ref[1], place_ref[2]
        to_y = lax.rem(y + 1 + slot // (nz * owned), ny)
        to_z = lax.rem(z + lax.rem(slot // owned, nz), nz)
        wanted = ((to_z * ny + to_y) * CORES + core) * owned + lax.rem(slot, owned)
        pick = jnp.where(wanted == column, 1.0, 0.0).astype(jnp.bfloat16)
        rotated = (mine_ref[...] + other_ref[...]).astype(jnp.bfloat16)
        picked = lax.dot_general(
            pick, rotated, (((1,), (1,)), ((), ())), preferred_element_type=jnp.float32
        )
        o_ref[...] = picked.astype(jnp.bfloat16)

    return pl.pallas_call(
        kernel,
        in_specs=[IN_SMEM, IN_VMEM, IN_VMEM],
        out_specs=IN_VMEM,
        out_shape=jax.ShapeDtypeStruct((kept, tokens), jnp.bfloat16),
        cost_estimate=pl.CostEstimate(
            flops=2 * kept * width * tokens,
            bytes_accessed=8 * tokens * width + 2 * kept * tokens,
            transcendentals=0,
        ),
        compiler_params=params(),
        name="owned_gradients",
    )(place, mine, other)


def chip_sums(layout, grads, mine, other, positions, lengths, owned, cut):
    nz, ny = layout.nz, layout.ny
    tokens, width = mine.shape
    seqs = lengths.shape[0]
    stay = nz * owned
    rest = width - cut

    def kernel(lengths_ref, grads_ref, mine_ref, other_ref, positions_ref, *refs):
        rotated = mine_ref[...] + other_ref[...]
        position = positions_ref[...]
        begin = jnp.int32(0)
        for s in range(seqs):
            end = begin + lengths_ref[s]
            inside = (position >= begin) & (position < end)
            part = jnp.where(inside, rotated, 0.0).astype(jnp.bfloat16)
            sums = jnp.dot(grads_ref[...], part, preferred_element_type=jnp.float32)
            at = pl.ds(s * cut, cut)
            for d in range(nz):
                for h in range(ny):
                    block = sums[h * stay + d * owned:h * stay + (d + 1) * owned, :cut]
                    refs[d][pl.ds(h * owned, owned), at] = block.astype(refs[d].dtype)
            if rest:
                at = pl.ds(s * rest, rest)
                refs[nz][:, at] = sums[stay:, cut:]
                refs[nz + 1][:, at] = sums[:stay, cut:].astype(jnp.bfloat16)
            begin = end

    shapes = [jax.ShapeDtypeStruct((ny * owned, seqs * cut), jnp.float32)]
    shapes += [jax.ShapeDtypeStruct((ny * owned, seqs * cut), jnp.bfloat16)] * (nz - 1)
    if rest:
        shapes.append(jax.ShapeDtypeStruct((stay, seqs * rest), jnp.float32))
        shapes.append(jax.ShapeDtypeStruct((stay, seqs * rest), jnp.bfloat16))
    return pl.pallas_call(
        kernel,
        in_specs=[IN_SMEM] + [IN_VMEM] * 4,
        out_specs=[IN_VMEM] * len(shapes),
        out_shape=shapes,
        cost_estimate=pl.CostEstimate(
            flops=2 * grads.size * seqs * width,
            bytes_accessed=8 * tokens * width + 2 * grads.shape[0] * seqs * width,
            transcendentals=0,
        ),
        compiler_params=params(),
        name="chip_sums",
    )(lengths, grads, mine, other, positions)


def add_up(kept, came, owned, own):
    count = kept.shape[0] // owned
    width = kept.shape[1]

    def kernel(*refs):
        total = refs[0][...]
        for i in range(len(came)):
            total += refs[1 + i][...].astype(jnp.float32)
        outs = refs[1 + len(came):]
        for i in range(count):
            outs[i][...] = total[i * owned:(i + 1) * owned].astype(outs[i].dtype)

    shapes = [
        jax.ShapeDtypeStruct((owned, width), jnp.float32 if i == own else jnp.bfloat16)
        for i in range(count)
    ]
    return pl.pallas_call(
        kernel,
        in_specs=[IN_VMEM] * (1 + len(came)),
        out_specs=[IN_VMEM] * count,
        out_shape=shapes,
        cost_estimate=pl.CostEstimate(
            flops=kept.size * len(came), bytes_accessed=8 * kept.size, transcendentals=0
        ),
        compiler_params=params(),
        name="add_up",
    )(kept, *came)


def squares(groups, lengths, owned):
    seqs = lengths.shape[0]
    widths = [group[0].shape[1] // seqs for group in groups]

    def kernel(lengths_ref, *refs):
        o_ref = refs[-1]
        tokens = lengths_ref[0]
        for s in range(1, seqs):
            tokens = tokens + lengths_ref[s]
        at, k = 0, 0
        for group, width in zip(groups, widths):
            over = jnp.full((owned, width), tokens, jnp.int32).astype(jnp.float32)
            sums = refs[k][...]
            for ref in refs[k + 1:k + len(group)]:
                sums = sums + ref[...].astype(jnp.float32)
            k += len(group)
            sums = sums * sums
            acc = sums[:, :width]
            for s in range(1, seqs):
                acc = acc + sums[:, s * width:(s + 1) * width]
            o_ref[:, pl.ds(at, width)] = acc / over
            at += width

    flat = [x for group in groups for x in group]
    return pl.pallas_call(
        kernel,
        in_specs=[IN_SMEM] + [IN_VMEM] * len(flat),
        out_specs=IN_VMEM,
        out_shape=jax.ShapeDtypeStruct((owned, sum(widths)), jnp.float32),
        cost_estimate=pl.CostEstimate(
            flops=2 * sum(x.size for x in flat),
            bytes_accessed=2 * sum(x.size for x in flat),
            transcendentals=0,
        ),
        compiler_params=params(),
        name="squares",
    )(lengths, *flat)


def scatter_sums(layout, sums, owned):
    nz, ny = layout.nz, layout.ny
    if ny == 1:
        return [[sums[0]] + [layout.along_z(sums[d], d) for d in range(1, nz)]]
    crossed = [layout.along_y(sums[nz + 1])]
    came = [layout.along_z(sums[d], d) for d in range(1, nz)]
    by_z = add_up(sums[nz], crossed, owned, 0)
    second = [by_z[0]] + [layout.along_z(by_z[d], d) for d in range(1, nz)]
    by_y = add_up(sums[0], came, owned, 1)
    return [[by_y[1], layout.along_y(by_y[0])], second]


def shards(layout, activations, gradients, basis_a, basis_g, token_index, seq_lengths):
    nz, ny, chips = layout.nz, layout.ny, layout.chips
    rows = activations.shape[0]
    owned = basis_g.shape[1] // (chips * CORES)
    me = lax.axis_index("row")
    core = lax.rem(me, CORES)
    y = lax.rem(me // CORES, ny)
    z = me // (CORES * ny)
    place = jnp.stack([z, y, core]).astype(jnp.int32)

    sib_index = layout.to_sibling(token_index)
    first = core == 0
    positions = jnp.concatenate(
        [jnp.where(first, token_index, sib_index), jnp.where(first, sib_index, token_index)]
    ).reshape(CORES * rows, 1)

    links = Links(layout, 2)
    sib_g = layout.to_sibling(gradients)
    sib_a = layout.to_sibling(activations)
    split = [basis_g.shape[0] * 4 // 7, basis_a.shape[0] // 2] if ny > 1 else [0, 0]
    early = []

    def rotate_early(found):
        early.append(partial_rotation(layout, gradients, sib_g, found[:4], place))
        return early[0]

    begun = {}

    def begin_a():
        for h in range(1, ny):
            links.after(sib_a)
            begun[h] = links.send("y", basis_a, h)
        return list(begun.values())

    gates = {
        ("y", 1): begin_a,
        nz // 2: lambda by_z: [by_z[nz - 1], sib_g, sib_a, *begun.values()],
        -1: rotate_early,
    }
    found_g = gather_columns(links, basis_g, split[0], gates)
    if not early:
        rotate_early(found_g)
    mine_g = partial_rotation(layout, gradients, sib_g, found_g[4:], place, early[0])
    links.after(early[0])
    found_a = gather_columns(links, basis_a, split[1], {("y", nz - 1): [mine_g]}, begun)
    grads = owned_gradients(layout, mine_g, layout.to_sibling(mine_g), place, owned)

    most, rows_left = partial_rotation(
        layout, activations, sib_a, found_a[:-2], place, None, found_a[-2:]
    )
    most, positions = lax.optimization_barrier((most, positions))
    mine_a = last_rotation(most, rows_left, found_a[-2:])
    cut = basis_a.shape[1] // ny**2
    sums = chip_sums(
        layout, grads, mine_a, layout.to_sibling(mine_a), positions, seq_lengths, owned, cut
    )
    return squares(scatter_sums(layout, sums, owned), seq_lengths, owned)


def solution(mesh):
    return jax.shard_map(
        functools.partial(shards, Layout(mesh)),
        mesh=mesh,
        in_specs=(
            P(("grp", "row"), None),
            P(("grp", "row"), None),
            P(("grp", "row"), None),
            P(("grp", "row"), None),
            P(("grp", "row")),
            P("grp"),
        ),
        out_specs=P(("grp", "row"), None),
        check_vma=False,
    )
```

```python
import functools

import jax
import jax.numpy as jnp
from jax import lax
from jax.experimental import pallas as pl
from jax.experimental.pallas import tpu as pltpu
from jax.sharding import PartitionSpec as P

CORES = 2
MIB = 1024 * 1024


def params(mib=8):
    return pltpu.CompilerParams(vmem_limit_bytes=mib * MIB)


IN_VMEM = pl.BlockSpec(memory_space=pltpu.VMEM)
IN_SMEM = pl.BlockSpec(memory_space=pltpu.SMEM)
ANYWHERE = pl.BlockSpec(memory_space=pl.ANY)


def in_hbm(x):
    return pltpu.with_memory_space_constraint(x, pltpu.HBM)


class Layout:
    def __init__(self, mesh):
        self.chips = mesh.shape["row"] // CORES
        self.ny = max(1, 4 // mesh.shape["grp"])
        if self.chips % self.ny:
            self.ny = 1
        self.nz = self.chips // self.ny

    def device(self, z, y, core):
        return ((z % self.nz) * self.ny + y % self.ny) * CORES + core

    def everyone(self):
        return [(z, y, c) for z in range(self.nz) for y in range(self.ny) for c in range(CORES)]

    def origin(self, z, y, d, h):
        return lax.rem(z + (self.nz - d), self.nz) * self.ny + lax.rem(y + (self.ny - h), self.ny)

    def along_z(self, x, hops):
        pairs = [(self.device(z, y, c), self.device(z + hops, y, c)) for z, y, c in self.everyone()]
        return lax.ppermute(x, "row", pairs)

    def along_y(self, x, hops=1):
        pairs = [(self.device(z, y, c), self.device(z, y + hops, c)) for z, y, c in self.everyone()]
        return lax.ppermute(x, "row", pairs)

    def to_sibling(self, x):
        pairs = [(self.device(z, y, c), self.device(z, y, 1 - c)) for z, y, c in self.everyone()]
        return lax.ppermute(x, "row", pairs)


def split_columns(act, core, chips):
    rows, depth = act.shape
    kc = depth // (chips * CORES)
    mine = lax.dynamic_index_in_dim(act.reshape(rows, chips, CORES, kc), core, 2, keepdims=False)
    return mine.transpose(1, 0, 2)


class Links:
    def __init__(self, layout, window):
        self.layout, self.window = layout, window
        self.done = {"z": [], "y": []}
        self.first = []

    def after(self, *first):
        self.first += first

    def send(self, kind, x, hops):
        done = self.done[kind]
        first = self.first + done[-self.window:len(done) - self.window + 1]
        self.first = []
        if first:
            x = lax.optimization_barrier((x, *first))[0]
        move = self.layout.along_z if kind == "z" else self.layout.along_y
        done.append(move(x, hops))
        return done[-1]


def gather_columns(links, piece, split, gates, begun={}):
    nz, ny = links.layout.nz, links.layout.ny
    middle = nz // 2
    steps = [(d, 1) for d in range(1, middle + 1)] + [(d, -1) for d in range(nz - 1, middle, -1)]
    steps = sorted(steps, key=lambda s: (min(s[0], nz - s[0]), -s[1]))
    by_z, crossed, found = {0: piece}, {}, [([piece], 0, 0)]

    def cross(d):
        for h in range(1, ny):
            if d == middle and split:
                head = links.send("z", crossed[d - 1, h][:split], 1)
                if -1 in gates:
                    links.after(gates[-1](found))
                if split == piece.shape[0]:
                    got = [head]
                else:
                    got = [head, links.send("y", by_z[d][split:], h)]
            else:
                gate = gates.get(("y", d), ())
                links.after(*(gate() if callable(gate) else gate))
                got = [begun[h]] if d == 0 and h in begun else [links.send("y", by_z[d], h)]
            crossed[d, h] = got[0]
            found.append((got, d, h))

    last = 0
    for d, sign in steps:
        gate = gates.get(d, ())
        links.after(*(gate(by_z) if callable(gate) else gate))
        by_z[d] = links.send("z", by_z[(d - sign) % nz], sign)
        found.append(([by_z[d]], d, 0))
        cross(last)
        last = d
    cross(last)
    links.first = []
    return found


def partial_rotation(layout, act, sib, found, place, total=None, left=()):
    rows = act.shape[0]
    count = len(found)
    blocks = [x for parts, _, _ in found for x in parts]
    kc = sum(x.shape[0] for x in found[0][0])
    width = blocks[0].shape[1]
    unaligned = kc % 128 != 0
    if unaligned:
        act = split_columns(act, place[2], layout.chips)
        sib = split_columns(sib, place[2], layout.chips)

    extra = [] if total is None else [total]

    def kernel(place_ref, act_ref, sib_ref, *refs):
        block_refs, refs = refs[:len(blocks)], refs[len(blocks):]
        o_ref = refs[len(extra)]
        rows_buf, block_buf, sems = refs[-3:]
        z, y, core = place_ref[0], place_ref[1], place_ref[2]
        mine = pl.ds(pl.multiple_of(core * rows, 16), rows)
        other = pl.ds(pl.multiple_of((1 - core) * rows, 16), rows)

        def bring_rows(d, h, to, i):
            q = layout.origin(z, y, d, h)
            at = 0 if unaligned else pl.ds(pl.multiple_of((CORES * q + core) * kc, 128), kc)
            own, its = [ref.at[q] if unaligned else ref.at[:, at] for ref in (act_ref, sib_ref)]
            return [
                pltpu.make_async_copy(own, to.at[mine], sems.at[i, 0]),
                pltpu.make_async_copy(its, to.at[other], sems.at[i, 1]),
            ]

        copies, k = [], 0
        for i in range(count):
            parts, d, h = found[i]
            step, at = bring_rows(d, h, rows_buf.at[i], i), 0
            for j, x in enumerate(parts):
                to = block_buf.at[i, pl.ds(at, x.shape[0])]
                step.append(pltpu.make_async_copy(block_refs[k], to, sems.at[i, 2 + j]))
                at += x.shape[0]
                k += 1
            copies.append(step)
        for j, (_, d, h) in enumerate(left):
            copies.append(bring_rows(d, h, refs[len(extra) + 1].at[j], count + j))
        for step in copies:
            for copy in step:
                copy.start()
        for i, step in enumerate(copies):
            for copy in step:
                copy.wait()
            if i >= count:
                continue
            product = jnp.dot(rows_buf[i], block_buf[i], preferred_element_type=jnp.float32)
            if i > 0:
                o_ref[...] += product
            elif extra:
                o_ref[...] = refs[0][...] + product
            else:
                o_ref[...] = product

    shapes = [jax.ShapeDtypeStruct((CORES * rows, width), jnp.float32)]
    if left:
        shapes.append(jax.ShapeDtypeStruct((len(left), CORES * rows, kc), act.dtype))
    outs = pl.pallas_call(
        kernel,
        in_specs=[IN_SMEM] + [ANYWHERE] * (2 + len(blocks)) + [IN_VMEM] * len(extra),
        out_specs=[IN_VMEM] * len(shapes),
        out_shape=shapes,
        scratch_shapes=[
            pltpu.VMEM((count, CORES * rows, kc), act.dtype),
            pltpu.VMEM((count, kc, width), act.dtype),
            pltpu.SemaphoreType.DMA((count + len(left), 4)),
        ],
        cost_estimate=pl.CostEstimate(
            flops=4 * rows * kc * count * width,
            bytes_accessed=2 * count * kc * (2 * rows + width) + 8 * rows * width,
            transcendentals=0,
        ),
        compiler_params=params(24),
        name="partial_rotation",
    )(place, *[in_hbm(x) for x in (act, sib, *blocks)], *extra)
    return outs if left else outs[0]


def last_rotation(total, rows, found):
    width = total.shape[1]
    blocks = [x for parts, _, _ in found for x in parts]

    def kernel(total_ref, rows_ref, *refs):
        sums, k = total_ref[...], 0
        for i, (parts, _, _) in enumerate(found):
            at = 0
            for part in parts:
                x = rows_ref[i, :, pl.ds(at, part.shape[0])]
                sums += jnp.dot(x, refs[k][...], preferred_element_type=jnp.float32)
                at += part.shape[0]
                k += 1
        refs[-1][...] = sums

    return pl.pallas_call(
        kernel,
        in_specs=[IN_VMEM] * (2 + len(blocks)),
        out_specs=IN_VMEM,
        out_shape=jax.ShapeDtypeStruct(total.shape, jnp.float32),
        cost_estimate=pl.CostEstimate(
            flops=2 * rows.size * width,
            bytes_accessed=2 * rows.size + 8 * total.size,
            transcendentals=0,
        ),
        compiler_params=params(),
        name="last_rotation",
    )(total, rows, *blocks)


def owned_gradients(layout, mine, other, place, owned):
    nz, ny = layout.nz, layout.ny
    tokens, width = mine.shape
    kept = nz * ny * owned

    def kernel(place_ref, mine_ref, other_ref, o_ref):
        slot = lax.broadcasted_iota(jnp.int32, (kept, width), 0)
        column = lax.broadcasted_iota(jnp.int32, (kept, width), 1)
        z, y, core = place_ref[0], place_ref[1], place_ref[2]
        to_y = lax.rem(y + 1 + slot // (nz * owned), ny)
        to_z = lax.rem(z + lax.rem(slot // owned, nz), nz)
        wanted = ((to_z * ny + to_y) * CORES + core) * owned + lax.rem(slot, owned)
        pick = jnp.where(wanted == column, 1.0, 0.0).astype(jnp.bfloat16)
        rotated = (mine_ref[...] + other_ref[...]).astype(jnp.bfloat16)
        picked = lax.dot_general(
            pick, rotated, (((1,), (1,)), ((), ())), preferred_element_type=jnp.float32
        )
        o_ref[...] = picked.astype(jnp.bfloat16)

    return pl.pallas_call(
        kernel,
        in_specs=[IN_SMEM, IN_VMEM, IN_VMEM],
        out_specs=IN_VMEM,
        out_shape=jax.ShapeDtypeStruct((kept, tokens), jnp.bfloat16),
        cost_estimate=pl.CostEstimate(
            flops=2 * kept * width * tokens,
            bytes_accessed=8 * tokens * width + 2 * kept * tokens,
            transcendentals=0,
        ),
        compiler_params=params(),
        name="owned_gradients",
    )(place, mine, other)


def chip_sums(layout, grads, mine, other, positions, lengths, owned, cut):
    nz, ny = layout.nz, layout.ny
    tokens, width = mine.shape
    seqs = lengths.shape[0]
    stay = nz * owned
    rest = width - cut

    def kernel(lengths_ref, grads_ref, mine_ref, other_ref, positions_ref, *refs):
        rotated = mine_ref[...] + other_ref[...]
        position = positions_ref[...]
        begin = jnp.int32(0)
        for s in range(seqs):
            end = begin + lengths_ref[s]
            inside = (position >= begin) & (position < end)
            part = jnp.where(inside, rotated, 0.0).astype(jnp.bfloat16)
            sums = jnp.dot(grads_ref[...], part, preferred_element_type=jnp.float32)
            at = pl.ds(s * cut, cut)
            for d in range(nz):
                for h in range(ny):
                    block = sums[h * stay + d * owned:h * stay + (d + 1) * owned, :cut]
                    refs[d][pl.ds(h * owned, owned), at] = block.astype(refs[d].dtype)
            if rest:
                at = pl.ds(s * rest, rest)
                refs[nz][:, at] = sums[stay:, cut:]
                refs[nz + 1][:, at] = sums[:stay, cut:].astype(jnp.bfloat16)
            begin = end

    shapes = [jax.ShapeDtypeStruct((ny * owned, seqs * cut), jnp.float32)]
    shapes += [jax.ShapeDtypeStruct((ny * owned, seqs * cut), jnp.bfloat16)] * (nz - 1)
    if rest:
        shapes.append(jax.ShapeDtypeStruct((stay, seqs * rest), jnp.float32))
        shapes.append(jax.ShapeDtypeStruct((stay, seqs * rest), jnp.bfloat16))
    return pl.pallas_call(
        kernel,
        in_specs=[IN_SMEM] + [IN_VMEM] * 4,
        out_specs=[IN_VMEM] * len(shapes),
        out_shape=shapes,
        cost_estimate=pl.CostEstimate(
            flops=2 * grads.size * seqs * width,
            bytes_accessed=8 * tokens * width + 2 * grads.shape[0] * seqs * width,
            transcendentals=0,
        ),
        compiler_params=params(),
        name="chip_sums",
    )(lengths, grads, mine, other, positions)


def add_up(kept, came, owned, own):
    count = kept.shape[0] // owned
    width = kept.shape[1]

    def kernel(*refs):
        total = refs[0][...]
        for i in range(len(came)):
            total += refs[1 + i][...].astype(jnp.float32)
        outs = refs[1 + len(came):]
        for i in range(count):
            outs[i][...] = total[i * owned:(i + 1) * owned].astype(outs[i].dtype)

    shapes = [
        jax.ShapeDtypeStruct((owned, width), jnp.float32 if i == own else jnp.bfloat16)
        for i in range(count)
    ]
    return pl.pallas_call(
        kernel,
        in_specs=[IN_VMEM] * (1 + len(came)),
        out_specs=[IN_VMEM] * count,
        out_shape=shapes,
        cost_estimate=pl.CostEstimate(
            flops=kept.size * len(came), bytes_accessed=8 * kept.size, transcendentals=0
        ),
        compiler_params=params(),
        name="add_up",
    )(kept, *came)


def squares(groups, lengths, owned):
    seqs = lengths.shape[0]
    widths = [group[0].shape[1] // seqs for group in groups]

    def kernel(lengths_ref, *refs):
        o_ref = refs[-1]
        tokens = lengths_ref[0]
        for s in range(1, seqs):
            tokens = tokens + lengths_ref[s]
        at, k = 0, 0
        for group, width in zip(groups, widths):
            over = jnp.full((owned, width), tokens, jnp.int32).astype(jnp.float32)
            sums = refs[k][...]
            for ref in refs[k + 1:k + len(group)]:
                sums = sums + ref[...].astype(jnp.float32)
            k += len(group)
            sums = sums * sums
            acc = sums[:, :width]
            for s in range(1, seqs):
                acc = acc + sums[:, s * width:(s + 1) * width]
            o_ref[:, pl.ds(at, width)] = acc / over
            at += width

    flat = [x for group in groups for x in group]
    return pl.pallas_call(
        kernel,
        in_specs=[IN_SMEM] + [IN_VMEM] * len(flat),
        out_specs=IN_VMEM,
        out_shape=jax.ShapeDtypeStruct((owned, sum(widths)), jnp.float32),
        cost_estimate=pl.CostEstimate(
            flops=2 * sum(x.size for x in flat),
            bytes_accessed=2 * sum(x.size for x in flat),
            transcendentals=0,
        ),
        compiler_params=params(),
        name="squares",
    )(lengths, *flat)


def scatter_sums(layout, sums, owned):
    nz, ny = layout.nz, layout.ny
    if ny == 1:
        return [[sums[0]] + [layout.along_z(sums[d], d) for d in range(1, nz)]]
    crossed = [layout.along_y(sums[nz + 1])]
    came = [layout.along_z(sums[d], d) for d in range(1, nz)]
    by_z = add_up(sums[nz], crossed, owned, 0)
    second = [by_z[0]] + [layout.along_z(by_z[d], d) for d in range(1, nz)]
    by_y = add_up(sums[0], came, owned, 1)
    return [[by_y[1], layout.along_y(by_y[0])], second]


def shards(layout, activations, gradients, basis_a, basis_g, token_index, seq_lengths):
    nz, ny, chips = layout.nz, layout.ny, layout.chips
    rows = activations.shape[0]
    owned = basis_g.shape[1] // (chips * CORES)
    me = lax.axis_index("row")
    core = lax.rem(me, CORES)
    y = lax.rem(me // CORES, ny)
    z = me // (CORES * ny)
    place = jnp.stack([z, y, core]).astype(jnp.int32)

    sib_index = layout.to_sibling(token_index)
    first = core == 0
    positions = jnp.concatenate(
        [jnp.where(first, token_index, sib_index), jnp.where(first, sib_index, token_index)]
    ).reshape(CORES * rows, 1)

    links = Links(layout, 2)
    sib_g = layout.to_sibling(gradients)
    sib_a = layout.to_sibling(activations)
    split = [basis_g.shape[0] * 4 // 7, basis_a.shape[0] // 2] if ny > 1 else [0, 0]
    early = []

    def rotate_early(found):
        early.append(partial_rotation(layout, gradients, sib_g, found[:4], place))
        return early[0]

    begun = {}

    def begin_a():
        for h in range(1, ny):
            links.after(sib_a)
            begun[h] = links.send("y", basis_a, h)
        return list(begun.values())

    gates = {
        ("y", 1): begin_a,
        nz - 1: [sib_a],
        nz // 2: lambda by_z: [by_z[nz - 1], sib_g, sib_a, *begun.values()],
        -1: rotate_early,
    }
    found_g = gather_columns(links, basis_g, split[0], gates)
    if not early:
        rotate_early(found_g)
    mine_g = partial_rotation(layout, gradients, sib_g, found_g[4:], place, early[0])
    links.after(early[0])
    found_a = gather_columns(links, basis_a, split[1], {("y", nz - 1): [mine_g]}, begun)
    grads = owned_gradients(layout, mine_g, layout.to_sibling(mine_g), place, owned)

    most, rows_left = partial_rotation(
        layout, activations, sib_a, found_a[:-2], place, None, found_a[-2:]
    )
    most, positions = lax.optimization_barrier((most, positions))
    mine_a = last_rotation(most, rows_left, found_a[-2:])
    cut = basis_a.shape[1] // ny**2
    sums = chip_sums(
        layout, grads, mine_a, layout.to_sibling(mine_a), positions, seq_lengths, owned, cut
    )
    return squares(scatter_sums(layout, sums, owned), seq_lengths, owned)


def solution(mesh):
    return jax.shard_map(
        functools.partial(shards, Layout(mesh)),
        mesh=mesh,
        in_specs=(
            P(("grp", "row"), None),
            P(("grp", "row"), None),
            P(("grp", "row"), None),
            P(("grp", "row"), None),
            P(("grp", "row")),
            P("grp"),
        ),
        out_specs=P(("grp", "row"), None),
        check_vma=False,
    )
```

```python
import functools

import jax
import jax.numpy as jnp
from jax import lax
from jax.experimental import pallas as pl
from jax.experimental.pallas import tpu as pltpu
from jax.sharding import PartitionSpec as P

CORES = 2
MIB = 1024 * 1024


def params(mib=8):
    return pltpu.CompilerParams(vmem_limit_bytes=mib * MIB)


IN_VMEM = pl.BlockSpec(memory_space=pltpu.VMEM)
IN_SMEM = pl.BlockSpec(memory_space=pltpu.SMEM)
ANYWHERE = pl.BlockSpec(memory_space=pl.ANY)


def in_hbm(x):
    return pltpu.with_memory_space_constraint(x, pltpu.HBM)


class Layout:
    def __init__(self, mesh):
        self.chips = mesh.shape["row"] // CORES
        self.ny = max(1, 4 // mesh.shape["grp"])
        if self.chips % self.ny:
            self.ny = 1
        self.nz = self.chips // self.ny

    def device(self, z, y, core):
        return ((z % self.nz) * self.ny + y % self.ny) * CORES + core

    def everyone(self):
        return [(z, y, c) for z in range(self.nz) for y in range(self.ny) for c in range(CORES)]

    def origin(self, z, y, d, h):
        return lax.rem(z + (self.nz - d), self.nz) * self.ny + lax.rem(y + (self.ny - h), self.ny)

    def along_z(self, x, hops):
        pairs = [(self.device(z, y, c), self.device(z + hops, y, c)) for z, y, c in self.everyone()]
        return lax.ppermute(x, "row", pairs)

    def along_y(self, x, hops=1):
        pairs = [(self.device(z, y, c), self.device(z, y + hops, c)) for z, y, c in self.everyone()]
        return lax.ppermute(x, "row", pairs)

    def to_sibling(self, x):
        pairs = [(self.device(z, y, c), self.device(z, y, 1 - c)) for z, y, c in self.everyone()]
        return lax.ppermute(x, "row", pairs)


def split_columns(act, core, chips):
    rows, depth = act.shape
    kc = depth // (chips * CORES)
    mine = lax.dynamic_index_in_dim(act.reshape(rows, chips, CORES, kc), core, 2, keepdims=False)
    return mine.transpose(1, 0, 2)


class Links:
    def __init__(self, layout, window):
        self.layout, self.window = layout, window
        self.done = {"z": [], "y": []}
        self.first = []

    def after(self, *first):
        self.first += first

    def send(self, kind, x, hops):
        done = self.done[kind]
        first = self.first + done[-self.window:len(done) - self.window + 1]
        self.first = []
        if first:
            x = lax.optimization_barrier((x, *first))[0]
        move = self.layout.along_z if kind == "z" else self.layout.along_y
        done.append(move(x, hops))
        return done[-1]


def gather_columns(links, piece, split, gates, begun={}):
    nz, ny = links.layout.nz, links.layout.ny
    middle = nz // 2
    steps = [(d, 1) for d in range(1, middle + 1)] + [(d, -1) for d in range(nz - 1, middle, -1)]
    steps = sorted(steps, key=lambda s: (min(s[0], nz - s[0]), -s[1]))
    by_z, crossed, found = {0: piece}, {}, [([piece], 0, 0)]

    def cross(d):
        for h in range(1, ny):
            if d == middle and split:
                head = links.send("z", crossed[d - 1, h][:split], 1)
                if -1 in gates:
                    links.after(gates[-1](found))
                if split == piece.shape[0]:
                    got = [head]
                else:
                    got = [head, links.send("y", by_z[d][split:], h)]
            else:
                gate = gates.get(("y", d), ())
                links.after(*(gate() if callable(gate) else gate))
                got = [begun[h]] if d == 0 and h in begun else [links.send("y", by_z[d], h)]
            crossed[d, h] = got[0]
            found.append((got, d, h))

    last = 0
    for d, sign in steps:
        gate = gates.get(d, ())
        links.after(*(gate(by_z) if callable(gate) else gate))
        by_z[d] = links.send("z", by_z[(d - sign) % nz], sign)
        found.append(([by_z[d]], d, 0))
        cross(last)
        last = d
    cross(last)
    links.first = []
    return found


def partial_rotation(layout, act, sib, found, place, total=None, left=()):
    rows = act.shape[0]
    count = len(found)
    blocks = [x for parts, _, _ in found for x in parts]
    kc = sum(x.shape[0] for x in found[0][0])
    width = blocks[0].shape[1]
    unaligned = kc % 128 != 0
    if unaligned:
        act = split_columns(act, place[2], layout.chips)
        sib = split_columns(sib, place[2], layout.chips)

    extra = [] if total is None else [total]

    def kernel(place_ref, act_ref, sib_ref, *refs):
        block_refs, refs = refs[:len(blocks)], refs[len(blocks):]
        o_ref = refs[len(extra)]
        rows_buf, block_buf, sems = refs[-3:]
        z, y, core = place_ref[0], place_ref[1], place_ref[2]
        mine = pl.ds(pl.multiple_of(core * rows, 16), rows)
        other = pl.ds(pl.multiple_of((1 - core) * rows, 16), rows)

        def bring_rows(d, h, to, i):
            q = layout.origin(z, y, d, h)
            at = 0 if unaligned else pl.ds(pl.multiple_of((CORES * q + core) * kc, 128), kc)
            own, its = [ref.at[q] if unaligned else ref.at[:, at] for ref in (act_ref, sib_ref)]
            return [
                pltpu.make_async_copy(own, to.at[mine], sems.at[i, 0]),
                pltpu.make_async_copy(its, to.at[other], sems.at[i, 1]),
            ]

        copies, k = [], 0
        for i in range(count):
            parts, d, h = found[i]
            step, at = bring_rows(d, h, rows_buf.at[i], i), 0
            for j, x in enumerate(parts):
                to = block_buf.at[i, pl.ds(at, x.shape[0])]
                step.append(pltpu.make_async_copy(block_refs[k], to, sems.at[i, 2 + j]))
                at += x.shape[0]
                k += 1
            copies.append(step)
        for j, (_, d, h) in enumerate(left):
            copies.append(bring_rows(d, h, refs[len(extra) + 1].at[j], count + j))
        for step in copies:
            for copy in step:
                copy.start()
        for i, step in enumerate(copies):
            for copy in step:
                copy.wait()
            if i >= count:
                continue
            product = jnp.dot(rows_buf[i], block_buf[i], preferred_element_type=jnp.float32)
            if i > 0:
                o_ref[...] += product
            elif extra:
                o_ref[...] = refs[0][...] + product
            else:
                o_ref[...] = product

    shapes = [jax.ShapeDtypeStruct((CORES * rows, width), jnp.float32)]
    if left:
        shapes.append(jax.ShapeDtypeStruct((len(left), CORES * rows, kc), act.dtype))
    outs = pl.pallas_call(
        kernel,
        in_specs=[IN_SMEM] + [ANYWHERE] * (2 + len(blocks)) + [IN_VMEM] * len(extra),
        out_specs=[IN_VMEM] * len(shapes),
        out_shape=shapes,
        scratch_shapes=[
            pltpu.VMEM((count, CORES * rows, kc), act.dtype),
            pltpu.VMEM((count, kc, width), act.dtype),
            pltpu.SemaphoreType.DMA((count + len(left), 4)),
        ],
        cost_estimate=pl.CostEstimate(
            flops=4 * rows * kc * count * width,
            bytes_accessed=2 * count * kc * (2 * rows + width) + 8 * rows * width,
            transcendentals=0,
        ),
        compiler_params=params(24),
        name="partial_rotation",
    )(place, *[in_hbm(x) for x in (act, sib, *blocks)], *extra)
    return outs if left else outs[0]


def last_rotation(total, rows, found):
    width = total.shape[1]
    blocks = [x for parts, _, _ in found for x in parts]

    def kernel(total_ref, rows_ref, *refs):
        sums, k = total_ref[...], 0
        for i, (parts, _, _) in enumerate(found):
            at = 0
            for part in parts:
                x = rows_ref[i, :, pl.ds(at, part.shape[0])]
                sums += jnp.dot(x, refs[k][...], preferred_element_type=jnp.float32)
                at += part.shape[0]
                k += 1
        refs[-1][...] = sums

    return pl.pallas_call(
        kernel,
        in_specs=[IN_VMEM] * (2 + len(blocks)),
        out_specs=IN_VMEM,
        out_shape=jax.ShapeDtypeStruct(total.shape, jnp.float32),
        cost_estimate=pl.CostEstimate(
            flops=2 * rows.size * width,
            bytes_accessed=2 * rows.size + 8 * total.size,
            transcendentals=0,
        ),
        compiler_params=params(),
        name="last_rotation",
    )(total, rows, *blocks)


def owned_gradients(layout, mine, other, place, owned):
    nz, ny = layout.nz, layout.ny
    tokens, width = mine.shape
    kept = nz * ny * owned

    def kernel(place_ref, mine_ref, other_ref, o_ref):
        slot = lax.broadcasted_iota(jnp.int32, (kept, width), 0)
        column = lax.broadcasted_iota(jnp.int32, (kept, width), 1)
        z, y, core = place_ref[0], place_ref[1], place_ref[2]
        to_y = lax.rem(y + 1 + slot // (nz * owned), ny)
        to_z = lax.rem(z + lax.rem(slot // owned, nz), nz)
        wanted = ((to_z * ny + to_y) * CORES + core) * owned + lax.rem(slot, owned)
        pick = jnp.where(wanted == column, 1.0, 0.0).astype(jnp.bfloat16)
        rotated = (mine_ref[...] + other_ref[...]).astype(jnp.bfloat16)
        picked = lax.dot_general(
            pick, rotated, (((1,), (1,)), ((), ())), preferred_element_type=jnp.float32
        )
        o_ref[...] = picked.astype(jnp.bfloat16)

    return pl.pallas_call(
        kernel,
        in_specs=[IN_SMEM, IN_VMEM, IN_VMEM],
        out_specs=IN_VMEM,
        out_shape=jax.ShapeDtypeStruct((kept, tokens), jnp.bfloat16),
        cost_estimate=pl.CostEstimate(
            flops=2 * kept * width * tokens,
            bytes_accessed=8 * tokens * width + 2 * kept * tokens,
            transcendentals=0,
        ),
        compiler_params=params(),
        name="owned_gradients",
    )(place, mine, other)


def chip_sums(layout, grads, mine, other, positions, lengths, owned, cut):
    nz, ny = layout.nz, layout.ny
    tokens, width = mine.shape
    seqs = lengths.shape[0]
    stay = nz * owned
    rest = width - cut

    def kernel(lengths_ref, grads_ref, mine_ref, other_ref, positions_ref, *refs):
        rotated = mine_ref[...] + other_ref[...]
        position = positions_ref[...]
        begin = jnp.int32(0)
        for s in range(seqs):
            end = begin + lengths_ref[s]
            inside = (position >= begin) & (position < end)
            part = jnp.where(inside, rotated, 0.0).astype(jnp.bfloat16)
            sums = jnp.dot(grads_ref[...], part, preferred_element_type=jnp.float32)
            at = pl.ds(s * cut, cut)
            for d in range(nz):
                for h in range(ny):
                    block = sums[h * stay + d * owned:h * stay + (d + 1) * owned, :cut]
                    refs[d][pl.ds(h * owned, owned), at] = block.astype(refs[d].dtype)
            if rest:
                at = pl.ds(s * rest, rest)
                refs[nz][:, at] = sums[stay:, cut:]
                refs[nz + 1][:, at] = sums[:stay, cut:].astype(jnp.bfloat16)
            begin = end

    shapes = [jax.ShapeDtypeStruct((ny * owned, seqs * cut), jnp.float32)]
    shapes += [jax.ShapeDtypeStruct((ny * owned, seqs * cut), jnp.bfloat16)] * (nz - 1)
    if rest:
        shapes.append(jax.ShapeDtypeStruct((stay, seqs * rest), jnp.float32))
        shapes.append(jax.ShapeDtypeStruct((stay, seqs * rest), jnp.bfloat16))
    return pl.pallas_call(
        kernel,
        in_specs=[IN_SMEM] + [IN_VMEM] * 4,
        out_specs=[IN_VMEM] * len(shapes),
        out_shape=shapes,
        cost_estimate=pl.CostEstimate(
            flops=2 * grads.size * seqs * width,
            bytes_accessed=8 * tokens * width + 2 * grads.shape[0] * seqs * width,
            transcendentals=0,
        ),
        compiler_params=params(),
        name="chip_sums",
    )(lengths, grads, mine, other, positions)


def add_up(kept, came, owned, own):
    count = kept.shape[0] // owned
    width = kept.shape[1]

    def kernel(*refs):
        total = refs[0][...]
        for i in range(len(came)):
            total += refs[1 + i][...].astype(jnp.float32)
        outs = refs[1 + len(came):]
        for i in range(count):
            outs[i][...] = total[i * owned:(i + 1) * owned].astype(outs[i].dtype)

    shapes = [
        jax.ShapeDtypeStruct((owned, width), jnp.float32 if i == own else jnp.bfloat16)
        for i in range(count)
    ]
    return pl.pallas_call(
        kernel,
        in_specs=[IN_VMEM] * (1 + len(came)),
        out_specs=[IN_VMEM] * count,
        out_shape=shapes,
        cost_estimate=pl.CostEstimate(
            flops=kept.size * len(came), bytes_accessed=8 * kept.size, transcendentals=0
        ),
        compiler_params=params(),
        name="add_up",
    )(kept, *came)


def squares(groups, lengths, owned):
    seqs = lengths.shape[0]
    widths = [group[0].shape[1] // seqs for group in groups]

    def kernel(lengths_ref, *refs):
        o_ref = refs[-1]
        tokens = lengths_ref[0]
        for s in range(1, seqs):
            tokens = tokens + lengths_ref[s]
        at, k = 0, 0
        for group, width in zip(groups, widths):
            over = jnp.full((owned, width), tokens, jnp.int32).astype(jnp.float32)
            sums = refs[k][...]
            for ref in refs[k + 1:k + len(group)]:
                sums = sums + ref[...].astype(jnp.float32)
            k += len(group)
            sums = sums * sums
            acc = sums[:, :width]
            for s in range(1, seqs):
                acc = acc + sums[:, s * width:(s + 1) * width]
            o_ref[:, pl.ds(at, width)] = acc / over
            at += width

    flat = [x for group in groups for x in group]
    return pl.pallas_call(
        kernel,
        in_specs=[IN_SMEM] + [IN_VMEM] * len(flat),
        out_specs=IN_VMEM,
        out_shape=jax.ShapeDtypeStruct((owned, sum(widths)), jnp.float32),
        cost_estimate=pl.CostEstimate(
            flops=2 * sum(x.size for x in flat),
            bytes_accessed=2 * sum(x.size for x in flat),
            transcendentals=0,
        ),
        compiler_params=params(),
        name="squares",
    )(lengths, *flat)


def scatter_sums(layout, sums, owned):
    nz, ny = layout.nz, layout.ny
    if ny == 1:
        return [[sums[0]] + [layout.along_z(sums[d], d) for d in range(1, nz)]]
    crossed = [layout.along_y(sums[nz + 1])]
    came = [layout.along_z(sums[d], d) for d in range(1, nz)]
    by_z = add_up(sums[nz], crossed, owned, 0)
    second = [by_z[0]] + [layout.along_z(by_z[d], d) for d in range(1, nz)]
    by_y = add_up(sums[0], came, owned, 1)
    return [[by_y[1], layout.along_y(by_y[0])], second]


def shards(layout, activations, gradients, basis_a, basis_g, token_index, seq_lengths):
    nz, ny, chips = layout.nz, layout.ny, layout.chips
    rows = activations.shape[0]
    owned = basis_g.shape[1] // (chips * CORES)
    me = lax.axis_index("row")
    core = lax.rem(me, CORES)
    y = lax.rem(me // CORES, ny)
    z = me // (CORES * ny)
    place = jnp.stack([z, y, core]).astype(jnp.int32)

    sib_index = layout.to_sibling(token_index)
    first = core == 0
    positions = jnp.concatenate(
        [jnp.where(first, token_index, sib_index), jnp.where(first, sib_index, token_index)]
    ).reshape(CORES * rows, 1)

    links = Links(layout, 2)
    sib_g = layout.to_sibling(gradients)
    sib_a = layout.to_sibling(activations)
    split = [basis_g.shape[0] * 4 // 7, basis_a.shape[0] // 2] if ny > 1 else [0, 0]
    early = []

    def rotate_early(found):
        early.append(partial_rotation(layout, gradients, sib_g, found[:4], place))
        return early[0]

    begun = {}

    def begin_a():
        for h in range(1, ny):
            links.after(sib_a)
            begun[h] = links.send("y", basis_a, h)
        return list(begun.values())

    gates = {
        ("y", 1): begin_a,
        nz - 1: [sib_a],
        nz // 2: lambda by_z: [sib_g, sib_a, *begun.values()],
        -1: rotate_early,
    }
    found_g = gather_columns(links, basis_g, split[0], gates)
    if not early:
        rotate_early(found_g)
    mine_g = partial_rotation(layout, gradients, sib_g, found_g[4:], place, early[0])
    links.after(early[0])
    found_a = gather_columns(links, basis_a, split[1], {("y", nz - 1): [mine_g]}, begun)
    grads = owned_gradients(layout, mine_g, layout.to_sibling(mine_g), place, owned)

    most, rows_left = partial_rotation(
        layout, activations, sib_a, found_a[:-2], place, None, found_a[-2:]
    )
    most, positions = lax.optimization_barrier((most, positions))
    mine_a = last_rotation(most, rows_left, found_a[-2:])
    cut = basis_a.shape[1] // ny**2
    sums = chip_sums(
        layout, grads, mine_a, layout.to_sibling(mine_a), positions, seq_lengths, owned, cut
    )
    return squares(scatter_sums(layout, sums, owned), seq_lengths, owned)


def solution(mesh):
    return jax.shard_map(
        functools.partial(shards, Layout(mesh)),
        mesh=mesh,
        in_specs=(
            P(("grp", "row"), None),
            P(("grp", "row"), None),
            P(("grp", "row"), None),
            P(("grp", "row"), None),
            P(("grp", "row")),
            P("grp"),
        ),
        out_specs=P(("grp", "row"), None),
        check_vma=False,
    )
```

```python
import functools

import jax
import jax.numpy as jnp
from jax import lax
from jax.experimental import pallas as pl
from jax.experimental.pallas import tpu as pltpu
from jax.sharding import PartitionSpec as P

CORES = 2
MIB = 1024 * 1024


def params(mib=8):
    return pltpu.CompilerParams(vmem_limit_bytes=mib * MIB)


IN_VMEM = pl.BlockSpec(memory_space=pltpu.VMEM)
IN_SMEM = pl.BlockSpec(memory_space=pltpu.SMEM)
ANYWHERE = pl.BlockSpec(memory_space=pl.ANY)


def in_hbm(x):
    return pltpu.with_memory_space_constraint(x, pltpu.HBM)


class Layout:
    def __init__(self, mesh):
        self.chips = mesh.shape["row"] // CORES
        self.ny = max(1, 4 // mesh.shape["grp"])
        if self.chips % self.ny:
            self.ny = 1
        self.nz = self.chips // self.ny

    def device(self, z, y, core):
        return ((z % self.nz) * self.ny + y % self.ny) * CORES + core

    def everyone(self):
        return [(z, y, c) for z in range(self.nz) for y in range(self.ny) for c in range(CORES)]

    def origin(self, z, y, d, h):
        return lax.rem(z + (self.nz - d), self.nz) * self.ny + lax.rem(y + (self.ny - h), self.ny)

    def along_z(self, x, hops):
        pairs = [(self.device(z, y, c), self.device(z + hops, y, c)) for z, y, c in self.everyone()]
        return lax.ppermute(x, "row", pairs)

    def along_y(self, x, hops=1):
        pairs = [(self.device(z, y, c), self.device(z, y + hops, c)) for z, y, c in self.everyone()]
        return lax.ppermute(x, "row", pairs)

    def to_sibling(self, x):
        pairs = [(self.device(z, y, c), self.device(z, y, 1 - c)) for z, y, c in self.everyone()]
        return lax.ppermute(x, "row", pairs)


def split_columns(act, core, chips):
    rows, depth = act.shape
    kc = depth // (chips * CORES)
    mine = lax.dynamic_index_in_dim(act.reshape(rows, chips, CORES, kc), core, 2, keepdims=False)
    return mine.transpose(1, 0, 2)


class Links:
    def __init__(self, layout, window):
        self.layout, self.window = layout, window
        self.done = {"z": [], "y": []}
        self.first = []

    def after(self, *first):
        self.first += first

    def send(self, kind, x, hops):
        done = self.done[kind]
        first = self.first + done[-self.window:len(done) - self.window + 1]
        self.first = []
        if first:
            x = lax.optimization_barrier((x, *first))[0]
        move = self.layout.along_z if kind == "z" else self.layout.along_y
        done.append(move(x, hops))
        return done[-1]


def gather_columns(links, piece, split, gates, begun={}):
    nz, ny = links.layout.nz, links.layout.ny
    middle = nz // 2
    steps = [(d, 1) for d in range(1, middle + 1)] + [(d, -1) for d in range(nz - 1, middle, -1)]
    steps = sorted(steps, key=lambda s: (min(s[0], nz - s[0]), -s[1]))
    by_z, crossed, found = {0: piece}, {}, [([piece], 0, 0)]

    def cross(d):
        for h in range(1, ny):
            if d == middle and split:
                head = links.send("z", crossed[d - 1, h][:split], 1)
                if -1 in gates:
                    links.after(gates[-1](found))
                if split == piece.shape[0]:
                    got = [head]
                else:
                    got = [head, links.send("y", by_z[d][split:], h)]
            else:
                gate = gates.get(("y", d), ())
                links.after(*(gate() if callable(gate) else gate))
                got = [begun[h]] if d == 0 and h in begun else [links.send("y", by_z[d], h)]
            crossed[d, h] = got[0]
            found.append((got, d, h))

    last = 0
    for d, sign in steps:
        gate = gates.get(d, ())
        links.after(*(gate(by_z) if callable(gate) else gate))
        by_z[d] = links.send("z", by_z[(d - sign) % nz], sign)
        found.append(([by_z[d]], d, 0))
        cross(last)
        last = d
    cross(last)
    links.first = []
    return found


def partial_rotation(layout, act, sib, found, place, total=None, left=()):
    rows = act.shape[0]
    count = len(found)
    blocks = [x for parts, _, _ in found for x in parts]
    kc = sum(x.shape[0] for x in found[0][0])
    width = blocks[0].shape[1]
    unaligned = kc % 128 != 0
    if unaligned:
        act = split_columns(act, place[2], layout.chips)
        sib = split_columns(sib, place[2], layout.chips)

    extra = [] if total is None else [total]

    def kernel(place_ref, act_ref, sib_ref, *refs):
        block_refs, refs = refs[:len(blocks)], refs[len(blocks):]
        o_ref = refs[len(extra)]
        rows_buf, block_buf, sems = refs[-3:]
        z, y, core = place_ref[0], place_ref[1], place_ref[2]
        mine = pl.ds(pl.multiple_of(core * rows, 16), rows)
        other = pl.ds(pl.multiple_of((1 - core) * rows, 16), rows)

        def bring_rows(d, h, to, i):
            q = layout.origin(z, y, d, h)
            at = 0 if unaligned else pl.ds(pl.multiple_of((CORES * q + core) * kc, 128), kc)
            own, its = [ref.at[q] if unaligned else ref.at[:, at] for ref in (act_ref, sib_ref)]
            return [
                pltpu.make_async_copy(own, to.at[mine], sems.at[i, 0]),
                pltpu.make_async_copy(its, to.at[other], sems.at[i, 1]),
            ]

        copies, k = [], 0
        for i in range(count):
            parts, d, h = found[i]
            step, at = bring_rows(d, h, rows_buf.at[i], i), 0
            for j, x in enumerate(parts):
                to = block_buf.at[i, pl.ds(at, x.shape[0])]
                step.append(pltpu.make_async_copy(block_refs[k], to, sems.at[i, 2 + j]))
                at += x.shape[0]
                k += 1
            copies.append(step)
        for j, (_, d, h) in enumerate(left):
            copies.append(bring_rows(d, h, refs[len(extra) + 1].at[j], count + j))
        for step in copies:
            for copy in step:
                copy.start()
        for i, step in enumerate(copies):
            for copy in step:
                copy.wait()
            if i >= count:
                continue
            product = jnp.dot(rows_buf[i], block_buf[i], preferred_element_type=jnp.float32)
            if i > 0:
                o_ref[...] += product
            elif extra:
                o_ref[...] = refs[0][...] + product
            else:
                o_ref[...] = product

    shapes = [jax.ShapeDtypeStruct((CORES * rows, width), jnp.float32)]
    if left:
        shapes.append(jax.ShapeDtypeStruct((len(left), CORES * rows, kc), act.dtype))
    outs = pl.pallas_call(
        kernel,
        in_specs=[IN_SMEM] + [ANYWHERE] * (2 + len(blocks)) + [IN_VMEM] * len(extra),
        out_specs=[IN_VMEM] * len(shapes),
        out_shape=shapes,
        scratch_shapes=[
            pltpu.VMEM((count, CORES * rows, kc), act.dtype),
            pltpu.VMEM((count, kc, width), act.dtype),
            pltpu.SemaphoreType.DMA((count + len(left), 4)),
        ],
        cost_estimate=pl.CostEstimate(
            flops=4 * rows * kc * count * width,
            bytes_accessed=2 * count * kc * (2 * rows + width) + 8 * rows * width,
            transcendentals=0,
        ),
        compiler_params=params(24),
        name="partial_rotation",
    )(place, *[in_hbm(x) for x in (act, sib, *blocks)], *extra)
    return outs if left else outs[0]


def last_rotation(total, rows, found):
    width = total.shape[1]
    blocks = [x for parts, _, _ in found for x in parts]

    def kernel(total_ref, rows_ref, *refs):
        sums, k = total_ref[...], 0
        for i, (parts, _, _) in enumerate(found):
            at = 0
            for part in parts:
                x = rows_ref[i, :, pl.ds(at, part.shape[0])]
                sums += jnp.dot(x, refs[k][...], preferred_element_type=jnp.float32)
                at += part.shape[0]
                k += 1
        refs[-1][...] = sums

    return pl.pallas_call(
        kernel,
        in_specs=[IN_VMEM] * (2 + len(blocks)),
        out_specs=IN_VMEM,
        out_shape=jax.ShapeDtypeStruct(total.shape, jnp.float32),
        cost_estimate=pl.CostEstimate(
            flops=2 * rows.size * width,
            bytes_accessed=2 * rows.size + 8 * total.size,
            transcendentals=0,
        ),
        compiler_params=params(),
        name="last_rotation",
    )(total, rows, *blocks)


def owned_gradients(layout, mine, other, place, owned):
    nz, ny = layout.nz, layout.ny
    tokens, width = mine.shape
    kept = nz * ny * owned

    def kernel(place_ref, mine_ref, other_ref, o_ref):
        slot = lax.broadcasted_iota(jnp.int32, (kept, width), 0)
        column = lax.broadcasted_iota(jnp.int32, (kept, width), 1)
        z, y, core = place_ref[0], place_ref[1], place_ref[2]
        to_y = lax.rem(y + 1 + slot // (nz * owned), ny)
        to_z = lax.rem(z + lax.rem(slot // owned, nz), nz)
        wanted = ((to_z * ny + to_y) * CORES + core) * owned + lax.rem(slot, owned)
        pick = jnp.where(wanted == column, 1.0, 0.0).astype(jnp.bfloat16)
        rotated = (mine_ref[...] + other_ref[...]).astype(jnp.bfloat16)
        picked = lax.dot_general(
            pick, rotated, (((1,), (1,)), ((), ())), preferred_element_type=jnp.float32
        )
        o_ref[...] = picked.astype(jnp.bfloat16)

    return pl.pallas_call(
        kernel,
        in_specs=[IN_SMEM, IN_VMEM, IN_VMEM],
        out_specs=IN_VMEM,
        out_shape=jax.ShapeDtypeStruct((kept, tokens), jnp.bfloat16),
        cost_estimate=pl.CostEstimate(
            flops=2 * kept * width * tokens,
            bytes_accessed=8 * tokens * width + 2 * kept * tokens,
            transcendentals=0,
        ),
        compiler_params=params(),
        name="owned_gradients",
    )(place, mine, other)


def chip_sums(layout, grads, mine, other, positions, lengths, owned, cut):
    nz, ny = layout.nz, layout.ny
    tokens, width = mine.shape
    seqs = lengths.shape[0]
    stay = nz * owned
    rest = width - cut

    def kernel(lengths_ref, grads_ref, mine_ref, other_ref, positions_ref, *refs):
        rotated = mine_ref[...] + other_ref[...]
        position = positions_ref[...]
        begin = jnp.int32(0)
        for s in range(seqs):
            end = begin + lengths_ref[s]
            inside = (position >= begin) & (position < end)
            part = jnp.where(inside, rotated, 0.0).astype(jnp.bfloat16)
            sums = jnp.dot(grads_ref[...], part, preferred_element_type=jnp.float32)
            at = pl.ds(s * cut, cut)
            for d in range(nz):
                for h in range(ny):
                    block = sums[h * stay + d * owned:h * stay + (d + 1) * owned, :cut]
                    refs[d][pl.ds(h * owned, owned), at] = block.astype(refs[d].dtype)
            if rest:
                at = pl.ds(s * rest, rest)
                refs[nz][:, at] = sums[stay:, cut:]
                refs[nz + 1][:, at] = sums[:stay, cut:].astype(jnp.bfloat16)
            begin = end

    shapes = [jax.ShapeDtypeStruct((ny * owned, seqs * cut), jnp.float32)]
    shapes += [jax.ShapeDtypeStruct((ny * owned, seqs * cut), jnp.bfloat16)] * (nz - 1)
    if rest:
        shapes.append(jax.ShapeDtypeStruct((stay, seqs * rest), jnp.float32))
        shapes.append(jax.ShapeDtypeStruct((stay, seqs * rest), jnp.bfloat16))
    return pl.pallas_call(
        kernel,
        in_specs=[IN_SMEM] + [IN_VMEM] * 4,
        out_specs=[IN_VMEM] * len(shapes),
        out_shape=shapes,
        cost_estimate=pl.CostEstimate(
            flops=2 * grads.size * seqs * width,
            bytes_accessed=8 * tokens * width + 2 * grads.shape[0] * seqs * width,
            transcendentals=0,
        ),
        compiler_params=params(),
        name="chip_sums",
    )(lengths, grads, mine, other, positions)


def add_up(kept, came, owned, own):
    count = kept.shape[0] // owned
    width = kept.shape[1]

    def kernel(*refs):
        total = refs[0][...]
        for i in range(len(came)):
            total += refs[1 + i][...].astype(jnp.float32)
        outs = refs[1 + len(came):]
        for i in range(count):
            outs[i][...] = total[i * owned:(i + 1) * owned].astype(outs[i].dtype)

    shapes = [
        jax.ShapeDtypeStruct((owned, width), jnp.float32 if i == own else jnp.bfloat16)
        for i in range(count)
    ]
    return pl.pallas_call(
        kernel,
        in_specs=[IN_VMEM] * (1 + len(came)),
        out_specs=[IN_VMEM] * count,
        out_shape=shapes,
        cost_estimate=pl.CostEstimate(
            flops=kept.size * len(came), bytes_accessed=8 * kept.size, transcendentals=0
        ),
        compiler_params=params(),
        name="add_up",
    )(kept, *came)


def squares(groups, lengths, owned):
    seqs = lengths.shape[0]
    widths = [group[0].shape[1] // seqs for group in groups]

    def kernel(lengths_ref, *refs):
        o_ref = refs[-1]
        tokens = lengths_ref[0]
        for s in range(1, seqs):
            tokens = tokens + lengths_ref[s]
        at, k = 0, 0
        for group, width in zip(groups, widths):
            over = jnp.full((owned, width), tokens, jnp.int32).astype(jnp.float32)
            sums = refs[k][...]
            for ref in refs[k + 1:k + len(group)]:
                sums = sums + ref[...].astype(jnp.float32)
            k += len(group)
            sums = sums * sums
            acc = sums[:, :width]
            for s in range(1, seqs):
                acc = acc + sums[:, s * width:(s + 1) * width]
            o_ref[:, pl.ds(at, width)] = acc / over
            at += width

    flat = [x for group in groups for x in group]
    return pl.pallas_call(
        kernel,
        in_specs=[IN_SMEM] + [IN_VMEM] * len(flat),
        out_specs=IN_VMEM,
        out_shape=jax.ShapeDtypeStruct((owned, sum(widths)), jnp.float32),
        cost_estimate=pl.CostEstimate(
            flops=2 * sum(x.size for x in flat),
            bytes_accessed=2 * sum(x.size for x in flat),
            transcendentals=0,
        ),
        compiler_params=params(),
        name="squares",
    )(lengths, *flat)


def scatter_sums(layout, sums, owned):
    nz, ny = layout.nz, layout.ny
    if ny == 1:
        return [[sums[0]] + [layout.along_z(sums[d], d) for d in range(1, nz)]]
    crossed = [layout.along_y(sums[nz + 1])]
    came = [layout.along_z(sums[d], d) for d in range(1, nz)]
    by_z = add_up(sums[nz], crossed, owned, 0)
    second = [by_z[0]] + [layout.along_z(by_z[d], d) for d in range(1, nz)]
    by_y = add_up(sums[0], came, owned, 1)
    return [[by_y[1], layout.along_y(by_y[0])], second]


def shards(layout, activations, gradients, basis_a, basis_g, token_index, seq_lengths):
    nz, ny, chips = layout.nz, layout.ny, layout.chips
    rows = activations.shape[0]
    owned = basis_g.shape[1] // (chips * CORES)
    me = lax.axis_index("row")
    core = lax.rem(me, CORES)
    y = lax.rem(me // CORES, ny)
    z = me // (CORES * ny)
    place = jnp.stack([z, y, core]).astype(jnp.int32)

    sib_index = layout.to_sibling(token_index)
    first = core == 0
    positions = jnp.concatenate(
        [jnp.where(first, token_index, sib_index), jnp.where(first, sib_index, token_index)]
    ).reshape(CORES * rows, 1)

    links = Links(layout, 2)
    sib_g = layout.to_sibling(gradients)
    sib_a = layout.to_sibling(activations)
    split = [basis_g.shape[0] * 4 // 7, basis_a.shape[0] * 3 // 4] if ny > 1 else [0, 0]
    early = []

    def rotate_early(found):
        early.append(partial_rotation(layout, gradients, sib_g, found[:4], place))
        return early[0]

    begun = {}

    def begin_a():
        for h in range(1, ny):
            links.after(sib_a)
            begun[h] = links.send("y", basis_a, h)
        return list(begun.values())

    gates = {
        ("y", 1): begin_a,
        nz - 1: [sib_a],
        nz // 2: lambda by_z: [sib_g, sib_a, *begun.values()],
        -1: rotate_early,
    }
    found_g = gather_columns(links, basis_g, split[0], gates)
    if not early:
        rotate_early(found_g)
    mine_g = partial_rotation(layout, gradients, sib_g, found_g[4:], place, early[0])
    links.after(early[0])
    found_a = gather_columns(links, basis_a, split[1], {("y", nz - 1): [mine_g]}, begun)
    grads = owned_gradients(layout, mine_g, layout.to_sibling(mine_g), place, owned)

    most, rows_left = partial_rotation(
        layout, activations, sib_a, found_a[:-2], place, None, found_a[-2:]
    )
    most, positions = lax.optimization_barrier((most, positions))
    mine_a = last_rotation(most, rows_left, found_a[-2:])
    cut = basis_a.shape[1] // ny**2
    sums = chip_sums(
        layout, grads, mine_a, layout.to_sibling(mine_a), positions, seq_lengths, owned, cut
    )
    return squares(scatter_sums(layout, sums, owned), seq_lengths, owned)


def solution(mesh):
    return jax.shard_map(
        functools.partial(shards, Layout(mesh)),
        mesh=mesh,
        in_specs=(
            P(("grp", "row"), None),
            P(("grp", "row"), None),
            P(("grp", "row"), None),
            P(("grp", "row"), None),
            P(("grp", "row")),
            P("grp"),
        ),
        out_specs=P(("grp", "row"), None),
        check_vma=False,
    )
```

```python
import functools

import jax
import jax.numpy as jnp
from jax import lax
from jax.experimental import pallas as pl
from jax.experimental.pallas import tpu as pltpu
from jax.sharding import PartitionSpec as P

CORES = 2
MIB = 1024 * 1024


def params(mib=8):
    return pltpu.CompilerParams(vmem_limit_bytes=mib * MIB)


IN_VMEM = pl.BlockSpec(memory_space=pltpu.VMEM)
IN_SMEM = pl.BlockSpec(memory_space=pltpu.SMEM)
ANYWHERE = pl.BlockSpec(memory_space=pl.ANY)


def in_hbm(x):
    return pltpu.with_memory_space_constraint(x, pltpu.HBM)


class Layout:
    def __init__(self, mesh):
        self.chips = mesh.shape["row"] // CORES
        self.ny = max(1, 4 // mesh.shape["grp"])
        if self.chips % self.ny:
            self.ny = 1
        self.nz = self.chips // self.ny

    def device(self, z, y, core):
        return ((z % self.nz) * self.ny + y % self.ny) * CORES + core

    def everyone(self):
        return [(z, y, c) for z in range(self.nz) for y in range(self.ny) for c in range(CORES)]

    def origin(self, z, y, d, h):
        return lax.rem(z + (self.nz - d), self.nz) * self.ny + lax.rem(y + (self.ny - h), self.ny)

    def along_z(self, x, hops):
        pairs = [(self.device(z, y, c), self.device(z + hops, y, c)) for z, y, c in self.everyone()]
        return lax.ppermute(x, "row", pairs)

    def along_y(self, x, hops=1):
        pairs = [(self.device(z, y, c), self.device(z, y + hops, c)) for z, y, c in self.everyone()]
        return lax.ppermute(x, "row", pairs)

    def to_sibling(self, x):
        pairs = [(self.device(z, y, c), self.device(z, y, 1 - c)) for z, y, c in self.everyone()]
        return lax.ppermute(x, "row", pairs)


def split_columns(act, core, chips):
    rows, depth = act.shape
    kc = depth // (chips * CORES)
    mine = lax.dynamic_index_in_dim(act.reshape(rows, chips, CORES, kc), core, 2, keepdims=False)
    return mine.transpose(1, 0, 2)


class Links:
    def __init__(self, layout, window):
        self.layout, self.window = layout, window
        self.done = {"z": [], "y": []}
        self.first = []

    def after(self, *first):
        self.first += first

    def send(self, kind, x, hops):
        done = self.done[kind]
        first = self.first + done[-self.window:len(done) - self.window + 1]
        self.first = []
        if first:
            x = lax.optimization_barrier((x, *first))[0]
        move = self.layout.along_z if kind == "z" else self.layout.along_y
        done.append(move(x, hops))
        return done[-1]


def gather_columns(links, piece, split, gates, begun={}):
    nz, ny = links.layout.nz, links.layout.ny
    middle = nz // 2
    steps = [(d, 1) for d in range(1, middle + 1)] + [(d, -1) for d in range(nz - 1, middle, -1)]
    steps = sorted(steps, key=lambda s: (min(s[0], nz - s[0]), -s[1]))
    by_z, crossed, found = {0: piece}, {}, [([piece], 0, 0)]

    def cross(d):
        for h in range(1, ny):
            if d == middle and split:
                head = links.send("z", crossed[d - 1, h][:split], 1)
                if -1 in gates:
                    links.after(gates[-1](found))
                if split == piece.shape[0]:
                    got = [head]
                else:
                    got = [head, links.send("y", by_z[d][split:], h)]
            else:
                gate = gates.get(("y", d), ())
                links.after(*(gate() if callable(gate) else gate))
                got = [begun[h]] if d == 0 and h in begun else [links.send("y", by_z[d], h)]
            crossed[d, h] = got[0]
            found.append((got, d, h))

    last = 0
    for d, sign in steps:
        gate = gates.get(d, ())
        links.after(*(gate(by_z) if callable(gate) else gate))
        by_z[d] = links.send("z", by_z[(d - sign) % nz], sign)
        found.append(([by_z[d]], d, 0))
        cross(last)
        last = d
    cross(last)
    links.first = []
    return found


def partial_rotation(layout, act, sib, found, place, total=None, left=()):
    rows = act.shape[0]
    count = len(found)
    blocks = [x for parts, _, _ in found for x in parts]
    kc = sum(x.shape[0] for x in found[0][0])
    width = blocks[0].shape[1]
    unaligned = kc % 128 != 0
    if unaligned:
        act = split_columns(act, place[2], layout.chips)
        sib = split_columns(sib, place[2], layout.chips)

    extra = [] if total is None else [total]

    def kernel(place_ref, act_ref, sib_ref, *refs):
        block_refs, refs = refs[:len(blocks)], refs[len(blocks):]
        o_ref = refs[len(extra)]
        rows_buf, block_buf, sems = refs[-3:]
        z, y, core = place_ref[0], place_ref[1], place_ref[2]
        mine = pl.ds(pl.multiple_of(core * rows, 16), rows)
        other = pl.ds(pl.multiple_of((1 - core) * rows, 16), rows)

        def bring_rows(d, h, to, i):
            q = layout.origin(z, y, d, h)
            at = 0 if unaligned else pl.ds(pl.multiple_of((CORES * q + core) * kc, 128), kc)
            own, its = [ref.at[q] if unaligned else ref.at[:, at] for ref in (act_ref, sib_ref)]
            return [
                pltpu.make_async_copy(own, to.at[mine], sems.at[i, 0]),
                pltpu.make_async_copy(its, to.at[other], sems.at[i, 1]),
            ]

        copies, k = [], 0
        for i in range(count):
            parts, d, h = found[i]
            step, at = bring_rows(d, h, rows_buf.at[i], i), 0
            for j, x in enumerate(parts):
                to = block_buf.at[i, pl.ds(at, x.shape[0])]
                step.append(pltpu.make_async_copy(block_refs[k], to, sems.at[i, 2 + j]))
                at += x.shape[0]
                k += 1
            copies.append(step)
        for j, (_, d, h) in enumerate(left):
            copies.append(bring_rows(d, h, refs[len(extra) + 1].at[j], count + j))
        for step in copies:
            for copy in step:
                copy.start()
        for i, step in enumerate(copies):
            for copy in step:
                copy.wait()
            if i >= count:
                continue
            product = jnp.dot(rows_buf[i], block_buf[i], preferred_element_type=jnp.float32)
            if i > 0:
                o_ref[...] += product
            elif extra:
                o_ref[...] = refs[0][...] + product
            else:
                o_ref[...] = product

    shapes = [jax.ShapeDtypeStruct((CORES * rows, width), jnp.float32)]
    if left:
        shapes.append(jax.ShapeDtypeStruct((len(left), CORES * rows, kc), act.dtype))
    outs = pl.pallas_call(
        kernel,
        in_specs=[IN_SMEM] + [ANYWHERE] * (2 + len(blocks)) + [IN_VMEM] * len(extra),
        out_specs=[IN_VMEM] * len(shapes),
        out_shape=shapes,
        scratch_shapes=[
            pltpu.VMEM((count, CORES * rows, kc), act.dtype),
            pltpu.VMEM((count, kc, width), act.dtype),
            pltpu.SemaphoreType.DMA((count + len(left), 4)),
        ],
        cost_estimate=pl.CostEstimate(
            flops=4 * rows * kc * count * width,
            bytes_accessed=2 * count * kc * (2 * rows + width) + 8 * rows * width,
            transcendentals=0,
        ),
        compiler_params=params(24),
        name="partial_rotation",
    )(place, *[in_hbm(x) for x in (act, sib, *blocks)], *extra)
    return outs if left else outs[0]


def last_rotation(total, rows, found):
    width = total.shape[1]
    blocks = [x for parts, _, _ in found for x in parts]

    def kernel(total_ref, rows_ref, *refs):
        sums, k = total_ref[...], 0
        for i, (parts, _, _) in enumerate(found):
            at = 0
            for part in parts:
                x = rows_ref[i, :, pl.ds(at, part.shape[0])]
                sums += jnp.dot(x, refs[k][...], preferred_element_type=jnp.float32)
                at += part.shape[0]
                k += 1
        refs[-2][...] = sums
        refs[-1][...] = sums.astype(jnp.bfloat16)

    return pl.pallas_call(
        kernel,
        in_specs=[IN_VMEM] * (2 + len(blocks)),
        out_specs=[IN_VMEM] * 2,
        out_shape=[
            jax.ShapeDtypeStruct(total.shape, jnp.float32),
            jax.ShapeDtypeStruct(total.shape, jnp.bfloat16),
        ],
        cost_estimate=pl.CostEstimate(
            flops=2 * rows.size * width,
            bytes_accessed=2 * rows.size + 8 * total.size,
            transcendentals=0,
        ),
        compiler_params=params(),
        name="last_rotation",
    )(total, rows, *blocks)


def owned_gradients(layout, mine, other, place, owned):
    nz, ny = layout.nz, layout.ny
    tokens, width = mine.shape
    kept = nz * ny * owned

    def kernel(place_ref, mine_ref, other_ref, o_ref):
        slot = lax.broadcasted_iota(jnp.int32, (kept, width), 0)
        column = lax.broadcasted_iota(jnp.int32, (kept, width), 1)
        z, y, core = place_ref[0], place_ref[1], place_ref[2]
        to_y = lax.rem(y + 1 + slot // (nz * owned), ny)
        to_z = lax.rem(z + lax.rem(slot // owned, nz), nz)
        wanted = ((to_z * ny + to_y) * CORES + core) * owned + lax.rem(slot, owned)
        pick = jnp.where(wanted == column, 1.0, 0.0).astype(jnp.bfloat16)
        rotated = (mine_ref[...] + other_ref[...]).astype(jnp.bfloat16)
        picked = lax.dot_general(
            pick, rotated, (((1,), (1,)), ((), ())), preferred_element_type=jnp.float32
        )
        o_ref[...] = picked.astype(jnp.bfloat16)

    return pl.pallas_call(
        kernel,
        in_specs=[IN_SMEM, IN_VMEM, IN_VMEM],
        out_specs=IN_VMEM,
        out_shape=jax.ShapeDtypeStruct((kept, tokens), jnp.bfloat16),
        cost_estimate=pl.CostEstimate(
            flops=2 * kept * width * tokens,
            bytes_accessed=8 * tokens * width + 2 * kept * tokens,
            transcendentals=0,
        ),
        compiler_params=params(),
        name="owned_gradients",
    )(place, mine, other)


def chip_sums(layout, grads, mine, other, positions, lengths, owned, cut):
    nz, ny = layout.nz, layout.ny
    tokens, width = mine.shape
    seqs = lengths.shape[0]
    stay = nz * owned
    rest = width - cut

    def kernel(lengths_ref, grads_ref, mine_ref, other_ref, positions_ref, *refs):
        rotated = mine_ref[...] + other_ref[...].astype(jnp.float32)
        position = positions_ref[...]

        def one(s, begin):
            end = begin + lengths_ref[s]
            inside = (position >= begin) & (position < end)
            part = jnp.where(inside, rotated, 0.0).astype(jnp.bfloat16)
            sums = jnp.dot(grads_ref[...], part, preferred_element_type=jnp.float32)
            at = pl.ds(pl.multiple_of(s * cut, cut), cut)
            for d in range(nz):
                for h in range(ny):
                    block = sums[h * stay + d * owned:h * stay + (d + 1) * owned, :cut]
                    refs[d][pl.ds(h * owned, owned), at] = block.astype(refs[d].dtype)
            if rest:
                at = pl.ds(pl.multiple_of(s * rest, rest), rest)
                refs[nz][:, at] = sums[stay:, cut:]
                refs[nz + 1][:, at] = sums[:stay, cut:].astype(jnp.bfloat16)
            return end

        lax.fori_loop(0, seqs, one, jnp.int32(0))

    shapes = [jax.ShapeDtypeStruct((ny * owned, seqs * cut), jnp.float32)]
    shapes += [jax.ShapeDtypeStruct((ny * owned, seqs * cut), jnp.bfloat16)] * (nz - 1)
    if rest:
        shapes.append(jax.ShapeDtypeStruct((stay, seqs * rest), jnp.float32))
        shapes.append(jax.ShapeDtypeStruct((stay, seqs * rest), jnp.bfloat16))
    return pl.pallas_call(
        kernel,
        in_specs=[IN_SMEM] + [IN_VMEM] * 4,
        out_specs=[IN_VMEM] * len(shapes),
        out_shape=shapes,
        cost_estimate=pl.CostEstimate(
            flops=2 * grads.size * seqs * width,
            bytes_accessed=8 * tokens * width + 2 * grads.shape[0] * seqs * width,
            transcendentals=0,
        ),
        compiler_params=params(),
        name="chip_sums",
    )(lengths, grads, mine, other, positions)


def add_up(kept, came, owned, own):
    count = kept.shape[0] // owned
    width = kept.shape[1]

    def kernel(*refs):
        total = refs[0][...]
        for i in range(len(came)):
            total += refs[1 + i][...].astype(jnp.float32)
        outs = refs[1 + len(came):]
        for i in range(count):
            outs[i][...] = total[i * owned:(i + 1) * owned].astype(outs[i].dtype)

    shapes = [
        jax.ShapeDtypeStruct((owned, width), jnp.float32 if i == own else jnp.bfloat16)
        for i in range(count)
    ]
    return pl.pallas_call(
        kernel,
        in_specs=[IN_VMEM] * (1 + len(came)),
        out_specs=[IN_VMEM] * count,
        out_shape=shapes,
        cost_estimate=pl.CostEstimate(
            flops=kept.size * len(came), bytes_accessed=8 * kept.size, transcendentals=0
        ),
        compiler_params=params(),
        name="add_up",
    )(kept, *came)


def squares(groups, lengths, owned):
    seqs = lengths.shape[0]
    widths = [group[0].shape[1] // seqs for group in groups]

    def kernel(lengths_ref, *refs):
        o_ref = refs[-1]
        tokens = lengths_ref[0]
        for s in range(1, seqs):
            tokens = tokens + lengths_ref[s]
        at, k = 0, 0
        for group, width in zip(groups, widths):
            over = jnp.full((owned, width), tokens, jnp.int32).astype(jnp.float32)
            sums = refs[k][...]
            for ref in refs[k + 1:k + len(group)]:
                sums = sums + ref[...].astype(jnp.float32)
            k += len(group)
            sums = sums * sums
            acc = sums[:, :width]
            for s in range(1, seqs):
                acc = acc + sums[:, s * width:(s + 1) * width]
            o_ref[:, pl.ds(at, width)] = acc / over
            at += width

    flat = [x for group in groups for x in group]
    return pl.pallas_call(
        kernel,
        in_specs=[IN_SMEM] + [IN_VMEM] * len(flat),
        out_specs=IN_VMEM,
        out_shape=jax.ShapeDtypeStruct((owned, sum(widths)), jnp.float32),
        cost_estimate=pl.CostEstimate(
            flops=2 * sum(x.size for x in flat),
            bytes_accessed=2 * sum(x.size for x in flat),
            transcendentals=0,
        ),
        compiler_params=params(),
        name="squares",
    )(lengths, *flat)


def scatter_sums(layout, sums, owned):
    nz, ny = layout.nz, layout.ny
    if ny == 1:
        return [[sums[0]] + [layout.along_z(sums[d], d) for d in range(1, nz)]]
    crossed = [layout.along_y(sums[nz + 1])]
    came = [layout.along_z(sums[d], d) for d in range(1, nz)]
    by_z = add_up(sums[nz], crossed, owned, 0)
    second = [by_z[0]] + [layout.along_z(by_z[d], d) for d in range(1, nz)]
    by_y = add_up(sums[0], came, owned, 1)
    return [[by_y[1], layout.along_y(by_y[0])], second]


def shards(layout, activations, gradients, basis_a, basis_g, token_index, seq_lengths):
    nz, ny, chips = layout.nz, layout.ny, layout.chips
    rows = activations.shape[0]
    owned = basis_g.shape[1] // (chips * CORES)
    me = lax.axis_index("row")
    core = lax.rem(me, CORES)
    y = lax.rem(me // CORES, ny)
    z = me // (CORES * ny)
    place = jnp.stack([z, y, core]).astype(jnp.int32)

    sib_index = layout.to_sibling(token_index)
    first = core == 0
    positions = jnp.concatenate(
        [jnp.where(first, token_index, sib_index), jnp.where(first, sib_index, token_index)]
    ).reshape(CORES * rows, 1)

    links = Links(layout, 2)
    sib_g = layout.to_sibling(gradients)
    sib_a = layout.to_sibling(activations)
    split = [basis_g.shape[0] * 4 // 7, basis_a.shape[0] * 3 // 4] if ny > 1 else [0, 0]
    early = []

    def rotate_early(found):
        early.append(partial_rotation(layout, gradients, sib_g, found[:4], place))
        return early[0]

    begun = {}

    def begin_a():
        for h in range(1, ny):
            links.after(sib_a)
            begun[h] = links.send("y", basis_a, h)
        return list(begun.values())

    gates = {
        ("y", 1): begin_a,
        nz - 1: [sib_a],
        nz // 2: lambda by_z: [sib_g, sib_a, *begun.values()],
        -1: rotate_early,
    }
    found_g = gather_columns(links, basis_g, split[0], gates)
    if not early:
        rotate_early(found_g)
    mine_g = partial_rotation(layout, gradients, sib_g, found_g[4:], place, early[0])
    links.after(early[0])
    found_a = gather_columns(links, basis_a, split[1], {("y", nz - 1): [mine_g]}, begun)
    grads = owned_gradients(layout, mine_g, layout.to_sibling(mine_g), place, owned)

    most, rows_left = partial_rotation(
        layout, activations, sib_a, found_a[:-2], place, None, found_a[-2:]
    )
    most, positions = lax.optimization_barrier((most, positions))
    mine_a, sent_a = last_rotation(most, rows_left, found_a[-2:])
    cut = basis_a.shape[1] // ny**2
    sums = chip_sums(
        layout, grads, mine_a, layout.to_sibling(sent_a), positions, seq_lengths, owned, cut
    )
    return squares(scatter_sums(layout, sums, owned), seq_lengths, owned)


def solution(mesh):
    return jax.shard_map(
        functools.partial(shards, Layout(mesh)),
        mesh=mesh,
        in_specs=(
            P(("grp", "row"), None),
            P(("grp", "row"), None),
            P(("grp", "row"), None),
            P(("grp", "row"), None),
            P(("grp", "row")),
            P("grp"),
        ),
        out_specs=P(("grp", "row"), None),
        check_vma=False,
    )
```

```python
import functools

import jax
import jax.numpy as jnp
from jax import lax
from jax.experimental import pallas as pl
from jax.experimental.pallas import tpu as pltpu
from jax.sharding import PartitionSpec as P

CORES = 2
MIB = 1024 * 1024


def params(mib=8):
    return pltpu.CompilerParams(vmem_limit_bytes=mib * MIB)


IN_VMEM = pl.BlockSpec(memory_space=pltpu.VMEM)
IN_SMEM = pl.BlockSpec(memory_space=pltpu.SMEM)
ANYWHERE = pl.BlockSpec(memory_space=pl.ANY)


def in_hbm(x):
    return pltpu.with_memory_space_constraint(x, pltpu.HBM)


class Layout:
    def __init__(self, mesh):
        self.chips = mesh.shape["row"] // CORES
        self.ny = max(1, 4 // mesh.shape["grp"])
        if self.chips % self.ny:
            self.ny = 1
        self.nz = self.chips // self.ny

    def device(self, z, y, core):
        return ((z % self.nz) * self.ny + y % self.ny) * CORES + core

    def everyone(self):
        return [(z, y, c) for z in range(self.nz) for y in range(self.ny) for c in range(CORES)]

    def origin(self, z, y, d, h):
        return lax.rem(z + (self.nz - d), self.nz) * self.ny + lax.rem(y + (self.ny - h), self.ny)

    def along_z(self, x, hops):
        pairs = [(self.device(z, y, c), self.device(z + hops, y, c)) for z, y, c in self.everyone()]
        return lax.ppermute(x, "row", pairs)

    def along_y(self, x, hops=1):
        pairs = [(self.device(z, y, c), self.device(z, y + hops, c)) for z, y, c in self.everyone()]
        return lax.ppermute(x, "row", pairs)

    def to_sibling(self, x):
        pairs = [(self.device(z, y, c), self.device(z, y, 1 - c)) for z, y, c in self.everyone()]
        return lax.ppermute(x, "row", pairs)


def split_columns(act, core, chips):
    rows, depth = act.shape
    kc = depth // (chips * CORES)
    mine = lax.dynamic_index_in_dim(act.reshape(rows, chips, CORES, kc), core, 2, keepdims=False)
    return mine.transpose(1, 0, 2)


class Links:
    def __init__(self, layout, window):
        self.layout, self.window = layout, window
        self.done = {"z": [], "y": []}
        self.first = []

    def after(self, *first):
        self.first += first

    def send(self, kind, x, hops):
        done = self.done[kind]
        first = self.first + done[-self.window:len(done) - self.window + 1]
        self.first = []
        if first:
            x = lax.optimization_barrier((x, *first))[0]
        move = self.layout.along_z if kind == "z" else self.layout.along_y
        done.append(move(x, hops))
        return done[-1]


def gather_columns(links, piece, split, gates, begun={}):
    nz, ny = links.layout.nz, links.layout.ny
    middle = nz // 2
    steps = [(d, 1) for d in range(1, middle + 1)] + [(d, -1) for d in range(nz - 1, middle, -1)]
    steps = sorted(steps, key=lambda s: (min(s[0], nz - s[0]), -s[1]))
    by_z, crossed, found = {0: piece}, {}, [([piece], 0, 0)]

    def cross(d):
        for h in range(1, ny):
            if d == middle and split:
                head = links.send("z", crossed[d - 1, h][:split], 1)
                if -1 in gates:
                    links.after(gates[-1](found))
                if split == piece.shape[0]:
                    got = [head]
                else:
                    got = [head, links.send("y", by_z[d][split:], h)]
            else:
                gate = gates.get(("y", d), ())
                links.after(*(gate() if callable(gate) else gate))
                got = [begun[h]] if d == 0 and h in begun else [links.send("y", by_z[d], h)]
            crossed[d, h] = got[0]
            found.append((got, d, h))

    last = 0
    for d, sign in steps:
        gate = gates.get(d, ())
        links.after(*(gate(by_z) if callable(gate) else gate))
        by_z[d] = links.send("z", by_z[(d - sign) % nz], sign)
        found.append(([by_z[d]], d, 0))
        cross(last)
        last = d
    cross(last)
    links.first = []
    return found


def partial_rotation(layout, act, sib, found, place, total=None, left=()):
    rows = act.shape[0]
    count = len(found)
    blocks = [x for parts, _, _ in found for x in parts]
    kc = sum(x.shape[0] for x in found[0][0])
    width = blocks[0].shape[1]
    unaligned = kc % 128 != 0
    if unaligned:
        act = split_columns(act, place[2], layout.chips)
        sib = split_columns(sib, place[2], layout.chips)

    extra = [] if total is None else [total]

    def kernel(place_ref, act_ref, sib_ref, *refs):
        block_refs, refs = refs[:len(blocks)], refs[len(blocks):]
        o_ref = refs[len(extra)]
        rows_buf, block_buf, sems = refs[-3:]
        z, y, core = place_ref[0], place_ref[1], place_ref[2]
        mine = pl.ds(pl.multiple_of(core * rows, 16), rows)
        other = pl.ds(pl.multiple_of((1 - core) * rows, 16), rows)

        def bring_rows(d, h, to, i):
            q = layout.origin(z, y, d, h)
            at = 0 if unaligned else pl.ds(pl.multiple_of((CORES * q + core) * kc, 128), kc)
            own, its = [ref.at[q] if unaligned else ref.at[:, at] for ref in (act_ref, sib_ref)]
            return [
                pltpu.make_async_copy(own, to.at[mine], sems.at[i, 0]),
                pltpu.make_async_copy(its, to.at[other], sems.at[i, 1]),
            ]

        copies, k = [], 0
        for i in range(count):
            parts, d, h = found[i]
            step, at = bring_rows(d, h, rows_buf.at[i], i), 0
            for j, x in enumerate(parts):
                to = block_buf.at[i, pl.ds(at, x.shape[0])]
                step.append(pltpu.make_async_copy(block_refs[k], to, sems.at[i, 2 + j]))
                at += x.shape[0]
                k += 1
            copies.append(step)
        for j, (_, d, h) in enumerate(left):
            copies.append(bring_rows(d, h, refs[len(extra) + 1].at[j], count + j))
        for step in copies:
            for copy in step:
                copy.start()
        for i, step in enumerate(copies):
            for copy in step:
                copy.wait()
            if i >= count:
                continue
            product = jnp.dot(rows_buf[i], block_buf[i], preferred_element_type=jnp.float32)
            if i > 0:
                o_ref[...] += product
            elif extra:
                o_ref[...] = refs[0][...] + product
            else:
                o_ref[...] = product

    shapes = [jax.ShapeDtypeStruct((CORES * rows, width), jnp.float32)]
    if left:
        shapes.append(jax.ShapeDtypeStruct((len(left), CORES * rows, kc), act.dtype))
    outs = pl.pallas_call(
        kernel,
        in_specs=[IN_SMEM] + [ANYWHERE] * (2 + len(blocks)) + [IN_VMEM] * len(extra),
        out_specs=[IN_VMEM] * len(shapes),
        out_shape=shapes,
        scratch_shapes=[
            pltpu.VMEM((count, CORES * rows, kc), act.dtype),
            pltpu.VMEM((count, kc, width), act.dtype),
            pltpu.SemaphoreType.DMA((count + len(left), 4)),
        ],
        cost_estimate=pl.CostEstimate(
            flops=4 * rows * kc * count * width,
            bytes_accessed=2 * count * kc * (2 * rows + width) + 8 * rows * width,
            transcendentals=0,
        ),
        compiler_params=params(24),
        name="partial_rotation",
    )(place, *[in_hbm(x) for x in (act, sib, *blocks)], *extra)
    return outs if left else outs[0]


def last_rotation(total, rows, found):
    width = total.shape[1]
    blocks = [x for parts, _, _ in found for x in parts]

    def kernel(total_ref, rows_ref, *refs):
        sums, k = total_ref[...], 0
        for i, (parts, _, _) in enumerate(found):
            at = 0
            for part in parts:
                x = rows_ref[i, :, pl.ds(at, part.shape[0])]
                sums += jnp.dot(x, refs[k][...], preferred_element_type=jnp.float32)
                at += part.shape[0]
                k += 1
        refs[-1][...] = sums

    return pl.pallas_call(
        kernel,
        in_specs=[IN_VMEM] * (2 + len(blocks)),
        out_specs=IN_VMEM,
        out_shape=jax.ShapeDtypeStruct(total.shape, jnp.float32),
        cost_estimate=pl.CostEstimate(
            flops=2 * rows.size * width,
            bytes_accessed=2 * rows.size + 8 * total.size,
            transcendentals=0,
        ),
        compiler_params=params(),
        name="last_rotation",
    )(total, rows, *blocks)


def owned_gradients(layout, mine, other, place, owned):
    nz, ny = layout.nz, layout.ny
    tokens, width = mine.shape
    kept = nz * ny * owned

    def kernel(place_ref, mine_ref, other_ref, o_ref):
        slot = lax.broadcasted_iota(jnp.int32, (kept, width), 0)
        column = lax.broadcasted_iota(jnp.int32, (kept, width), 1)
        z, y, core = place_ref[0], place_ref[1], place_ref[2]
        to_y = lax.rem(y + 1 + slot // (nz * owned), ny)
        to_z = lax.rem(z + lax.rem(slot // owned, nz), nz)
        wanted = ((to_z * ny + to_y) * CORES + core) * owned + lax.rem(slot, owned)
        pick = jnp.where(wanted == column, 1.0, 0.0).astype(jnp.bfloat16)
        rotated = (mine_ref[...] + other_ref[...]).astype(jnp.bfloat16)
        picked = lax.dot_general(
            pick, rotated, (((1,), (1,)), ((), ())), preferred_element_type=jnp.float32
        )
        o_ref[...] = picked.astype(jnp.bfloat16)

    return pl.pallas_call(
        kernel,
        in_specs=[IN_SMEM, IN_VMEM, IN_VMEM],
        out_specs=IN_VMEM,
        out_shape=jax.ShapeDtypeStruct((kept, tokens), jnp.bfloat16),
        cost_estimate=pl.CostEstimate(
            flops=2 * kept * width * tokens,
            bytes_accessed=8 * tokens * width + 2 * kept * tokens,
            transcendentals=0,
        ),
        compiler_params=params(),
        name="owned_gradients",
    )(place, mine, other)


def chip_sums(layout, grads, mine, other, positions, lengths, owned, cut):
    nz, ny = layout.nz, layout.ny
    tokens, width = mine.shape
    seqs = lengths.shape[0]
    stay = nz * owned
    rest = width - cut

    def kernel(lengths_ref, grads_ref, mine_ref, other_ref, positions_ref, *refs):
        rotated = mine_ref[...] + other_ref[...]
        position = positions_ref[...]
        begin = jnp.int32(0)
        for s in range(seqs):
            end = begin + lengths_ref[s]
            inside = (position >= begin) & (position < end)
            part = jnp.where(inside, rotated, 0.0).astype(jnp.bfloat16)
            sums = jnp.dot(grads_ref[...], part, preferred_element_type=jnp.float32)
            at = pl.ds(s * cut, cut)
            for d in range(nz):
                for h in range(ny):
                    block = sums[h * stay + d * owned:h * stay + (d + 1) * owned, :cut]
                    refs[d][pl.ds(h * owned, owned), at] = block.astype(refs[d].dtype)
            if rest:
                at = pl.ds(s * rest, rest)
                refs[nz][:, at] = sums[stay:, cut:]
                refs[nz + 1][:, at] = sums[:stay, cut:].astype(jnp.bfloat16)
            begin = end

    shapes = [jax.ShapeDtypeStruct((ny * owned, seqs * cut), jnp.float32)]
    shapes += [jax.ShapeDtypeStruct((ny * owned, seqs * cut), jnp.bfloat16)] * (nz - 1)
    if rest:
        shapes.append(jax.ShapeDtypeStruct((stay, seqs * rest), jnp.float32))
        shapes.append(jax.ShapeDtypeStruct((stay, seqs * rest), jnp.bfloat16))
    return pl.pallas_call(
        kernel,
        in_specs=[IN_SMEM] + [IN_VMEM] * 4,
        out_specs=[IN_VMEM] * len(shapes),
        out_shape=shapes,
        cost_estimate=pl.CostEstimate(
            flops=2 * grads.size * seqs * width,
            bytes_accessed=8 * tokens * width + 2 * grads.shape[0] * seqs * width,
            transcendentals=0,
        ),
        compiler_params=params(),
        name="chip_sums",
    )(lengths, grads, mine, other, positions)


def add_up(kept, came, owned, own):
    count = kept.shape[0] // owned
    width = kept.shape[1]

    def kernel(*refs):
        total = refs[0][...]
        for i in range(len(came)):
            total += refs[1 + i][...].astype(jnp.float32)
        outs = refs[1 + len(came):]
        for i in range(count):
            outs[i][...] = total[i * owned:(i + 1) * owned].astype(outs[i].dtype)

    shapes = [
        jax.ShapeDtypeStruct((owned, width), jnp.float32 if i == own else jnp.bfloat16)
        for i in range(count)
    ]
    return pl.pallas_call(
        kernel,
        in_specs=[IN_VMEM] * (1 + len(came)),
        out_specs=[IN_VMEM] * count,
        out_shape=shapes,
        cost_estimate=pl.CostEstimate(
            flops=kept.size * len(came), bytes_accessed=8 * kept.size, transcendentals=0
        ),
        compiler_params=params(),
        name="add_up",
    )(kept, *came)


def squares(groups, lengths, owned):
    seqs = lengths.shape[0]
    widths = [group[0].shape[1] // seqs for group in groups]

    def kernel(lengths_ref, *refs):
        o_ref = refs[-1]
        tokens = lengths_ref[0]
        for s in range(1, seqs):
            tokens = tokens + lengths_ref[s]
        at, k = 0, 0
        for group, width in zip(groups, widths):
            over = jnp.full((owned, width), tokens, jnp.int32).astype(jnp.float32)
            sums = refs[k][...]
            for ref in refs[k + 1:k + len(group)]:
                sums = sums + ref[...].astype(jnp.float32)
            k += len(group)
            sums = sums * sums
            acc = sums[:, :width]
            for s in range(1, seqs):
                acc = acc + sums[:, s * width:(s + 1) * width]
            o_ref[:, pl.ds(at, width)] = acc / over
            at += width

    flat = [x for group in groups for x in group]
    return pl.pallas_call(
        kernel,
        in_specs=[IN_SMEM] + [IN_VMEM] * len(flat),
        out_specs=IN_VMEM,
        out_shape=jax.ShapeDtypeStruct((owned, sum(widths)), jnp.float32),
        cost_estimate=pl.CostEstimate(
            flops=2 * sum(x.size for x in flat),
            bytes_accessed=2 * sum(x.size for x in flat),
            transcendentals=0,
        ),
        compiler_params=params(),
        name="squares",
    )(lengths, *flat)


def scatter_sums(layout, sums, owned):
    nz, ny = layout.nz, layout.ny
    if ny == 1:
        return [[sums[0]] + [layout.along_z(sums[d], d) for d in range(1, nz)]]
    crossed = [layout.along_y(sums[nz + 1])]
    came = [layout.along_z(sums[d], d) for d in range(1, nz)]
    by_z = add_up(sums[nz], crossed, owned, 0)
    second = [by_z[0]] + [layout.along_z(by_z[d], d) for d in range(1, nz)]
    by_y = add_up(sums[0], came, owned, 1)
    return [[by_y[1], layout.along_y(by_y[0])], second]


def shards(layout, activations, gradients, basis_a, basis_g, token_index, seq_lengths):
    nz, ny, chips = layout.nz, layout.ny, layout.chips
    rows = activations.shape[0]
    owned = basis_g.shape[1] // (chips * CORES)
    me = lax.axis_index("row")
    core = lax.rem(me, CORES)
    y = lax.rem(me // CORES, ny)
    z = me // (CORES * ny)
    place = jnp.stack([z, y, core]).astype(jnp.int32)

    sib_index = layout.to_sibling(token_index)
    first = core == 0
    positions = jnp.concatenate(
        [jnp.where(first, token_index, sib_index), jnp.where(first, sib_index, token_index)]
    ).reshape(CORES * rows, 1)

    links = Links(layout, 2)
    sib_g = layout.to_sibling(gradients)
    sib_a = layout.to_sibling(activations)
    split = [basis_g.shape[0] * 3 // 7, basis_a.shape[0] * 3 // 4] if ny > 1 else [0, 0]
    early = []

    def rotate_early(found):
        early.append(partial_rotation(layout, gradients, sib_g, found[:4], place))
        return early[0]

    begun = {}

    def begin_a():
        for h in range(1, ny):
            links.after(sib_a)
            begun[h] = links.send("y", basis_a, h)
        return list(begun.values())

    gates = {
        ("y", 1): begin_a,
        nz - 1: [sib_a],
        nz // 2: lambda by_z: [sib_g, sib_a, *begun.values()],
        -1: rotate_early,
    }
    found_g = gather_columns(links, basis_g, split[0], gates)
    if not early:
        rotate_early(found_g)
    mine_g = partial_rotation(layout, gradients, sib_g, found_g[4:], place, early[0])
    links.after(early[0])
    found_a = gather_columns(links, basis_a, split[1], {("y", nz - 1): [mine_g]}, begun)
    grads = owned_gradients(layout, mine_g, layout.to_sibling(mine_g), place, owned)

    most, rows_left = partial_rotation(
        layout, activations, sib_a, found_a[:-2], place, None, found_a[-2:]
    )
    most, positions = lax.optimization_barrier((most, positions))
    mine_a = last_rotation(most, rows_left, found_a[-2:])
    cut = basis_a.shape[1] // ny**2
    sums = chip_sums(
        layout, grads, mine_a, layout.to_sibling(mine_a), positions, seq_lengths, owned, cut
    )
    return squares(scatter_sums(layout, sums, owned), seq_lengths, owned)


def solution(mesh):
    return jax.shard_map(
        functools.partial(shards, Layout(mesh)),
        mesh=mesh,
        in_specs=(
            P(("grp", "row"), None),
            P(("grp", "row"), None),
            P(("grp", "row"), None),
            P(("grp", "row"), None),
            P(("grp", "row")),
            P("grp"),
        ),
        out_specs=P(("grp", "row"), None),
        check_vma=False,
    )
```

```python
import functools

import jax
import jax.numpy as jnp
from jax import lax
from jax.experimental import pallas as pl
from jax.experimental.pallas import tpu as pltpu
from jax.sharding import PartitionSpec as P

CORES = 2
MIB = 1024 * 1024


def params(mib=8):
    return pltpu.CompilerParams(vmem_limit_bytes=mib * MIB)


IN_VMEM = pl.BlockSpec(memory_space=pltpu.VMEM)
IN_SMEM = pl.BlockSpec(memory_space=pltpu.SMEM)
ANYWHERE = pl.BlockSpec(memory_space=pl.ANY)


def in_hbm(x):
    return pltpu.with_memory_space_constraint(x, pltpu.HBM)


class Layout:
    def __init__(self, mesh):
        self.chips = mesh.shape["row"] // CORES
        self.ny = max(1, 4 // mesh.shape["grp"])
        if self.chips % self.ny:
            self.ny = 1
        self.nz = self.chips // self.ny

    def device(self, z, y, core):
        return ((z % self.nz) * self.ny + y % self.ny) * CORES + core

    def everyone(self):
        return [(z, y, c) for z in range(self.nz) for y in range(self.ny) for c in range(CORES)]

    def origin(self, z, y, d, h):
        return lax.rem(z + (self.nz - d), self.nz) * self.ny + lax.rem(y + (self.ny - h), self.ny)

    def along_z(self, x, hops):
        pairs = [(self.device(z, y, c), self.device(z + hops, y, c)) for z, y, c in self.everyone()]
        return lax.ppermute(x, "row", pairs)

    def along_y(self, x, hops=1):
        pairs = [(self.device(z, y, c), self.device(z, y + hops, c)) for z, y, c in self.everyone()]
        return lax.ppermute(x, "row", pairs)

    def to_sibling(self, x):
        pairs = [(self.device(z, y, c), self.device(z, y, 1 - c)) for z, y, c in self.everyone()]
        return lax.ppermute(x, "row", pairs)


def split_columns(act, core, chips):
    rows, depth = act.shape
    kc = depth // (chips * CORES)
    mine = lax.dynamic_index_in_dim(act.reshape(rows, chips, CORES, kc), core, 2, keepdims=False)
    return mine.transpose(1, 0, 2)


class Links:
    def __init__(self, layout, window):
        self.layout, self.window = layout, window
        self.done = {"z": [], "y": []}
        self.first = []

    def after(self, *first):
        self.first += first

    def send(self, kind, x, hops):
        done = self.done[kind]
        first = self.first + done[-self.window:len(done) - self.window + 1]
        self.first = []
        if first:
            x = lax.optimization_barrier((x, *first))[0]
        move = self.layout.along_z if kind == "z" else self.layout.along_y
        done.append(move(x, hops))
        return done[-1]


def gather_columns(links, piece, split, gates, begun={}):
    nz, ny = links.layout.nz, links.layout.ny
    middle = nz // 2
    steps = [(d, 1) for d in range(1, middle + 1)] + [(d, -1) for d in range(nz - 1, middle, -1)]
    steps = sorted(steps, key=lambda s: (min(s[0], nz - s[0]), -s[1]))
    by_z, crossed, found = {0: piece}, {}, [([piece], 0, 0)]

    def cross(d):
        for h in range(1, ny):
            if d == middle and split:
                head = links.send("z", crossed[d - 1, h][:split], 1)
                if -1 in gates:
                    links.after(gates[-1](found))
                if split == piece.shape[0]:
                    got = [head]
                else:
                    got = [head, links.send("y", by_z[d][split:], h)]
            else:
                gate = gates.get(("y", d), ())
                links.after(*(gate() if callable(gate) else gate))
                got = [begun[h]] if d == 0 and h in begun else [links.send("y", by_z[d], h)]
            crossed[d, h] = got[0]
            found.append((got, d, h))

    last = 0
    for d, sign in steps:
        gate = gates.get(d, ())
        links.after(*(gate(by_z) if callable(gate) else gate))
        by_z[d] = links.send("z", by_z[(d - sign) % nz], sign)
        found.append(([by_z[d]], d, 0))
        cross(last)
        last = d
    cross(last)
    links.first = []
    return found


def partial_rotation(layout, act, sib, found, place, total=None, left=()):
    rows = act.shape[0]
    count = len(found)
    blocks = [x for parts, _, _ in found for x in parts]
    kc = sum(x.shape[0] for x in found[0][0])
    width = blocks[0].shape[1]
    unaligned = kc % 128 != 0
    if unaligned:
        act = split_columns(act, place[2], layout.chips)
        sib = split_columns(sib, place[2], layout.chips)

    extra = [] if total is None else [total]

    def kernel(place_ref, act_ref, sib_ref, *refs):
        block_refs, refs = refs[:len(blocks)], refs[len(blocks):]
        o_ref = refs[len(extra)]
        rows_buf, block_buf, sems = refs[-3:]
        z, y, core = place_ref[0], place_ref[1], place_ref[2]
        mine = pl.ds(pl.multiple_of(core * rows, 16), rows)
        other = pl.ds(pl.multiple_of((1 - core) * rows, 16), rows)

        def bring_rows(d, h, to, i):
            q = layout.origin(z, y, d, h)
            at = 0 if unaligned else pl.ds(pl.multiple_of((CORES * q + core) * kc, 128), kc)
            own, its = [ref.at[q] if unaligned else ref.at[:, at] for ref in (act_ref, sib_ref)]
            return [
                pltpu.make_async_copy(own, to.at[mine], sems.at[i, 0]),
                pltpu.make_async_copy(its, to.at[other], sems.at[i, 1]),
            ]

        copies, k = [], 0
        for i in range(count):
            parts, d, h = found[i]
            step, at = bring_rows(d, h, rows_buf.at[i], i), 0
            for j, x in enumerate(parts):
                to = block_buf.at[i, pl.ds(at, x.shape[0])]
                step.append(pltpu.make_async_copy(block_refs[k], to, sems.at[i, 2 + j]))
                at += x.shape[0]
                k += 1
            copies.append(step)
        for j, (_, d, h) in enumerate(left):
            copies.append(bring_rows(d, h, refs[len(extra) + 1].at[j], count + j))
        for step in copies:
            for copy in step:
                copy.start()
        for i, step in enumerate(copies):
            for copy in step:
                copy.wait()
            if i >= count:
                continue
            product = jnp.dot(rows_buf[i], block_buf[i], preferred_element_type=jnp.float32)
            if i > 0:
                o_ref[...] += product
            elif extra:
                o_ref[...] = refs[0][...] + product
            else:
                o_ref[...] = product

    shapes = [jax.ShapeDtypeStruct((CORES * rows, width), jnp.float32)]
    if left:
        shapes.append(jax.ShapeDtypeStruct((len(left), CORES * rows, kc), act.dtype))
    outs = pl.pallas_call(
        kernel,
        in_specs=[IN_SMEM] + [ANYWHERE] * (2 + len(blocks)) + [IN_VMEM] * len(extra),
        out_specs=[IN_VMEM] * len(shapes),
        out_shape=shapes,
        scratch_shapes=[
            pltpu.VMEM((count, CORES * rows, kc), act.dtype),
            pltpu.VMEM((count, kc, width), act.dtype),
            pltpu.SemaphoreType.DMA((count + len(left), 4)),
        ],
        cost_estimate=pl.CostEstimate(
            flops=4 * rows * kc * count * width,
            bytes_accessed=2 * count * kc * (2 * rows + width) + 8 * rows * width,
            transcendentals=0,
        ),
        compiler_params=params(24),
        name="partial_rotation",
    )(place, *[in_hbm(x) for x in (act, sib, *blocks)], *extra)
    return outs if left else outs[0]


def last_rotation(total, rows, found):
    width = total.shape[1]
    blocks = [x for parts, _, _ in found for x in parts]

    def kernel(total_ref, rows_ref, *refs):
        sums, k = total_ref[...], 0
        for i, (parts, _, _) in enumerate(found):
            at = 0
            for part in parts:
                x = rows_ref[i, :, pl.ds(at, part.shape[0])]
                sums += jnp.dot(x, refs[k][...], preferred_element_type=jnp.float32)
                at += part.shape[0]
                k += 1
        refs[-1][...] = sums

    return pl.pallas_call(
        kernel,
        in_specs=[IN_VMEM] * (2 + len(blocks)),
        out_specs=IN_VMEM,
        out_shape=jax.ShapeDtypeStruct(total.shape, jnp.float32),
        cost_estimate=pl.CostEstimate(
            flops=2 * rows.size * width,
            bytes_accessed=2 * rows.size + 8 * total.size,
            transcendentals=0,
        ),
        compiler_params=params(),
        name="last_rotation",
    )(total, rows, *blocks)


def owned_gradients(layout, mine, other, place, owned):
    nz, ny = layout.nz, layout.ny
    tokens, width = mine.shape
    kept = nz * ny * owned

    def kernel(place_ref, mine_ref, other_ref, o_ref):
        slot = lax.broadcasted_iota(jnp.int32, (kept, width), 0)
        column = lax.broadcasted_iota(jnp.int32, (kept, width), 1)
        z, y, core = place_ref[0], place_ref[1], place_ref[2]
        to_y = lax.rem(y + 1 + slot // (nz * owned), ny)
        to_z = lax.rem(z + lax.rem(slot // owned, nz), nz)
        wanted = ((to_z * ny + to_y) * CORES + core) * owned + lax.rem(slot, owned)
        pick = jnp.where(wanted == column, 1.0, 0.0).astype(jnp.bfloat16)
        rotated = (mine_ref[...] + other_ref[...]).astype(jnp.bfloat16)
        picked = lax.dot_general(
            pick, rotated, (((1,), (1,)), ((), ())), preferred_element_type=jnp.float32
        )
        o_ref[...] = picked.astype(jnp.bfloat16)

    return pl.pallas_call(
        kernel,
        in_specs=[IN_SMEM, IN_VMEM, IN_VMEM],
        out_specs=IN_VMEM,
        out_shape=jax.ShapeDtypeStruct((kept, tokens), jnp.bfloat16),
        cost_estimate=pl.CostEstimate(
            flops=2 * kept * width * tokens,
            bytes_accessed=8 * tokens * width + 2 * kept * tokens,
            transcendentals=0,
        ),
        compiler_params=params(),
        name="owned_gradients",
    )(place, mine, other)


def chip_sums(layout, grads, mine, other, positions, lengths, owned, cut):
    nz, ny = layout.nz, layout.ny
    tokens, width = mine.shape
    seqs = lengths.shape[0]
    stay = nz * owned
    rest = width - cut

    def kernel(lengths_ref, grads_ref, mine_ref, other_ref, positions_ref, *refs):
        rotated = mine_ref[...] + other_ref[...]
        position = positions_ref[...]
        begin = jnp.int32(0)
        for s in range(seqs):
            end = begin + lengths_ref[s]
            inside = (position >= begin) & (position < end)
            part = jnp.where(inside, rotated, 0.0).astype(jnp.bfloat16)
            sums = jnp.dot(grads_ref[...], part, preferred_element_type=jnp.float32)
            at = pl.ds(s * cut, cut)
            for d in range(nz):
                for h in range(ny):
                    block = sums[h * stay + d * owned:h * stay + (d + 1) * owned, :cut]
                    refs[d][pl.ds(h * owned, owned), at] = block.astype(refs[d].dtype)
            if rest:
                at = pl.ds(s * rest, rest)
                refs[nz][:, at] = sums[stay:, cut:]
                refs[nz + 1][:, at] = sums[:stay, cut:].astype(jnp.bfloat16)
            begin = end

    shapes = [jax.ShapeDtypeStruct((ny * owned, seqs * cut), jnp.float32)]
    shapes += [jax.ShapeDtypeStruct((ny * owned, seqs * cut), jnp.bfloat16)] * (nz - 1)
    if rest:
        shapes.append(jax.ShapeDtypeStruct((stay, seqs * rest), jnp.float32))
        shapes.append(jax.ShapeDtypeStruct((stay, seqs * rest), jnp.bfloat16))
    return pl.pallas_call(
        kernel,
        in_specs=[IN_SMEM] + [IN_VMEM] * 4,
        out_specs=[IN_VMEM] * len(shapes),
        out_shape=shapes,
        cost_estimate=pl.CostEstimate(
            flops=2 * grads.size * seqs * width,
            bytes_accessed=8 * tokens * width + 2 * grads.shape[0] * seqs * width,
            transcendentals=0,
        ),
        compiler_params=params(),
        name="chip_sums",
    )(lengths, grads, mine, other, positions)


def add_up(kept, came, owned, own):
    count = kept.shape[0] // owned
    width = kept.shape[1]

    def kernel(*refs):
        total = refs[0][...]
        for i in range(len(came)):
            total += refs[1 + i][...].astype(jnp.float32)
        outs = refs[1 + len(came):]
        for i in range(count):
            outs[i][...] = total[i * owned:(i + 1) * owned].astype(outs[i].dtype)

    shapes = [
        jax.ShapeDtypeStruct((owned, width), jnp.float32 if i == own else jnp.bfloat16)
        for i in range(count)
    ]
    return pl.pallas_call(
        kernel,
        in_specs=[IN_VMEM] * (1 + len(came)),
        out_specs=[IN_VMEM] * count,
        out_shape=shapes,
        cost_estimate=pl.CostEstimate(
            flops=kept.size * len(came), bytes_accessed=8 * kept.size, transcendentals=0
        ),
        compiler_params=params(),
        name="add_up",
    )(kept, *came)


def squares(groups, lengths, owned):
    seqs = lengths.shape[0]
    widths = [group[0].shape[1] // seqs for group in groups]

    def kernel(lengths_ref, *refs):
        o_ref = refs[-1]
        tokens = lengths_ref[0]
        for s in range(1, seqs):
            tokens = tokens + lengths_ref[s]
        at, k = 0, 0
        for group, width in zip(groups, widths):
            over = jnp.full((owned, width), tokens, jnp.int32).astype(jnp.float32)
            sums = refs[k][...]
            for ref in refs[k + 1:k + len(group)]:
                sums = sums + ref[...].astype(jnp.float32)
            k += len(group)
            sums = sums * sums
            acc = sums[:, :width]
            for s in range(1, seqs):
                acc = acc + sums[:, s * width:(s + 1) * width]
            o_ref[:, pl.ds(at, width)] = acc / over
            at += width

    flat = [x for group in groups for x in group]
    return pl.pallas_call(
        kernel,
        in_specs=[IN_SMEM] + [IN_VMEM] * len(flat),
        out_specs=IN_VMEM,
        out_shape=jax.ShapeDtypeStruct((owned, sum(widths)), jnp.float32),
        cost_estimate=pl.CostEstimate(
            flops=2 * sum(x.size for x in flat),
            bytes_accessed=2 * sum(x.size for x in flat),
            transcendentals=0,
        ),
        compiler_params=params(),
        name="squares",
    )(lengths, *flat)


def scatter_sums(layout, sums, owned):
    nz, ny = layout.nz, layout.ny
    if ny == 1:
        return [[sums[0]] + [layout.along_z(sums[d], d) for d in range(1, nz)]]
    crossed = [layout.along_y(sums[nz + 1])]
    came = [layout.along_z(sums[d], d) for d in range(1, nz)]
    by_z = add_up(sums[nz], crossed, owned, 0)
    second = [by_z[0]] + [layout.along_z(by_z[d], d) for d in range(1, nz)]
    by_y = add_up(sums[0], came, owned, 1)
    return [[by_y[1], layout.along_y(by_y[0])], second]


def shards(layout, activations, gradients, basis_a, basis_g, token_index, seq_lengths):
    nz, ny, chips = layout.nz, layout.ny, layout.chips
    rows = activations.shape[0]
    owned = basis_g.shape[1] // (chips * CORES)
    me = lax.axis_index("row")
    core = lax.rem(me, CORES)
    y = lax.rem(me // CORES, ny)
    z = me // (CORES * ny)
    place = jnp.stack([z, y, core]).astype(jnp.int32)

    sib_index = layout.to_sibling(token_index)
    first = core == 0
    positions = jnp.concatenate(
        [jnp.where(first, token_index, sib_index), jnp.where(first, sib_index, token_index)]
    ).reshape(CORES * rows, 1)

    links = Links(layout, 2)
    sib_g = layout.to_sibling(gradients)
    sib_a = layout.to_sibling(activations)
    split = [basis_g.shape[0] * 4 // 7, basis_a.shape[0] * 3 // 4] if ny > 1 else [0, 0]
    early = []

    def rotate_early(found):
        early.append(partial_rotation(layout, gradients, sib_g, found[:4], place))
        return early[0]

    begun = {}

    def begin_a():
        for h in range(1, ny):
            begun[h] = links.send("y", basis_a, h)
        return list(begun.values())

    gates = {
        ("y", 1): begin_a,
        nz - 1: [sib_a],
        nz // 2: lambda by_z: [sib_g, sib_a, *begun.values()],
        -1: rotate_early,
    }
    found_g = gather_columns(links, basis_g, split[0], gates)
    if not early:
        rotate_early(found_g)
    mine_g = partial_rotation(layout, gradients, sib_g, found_g[4:], place, early[0])
    links.after(early[0])
    found_a = gather_columns(links, basis_a, split[1], {("y", nz - 1): [mine_g]}, begun)
    grads = owned_gradients(layout, mine_g, layout.to_sibling(mine_g), place, owned)

    most, rows_left = partial_rotation(
        layout, activations, sib_a, found_a[:-2], place, None, found_a[-2:]
    )
    most, positions = lax.optimization_barrier((most, positions))
    mine_a = last_rotation(most, rows_left, found_a[-2:])
    cut = basis_a.shape[1] // ny**2
    sums = chip_sums(
        layout, grads, mine_a, layout.to_sibling(mine_a), positions, seq_lengths, owned, cut
    )
    return squares(scatter_sums(layout, sums, owned), seq_lengths, owned)


def solution(mesh):
    return jax.shard_map(
        functools.partial(shards, Layout(mesh)),
        mesh=mesh,
        in_specs=(
            P(("grp", "row"), None),
            P(("grp", "row"), None),
            P(("grp", "row"), None),
            P(("grp", "row"), None),
            P(("grp", "row")),
            P("grp"),
        ),
        out_specs=P(("grp", "row"), None),
        check_vma=False,
    )
```

```python
import functools

import jax
import jax.numpy as jnp
from jax import lax
from jax.experimental import pallas as pl
from jax.experimental.pallas import tpu as pltpu
from jax.sharding import PartitionSpec as P

CORES = 2
MIB = 1024 * 1024


def params(mib=8):
    return pltpu.CompilerParams(vmem_limit_bytes=mib * MIB)


IN_VMEM = pl.BlockSpec(memory_space=pltpu.VMEM)
IN_SMEM = pl.BlockSpec(memory_space=pltpu.SMEM)
ANYWHERE = pl.BlockSpec(memory_space=pl.ANY)


def in_hbm(x):
    return pltpu.with_memory_space_constraint(x, pltpu.HBM)


class Layout:
    def __init__(self, mesh):
        self.chips = mesh.shape["row"] // CORES
        self.ny = max(1, 4 // mesh.shape["grp"])
        if self.chips % self.ny:
            self.ny = 1
        self.nz = self.chips // self.ny

    def device(self, z, y, core):
        return ((z % self.nz) * self.ny + y % self.ny) * CORES + core

    def everyone(self):
        return [(z, y, c) for z in range(self.nz) for y in range(self.ny) for c in range(CORES)]

    def origin(self, z, y, d, h):
        return lax.rem(z + (self.nz - d), self.nz) * self.ny + lax.rem(y + (self.ny - h), self.ny)

    def along_z(self, x, hops):
        pairs = [(self.device(z, y, c), self.device(z + hops, y, c)) for z, y, c in self.everyone()]
        return lax.ppermute(x, "row", pairs)

    def along_y(self, x, hops=1):
        pairs = [(self.device(z, y, c), self.device(z, y + hops, c)) for z, y, c in self.everyone()]
        return lax.ppermute(x, "row", pairs)

    def to_sibling(self, x):
        pairs = [(self.device(z, y, c), self.device(z, y, 1 - c)) for z, y, c in self.everyone()]
        return lax.ppermute(x, "row", pairs)


def split_columns(act, core, chips):
    rows, depth = act.shape
    kc = depth // (chips * CORES)
    mine = lax.dynamic_index_in_dim(act.reshape(rows, chips, CORES, kc), core, 2, keepdims=False)
    return mine.transpose(1, 0, 2)


class Links:
    def __init__(self, layout, window):
        self.layout, self.window = layout, window
        self.done = {"z": [], "y": []}
        self.first = []

    def after(self, *first):
        self.first += first

    def send(self, kind, x, hops):
        done = self.done[kind]
        first = self.first + done[-self.window:len(done) - self.window + 1]
        self.first = []
        if first:
            x = lax.optimization_barrier((x, *first))[0]
        move = self.layout.along_z if kind == "z" else self.layout.along_y
        done.append(move(x, hops))
        return done[-1]


def gather_columns(links, piece, split, gates, begun={}):
    nz, ny = links.layout.nz, links.layout.ny
    middle = nz // 2
    steps = [(d, 1) for d in range(1, middle + 1)] + [(d, -1) for d in range(nz - 1, middle, -1)]
    steps = sorted(steps, key=lambda s: (min(s[0], nz - s[0]), -s[1]))
    by_z, crossed, found = {0: piece}, {}, [([piece], 0, 0)]

    def cross(d):
        for h in range(1, ny):
            if d == middle and split:
                head = links.send("z", crossed[d - 1, h][:split], 1)
                if -1 in gates:
                    links.after(gates[-1](found))
                if split == piece.shape[0]:
                    got = [head]
                else:
                    got = [head, links.send("y", by_z[d][split:], h)]
            else:
                gate = gates.get(("y", d), ())
                links.after(*(gate() if callable(gate) else gate))
                got = [begun[h]] if d == 0 and h in begun else [links.send("y", by_z[d], h)]
            crossed[d, h] = got[0]
            found.append((got, d, h))

    last = 0
    for d, sign in steps:
        gate = gates.get(d, ())
        links.after(*(gate(by_z) if callable(gate) else gate))
        by_z[d] = links.send("z", by_z[(d - sign) % nz], sign)
        found.append(([by_z[d]], d, 0))
        cross(last)
        last = d
    cross(last)
    links.first = []
    return found


def partial_rotation(layout, act, sib, found, place, total=None, left=()):
    rows = act.shape[0]
    count = len(found)
    blocks = [x for parts, _, _ in found for x in parts]
    kc = sum(x.shape[0] for x in found[0][0])
    width = blocks[0].shape[1]
    unaligned = kc % 128 != 0
    if unaligned:
        act = split_columns(act, place[2], layout.chips)
        sib = split_columns(sib, place[2], layout.chips)

    extra = [] if total is None else [total]

    def kernel(place_ref, act_ref, sib_ref, *refs):
        block_refs, refs = refs[:len(blocks)], refs[len(blocks):]
        o_ref = refs[len(extra)]
        rows_buf, block_buf, sems = refs[-3:]
        z, y, core = place_ref[0], place_ref[1], place_ref[2]
        mine = pl.ds(pl.multiple_of(core * rows, 16), rows)
        other = pl.ds(pl.multiple_of((1 - core) * rows, 16), rows)

        def bring_rows(d, h, to, i):
            q = layout.origin(z, y, d, h)
            at = 0 if unaligned else pl.ds(pl.multiple_of((CORES * q + core) * kc, 128), kc)
            own, its = [ref.at[q] if unaligned else ref.at[:, at] for ref in (act_ref, sib_ref)]
            return [
                pltpu.make_async_copy(own, to.at[mine], sems.at[i, 0]),
                pltpu.make_async_copy(its, to.at[other], sems.at[i, 1]),
            ]

        copies, k = [], 0
        for i in range(count):
            parts, d, h = found[i]
            step, at = bring_rows(d, h, rows_buf.at[i], i), 0
            for j, x in enumerate(parts):
                to = block_buf.at[i, pl.ds(at, x.shape[0])]
                step.append(pltpu.make_async_copy(block_refs[k], to, sems.at[i, 2 + j]))
                at += x.shape[0]
                k += 1
            copies.append(step)
        for j, (_, d, h) in enumerate(left):
            copies.append(bring_rows(d, h, refs[len(extra) + 1].at[j], count + j))
        for step in copies:
            for copy in step:
                copy.start()
        for i, step in enumerate(copies):
            for copy in step:
                copy.wait()
            if i >= count:
                continue
            product = jnp.dot(rows_buf[i], block_buf[i], preferred_element_type=jnp.float32)
            if i > 0:
                o_ref[...] += product
            elif extra:
                o_ref[...] = refs[0][...] + product
            else:
                o_ref[...] = product

    shapes = [jax.ShapeDtypeStruct((CORES * rows, width), jnp.float32)]
    if left:
        shapes.append(jax.ShapeDtypeStruct((len(left), CORES * rows, kc), act.dtype))
    outs = pl.pallas_call(
        kernel,
        in_specs=[IN_SMEM] + [ANYWHERE] * (2 + len(blocks)) + [IN_VMEM] * len(extra),
        out_specs=[IN_VMEM] * len(shapes),
        out_shape=shapes,
        scratch_shapes=[
            pltpu.VMEM((count, CORES * rows, kc), act.dtype),
            pltpu.VMEM((count, kc, width), act.dtype),
            pltpu.SemaphoreType.DMA((count + len(left), 4)),
        ],
        cost_estimate=pl.CostEstimate(
            flops=4 * rows * kc * count * width,
            bytes_accessed=2 * count * kc * (2 * rows + width) + 8 * rows * width,
            transcendentals=0,
        ),
        compiler_params=params(24),
        name="partial_rotation",
    )(place, *[in_hbm(x) for x in (act, sib, *blocks)], *extra)
    return outs if left else outs[0]


def last_rotation(total, rows, found):
    width = total.shape[1]
    blocks = [x for parts, _, _ in found for x in parts]

    def kernel(total_ref, rows_ref, *refs):
        sums, k = total_ref[...], 0
        for i, (parts, _, _) in enumerate(found):
            at = 0
            for part in parts:
                x = rows_ref[i, :, pl.ds(at, part.shape[0])]
                sums += jnp.dot(x, refs[k][...], preferred_element_type=jnp.float32)
                at += part.shape[0]
                k += 1
        refs[-1][...] = sums

    return pl.pallas_call(
        kernel,
        in_specs=[IN_VMEM] * (2 + len(blocks)),
        out_specs=IN_VMEM,
        out_shape=jax.ShapeDtypeStruct(total.shape, jnp.float32),
        cost_estimate=pl.CostEstimate(
            flops=2 * rows.size * width,
            bytes_accessed=2 * rows.size + 8 * total.size,
            transcendentals=0,
        ),
        compiler_params=params(),
        name="last_rotation",
    )(total, rows, *blocks)


def owned_gradients(layout, mine, other, place, positions, lengths, owned):
    nz, ny = layout.nz, layout.ny
    tokens, width = mine.shape
    kept = nz * ny * owned
    seqs = lengths.shape[0]

    def kernel(place_ref, lengths_ref, mine_ref, other_ref, positions_ref, o_ref):
        slot = lax.broadcasted_iota(jnp.int32, (kept, width), 0)
        column = lax.broadcasted_iota(jnp.int32, (kept, width), 1)
        z, y, core = place_ref[0], place_ref[1], place_ref[2]
        to_y = lax.rem(y + 1 + slot // (nz * owned), ny)
        to_z = lax.rem(z + lax.rem(slot // owned, nz), nz)
        wanted = ((to_z * ny + to_y) * CORES + core) * owned + lax.rem(slot, owned)
        pick = jnp.where(wanted == column, 1.0, 0.0).astype(jnp.bfloat16)
        rotated = (mine_ref[...] + other_ref[...]).astype(jnp.bfloat16)
        picked = lax.dot_general(
            pick, rotated, (((1,), (1,)), ((), ())), preferred_element_type=jnp.float32
        )
        position = positions_ref[...]
        begin = jnp.int32(0)
        for s in range(seqs):
            end = begin + lengths_ref[s]
            inside = (position >= begin) & (position < end)
            part = jnp.where(inside, picked, 0.0).astype(jnp.bfloat16)
            o_ref[pl.ds(s * kept, kept), :] = part
            begin = end

    return pl.pallas_call(
        kernel,
        in_specs=[IN_SMEM, IN_SMEM, IN_VMEM, IN_VMEM, IN_VMEM],
        out_specs=IN_VMEM,
        out_shape=jax.ShapeDtypeStruct((seqs * kept, tokens), jnp.bfloat16),
        cost_estimate=pl.CostEstimate(
            flops=2 * kept * width * tokens,
            bytes_accessed=8 * tokens * width + 2 * kept * tokens,
            transcendentals=0,
        ),
        compiler_params=params(),
        name="owned_gradients",
    )(place, lengths, mine, other, positions)


def chip_sums(layout, grads, mine, other, seqs, owned, cut):
    nz, ny = layout.nz, layout.ny
    tokens, width = mine.shape
    stay = nz * owned
    rest = width - cut

    kept = grads.shape[0] // seqs

    def kernel(grads_ref, mine_ref, other_ref, *refs):
        rotated = (mine_ref[...] + other_ref[...]).astype(jnp.bfloat16)
        products = jnp.dot(grads_ref[...], rotated, preferred_element_type=jnp.float32)
        for s in range(seqs):
            sums = products[s * kept:(s + 1) * kept]
            at = pl.ds(s * cut, cut)
            for d in range(nz):
                for h in range(ny):
                    block = sums[h * stay + d * owned:h * stay + (d + 1) * owned, :cut]
                    refs[d][pl.ds(h * owned, owned), at] = block.astype(refs[d].dtype)
            if rest:
                at = pl.ds(s * rest, rest)
                refs[nz][:, at] = sums[stay:, cut:]
                refs[nz + 1][:, at] = sums[:stay, cut:].astype(jnp.bfloat16)

    shapes = [jax.ShapeDtypeStruct((ny * owned, seqs * cut), jnp.float32)]
    shapes += [jax.ShapeDtypeStruct((ny * owned, seqs * cut), jnp.bfloat16)] * (nz - 1)
    if rest:
        shapes.append(jax.ShapeDtypeStruct((stay, seqs * rest), jnp.float32))
        shapes.append(jax.ShapeDtypeStruct((stay, seqs * rest), jnp.bfloat16))
    return pl.pallas_call(
        kernel,
        in_specs=[IN_VMEM] * 3,
        out_specs=[IN_VMEM] * len(shapes),
        out_shape=shapes,
        cost_estimate=pl.CostEstimate(
            flops=2 * grads.size * width,
            bytes_accessed=8 * tokens * width + 2 * grads.shape[0] * width,
            transcendentals=0,
        ),
        compiler_params=params(),
        name="chip_sums",
    )(grads, mine, other)


def add_up(kept, came, owned, own):
    count = kept.shape[0] // owned
    width = kept.shape[1]

    def kernel(*refs):
        total = refs[0][...]
        for i in range(len(came)):
            total += refs[1 + i][...].astype(jnp.float32)
        outs = refs[1 + len(came):]
        for i in range(count):
            outs[i][...] = total[i * owned:(i + 1) * owned].astype(outs[i].dtype)

    shapes = [
        jax.ShapeDtypeStruct((owned, width), jnp.float32 if i == own else jnp.bfloat16)
        for i in range(count)
    ]
    return pl.pallas_call(
        kernel,
        in_specs=[IN_VMEM] * (1 + len(came)),
        out_specs=[IN_VMEM] * count,
        out_shape=shapes,
        cost_estimate=pl.CostEstimate(
            flops=kept.size * len(came), bytes_accessed=8 * kept.size, transcendentals=0
        ),
        compiler_params=params(),
        name="add_up",
    )(kept, *came)


def squares(groups, lengths, owned):
    seqs = lengths.shape[0]
    widths = [group[0].shape[1] // seqs for group in groups]

    def kernel(lengths_ref, *refs):
        o_ref = refs[-1]
        tokens = lengths_ref[0]
        for s in range(1, seqs):
            tokens = tokens + lengths_ref[s]
        at, k = 0, 0
        for group, width in zip(groups, widths):
            over = jnp.full((owned, width), tokens, jnp.int32).astype(jnp.float32)
            sums = refs[k][...]
            for ref in refs[k + 1:k + len(group)]:
                sums = sums + ref[...].astype(jnp.float32)
            k += len(group)
            sums = sums * sums
            acc = sums[:, :width]
            for s in range(1, seqs):
                acc = acc + sums[:, s * width:(s + 1) * width]
            o_ref[:, pl.ds(at, width)] = acc / over
            at += width

    flat = [x for group in groups for x in group]
    return pl.pallas_call(
        kernel,
        in_specs=[IN_SMEM] + [IN_VMEM] * len(flat),
        out_specs=IN_VMEM,
        out_shape=jax.ShapeDtypeStruct((owned, sum(widths)), jnp.float32),
        cost_estimate=pl.CostEstimate(
            flops=2 * sum(x.size for x in flat),
            bytes_accessed=2 * sum(x.size for x in flat),
            transcendentals=0,
        ),
        compiler_params=params(),
        name="squares",
    )(lengths, *flat)


def scatter_sums(layout, sums, owned):
    nz, ny = layout.nz, layout.ny
    if ny == 1:
        return [[sums[0]] + [layout.along_z(sums[d], d) for d in range(1, nz)]]
    crossed = [layout.along_y(sums[nz + 1])]
    came = [layout.along_z(sums[d], d) for d in range(1, nz)]
    by_z = add_up(sums[nz], crossed, owned, 0)
    second = [by_z[0]] + [layout.along_z(by_z[d], d) for d in range(1, nz)]
    by_y = add_up(sums[0], came, owned, 1)
    return [[by_y[1], layout.along_y(by_y[0])], second]


def shards(layout, activations, gradients, basis_a, basis_g, token_index, seq_lengths):
    nz, ny, chips = layout.nz, layout.ny, layout.chips
    rows = activations.shape[0]
    owned = basis_g.shape[1] // (chips * CORES)
    me = lax.axis_index("row")
    core = lax.rem(me, CORES)
    y = lax.rem(me // CORES, ny)
    z = me // (CORES * ny)
    place = jnp.stack([z, y, core]).astype(jnp.int32)

    sib_index = layout.to_sibling(token_index)
    first = core == 0
    positions = jnp.concatenate(
        [jnp.where(first, token_index, sib_index), jnp.where(first, sib_index, token_index)]
    ).reshape(1, CORES * rows)

    links = Links(layout, 2)
    sib_g = layout.to_sibling(gradients)
    sib_a = layout.to_sibling(activations)
    split = [basis_g.shape[0] * 4 // 7, basis_a.shape[0] * 3 // 4] if ny > 1 else [0, 0]
    early = []

    def rotate_early(found):
        early.append(partial_rotation(layout, gradients, sib_g, found[:4], place))
        return early[0]

    begun = {}

    def begin_a():
        for h in range(1, ny):
            begun[h] = links.send("y", basis_a, h)
        return list(begun.values())

    gates = {
        ("y", 1): begin_a,
        nz - 1: [sib_a],
        nz // 2: lambda by_z: [sib_g, sib_a, *begun.values()],
        -1: rotate_early,
    }
    found_g = gather_columns(links, basis_g, split[0], gates)
    if not early:
        rotate_early(found_g)
    mine_g = partial_rotation(layout, gradients, sib_g, found_g[4:], place, early[0])
    links.after(early[0])
    found_a = gather_columns(links, basis_a, split[1], {("y", nz - 1): [mine_g]}, begun)
    grads = owned_gradients(
        layout, mine_g, layout.to_sibling(mine_g), place, positions, seq_lengths, owned
    )

    most, rows_left = partial_rotation(
        layout, activations, sib_a, found_a[:-2], place, None, found_a[-2:]
    )
    most, positions = lax.optimization_barrier((most, positions))
    mine_a = last_rotation(most, rows_left, found_a[-2:])
    cut = basis_a.shape[1] // ny**2
    sums = chip_sums(
        layout, grads, mine_a, layout.to_sibling(mine_a), seq_lengths.shape[0], owned, cut
    )
    return squares(scatter_sums(layout, sums, owned), seq_lengths, owned)


def solution(mesh):
    return jax.shard_map(
        functools.partial(shards, Layout(mesh)),
        mesh=mesh,
        in_specs=(
            P(("grp", "row"), None),
            P(("grp", "row"), None),
            P(("grp", "row"), None),
            P(("grp", "row"), None),
            P(("grp", "row")),
            P("grp"),
        ),
        out_specs=P(("grp", "row"), None),
        check_vma=False,
    )
```

```python
import functools

import jax
import jax.numpy as jnp
from jax import lax
from jax.experimental import pallas as pl
from jax.experimental.pallas import tpu as pltpu
from jax.sharding import PartitionSpec as P

CORES = 2
MIB = 1024 * 1024


def params(mib=8):
    return pltpu.CompilerParams(vmem_limit_bytes=mib * MIB)


IN_VMEM = pl.BlockSpec(memory_space=pltpu.VMEM)
IN_SMEM = pl.BlockSpec(memory_space=pltpu.SMEM)
ANYWHERE = pl.BlockSpec(memory_space=pl.ANY)


def in_hbm(x):
    return pltpu.with_memory_space_constraint(x, pltpu.HBM)


class Layout:
    def __init__(self, mesh):
        self.chips = mesh.shape["row"] // CORES
        self.ny = max(1, 4 // mesh.shape["grp"])
        if self.chips % self.ny:
            self.ny = 1
        self.nz = self.chips // self.ny

    def device(self, z, y, core):
        return ((z % self.nz) * self.ny + y % self.ny) * CORES + core

    def everyone(self):
        return [(z, y, c) for z in range(self.nz) for y in range(self.ny) for c in range(CORES)]

    def origin(self, z, y, d, h):
        return lax.rem(z + (self.nz - d), self.nz) * self.ny + lax.rem(y + (self.ny - h), self.ny)

    def along_z(self, x, hops):
        pairs = [(self.device(z, y, c), self.device(z + hops, y, c)) for z, y, c in self.everyone()]
        return lax.ppermute(x, "row", pairs)

    def along_y(self, x, hops=1):
        pairs = [(self.device(z, y, c), self.device(z, y + hops, c)) for z, y, c in self.everyone()]
        return lax.ppermute(x, "row", pairs)

    def to_sibling(self, x):
        pairs = [(self.device(z, y, c), self.device(z, y, 1 - c)) for z, y, c in self.everyone()]
        return lax.ppermute(x, "row", pairs)


def split_columns(act, core, chips):
    rows, depth = act.shape
    kc = depth // (chips * CORES)
    mine = lax.dynamic_index_in_dim(act.reshape(rows, chips, CORES, kc), core, 2, keepdims=False)
    return mine.transpose(1, 0, 2)


class Links:
    def __init__(self, layout, window):
        self.layout, self.window = layout, window
        self.done = {"z": [], "y": []}
        self.first = []

    def after(self, *first):
        self.first += first

    def send(self, kind, x, hops):
        done = self.done[kind]
        first = self.first + done[-self.window:len(done) - self.window + 1]
        self.first = []
        if first:
            x = lax.optimization_barrier((x, *first))[0]
        move = self.layout.along_z if kind == "z" else self.layout.along_y
        done.append(move(x, hops))
        return done[-1]


def gather_columns(links, piece, split, gates, begun={}):
    nz, ny = links.layout.nz, links.layout.ny
    middle = nz // 2
    steps = [(d, 1) for d in range(1, middle + 1)] + [(d, -1) for d in range(nz - 1, middle, -1)]
    steps = sorted(steps, key=lambda s: (min(s[0], nz - s[0]), -s[1]))
    by_z, crossed, found = {0: piece}, {}, [([piece], 0, 0)]

    def cross(d):
        for h in range(1, ny):
            if d == middle and split:
                head = links.send("z", crossed[d - 1, h][:split], 1)
                if -1 in gates:
                    links.after(gates[-1](found))
                if split == piece.shape[0]:
                    got = [head]
                else:
                    got = [head, links.send("y", by_z[d][split:], h)]
            else:
                gate = gates.get(("y", d), ())
                links.after(*(gate() if callable(gate) else gate))
                got = [begun[h]] if d == 0 and h in begun else [links.send("y", by_z[d], h)]
            crossed[d, h] = got[0]
            found.append((got, d, h))

    last = 0
    for d, sign in steps:
        gate = gates.get(d, ())
        links.after(*(gate(by_z) if callable(gate) else gate))
        by_z[d] = links.send("z", by_z[(d - sign) % nz], sign)
        found.append(([by_z[d]], d, 0))
        cross(last)
        last = d
    cross(last)
    links.first = []
    return found


def partial_rotation(layout, act, sib, found, place, total=None, left=()):
    rows = act.shape[0]
    count = len(found)
    blocks = [x for parts, _, _ in found for x in parts]
    kc = sum(x.shape[0] for x in found[0][0])
    width = blocks[0].shape[1]
    unaligned = kc % 128 != 0
    if unaligned:
        act = split_columns(act, place[2], layout.chips)
        sib = split_columns(sib, place[2], layout.chips)

    extra = [] if total is None else [total]

    def kernel(place_ref, act_ref, sib_ref, *refs):
        block_refs, refs = refs[:len(blocks)], refs[len(blocks):]
        o_ref = refs[len(extra)]
        rows_buf, block_buf, sems = refs[-3:]
        z, y, core = place_ref[0], place_ref[1], place_ref[2]
        mine = pl.ds(pl.multiple_of(core * rows, 16), rows)
        other = pl.ds(pl.multiple_of((1 - core) * rows, 16), rows)

        def bring_rows(d, h, to, i):
            q = layout.origin(z, y, d, h)
            at = 0 if unaligned else pl.ds(pl.multiple_of((CORES * q + core) * kc, 128), kc)
            own, its = [ref.at[q] if unaligned else ref.at[:, at] for ref in (act_ref, sib_ref)]
            return [
                pltpu.make_async_copy(own, to.at[mine], sems.at[i, 0]),
                pltpu.make_async_copy(its, to.at[other], sems.at[i, 1]),
            ]

        copies, k = [], 0
        for i in range(count):
            parts, d, h = found[i]
            step, at = bring_rows(d, h, rows_buf.at[i], i), 0
            for j, x in enumerate(parts):
                to = block_buf.at[i, pl.ds(at, x.shape[0])]
                step.append(pltpu.make_async_copy(block_refs[k], to, sems.at[i, 2 + j]))
                at += x.shape[0]
                k += 1
            copies.append(step)
        for j, (_, d, h) in enumerate(left):
            copies.append(bring_rows(d, h, refs[len(extra) + 1].at[j], count + j))
        for step in copies:
            for copy in step:
                copy.start()
        for i, step in enumerate(copies):
            for copy in step:
                copy.wait()
            if i >= count:
                continue
            product = jnp.dot(rows_buf[i], block_buf[i], preferred_element_type=jnp.float32)
            if i > 0:
                o_ref[...] += product
            elif extra:
                o_ref[...] = refs[0][...] + product
            else:
                o_ref[...] = product

    shapes = [jax.ShapeDtypeStruct((CORES * rows, width), jnp.float32)]
    if left:
        shapes.append(jax.ShapeDtypeStruct((len(left), CORES * rows, kc), act.dtype))
    outs = pl.pallas_call(
        kernel,
        in_specs=[IN_SMEM] + [ANYWHERE] * (2 + len(blocks)) + [IN_VMEM] * len(extra),
        out_specs=[IN_VMEM] * len(shapes),
        out_shape=shapes,
        scratch_shapes=[
            pltpu.VMEM((count, CORES * rows, kc), act.dtype),
            pltpu.VMEM((count, kc, width), act.dtype),
            pltpu.SemaphoreType.DMA((count + len(left), 4)),
        ],
        cost_estimate=pl.CostEstimate(
            flops=4 * rows * kc * count * width,
            bytes_accessed=2 * count * kc * (2 * rows + width) + 8 * rows * width,
            transcendentals=0,
        ),
        compiler_params=params(24),
        name="partial_rotation",
    )(place, in_hbm(act), in_hbm(sib), *blocks, *extra)
    return outs if left else outs[0]


def last_rotation(total, rows, found):
    width = total.shape[1]
    blocks = [x for parts, _, _ in found for x in parts]

    def kernel(total_ref, rows_ref, *refs):
        sums, k = total_ref[...], 0
        for i, (parts, _, _) in enumerate(found):
            at = 0
            for part in parts:
                x = rows_ref[i, :, pl.ds(at, part.shape[0])]
                sums += jnp.dot(x, refs[k][...], preferred_element_type=jnp.float32)
                at += part.shape[0]
                k += 1
        refs[-1][...] = sums

    return pl.pallas_call(
        kernel,
        in_specs=[IN_VMEM] * (2 + len(blocks)),
        out_specs=IN_VMEM,
        out_shape=jax.ShapeDtypeStruct(total.shape, jnp.float32),
        cost_estimate=pl.CostEstimate(
            flops=2 * rows.size * width,
            bytes_accessed=2 * rows.size + 8 * total.size,
            transcendentals=0,
        ),
        compiler_params=params(),
        name="last_rotation",
    )(total, rows, *blocks)


def owned_gradients(layout, mine, other, place, positions, lengths, owned):
    nz, ny = layout.nz, layout.ny
    tokens, width = mine.shape
    kept = nz * ny * owned
    seqs = lengths.shape[0]

    def kernel(place_ref, lengths_ref, mine_ref, other_ref, positions_ref, o_ref):
        slot = lax.broadcasted_iota(jnp.int32, (kept, width), 0)
        column = lax.broadcasted_iota(jnp.int32, (kept, width), 1)
        z, y, core = place_ref[0], place_ref[1], place_ref[2]
        to_y = lax.rem(y + 1 + slot // (nz * owned), ny)
        to_z = lax.rem(z + lax.rem(slot // owned, nz), nz)
        wanted = ((to_z * ny + to_y) * CORES + core) * owned + lax.rem(slot, owned)
        pick = jnp.where(wanted == column, 1.0, 0.0).astype(jnp.bfloat16)
        rotated = (mine_ref[...] + other_ref[...]).astype(jnp.bfloat16)
        picked = lax.dot_general(
            pick, rotated, (((1,), (1,)), ((), ())), preferred_element_type=jnp.float32
        )
        position = positions_ref[...]
        begin = jnp.int32(0)
        for s in range(seqs):
            end = begin + lengths_ref[s]
            inside = (position >= begin) & (position < end)
            part = jnp.where(inside, picked, 0.0).astype(jnp.bfloat16)
            o_ref[pl.ds(s * kept, kept), :] = part
            begin = end

    return pl.pallas_call(
        kernel,
        in_specs=[IN_SMEM, IN_SMEM, IN_VMEM, IN_VMEM, IN_VMEM],
        out_specs=IN_VMEM,
        out_shape=jax.ShapeDtypeStruct((seqs * kept, tokens), jnp.bfloat16),
        cost_estimate=pl.CostEstimate(
            flops=2 * kept * width * tokens,
            bytes_accessed=8 * tokens * width + 2 * kept * tokens,
            transcendentals=0,
        ),
        compiler_params=params(),
        name="owned_gradients",
    )(place, lengths, mine, other, positions)


def chip_sums(layout, grads, mine, other, seqs, owned, cut):
    nz, ny = layout.nz, layout.ny
    tokens, width = mine.shape
    stay = nz * owned
    rest = width - cut

    kept = grads.shape[0] // seqs

    def kernel(grads_ref, mine_ref, other_ref, *refs):
        rotated = (mine_ref[...] + other_ref[...]).astype(jnp.bfloat16)
        products = jnp.dot(grads_ref[...], rotated, preferred_element_type=jnp.float32)
        for s in range(seqs):
            sums = products[s * kept:(s + 1) * kept]
            at = pl.ds(s * cut, cut)
            for d in range(nz):
                for h in range(ny):
                    block = sums[h * stay + d * owned:h * stay + (d + 1) * owned, :cut]
                    refs[d][pl.ds(h * owned, owned), at] = block.astype(refs[d].dtype)
            if rest:
                at = pl.ds(s * rest, rest)
                refs[nz][:, at] = sums[stay:, cut:]
                refs[nz + 1][:, at] = sums[:stay, cut:].astype(jnp.bfloat16)

    shapes = [jax.ShapeDtypeStruct((ny * owned, seqs * cut), jnp.float32)]
    shapes += [jax.ShapeDtypeStruct((ny * owned, seqs * cut), jnp.bfloat16)] * (nz - 1)
    if rest:
        shapes.append(jax.ShapeDtypeStruct((stay, seqs * rest), jnp.float32))
        shapes.append(jax.ShapeDtypeStruct((stay, seqs * rest), jnp.bfloat16))
    return pl.pallas_call(
        kernel,
        in_specs=[IN_VMEM] * 3,
        out_specs=[IN_VMEM] * len(shapes),
        out_shape=shapes,
        cost_estimate=pl.CostEstimate(
            flops=2 * grads.size * width,
            bytes_accessed=8 * tokens * width + 2 * grads.shape[0] * width,
            transcendentals=0,
        ),
        compiler_params=params(),
        name="chip_sums",
    )(grads, mine, other)


def add_up(kept, came, owned, own):
    count = kept.shape[0] // owned
    width = kept.shape[1]

    def kernel(*refs):
        total = refs[0][...]
        for i in range(len(came)):
            total += refs[1 + i][...].astype(jnp.float32)
        outs = refs[1 + len(came):]
        for i in range(count):
            outs[i][...] = total[i * owned:(i + 1) * owned].astype(outs[i].dtype)

    shapes = [
        jax.ShapeDtypeStruct((owned, width), jnp.float32 if i == own else jnp.bfloat16)
        for i in range(count)
    ]
    return pl.pallas_call(
        kernel,
        in_specs=[IN_VMEM] * (1 + len(came)),
        out_specs=[IN_VMEM] * count,
        out_shape=shapes,
        cost_estimate=pl.CostEstimate(
            flops=kept.size * len(came), bytes_accessed=8 * kept.size, transcendentals=0
        ),
        compiler_params=params(),
        name="add_up",
    )(kept, *came)


def squares(groups, lengths, owned):
    seqs = lengths.shape[0]
    widths = [group[0].shape[1] // seqs for group in groups]

    def kernel(lengths_ref, *refs):
        o_ref = refs[-1]
        tokens = lengths_ref[0]
        for s in range(1, seqs):
            tokens = tokens + lengths_ref[s]
        at, k = 0, 0
        for group, width in zip(groups, widths):
            over = jnp.full((owned, width), tokens, jnp.int32).astype(jnp.float32)
            sums = refs[k][...]
            for ref in refs[k + 1:k + len(group)]:
                sums = sums + ref[...].astype(jnp.float32)
            k += len(group)
            sums = sums * sums
            acc = sums[:, :width]
            for s in range(1, seqs):
                acc = acc + sums[:, s * width:(s + 1) * width]
            o_ref[:, pl.ds(at, width)] = acc / over
            at += width

    flat = [x for group in groups for x in group]
    return pl.pallas_call(
        kernel,
        in_specs=[IN_SMEM] + [IN_VMEM] * len(flat),
        out_specs=IN_VMEM,
        out_shape=jax.ShapeDtypeStruct((owned, sum(widths)), jnp.float32),
        cost_estimate=pl.CostEstimate(
            flops=2 * sum(x.size for x in flat),
            bytes_accessed=2 * sum(x.size for x in flat),
            transcendentals=0,
        ),
        compiler_params=params(),
        name="squares",
    )(lengths, *flat)


def scatter_sums(layout, sums, owned):
    nz, ny = layout.nz, layout.ny
    if ny == 1:
        return [[sums[0]] + [layout.along_z(sums[d], d) for d in range(1, nz)]]
    crossed = [layout.along_y(sums[nz + 1])]
    came = [layout.along_z(sums[d], d) for d in range(1, nz)]
    by_z = add_up(sums[nz], crossed, owned, 0)
    second = [by_z[0]] + [layout.along_z(by_z[d], d) for d in range(1, nz)]
    by_y = add_up(sums[0], came, owned, 1)
    return [[by_y[1], layout.along_y(by_y[0])], second]


def shards(layout, activations, gradients, basis_a, basis_g, token_index, seq_lengths):
    nz, ny, chips = layout.nz, layout.ny, layout.chips
    rows = activations.shape[0]
    owned = basis_g.shape[1] // (chips * CORES)
    me = lax.axis_index("row")
    core = lax.rem(me, CORES)
    y = lax.rem(me // CORES, ny)
    z = me // (CORES * ny)
    place = jnp.stack([z, y, core]).astype(jnp.int32)

    sib_index = layout.to_sibling(token_index)
    first = core == 0
    positions = jnp.concatenate(
        [jnp.where(first, token_index, sib_index), jnp.where(first, sib_index, token_index)]
    ).reshape(1, CORES * rows)

    links = Links(layout, 2)
    sib_g = layout.to_sibling(gradients)
    sib_a = layout.to_sibling(activations)
    split = [basis_g.shape[0] * 4 // 7, basis_a.shape[0] * 3 // 4] if ny > 1 else [0, 0]
    early = []

    def rotate_early(found):
        early.append(partial_rotation(layout, gradients, sib_g, found[:4], place))
        return early[0]

    begun = {}

    def begin_a():
        for h in range(1, ny):
            begun[h] = links.send("y", basis_a, h)
        return list(begun.values())

    gates = {
        ("y", 1): begin_a,
        nz - 1: [sib_a],
        nz // 2: lambda by_z: [sib_g, sib_a, *begun.values()],
        -1: rotate_early,
    }
    found_g = gather_columns(links, basis_g, split[0], gates)
    if not early:
        rotate_early(found_g)
    mine_g = partial_rotation(layout, gradients, sib_g, found_g[4:], place, early[0])
    links.after(early[0])
    found_a = gather_columns(links, basis_a, split[1], {("y", nz - 1): [mine_g]}, begun)
    grads = owned_gradients(
        layout, mine_g, layout.to_sibling(mine_g), place, positions, seq_lengths, owned
    )

    most, rows_left = partial_rotation(
        layout, activations, sib_a, found_a[:-2], place, None, found_a[-2:]
    )
    most, positions = lax.optimization_barrier((most, positions))
    mine_a = last_rotation(most, rows_left, found_a[-2:])
    cut = basis_a.shape[1] // ny**2
    sums = chip_sums(
        layout, grads, mine_a, layout.to_sibling(mine_a), seq_lengths.shape[0], owned, cut
    )
    return squares(scatter_sums(layout, sums, owned), seq_lengths, owned)


def solution(mesh):
    return jax.shard_map(
        functools.partial(shards, Layout(mesh)),
        mesh=mesh,
        in_specs=(
            P(("grp", "row"), None),
            P(("grp", "row"), None),
            P(("grp", "row"), None),
            P(("grp", "row"), None),
            P(("grp", "row")),
            P("grp"),
        ),
        out_specs=P(("grp", "row"), None),
        check_vma=False,
    )
```

```python
import functools

import jax
import jax.numpy as jnp
from jax import lax
from jax.experimental import pallas as pl
from jax.experimental.pallas import tpu as pltpu
from jax.sharding import PartitionSpec as P

CORES = 2
MIB = 1024 * 1024


def params(mib=8):
    return pltpu.CompilerParams(vmem_limit_bytes=mib * MIB)


IN_VMEM = pl.BlockSpec(memory_space=pltpu.VMEM)
IN_SMEM = pl.BlockSpec(memory_space=pltpu.SMEM)
ANYWHERE = pl.BlockSpec(memory_space=pl.ANY)


def in_hbm(x):
    return pltpu.with_memory_space_constraint(x, pltpu.HBM)


class Layout:
    def __init__(self, mesh):
        self.chips = mesh.shape["row"] // CORES
        self.ny = max(1, 4 // mesh.shape["grp"])
        if self.chips % self.ny:
            self.ny = 1
        self.nz = self.chips // self.ny

    def device(self, z, y, core):
        return ((z % self.nz) * self.ny + y % self.ny) * CORES + core

    def everyone(self):
        return [(z, y, c) for z in range(self.nz) for y in range(self.ny) for c in range(CORES)]

    def origin(self, z, y, d, h):
        return lax.rem(z + (self.nz - d), self.nz) * self.ny + lax.rem(y + (self.ny - h), self.ny)

    def along_z(self, x, hops):
        pairs = [(self.device(z, y, c), self.device(z + hops, y, c)) for z, y, c in self.everyone()]
        return lax.ppermute(x, "row", pairs)

    def along_y(self, x, hops=1):
        pairs = [(self.device(z, y, c), self.device(z, y + hops, c)) for z, y, c in self.everyone()]
        return lax.ppermute(x, "row", pairs)

    def to_sibling(self, x):
        pairs = [(self.device(z, y, c), self.device(z, y, 1 - c)) for z, y, c in self.everyone()]
        return lax.ppermute(x, "row", pairs)


def split_columns(act, core, chips):
    rows, depth = act.shape
    kc = depth // (chips * CORES)
    mine = lax.dynamic_index_in_dim(act.reshape(rows, chips, CORES, kc), core, 2, keepdims=False)
    return mine.transpose(1, 0, 2)


class Links:
    def __init__(self, layout, window):
        self.layout, self.window = layout, window
        self.done = {"z": [], "y": []}
        self.first = []

    def after(self, *first):
        self.first += first

    def send(self, kind, x, hops):
        done = self.done[kind]
        first = self.first + done[-self.window:len(done) - self.window + 1]
        self.first = []
        if first:
            x = lax.optimization_barrier((x, *first))[0]
        move = self.layout.along_z if kind == "z" else self.layout.along_y
        done.append(move(x, hops))
        return done[-1]


def gather_columns(links, piece, split, gates, begun={}):
    nz, ny = links.layout.nz, links.layout.ny
    middle = nz // 2
    steps = [(d, 1) for d in range(1, middle + 1)] + [(d, -1) for d in range(nz - 1, middle, -1)]
    steps = sorted(steps, key=lambda s: (min(s[0], nz - s[0]), -s[1]))
    by_z, crossed, found = {0: piece}, {}, [([piece], 0, 0)]

    def cross(d):
        for h in range(1, ny):
            if d == middle and split:
                head = links.send("z", crossed[d - 1, h][:split], 1)
                if -1 in gates:
                    links.after(gates[-1](found))
                if split == piece.shape[0]:
                    got = [head]
                else:
                    got = [head, links.send("y", by_z[d][split:], h)]
            else:
                gate = gates.get(("y", d), ())
                links.after(*(gate() if callable(gate) else gate))
                got = [begun[h]] if d == 0 and h in begun else [links.send("y", by_z[d], h)]
            crossed[d, h] = got[0]
            found.append((got, d, h))

    last = 0
    for d, sign in steps:
        gate = gates.get(d, ())
        links.after(*(gate(by_z) if callable(gate) else gate))
        by_z[d] = links.send("z", by_z[(d - sign) % nz], sign)
        found.append(([by_z[d]], d, 0))
        cross(last)
        last = d
    cross(last)
    links.first = []
    return found


def partial_rotation(layout, act, sib, found, place, total=None, left=()):
    rows = act.shape[0]
    count = len(found)
    blocks = [x for parts, _, _ in found for x in parts]
    kc = sum(x.shape[0] for x in found[0][0])
    width = blocks[0].shape[1]
    unaligned = kc % 128 != 0
    if unaligned:
        act = split_columns(act, place[2], layout.chips)
        sib = split_columns(sib, place[2], layout.chips)

    extra = [] if total is None else [total]

    def kernel(place_ref, act_ref, sib_ref, *refs):
        block_refs, refs = refs[:len(blocks)], refs[len(blocks):]
        o_ref = refs[len(extra)]
        rows_buf, block_buf, sems = refs[-3:]
        z, y, core = place_ref[0], place_ref[1], place_ref[2]
        mine = pl.ds(pl.multiple_of(core * rows, 16), rows)
        other = pl.ds(pl.multiple_of((1 - core) * rows, 16), rows)

        def bring_rows(d, h, to, i):
            q = layout.origin(z, y, d, h)
            at = 0 if unaligned else pl.ds(pl.multiple_of((CORES * q + core) * kc, 128), kc)
            own, its = [ref.at[q] if unaligned else ref.at[:, at] for ref in (act_ref, sib_ref)]
            return [
                pltpu.make_async_copy(own, to.at[mine], sems.at[i, 0]),
                pltpu.make_async_copy(its, to.at[other], sems.at[i, 1]),
            ]

        copies, k = [], 0
        for i in range(count):
            parts, d, h = found[i]
            step, at = bring_rows(d, h, rows_buf.at[i], i), 0
            for j, x in enumerate(parts):
                to = block_buf.at[i, pl.ds(at, x.shape[0])]
                step.append(pltpu.make_async_copy(block_refs[k], to, sems.at[i, 2 + j]))
                at += x.shape[0]
                k += 1
            copies.append(step)
        for j, (_, d, h) in enumerate(left):
            copies.append(bring_rows(d, h, refs[len(extra) + 1].at[j], count + j))
        for step in copies:
            for copy in step:
                copy.start()
        for i, step in enumerate(copies):
            for copy in step:
                copy.wait()
            if i >= count:
                continue
            product = jnp.dot(rows_buf[i], block_buf[i], preferred_element_type=jnp.float32)
            if i > 0:
                o_ref[...] += product
            elif extra:
                o_ref[...] = refs[0][...] + product
            else:
                o_ref[...] = product

    shapes = [jax.ShapeDtypeStruct((CORES * rows, width), jnp.float32)]
    if left:
        shapes.append(jax.ShapeDtypeStruct((len(left), CORES * rows, kc), act.dtype))
    outs = pl.pallas_call(
        kernel,
        in_specs=[IN_SMEM] + [ANYWHERE] * (2 + len(blocks)) + [IN_VMEM] * len(extra),
        out_specs=[IN_VMEM] * len(shapes),
        out_shape=shapes,
        scratch_shapes=[
            pltpu.VMEM((count, CORES * rows, kc), act.dtype),
            pltpu.VMEM((count, kc, width), act.dtype),
            pltpu.SemaphoreType.DMA((count + len(left), 4)),
        ],
        cost_estimate=pl.CostEstimate(
            flops=4 * rows * kc * count * width,
            bytes_accessed=2 * count * kc * (2 * rows + width) + 8 * rows * width,
            transcendentals=0,
        ),
        compiler_params=params(24),
        name="partial_rotation",
    )(place, *[in_hbm(x) for x in (act, sib, *blocks)], *extra)
    return outs if left else outs[0]


def last_rotation(total, rows, found):
    width = total.shape[1]
    blocks = [x for parts, _, _ in found for x in parts]

    def kernel(total_ref, rows_ref, *refs):
        sums, k = total_ref[...], 0
        for i, (parts, _, _) in enumerate(found):
            at = 0
            for part in parts:
                x = rows_ref[i, :, pl.ds(at, part.shape[0])]
                sums += jnp.dot(x, refs[k][...], preferred_element_type=jnp.float32)
                at += part.shape[0]
                k += 1
        refs[-1][...] = sums

    return pl.pallas_call(
        kernel,
        in_specs=[IN_VMEM] * (2 + len(blocks)),
        out_specs=IN_VMEM,
        out_shape=jax.ShapeDtypeStruct(total.shape, jnp.float32),
        cost_estimate=pl.CostEstimate(
            flops=2 * rows.size * width,
            bytes_accessed=2 * rows.size + 8 * total.size,
            transcendentals=0,
        ),
        compiler_params=params(),
        name="last_rotation",
    )(total, rows, *blocks)


def owned_gradients(layout, mine, other, place, positions, lengths, owned):
    nz, ny = layout.nz, layout.ny
    tokens, width = mine.shape
    kept = nz * ny * owned
    seqs = lengths.shape[0]

    def kernel(place_ref, lengths_ref, mine_ref, other_ref, positions_ref, o_ref):
        slot = lax.broadcasted_iota(jnp.int32, (kept, width), 0)
        column = lax.broadcasted_iota(jnp.int32, (kept, width), 1)
        z, y, core = place_ref[0], place_ref[1], place_ref[2]
        to_y = lax.rem(y + 1 + slot // (nz * owned), ny)
        to_z = lax.rem(z + lax.rem(slot // owned, nz), nz)
        wanted = ((to_z * ny + to_y) * CORES + core) * owned + lax.rem(slot, owned)
        pick = jnp.where(wanted == column, 1.0, 0.0).astype(jnp.bfloat16)
        rotated = (mine_ref[...] + other_ref[...]).astype(jnp.bfloat16)
        picked = lax.dot_general(
            pick, rotated, (((1,), (1,)), ((), ())), preferred_element_type=jnp.float32
        )
        position = positions_ref[...]
        begin = jnp.int32(0)
        for s in range(seqs):
            end = begin + lengths_ref[s]
            inside = (position >= begin) & (position < end)
            part = jnp.where(inside, picked, 0.0).astype(jnp.bfloat16)
            o_ref[pl.ds(s * kept, kept), :] = part
            begin = end

    return pl.pallas_call(
        kernel,
        in_specs=[IN_SMEM, IN_SMEM, IN_VMEM, IN_VMEM, IN_VMEM],
        out_specs=IN_VMEM,
        out_shape=jax.ShapeDtypeStruct((seqs * kept, tokens), jnp.bfloat16),
        cost_estimate=pl.CostEstimate(
            flops=2 * kept * width * tokens,
            bytes_accessed=8 * tokens * width + 2 * kept * tokens,
            transcendentals=0,
        ),
        compiler_params=params(),
        name="owned_gradients",
    )(place, lengths, mine, other, positions)


def chip_sums(layout, grads, mine, other, seqs, owned, cut):
    nz, ny = layout.nz, layout.ny
    tokens, width = mine.shape
    stay = nz * owned
    rest = width - cut

    kept = grads.shape[0] // seqs

    def kernel(grads_ref, mine_ref, other_ref, *refs):
        rotated = (mine_ref[...] + other_ref[...]).astype(jnp.bfloat16)
        products = jnp.dot(grads_ref[...], rotated, preferred_element_type=jnp.float32)
        for s in range(seqs):
            sums = products[s * kept:(s + 1) * kept]
            at = pl.ds(s * cut, cut)
            for d in range(nz):
                for h in range(ny):
                    block = sums[h * stay + d * owned:h * stay + (d + 1) * owned, :cut]
                    refs[d][pl.ds(h * owned, owned), at] = block.astype(refs[d].dtype)
            if rest:
                at = pl.ds(s * rest, rest)
                refs[nz][:, at] = sums[stay:, cut:]
                refs[nz + 1][:, at] = sums[:stay, cut:].astype(jnp.bfloat16)

    shapes = [jax.ShapeDtypeStruct((ny * owned, seqs * cut), jnp.float32)]
    shapes += [jax.ShapeDtypeStruct((ny * owned, seqs * cut), jnp.bfloat16)] * (nz - 1)
    if rest:
        shapes.append(jax.ShapeDtypeStruct((stay, seqs * rest), jnp.float32))
        shapes.append(jax.ShapeDtypeStruct((stay, seqs * rest), jnp.bfloat16))
    return pl.pallas_call(
        kernel,
        in_specs=[IN_VMEM] * 3,
        out_specs=[IN_VMEM] * len(shapes),
        out_shape=shapes,
        cost_estimate=pl.CostEstimate(
            flops=2 * grads.size * width,
            bytes_accessed=8 * tokens * width + 2 * grads.shape[0] * width,
            transcendentals=0,
        ),
        compiler_params=params(),
        name="chip_sums",
    )(grads, mine, other)


def add_up(kept, came, owned, own):
    count = kept.shape[0] // owned
    width = kept.shape[1]

    def kernel(*refs):
        total = refs[0][...]
        for i in range(len(came)):
            total += refs[1 + i][...].astype(jnp.float32)
        outs = refs[1 + len(came):]
        for i in range(count):
            outs[i][...] = total[i * owned:(i + 1) * owned].astype(outs[i].dtype)

    shapes = [
        jax.ShapeDtypeStruct((owned, width), jnp.float32 if i == own else jnp.bfloat16)
        for i in range(count)
    ]
    return pl.pallas_call(
        kernel,
        in_specs=[IN_VMEM] * (1 + len(came)),
        out_specs=[IN_VMEM] * count,
        out_shape=shapes,
        cost_estimate=pl.CostEstimate(
            flops=kept.size * len(came), bytes_accessed=8 * kept.size, transcendentals=0
        ),
        compiler_params=params(),
        name="add_up",
    )(kept, *came)


def squares(groups, lengths, owned):
    seqs = lengths.shape[0]
    widths = [group[0].shape[1] // seqs for group in groups]

    def kernel(lengths_ref, *refs):
        o_ref = refs[-1]
        tokens = lengths_ref[0]
        for s in range(1, seqs):
            tokens = tokens + lengths_ref[s]
        at, k = 0, 0
        for group, width in zip(groups, widths):
            over = jnp.full((owned, width), tokens, jnp.int32).astype(jnp.float32)
            sums = refs[k][...]
            for ref in refs[k + 1:k + len(group)]:
                sums = sums + ref[...].astype(jnp.float32)
            k += len(group)
            sums = sums * sums
            acc = sums[:, :width]
            for s in range(1, seqs):
                acc = acc + sums[:, s * width:(s + 1) * width]
            o_ref[:, pl.ds(at, width)] = acc / over
            at += width

    flat = [x for group in groups for x in group]
    return pl.pallas_call(
        kernel,
        in_specs=[IN_SMEM] + [IN_VMEM] * len(flat),
        out_specs=IN_VMEM,
        out_shape=jax.ShapeDtypeStruct((owned, sum(widths)), jnp.float32),
        cost_estimate=pl.CostEstimate(
            flops=2 * sum(x.size for x in flat),
            bytes_accessed=2 * sum(x.size for x in flat),
            transcendentals=0,
        ),
        compiler_params=params(),
        name="squares",
    )(lengths, *flat)


def scatter_sums(layout, sums, owned):
    nz, ny = layout.nz, layout.ny
    if ny == 1:
        return [[sums[0]] + [layout.along_z(sums[d], d) for d in range(1, nz)]]
    crossed = [layout.along_y(sums[nz + 1])]
    came = [layout.along_z(sums[d], d) for d in range(1, nz)]
    by_z = add_up(sums[nz], crossed, owned, 0)
    second = [by_z[0]] + [layout.along_z(by_z[d], d) for d in range(1, nz)]
    by_y = add_up(sums[0], came, owned, 1)
    return [[by_y[1], layout.along_y(by_y[0])], second]


def shards(layout, activations, gradients, basis_a, basis_g, token_index, seq_lengths):
    nz, ny, chips = layout.nz, layout.ny, layout.chips
    rows = activations.shape[0]
    owned = basis_g.shape[1] // (chips * CORES)
    me = lax.axis_index("row")
    core = lax.rem(me, CORES)
    y = lax.rem(me // CORES, ny)
    z = me // (CORES * ny)
    place = jnp.stack([z, y, core]).astype(jnp.int32)

    sib_index = layout.to_sibling(token_index)
    first = core == 0
    positions = jnp.concatenate(
        [jnp.where(first, token_index, sib_index), jnp.where(first, sib_index, token_index)]
    ).reshape(1, CORES * rows)

    links = Links(layout, 2)
    sib_g = layout.to_sibling(gradients)
    sib_a = layout.to_sibling(activations)
    split = [basis_g.shape[0] * 4 // 7, basis_a.shape[0] // 2] if ny > 1 else [0, 0]
    early = []

    def rotate_early(found):
        early.append(partial_rotation(layout, gradients, sib_g, found[:4], place))
        return early[0]

    begun = {}

    def begin_a():
        for h in range(1, ny):
            begun[h] = links.send("y", basis_a, h)
        return list(begun.values())

    gates = {
        ("y", 1): begin_a,
        nz - 1: [sib_a],
        nz // 2: lambda by_z: [sib_g, sib_a, *begun.values()],
        -1: rotate_early,
    }
    found_g = gather_columns(links, basis_g, split[0], gates)
    if not early:
        rotate_early(found_g)
    mine_g = partial_rotation(layout, gradients, sib_g, found_g[4:], place, early[0])
    links.after(early[0])
    found_a = gather_columns(links, basis_a, split[1], {("y", nz - 1): [mine_g]}, begun)
    grads = owned_gradients(
        layout, mine_g, layout.to_sibling(mine_g), place, positions, seq_lengths, owned
    )

    most, rows_left = partial_rotation(
        layout, activations, sib_a, found_a[:-2], place, None, found_a[-2:]
    )
    most, positions = lax.optimization_barrier((most, positions))
    mine_a = last_rotation(most, rows_left, found_a[-2:])
    cut = basis_a.shape[1] // ny**2
    sums = chip_sums(
        layout, grads, mine_a, layout.to_sibling(mine_a), seq_lengths.shape[0], owned, cut
    )
    return squares(scatter_sums(layout, sums, owned), seq_lengths, owned)


def solution(mesh):
    return jax.shard_map(
        functools.partial(shards, Layout(mesh)),
        mesh=mesh,
        in_specs=(
            P(("grp", "row"), None),
            P(("grp", "row"), None),
            P(("grp", "row"), None),
            P(("grp", "row"), None),
            P(("grp", "row")),
            P("grp"),
        ),
        out_specs=P(("grp", "row"), None),
        check_vma=False,
    )
```
